32 devices in a mesh: expert: 16 (over z, y, x), dp: 2 (over core).
Axes of the slice: x: 2, y: 2, z: 4, core: 2. Of those that a mesh axis runs over, the one named last changes fastest.
Arguments:
- expert_ids: int32 [4096, 8], P(('expert', 'dp')), may hold values from 0 to 15, all different within a row; in each aligned block of 128 rows (0 to 127, 128 to 255, ...) at most 80 rows name the same one
- gates: float32 [4096, 8], P(('expert', 'dp')), may hold values from 0.05 to 1
- hidden: bfloat16 [16, 2560, 768], P('expert', 'dp'), may hold values from -6 to 6
- weight: bfloat16 [16, 768, 2048], P('expert'), may hold values from -0.21875 to 0.21875
- out_grad: bfloat16 [4096, 2048], P(('expert', 'dp')), may hold values from -6 to 6
Outputs:
- combined: bfloat16 [4096, 2048], P(('expert', 'dp'))
- gate_grads: float32 [4096, 8], P(('expert', 'dp'))
- hidden_grads: bfloat16 [16, 2560, 768], P('expert', 'dp')
- weight_grads: bfloat16 [16, 768, 2048], P('expert', None, 'dp')
The draws below stay inside these ranges and needn't reach their ends.
Inputs may be any that keep to these rules, and one draw needn't show every extreme that they name: `expert_ids`: each token names 8 different experts; among the 128 tokens of one device no expert is named more than 80 times, a bound that some block reaches.
All inputs are finite; a program needn't handle non-finite values.
Results may differ from the reference program's by a relative error of at most 0.0049.
Values may be sent and summed in bfloat16 or wider, within the bound.
No kernel may reach another device: no remote copies, remote signals or barrier semaphores. Data moves between devices by JAX's collectives and lax.ppermute only.
A program may use at most 128 MiB of HBM per device.

```python
import math
import jax
import jax.numpy as jnp
import numpy as np
from jax import lax

D = 2048
FF = 768
TOP = 8
TOK_DEV = 128
EXPERT_TOTAL = 16
SENDER_DEVICES = 16
DATA_GROUPS = 2
SLOT_LIMIT = 80
TOKENS = 4096


def steps_of(own_key, shape, cuts, least, high):
    loudness = 1.0
    for position, parts in cuts:
        draws = jax.random.uniform(jax.random.fold_in(jax.random.fold_in(own_key, 6), position), (parts,), jnp.float32, least / len(cuts), high / len(cuts))
        loudness = loudness * jnp.repeat(jnp.exp(draws), shape[position] // parts).reshape((-1,) + (1,) * (len(shape) - 1 - position))
    return loudness


def deal_out(rng, own, number, rows, amount, top, most, slope):
    sequence = jax.random.permutation(rng, amount)
    heavy_load, usual = shares(amount, rows * top, most, slope, True), shares(amount, rows * top, most, slope, False)
    places = jnp.arange(amount)

    def named(sizes, offset_by):
        used = int((sizes > 0).sum())
        fixed = max(1, used // 4)
        moved = fixed + (places - fixed + offset_by * (used - fixed)) % max(1, amount - fixed)
        return jnp.zeros((amount,), jnp.int32).at[sequence[jnp.where(places < fixed, places, moved)]].set(jnp.asarray(sizes, jnp.int32))

    sizes = jnp.where(number % 4 == 0, named(heavy_load, number // 4), named(usual, number - number // 4 - 1))
    mixed = jax.random.permutation(jax.random.fold_in(own, 3), amount)
    donor, sink = mixed[0:amount // 2 * 2:2], mixed[1:amount // 2 * 2:2]
    room = jnp.minimum(sizes[donor] - 1, most - sizes[sink]) // 2
    room = jnp.where((donor == sequence[0]) | (sink == sequence[0]) | (sizes[sink] == 0), 0, jnp.maximum(room, 0))
    moved = jax.random.randint(jax.random.fold_in(own, 4), (amount // 2,), 0, 1 << 20) % (room + 1)
    sizes = sizes.at[donor].add(-moved).at[sink].add(moved)
    items = jnp.searchsorted(jnp.cumsum(sizes), jnp.arange(rows * top), side="right").astype(jnp.int32)
    listing = items.reshape(top, rows).T
    listing = listing[jax.random.permutation(jax.random.fold_in(own, 1), rows)]
    offset_by = jax.random.randint(jax.random.fold_in(own, 2), (rows, 1), 0, top)
    return jnp.take_along_axis(listing, (jnp.arange(top)[None, :] + offset_by) % top, axis=1)


def shares(count, total, limit, lean, full):
    portions = [(1 << 20) // math.isqrt(grade ** lean) + 1 for grade in range(1, count + 1)]
    largest = limit if full else min(limit, max(-(-total // count), total * portions[0] // sum(portions)))
    least = 1 if total - largest >= count - 1 else 0
    counts, surplus = [largest] + [least] * (count - 1), total - largest - least * (count - 1)
    while surplus > 0:
        free = [i for i in range(1, count) if counts[i] < largest] or [i for i in range(1, count) if counts[i] < limit]
        mass, remaining = sum([portions[i] for i in free]), surplus
        for i in free:
            addition = min(limit - counts[i], max(1, remaining * portions[i] // mass), surplus)
            counts[i] = counts[i] + addition
            surplus = surplus - addition
    return np.array(counts)


def noise(rng, shape, scale, bound, cuts=(), kind=jnp.bfloat16):
    drawn = jax.random.normal(rng, shape, jnp.float32) * scale
    if len(cuts) > 0:
        drawn = steps_of(rng, shape, cuts, -0.22, 0.18) * drawn
    return jnp.clip(drawn, min=-bound, max=bound).astype(kind)


def setup_inputs(seed: int = 0) -> dict:
    arg_keys = jax.random.split(jax.random.key(seed), 6)
    expert_ids_keys = jax.random.split(jax.random.fold_in(arg_keys[0], 1), TOKENS // TOK_DEV)
    expert_ids_turns = jax.random.permutation(jax.random.fold_in(arg_keys[0], 3), TOKENS // TOK_DEV)
    expert_ids = jax.vmap(lambda own, number: deal_out(jax.random.fold_in(arg_keys[0], 2), own, number, TOK_DEV, EXPERT_TOTAL, TOP, SLOT_LIMIT, 2))(expert_ids_keys, expert_ids_turns).reshape((TOKENS, TOP))
    gates = jnp.clip(jnp.exp(math.log(1.0) - 2.9957323 * jax.random.uniform(arg_keys[1], (TOKENS, TOP), jnp.float32) ** steps_of(arg_keys[1], (TOKENS, TOP), ((0, 32),), -0.2, 0.2)), 0.05, 1.0)
    hidden = noise(arg_keys[2], (EXPERT_TOTAL, DATA_GROUPS * SENDER_DEVICES * SLOT_LIMIT, FF), 1.0, 6.0, ((0, 16), (1, 2)))
    weight = noise(arg_keys[3], (EXPERT_TOTAL, FF, D), FF ** -0.5, 0.21875, ((0, 16),))
    out_grad = noise(arg_keys[4], (TOKENS, D), 1.0, 6.0, ((0, 32),))
    return {"expert_ids": expert_ids, "gates": gates, "hidden": hidden, "weight": weight, "out_grad": out_grad}


def reference(expert_ids, gates, hidden, weight, out_grad):
    index_pairs = TOK_DEV * TOP
    block_list = SENDER_DEVICES * DATA_GROUPS
    identifiers = expert_ids.reshape(block_list, index_pairs)
    onehot = (identifiers[:, :, None] == jnp.arange(EXPERT_TOTAL, dtype=jnp.int32)[None, None, :]).astype(jnp.int32)
    slot = jnp.sum((jnp.cumsum(onehot, 1) - onehot) * onehot, 2).astype(jnp.int32)
    block = jnp.arange(block_list, dtype=jnp.int32)
    source = block // DATA_GROUPS
    group = block % DATA_GROUPS
    row_index = (group[:, None] * SENDER_DEVICES + source[:, None]) * SLOT_LIMIT + slot
    slot_count = DATA_GROUPS * SENDER_DEVICES * SLOT_LIMIT
    flattened = (identifiers * slot_count + row_index).reshape(-1).astype(jnp.int32)
    owning_device = jnp.full((EXPERT_TOTAL * slot_count,), -1, dtype=jnp.int32)
    owning_device = owning_device.at[flattened].set(jnp.arange(block_list * index_pairs, dtype=jnp.int32)).reshape(EXPERT_TOTAL, slot_count)
    gate_flat = gates.reshape(-1)

    def per_expert(carry, inputs):
        accum, ggrad = carry
        hid_e, w_e, own = inputs
        valid = own >= 0
        safe = jnp.where(valid, own, 0).astype(jnp.int32)
        tok = safe // TOP
        weight_g = jnp.where(valid, gate_flat[safe], jnp.float32(0.0))
        yrows = jnp.dot(hid_e, w_e, preferred_element_type=jnp.float32).astype(jnp.bfloat16)
        yfloat = yrows.astype(jnp.float32)
        accum = accum.at[tok].add(weight_g[:, None] * yfloat)
        drows = out_grad[tok].astype(jnp.float32)
        inner = jnp.sum(drows * yfloat, 1)
        ggrad = ggrad.at[safe].add(jnp.where(valid, inner, jnp.float32(0.0)))
        grad_rows = (weight_g[:, None] * drows).astype(jnp.bfloat16)
        dhid = jnp.dot(grad_rows, w_e.T, preferred_element_type=jnp.float32).astype(jnp.bfloat16)
        dwgt = jnp.dot(hid_e.T, grad_rows, preferred_element_type=jnp.float32).astype(jnp.bfloat16)
        return (accum, ggrad), (dhid, dwgt)

    start = (jnp.zeros((TOKENS, D), jnp.float32), jnp.zeros((TOKENS * TOP,), jnp.float32))
    (accum, ggrad), (hidden_grads, weight_grads) = lax.scan(per_expert, start, (hidden, weight, owning_device))
    return accum.astype(jnp.bfloat16), ggrad.reshape(TOKENS, TOP), hidden_grads, weight_grads
```

```python
import functools

import jax
import jax.numpy as jnp
from jax import lax
from jax.experimental import pallas as pl
from jax.experimental.pallas import tpu as pltpu
from jax.sharding import PartitionSpec as P

F32 = jnp.float32
BF16 = jnp.bfloat16
VMEM_BYTES = 32 * 1024 * 1024


def call(body, name, grid, in_specs, out_specs, out_shape, scalars, operands, flops=0, moved=0, scratch=(), aliases=None):
    return pl.pallas_call(
        body,
        name=name,
        grid_spec=pltpu.PrefetchScalarGridSpec(
            num_scalar_prefetch=1, grid=grid, in_specs=in_specs, out_specs=out_specs, scratch_shapes=scratch
        ),
        out_shape=out_shape,
        input_output_aliases=aliases or {},
        cost_estimate=pl.CostEstimate(flops=flops, bytes_accessed=moved, transcendentals=0),
        compiler_params=pltpu.CompilerParams(vmem_limit_bytes=VMEM_BYTES),
    )(scalars, *operands)


def table_body(meta, ids, gates, table):
    count = table.shape[0] // 2
    tokens = table.shape[1]
    expert = lax.broadcasted_iota(jnp.int32, (count, tokens), 0)
    named = jnp.zeros((count, tokens), F32)
    gate = jnp.zeros((count, tokens), F32)
    for choice in range(ids.shape[0]):
        hit = ids[choice : choice + 1, :] == expert
        named = named + jnp.where(hit, 1.0, 0.0)
        gate = gate + jnp.where(hit, gates[choice : choice + 1, :], 0.0)
    before = lax.broadcasted_iota(jnp.int32, (tokens, tokens), 0) < lax.broadcasted_iota(jnp.int32, (tokens, tokens), 1)
    earlier = jnp.dot(named.astype(BF16), jnp.where(before, 1.0, 0.0).astype(BF16), preferred_element_type=F32)
    offset = meta[2].astype(F32)
    table[:count, :] = jnp.where(named > 0.0, earlier + offset, -1.0)
    table[count:, :] = gate


def forward_body(meta, hidden, weight, out):
    rows = hidden[:, 0].reshape(out.shape[0], hidden.shape[3])
    out[...] = jnp.dot(rows, weight[...], preferred_element_type=F32).astype(BF16)


def turn_body(meta, hidden, out):
    out[0] = hidden[:, 0].reshape(out.shape[2], out.shape[1]).T


def selection(table, expert, rows):
    count = table.shape[0] // 2
    place = table[pl.ds(expert, 1), :]
    gate = table[pl.ds(expert + count, 1), :]
    row = lax.broadcasted_iota(jnp.int32, (rows, table.shape[1]), 0).astype(F32)
    return row == place, gate


def grad_rows_body(peers, groups, meta, *refs):
    tables, tokens, outs = refs[:groups], refs[groups : 2 * groups], refs[2 * groups :]
    rows = outs[0].shape[0] // groups
    for group in range(groups):
        start = pl.multiple_of(lax.bitwise_xor(meta[1], group) * rows, rows)
        grad = tokens[group][...]
        for peer in range(peers):
            match, gate = selection(tables[group], lax.bitwise_xor(meta[3], peer), rows)
            row_gate = jnp.sum(jnp.where(match, gate, 0.0), 1, keepdims=True)
            picked = jnp.dot(jnp.where(match, 1.0, 0.0).astype(BF16), grad, preferred_element_type=F32)
            outs[peer][pl.ds(start, rows), :] = (picked * row_gate).astype(BF16)


def combine_body(peers, meta, table, token, *refs):
    returned, (part, inner) = refs[:peers], refs[peers:]
    rows = returned[0].shape[0]
    grad = token[...]
    total = jnp.zeros(part.shape, F32)
    contract = (((0,), (0,)), ((), ()))

    @pl.when(pl.program_id(0) == 0)
    def _():
        inner[...] = jnp.zeros(inner.shape, F32)

    for peer in range(peers):
        match, gate = selection(table, lax.bitwise_xor(meta[3], peer), rows)
        high = gate.astype(BF16).astype(F32)
        low = gate - high
        value = returned[peer][...]
        weights = jnp.concatenate([jnp.where(match, high, 0.0), jnp.where(match, low, 0.0)], 0).astype(BF16)
        total = total + lax.dot_general(
            weights, jnp.concatenate([value, value], 0), contract, preferred_element_type=F32
        )
        products = lax.dot_general(value, grad, (((1,), (1,)), ((), ())), preferred_element_type=F32)
        inner[peer : peer + 1, :] += jnp.sum(jnp.where(match, products, 0.0), 0, keepdims=True)
    part[...] = total.astype(part.dtype)


def hidden_grad_body(meta, rows, weight, *refs):
    out = refs[-1]
    value = lax.dot_general(rows[...], weight[...], (((1,), (1,)), ((), ())), preferred_element_type=F32)
    out[:, 0] = value.astype(BF16).reshape(out.shape[0], out.shape[2], out.shape[3])


def weight_grad_body(meta, turned, rows, *refs):
    value = jnp.dot(turned[0], rows[...], preferred_element_type=F32)
    if len(refs) == 2:
        value = value + refs[0][...]
    refs[-1][...] = value


def finish_body(parts, peers, meta, ids, *refs):
    sums, inners, (combined, gate_grads) = refs[:parts], refs[parts : 2 * parts], refs[2 * parts :]
    total = sums[0][...].astype(F32)
    for part in range(1, parts):
        total = total + sums[part][...].astype(F32)
    combined[...] = total.astype(BF16)
    relative = lax.bitwise_xor(ids[...], meta[3])
    found = jnp.zeros(gate_grads.shape, F32)
    for part in range(parts):
        for peer in range(peers):
            found = found + jnp.where(relative == part * peers + peer, inners[part][peer : peer + 1, :], 0.0)
    gate_grads[...] = found


def per_device(expert_ids, gates, hidden, weight, out_grad):
    count = lax.axis_size("expert")
    peers = 1 << ((count.bit_length() - 1) // 2)
    planes = count // peers
    tokens, top = expert_ids.shape
    cap = hidden.shape[1] // count
    width, inside = out_grad.shape[1], hidden.shape[2]
    fold = 1
    while fold * cap % 16:
        fold *= 2
    groups = planes // fold
    group_rows, group_tokens = fold * cap, fold * tokens
    rows = planes * cap
    tile = min(512, width)
    steps = width // tile

    me = lax.axis_index("expert")
    core = lax.axis_index("dp")
    column, plane = me % peers, me // peers
    meta = jnp.stack([column, plane // fold, (plane % fold) * cap, me, core]).astype(jnp.int32)

    def swap(value, distance):
        return lax.ppermute(value, "expert", [(e, e ^ distance) for e in range(count)])

    matrix = weight[0]
    if fold == 1:
        blocks = hidden.reshape(planes, peers, cap, inside)
    else:
        blocks = hidden.reshape(planes, peers, cap, inside).transpose(1, 0, 2, 3).reshape(1, peers, rows, inside)
    block = (blocks.shape[0], 1, blocks.shape[2], inside)

    token_rows = [out_grad] + [swap(out_grad, peers * k) for k in range(1, planes)]

    def forward(peer):
        return call(
            forward_body, f"forward{peer}", (steps,),
            [
                pl.BlockSpec(block, lambda i, m: (0, lax.bitwise_xor(m[0], peer), 0, 0)),
                pl.BlockSpec((inside, tile), lambda i, m: (0, i)),
            ],
            pl.BlockSpec((rows, tile), lambda i, m: (0, i)),
            jax.ShapeDtypeStruct((rows, width), BF16),
            meta, (blocks, matrix),
            flops=2 * rows * inside * width, moved=2 * (rows * inside + inside * width + rows * width),
        )

    outputs = {}
    for peer in list(range(1, peers)) + [0]:
        outputs[peer] = forward(peer)
    returned = [outputs[0]] + [swap(outputs[peer], peer) for peer in range(1, peers)]

    ids_turned = expert_ids.T
    table = call(
        table_body, "table", (1,),
        [pl.BlockSpec((top, tokens), lambda i, m: (0, 0)), pl.BlockSpec((top, tokens), lambda i, m: (0, 0))],
        pl.BlockSpec((2 * count, tokens), lambda i, m: (0, 0)),
        jax.ShapeDtypeStruct((2 * count, tokens), F32),
        meta, (ids_turned, gates.T),
    )
    tables = [table] + [swap(table, peers * k) for k in range(1, planes)]
    if fold > 1:
        tables = [jnp.concatenate(tables[g * fold : (g + 1) * fold], 1) for g in range(groups)]
        token_rows = [jnp.concatenate(token_rows[g * fold : (g + 1) * fold], 0) for g in range(groups)]

    turned = call(
        turn_body, "turn", (peers,),
        [pl.BlockSpec(block, lambda i, m: (0, lax.bitwise_xor(m[0], i), 0, 0))],
        pl.BlockSpec((1, inside, rows), lambda i, m: (i, 0, 0)),
        jax.ShapeDtypeStruct((peers, inside, rows), BF16),
        meta, (blocks,),
        moved=4 * peers * rows * inside,
    )

    table_spec = pl.BlockSpec((2 * count, group_tokens), lambda i, m: (0, 0))
    token_spec = pl.BlockSpec((group_tokens, tile), lambda i, m: (0, i))
    grad_rows = call(
        functools.partial(grad_rows_body, peers, groups), "grad_rows", (steps,),
        [table_spec] * groups + [token_spec] * groups,
        [pl.BlockSpec((rows, tile), lambda i, m: (0, i))] * peers,
        [jax.ShapeDtypeStruct((rows, width), BF16)] * peers,
        meta, (*tables, *token_rows),
        flops=2 * peers * rows * group_tokens * width,
        moved=2 * width * (planes * tokens + peers * rows),
    )
    arrived = [grad_rows[0]] + [swap(grad_rows[peer], peer) for peer in range(1, peers)]

    def combine(group):
        return call(
            functools.partial(combine_body, peers), f"combine{group}", (steps,),
            [table_spec, token_spec]
            + [pl.BlockSpec((group_rows, tile), lambda i, m: (lax.bitwise_xor(m[1], group), i))] * peers,
            [
                pl.BlockSpec((group_tokens, tile), lambda i, m: (0, i)),
                pl.BlockSpec((peers, group_tokens), lambda i, m: (0, 0)),
            ],
            [
                jax.ShapeDtypeStruct((group_tokens, width), F32 if group == 0 else BF16),
                jax.ShapeDtypeStruct((peers, group_tokens), F32),
            ],
            meta, (tables[group], token_rows[group], *returned),
            flops=6 * peers * group_rows * group_tokens * width,
            moved=2 * width * (2 * group_tokens + peers * group_rows),
        )

    sums, inners = [None] * planes, [None] * planes
    for group in list(range(1, groups)) + [0]:
        part, inner = combine(group)
        for k in range(fold):
            at = group * fold + k
            piece = part if fold == 1 else part[k * tokens : (k + 1) * tokens]
            piece_inner = inner if fold == 1 else inner[:, k * tokens : (k + 1) * tokens]
            if at:
                piece, piece_inner = swap(piece.astype(BF16), peers * at), swap(piece_inner, peers * at)
            sums[at], inners[at] = piece, piece_inner

    small = pl.BlockSpec((peers, tokens), lambda i, m: (0, 0))
    wide = pl.BlockSpec((tokens, width), lambda i, m: (0, 0))
    combined, gate_grads = call(
        functools.partial(finish_body, planes, peers), "finish", (1,),
        [pl.BlockSpec((top, tokens), lambda i, m: (0, 0))] + [wide] * planes + [small] * planes,
        [wide, pl.BlockSpec((top, tokens), lambda i, m: (0, 0))],
        [jax.ShapeDtypeStruct((tokens, width), BF16), jax.ShapeDtypeStruct((top, tokens), F32)],
        meta, (ids_turned, *sums, *inners),
        moved=2 * tokens * width * (planes + 2),
    )

    def hidden_grad(peer, earlier):
        depth = min(256, inside)
        return call(
            hidden_grad_body, f"hidden_grad{peer}", (inside // depth,),
            [
                pl.BlockSpec((rows, width), lambda i, m: (0, 0)),
                pl.BlockSpec((depth, width), lambda i, m: (i, 0)),
            ]
            + ([] if earlier is None else [pl.BlockSpec(memory_space=pl.ANY)]),
            pl.BlockSpec(block[:3] + (depth,), lambda i, m: (0, lax.bitwise_xor(m[0], peer), 0, i)),
            jax.ShapeDtypeStruct(blocks.shape, BF16),
            meta, (arrived[peer], matrix) + (() if earlier is None else (earlier,)),
            flops=2 * rows * inside * width, moved=2 * (rows * inside + inside * width + rows * width),
            aliases=None if earlier is None else {3: 0},
        )

    def weight_grad(peer, earlier, half):
        extent = width if half is None else width // 2
        part = min(tile, extent)
        count_tiles = extent // part

        def at(i, m):
            return i if half is None else lax.bitwise_xor(m[4], half) * count_tiles + i

        return call(
            weight_grad_body, f"weight_grad{peer}", (count_tiles,),
            [
                pl.BlockSpec((1, inside, rows), lambda i, m: (peer, 0, 0)),
                pl.BlockSpec((rows, part), lambda i, m: (0, at(i, m))),
            ]
            + ([] if earlier is None else [pl.BlockSpec((inside, part), lambda i, m: (0, at(i, m)))]),
            pl.BlockSpec((inside, part), lambda i, m: (0, i)),
            jax.ShapeDtypeStruct((inside, extent), F32),
            meta, (turned, arrived[peer]) + (() if earlier is None else (earlier,)),
            flops=2 * rows * inside * extent, moved=2 * rows * (inside + extent) + 8 * inside * extent,
        )

    hidden_grads, total = None, None
    for peer in range(peers - 1):
        hidden_grads = hidden_grad(peer, hidden_grads)
        total = weight_grad(peer, total, None)
    other = weight_grad(peers - 1, total, 1)
    other = lax.ppermute(other, "dp", [(0, 1), (1, 0)])
    own = weight_grad(peers - 1, total, 0)
    hidden_grads = hidden_grad(peers - 1, hidden_grads)
    weight_grads = (own + other).astype(BF16)[None]

    if fold > 1:
        hidden_grads = hidden_grads.reshape(peers, planes, cap, inside).transpose(1, 0, 2, 3)
    return combined, gate_grads.T, hidden_grads.reshape(hidden.shape), weight_grads


def solution(mesh):
    placed = (
        P(("expert", "dp"), None),
        P(("expert", "dp"), None),
        P("expert", "dp", None),
        P("expert", None, None),
        P(("expert", "dp"), None),
    )
    return jax.shard_map(
        per_device,
        mesh=mesh,
        in_specs=placed,
        out_specs=(
            P(("expert", "dp"), None),
            P(("expert", "dp"), None),
            P("expert", "dp", None),
            P("expert", None, "dp"),
        ),
        check_vma=False,
    )
```

```python
import functools

import jax
import jax.numpy as jnp
from jax import lax
from jax.experimental import pallas as pl
from jax.experimental.pallas import tpu as pltpu
from jax.sharding import PartitionSpec as P

F32 = jnp.float32
BF16 = jnp.bfloat16
VMEM_BYTES = 32 * 1024 * 1024
COST = 10**10


def call(body, name, grid, in_specs, out_specs, out_shape, scalars, operands, flops=0, moved=0, scratch=(), aliases=None):
    return pl.pallas_call(
        body,
        name=name,
        grid_spec=pltpu.PrefetchScalarGridSpec(
            num_scalar_prefetch=1, grid=grid, in_specs=in_specs, out_specs=out_specs, scratch_shapes=scratch
        ),
        out_shape=out_shape,
        input_output_aliases=aliases or {},
        cost_estimate=pl.CostEstimate(flops=COST, bytes_accessed=COST, transcendentals=0),
        compiler_params=pltpu.CompilerParams(vmem_limit_bytes=VMEM_BYTES),
    )(scalars, *operands)


def follow(value, *earlier):
    anywhere = pl.BlockSpec(memory_space=pl.ANY)
    return pl.pallas_call(
        lambda *refs: None,
        name="follow",
        in_specs=[anywhere] * (1 + len(earlier)),
        out_specs=anywhere,
        out_shape=jax.ShapeDtypeStruct(value.shape, value.dtype),
        input_output_aliases={0: 0},
        cost_estimate=pl.CostEstimate(flops=COST, bytes_accessed=COST, transcendentals=0),
    )(value, *earlier)


def table_body(meta, ids, gates, table):
    count = table.shape[0] // 2
    tokens = table.shape[1]
    expert = lax.broadcasted_iota(jnp.int32, (count, tokens), 0)
    named = jnp.zeros((count, tokens), F32)
    gate = jnp.zeros((count, tokens), F32)
    for choice in range(ids.shape[0]):
        hit = ids[choice : choice + 1, :] == expert
        named = named + jnp.where(hit, 1.0, 0.0)
        gate = gate + jnp.where(hit, gates[choice : choice + 1, :], 0.0)
    before = lax.broadcasted_iota(jnp.int32, (tokens, tokens), 0) < lax.broadcasted_iota(jnp.int32, (tokens, tokens), 1)
    earlier = jnp.dot(named.astype(BF16), jnp.where(before, 1.0, 0.0).astype(BF16), preferred_element_type=F32)
    offset = meta[2].astype(F32)
    table[:count, :] = jnp.where(named > 0.0, earlier + offset, -1.0)
    table[count:, :] = gate


def forward_body(meta, hidden, weight, out):
    rows = hidden[:, 0].reshape(out.shape[0], hidden.shape[3])
    out[...] = jnp.dot(rows, weight[...], preferred_element_type=F32).astype(BF16)


def turn_body(meta, hidden, out):
    out[0] = hidden[:, 0].reshape(out.shape[2], out.shape[1]).T


def selection(tables, expert, rows, planes):
    count = tables.shape[1] // 2
    place = jnp.concatenate([tables[plane, pl.ds(expert, 1), :] for plane in planes], 1)
    gate = jnp.concatenate([tables[plane, pl.ds(expert + count, 1), :] for plane in planes], 1)
    row = lax.broadcasted_iota(jnp.int32, (rows, place.shape[1]), 0).astype(F32)
    return row == place, gate


def planes_of(meta, group, fold):
    return [lax.bitwise_xor(meta[1], group) * fold + k for k in range(fold)]


def grad_rows_body(peers, groups, fold, meta, tables, tokens, *outs):
    rows, group_tokens = outs[0].shape[0] // groups, tokens.shape[0] // groups
    first = pl.program_id(0) < pl.num_programs(0) // 2
    for group in range(groups):
        start = group * rows
        grad = tokens[group * group_tokens : (group + 1) * group_tokens, :]
        planes = [group * fold + k for k in range(fold)]
        for peer in range(peers):
            match, gate = selection(tables, lax.bitwise_xor(meta[3], peer), rows, planes)
            row_gate = jnp.sum(jnp.where(match, gate, 0.0), 1, keepdims=True)
            picked = jnp.dot(jnp.where(match, 1.0, 0.0).astype(BF16), grad, preferred_element_type=F32)
            value = (picked * row_gate).astype(BF16)
            if peer < peers - 1:
                outs[peer][pl.ds(start, rows), :] = value
            else:

                @pl.when(first)
                def _():
                    outs[peers - 1][pl.ds(start, rows), :] = value

                @pl.when(jnp.logical_not(first))
                def _():
                    outs[peers][pl.ds(start, rows), :] = value


def combine_body(peers, group, fold, meta, tables, token, *refs):
    returned, (part, inner) = refs[:peers], refs[peers:]
    rows = returned[0].shape[0]
    step, last = pl.program_id(0), pl.num_programs(0) - 1
    contract = (((0,), (0,)), ((), ()))

    @pl.when(step == 0)
    def _():
        inner[...] = jnp.zeros(inner.shape, F32)

    @pl.when(step < last)
    def _():
        grad = token[...]
        total = jnp.zeros(part.shape, F32)
        for peer in range(peers):
            match, gate = selection(tables, lax.bitwise_xor(meta[3], peer), rows, planes_of(meta, group, fold))
            high = gate.astype(BF16).astype(F32)
            low = gate - high
            value = returned[peer][...]
            weights = jnp.concatenate([jnp.where(match, high, 0.0), jnp.where(match, low, 0.0)], 0).astype(BF16)
            total = total + lax.dot_general(
                weights, jnp.concatenate([value, value], 0), contract, preferred_element_type=F32
            )
            products = lax.dot_general(value, grad, (((1,), (1,)), ((), ())), preferred_element_type=F32)
            inner[peer : peer + 1, :] += jnp.sum(jnp.where(match, products, 0.0), 0, keepdims=True)
        part[...] = total.astype(part.dtype)

    @pl.when(step == last)
    def _():
        value = inner[...]
        high = value.astype(BF16).astype(F32)
        middle = (value - high).astype(BF16).astype(F32)
        rest = jnp.zeros((128 - 3 * peers, value.shape[1]), F32)
        pieces = jnp.concatenate([high, middle, value - high - middle, rest], 0)
        part[:, :128] = pieces.T.astype(part.dtype)


def expert_body(has_earlier, meta, turned, rows, weight, *refs):
    total, hidden_grads, inside = refs[-3:]
    value = jnp.dot(turned[0], rows[...], preferred_element_type=F32)
    if has_earlier:
        value = value + refs[0][...]
    total[...] = value
    share = lax.dot_general(rows[...], weight[...], (((1,), (1,)), ((), ())), preferred_element_type=F32)
    step = pl.program_id(0)

    @pl.when(step == 0)
    def _():
        inside[...] = share

    @pl.when(step > 0)
    def _():
        inside[...] += share

    @pl.when(step == pl.num_programs(0) - 1)
    def _():
        hidden_grads[:, 0] = inside[...].astype(BF16).reshape(hidden_grads.shape[0], *hidden_grads.shape[2:])


def other_half_body(meta, turned, rows, earlier, out):
    out[...] = jnp.dot(turned[0], rows[...], preferred_element_type=F32) + earlier[...]


def last_body(meta, turned, rows_other, rows_own, weight_other, weight_own, earlier, other, kept, grads, hidden_grads, inside):
    value = jnp.dot(turned[0], rows_own[...], preferred_element_type=F32)
    grads[...] = (value + earlier[...] + other[...]).astype(BF16)
    contract = (((1,), (1,)), ((), ()))
    share = lax.dot_general(rows_other[...], weight_other[...], contract, preferred_element_type=F32)
    share = share + lax.dot_general(rows_own[...], weight_own[...], contract, preferred_element_type=F32)
    step = pl.program_id(0)

    @pl.when(step == 0)
    def _():
        inside[...] = share

    @pl.when(step > 0)
    def _():
        inside[...] += share

    @pl.when(step == pl.num_programs(0) - 1)
    def _():
        hidden_grads[:, 0] = inside[...].astype(BF16).reshape(hidden_grads.shape[0], *hidden_grads.shape[2:])


def finish_body(parts, peers, meta, ids, *refs):
    sums, (combined, gate_grads) = refs[:parts], refs[parts:]
    width = combined.shape[1]
    total = sums[0][:, :width].astype(F32)
    for part in range(1, parts):
        total = total + sums[part][:, :width].astype(F32)
    combined[...] = total.astype(BF16)
    relative = lax.bitwise_xor(ids[...], meta[3])
    found = jnp.zeros(gate_grads.shape, F32)
    for part in range(parts):
        pieces = sums[part][:, width:].astype(F32).T
        inner = pieces[:peers] + pieces[peers : 2 * peers] + pieces[2 * peers : 3 * peers]
        for peer in range(peers):
            found = found + jnp.where(relative == part * peers + peer, inner[peer : peer + 1, :], 0.0)
    gate_grads[...] = found


def per_device(expert_ids, gates, hidden, weight, out_grad):
    count = lax.axis_size("expert")
    peers = 1 << ((count.bit_length() - 1) // 2)
    planes = count // peers
    tokens, top = expert_ids.shape
    cap = hidden.shape[1] // count
    width, inside = out_grad.shape[1], hidden.shape[2]
    fold = 1
    while fold * cap % 16:
        fold *= 2
    groups = planes // fold
    group_rows, group_tokens = fold * cap, fold * tokens
    rows = planes * cap
    tile = min(512, width // 2)
    steps = width // tile
    half = steps // 2
    last = peers - 1
    anywhere = pl.BlockSpec(memory_space=pl.ANY)

    me = lax.axis_index("expert")
    core = lax.axis_index("dp")
    column, plane = me % peers, me // peers
    meta = jnp.stack([column, plane // fold, (plane % fold) * cap, me, core, plane]).astype(jnp.int32)

    def swap(value, distance):
        return lax.ppermute(value, "expert", [(e, e ^ distance) for e in range(count)])

    matrix = weight[0]
    if fold == 1:
        blocks = hidden.reshape(planes, peers, cap, inside)
    else:
        blocks = hidden.reshape(planes, peers, cap, inside).transpose(1, 0, 2, 3).reshape(1, peers, rows, inside)
    block = (blocks.shape[0], 1, blocks.shape[2], inside)

    columns = [[p * peers + c for p in range(planes)] for c in range(peers)]
    token_rows = lax.all_gather(out_grad, "expert", axis_index_groups=columns, tiled=True)

    ids_turned = expert_ids.T
    table = call(
        table_body, "table", (1,),
        [pl.BlockSpec((top, tokens), lambda i, m: (0, 0)), pl.BlockSpec((top, tokens), lambda i, m: (0, 0))],
        pl.BlockSpec((2 * count, tokens), lambda i, m: (0, 0)),
        jax.ShapeDtypeStruct((2 * count, tokens), F32),
        meta, (ids_turned, gates.T),
    )
    tables = lax.all_gather(table, "expert", axis_index_groups=columns)

    def forward(peer, after):
        return call(
            lambda meta, *refs: forward_body(meta, refs[0], refs[1], refs[-1]), f"forward{peer}", (steps,),
            [
                pl.BlockSpec(block, lambda i, m: (0, lax.bitwise_xor(m[0], peer), 0, 0)),
                pl.BlockSpec((inside, tile), lambda i, m: (0, i)),
            ]
            + [anywhere] * len(after),
            pl.BlockSpec((rows, tile), lambda i, m: (0, i)),
            jax.ShapeDtypeStruct((rows, width), BF16),
            meta, (blocks, matrix, *after),
            flops=2 * rows * inside * width, moved=2 * (rows * inside + inside * width + rows * width),
        )

    outputs, after = {}, ()
    for peer in list(range(1, peers)) + [0]:
        outputs[peer] = forward(peer, after)
        after = (outputs[peer],)
    returned = [outputs[0]] + [swap(outputs[peer], peer) for peer in range(1, last)]
    final_output = follow(outputs[last], *returned[1:])
    returned.append(swap(final_output, last))

    turned = call(
        lambda meta, *refs: turn_body(meta, refs[0], refs[-1]), "turn", (peers,),
        [pl.BlockSpec(block, lambda i, m: (0, lax.bitwise_xor(m[0], i), 0, 0)), anywhere],
        pl.BlockSpec((1, inside, rows), lambda i, m: (i, 0, 0)),
        jax.ShapeDtypeStruct((peers, inside, rows), BF16),
        meta, (blocks, outputs[0]),
        moved=4 * peers * rows * inside,
    )

    table_spec = pl.BlockSpec(tables.shape, lambda i, m: (0, 0, 0))

    def turned_column(i, m):
        return lax.bitwise_xor(i, (1 - m[4]) * half)

    grad_rows = call(
        lambda meta, tables, tokens, turned, after, *outs: grad_rows_body(peers, groups, fold, meta, tables, tokens, *outs),
        "grad_rows", (steps,),
        [table_spec, pl.BlockSpec((planes * tokens, tile), lambda i, m: (0, turned_column(i, m))), anywhere, anywhere],
        [pl.BlockSpec((rows, tile), lambda i, m: (0, turned_column(i, m)))] * last
        + [
            pl.BlockSpec((rows, tile), lambda i, m: (0, jnp.minimum(i, half - 1))),
            pl.BlockSpec((rows, tile), lambda i, m: (0, jnp.maximum(i - half, 0))),
        ],
        [jax.ShapeDtypeStruct((rows, width), BF16)] * last + [jax.ShapeDtypeStruct((rows, width // 2), BF16)] * 2,
        meta, (tables, token_rows, turned, final_output),
        flops=2 * peers * rows * group_tokens * width,
        moved=2 * width * (planes * tokens + peers * rows),
    )
    arrived = [grad_rows[0]] + [swap(grad_rows[peer], peer) for peer in range(1, last)]

    padded = width + 128

    def combine(group, after):
        def part_of(i, m):
            return (lax.bitwise_xor(m[1], group), jnp.minimum(i, steps - 1))

        return call(
            lambda meta, tables, after, *refs: combine_body(peers, group, fold, meta, tables, *refs),
            f"combine{group}", (steps + 1,),
            [table_spec, anywhere, pl.BlockSpec((group_tokens, tile), part_of)]
            + [pl.BlockSpec((group_rows, tile), part_of)] * peers,
            pl.BlockSpec((group_tokens, tile), lambda i, m: (0, i)),
            jax.ShapeDtypeStruct((group_tokens, padded), F32 if group == 0 else BF16),
            meta, (tables, after, token_rows, *returned),
            flops=6 * peers * group_rows * group_tokens * width,
            moved=2 * width * (2 * group_tokens + peers * group_rows),
            scratch=[pltpu.VMEM((peers, group_tokens), F32)],
        )

    sums, after = [None] * planes, grad_rows[0]
    for group in list(range(1, groups)) + [0]:
        after = part = combine(group, after)
        for k in range(fold):
            at = group * fold + k
            piece = part
            if fold > 1:
                piece = lax.dynamic_slice_in_dim(part, lax.bitwise_xor(plane % fold, k) * tokens, tokens)
            sums[at] = swap(piece.astype(BF16), peers * at) if at else piece

    first_half = follow(grad_rows[last], *arrived[1:last], sums[0])
    arrived.append(swap(first_half, last))
    second_half = follow(grad_rows[peers], arrived[last])
    arrived.append(swap(second_half, last))

    wide = pl.BlockSpec((tokens, padded), lambda i, m: (0, 0))
    combined, gate_grads = call(
        functools.partial(finish_body, planes, peers), "finish", (1,),
        [pl.BlockSpec((top, tokens), lambda i, m: (0, 0))] + [wide] * planes,
        [pl.BlockSpec((tokens, width), lambda i, m: (0, 0)), pl.BlockSpec((top, tokens), lambda i, m: (0, 0))],
        [jax.ShapeDtypeStruct((tokens, width), BF16), jax.ShapeDtypeStruct((top, tokens), F32)],
        meta, (ids_turned, *sums),
        moved=2 * tokens * width * (planes + 2),
    )

    grads_shape = jax.ShapeDtypeStruct(blocks.shape, BF16)

    def expert(peer, earlier, after):
        column_spec = pl.BlockSpec((inside, tile), lambda i, m: (0, i))
        operands = [turned, arrived[peer], matrix] + list(earlier) + list(after)
        return call(
            functools.partial(expert_body, bool(earlier)), f"expert{peer}", (steps,),
            [
                pl.BlockSpec((1, inside, rows), lambda i, m: (peer, 0, 0)),
                pl.BlockSpec((rows, tile), lambda i, m: (0, i)),
                column_spec,
            ]
            + ([column_spec, anywhere] if earlier else [])
            + [anywhere] * len(after),
            [column_spec, pl.BlockSpec(block, lambda i, m: (0, lax.bitwise_xor(m[0], peer), 0, 0))],
            [jax.ShapeDtypeStruct((inside, width), F32), grads_shape],
            meta, operands,
            flops=4 * rows * inside * width, moved=2 * (2 * rows * inside + 5 * inside * width + rows * width),
            scratch=[pltpu.VMEM((rows, inside), F32)],
            aliases={5: 1} if earlier else None,
        )

    earlier = ()
    for peer in range(last):
        earlier = expert(peer, earlier, (first_half,) if peer else ())
    total, hidden_grads = earlier

    def own(i, m):
        return (0, m[4] * half + i)

    def others(i, m):
        return (0, (1 - m[4]) * half + i)

    turned_spec = pl.BlockSpec((1, inside, rows), lambda i, m: (last, 0, 0))
    rows_spec = pl.BlockSpec((rows, tile), lambda i, m: (0, i))
    half_spec = pl.BlockSpec((inside, tile), lambda i, m: (0, i))
    other = call(
        lambda meta, *refs: other_half_body(meta, *refs[:3], refs[-1]), "other_half", (half,),
        [turned_spec, rows_spec, pl.BlockSpec((inside, tile), others), anywhere, anywhere],
        half_spec,
        jax.ShapeDtypeStruct((inside, width // 2), F32),
        meta, (turned, arrived[last], total, combined, second_half),
        flops=rows * inside * width, moved=4 * inside * width,
    )
    other = lax.ppermute(other, "dp", [(0, 1), (1, 0)])
    weight_grads, hidden_grads = call(
        last_body, "last", (half,),
        [
            turned_spec, rows_spec, rows_spec,
            pl.BlockSpec((inside, tile), others), pl.BlockSpec((inside, tile), own), pl.BlockSpec((inside, tile), own),
            half_spec, anywhere,
        ],
        [half_spec, pl.BlockSpec(block, lambda i, m: (0, lax.bitwise_xor(m[0], last), 0, 0))],
        [jax.ShapeDtypeStruct((inside, width // 2), BF16), grads_shape],
        meta, (turned, arrived[last], arrived[peers], matrix, matrix, total, other, hidden_grads),
        flops=3 * rows * inside * width, moved=10 * inside * width,
        scratch=[pltpu.VMEM((rows, inside), F32)],
        aliases={8: 1},
    )

    if fold > 1:
        hidden_grads = hidden_grads.reshape(peers, planes, cap, inside).transpose(1, 0, 2, 3)
    return combined, gate_grads.T, hidden_grads.reshape(hidden.shape), weight_grads[None]


def solution(mesh):
    placed = (
        P(("expert", "dp"), None),
        P(("expert", "dp"), None),
        P("expert", "dp", None),
        P("expert", None, None),
        P(("expert", "dp"), None),
    )
    return jax.shard_map(
        per_device,
        mesh=mesh,
        in_specs=placed,
        out_specs=(
            P(("expert", "dp"), None),
            P(("expert", "dp"), None),
            P("expert", "dp", None),
            P("expert", None, "dp"),
        ),
        check_vma=False,
    )
```

```python
import functools

import jax
import jax.numpy as jnp
from jax import lax
from jax.experimental import pallas as pl
from jax.experimental.pallas import tpu as pltpu
from jax.sharding import PartitionSpec as P

F32 = jnp.float32
BF16 = jnp.bfloat16
VMEM_BYTES = 60 * 1024 * 1024
COST = 1024


def call(body, name, grid, in_specs, out_specs, out_shape, scalars, operands, scratch=(), aliases=None):
    return pl.pallas_call(
        body,
        name=name,
        grid_spec=pltpu.PrefetchScalarGridSpec(
            num_scalar_prefetch=1, grid=grid, in_specs=in_specs, out_specs=out_specs, scratch_shapes=scratch
        ),
        out_shape=out_shape,
        input_output_aliases=aliases or {},
        cost_estimate=pl.CostEstimate(flops=COST, bytes_accessed=COST, transcendentals=0),
        compiler_params=pltpu.CompilerParams(vmem_limit_bytes=VMEM_BYTES),
    )(scalars, *operands)


def follow(value, *earlier):
    anywhere = pl.BlockSpec(memory_space=pl.ANY)
    return pl.pallas_call(
        lambda *refs: None,
        name="follow",
        grid=(1,),
        in_specs=[anywhere] + [pl.BlockSpec((16, 128), lambda i: (0, 0))] * len(earlier),
        out_specs=anywhere,
        out_shape=jax.ShapeDtypeStruct(value.shape, value.dtype),
        input_output_aliases={0: 0},
        cost_estimate=pl.CostEstimate(flops=COST, bytes_accessed=COST, transcendentals=0),
        compiler_params=pltpu.CompilerParams(vmem_limit_bytes=VMEM_BYTES),
    )(value, *earlier)


def table_body(meta, ids, gates, table):
    count = table.shape[0] // 2
    tokens = table.shape[1]
    expert = lax.broadcasted_iota(jnp.int32, (count, tokens), 0)
    named = jnp.zeros((count, tokens), F32)
    gate = jnp.zeros((count, tokens), F32)
    for choice in range(ids.shape[0]):
        hit = ids[choice : choice + 1, :] == expert
        named = named + jnp.where(hit, 1.0, 0.0)
        gate = gate + jnp.where(hit, gates[choice : choice + 1, :], 0.0)
    before = lax.broadcasted_iota(jnp.int32, (tokens, tokens), 0) < lax.broadcasted_iota(jnp.int32, (tokens, tokens), 1)
    earlier = jnp.dot(named.astype(BF16), jnp.where(before, 1.0, 0.0).astype(BF16), preferred_element_type=F32)
    offset = meta[2].astype(F32)
    table[:count, :] = jnp.where(named > 0.0, earlier + offset, -1.0)
    table[count:, :] = gate


def forward_body(meta, hidden, weight, out):
    rows = hidden[:, 0].reshape(out.shape[0], hidden.shape[3])
    out[...] = jnp.dot(rows, weight[...], preferred_element_type=F32).astype(BF16)


def turn_body(meta, hidden, after, out, final):
    value = hidden[:, 0].reshape(final.shape)
    out[0] = value.T
    final[...] = value


def turn_other_body(meta, hidden, out):
    out[...] = hidden[...].T


def selection(tables, expert, rows, planes):
    count = tables.shape[1] // 2
    place = jnp.concatenate([tables[plane, pl.ds(expert, 1), :] for plane in planes], 1)
    gate = jnp.concatenate([tables[plane, pl.ds(expert + count, 1), :] for plane in planes], 1)
    row = lax.broadcasted_iota(jnp.int32, (rows, place.shape[1]), 0).astype(F32)
    return row == place, gate


def grad_rows_body(peers, groups, fold, meta, tables, tokens, *refs):
    outs, (choices, row_gates) = refs[:-2], refs[-2:]
    rows, group_tokens = outs[0].shape[0] // groups, tokens.shape[0] // groups

    @pl.when(pl.program_id(0) == 0)
    def _():
        for group in range(groups):
            planes = [group * fold + k for k in range(fold)]
            for peer in range(peers):
                match, gate = selection(tables, lax.bitwise_xor(meta[3], peer), rows, planes)
                part = pl.ds(peer * rows, rows)
                row_gates[group, part, :] = jnp.broadcast_to(
                    jnp.sum(jnp.where(match, gate, 0.0), 1, keepdims=True), (rows, 128)
                )
                choices[group, part, :] = jnp.where(match, 1.0, 0.0).astype(BF16)

    for group in range(groups):
        grad = tokens[group * group_tokens : (group + 1) * group_tokens, :]
        picked = jnp.dot(choices[group], grad, preferred_element_type=F32)
        value = (picked * row_gates[group][:, :1]).astype(BF16)
        place = pl.ds(group * rows, rows)
        for peer in range(peers):
            outs[peer][place, :] = value[peer * rows : (peer + 1) * rows]


def combine_body(peers, fold, stride, offset, meta, tables, token, *refs):
    returned, (part, weights, marks, inner) = refs[:peers], refs[peers:]
    rows, tokens = returned[0].shape[0], token.shape[0]
    count = tables.shape[1] // 2
    step, last = pl.program_id(1), pl.num_programs(1) - 1
    group = lax.bitwise_xor(meta[1], pl.program_id(0) * stride + offset)

    @pl.when(step == 0)
    def _():
        inner[...] = jnp.zeros(inner.shape, F32)
        planes = [group * fold + k for k in range(fold)]
        for peer in range(peers):
            match, gate = selection(tables, lax.bitwise_xor(meta[3], peer), rows, planes)
            here = pl.ds(peer * rows, rows)
            high = gate.astype(BF16).astype(F32)
            marks[here, :] = jnp.where(match, 1.0, 0.0)
            weights[here, :tokens] = jnp.where(match, high, 0.0).astype(BF16)
            weights[here, tokens:] = jnp.where(match, gate - high, 0.0).astype(BF16)

    @pl.when(step < last)
    def _():
        value = jnp.concatenate([ref[...] for ref in returned], 0)
        total = lax.dot_general(weights[...], value, (((0,), (0,)), ((), ())), preferred_element_type=F32)
        part[...] = (total[:tokens] + total[tokens:]).astype(part.dtype)
        products = lax.dot_general(value, token[...], (((1,), (1,)), ((), ())), preferred_element_type=F32)
        products = products * marks[...]
        for peer in range(peers):
            inner[peer : peer + 1, :] += jnp.sum(products[peer * rows : (peer + 1) * rows], 0, keepdims=True)

    @pl.when(step == last)
    def _():
        value = inner[...]
        high = value.astype(BF16).astype(F32)
        middle = (value - high).astype(BF16).astype(F32)
        pieces = (high, middle, value - high - middle)
        extent = -(-3 * count // 128) * 128
        row = lax.broadcasted_iota(jnp.int32, (extent, tokens), 0)
        placed = jnp.zeros((extent, tokens), F32)
        for number, piece in enumerate(pieces):
            for peer in range(peers):
                at = number * count + lax.bitwise_xor(meta[3], peer)
                placed = jnp.where(row == at, piece[peer : peer + 1, :], placed)
        part[:, :extent] = placed.T.astype(part.dtype)


def inside_body(meta, rows, weight, *refs):
    hidden_grads, inside = refs[-2:]
    share = lax.dot_general(rows[...], weight[...], (((1,), (1,)), ((), ())), preferred_element_type=F32)
    step = pl.program_id(0)

    @pl.when(step == 0)
    def _():
        inside[...] = share

    @pl.when(step > 0)
    def _():
        inside[...] += share

    @pl.when(step == pl.num_programs(0) - 1)
    def _():
        hidden_grads[:, 0] = inside[...].astype(BF16).reshape(hidden_grads.shape[0], *hidden_grads.shape[2:])


def expert_body(has_earlier, meta, turned, rows, weight, *refs):
    sums, (hidden_grads, inside) = refs[-4:-2], refs[-2:]
    value = jnp.dot(turned[0], rows[...], preferred_element_type=F32)
    half = pl.num_programs(0) // 2
    for side in range(2):

        @pl.when(pl.program_id(0) // half == side)
        def _():
            sums[side][...] = (value + refs[side][...] if has_earlier else value).astype(sums[side].dtype)

    inside_body(meta, rows, weight, hidden_grads, inside)


def last_body(meta, turned, rows, turned_other, rows_other, earlier, earlier_other, done, grads):
    value = jnp.dot(turned[0], rows[...], preferred_element_type=F32)
    value = value + jnp.dot(turned_other[...], rows_other[...], preferred_element_type=F32)
    grads[...] = (value + earlier[...] + earlier_other[...].astype(F32)).astype(BF16)


def finish_body(count, meta, after, ids, kept, arrived, combined, gate_grads):
    width = combined.shape[1]
    combined[...] = (kept[:, :width] + arrived[:, :width].astype(F32)).astype(BF16)
    pieces = (kept[:, width:] + arrived[:, width:].astype(F32)).T
    inner = pieces[:count] + pieces[count : 2 * count] + pieces[2 * count : 3 * count]
    named = ids[...]
    found = jnp.zeros(gate_grads.shape, F32)
    for expert in range(count):
        found = found + jnp.where(named == expert, inner[expert : expert + 1, :], 0.0)
    gate_grads[...] = found


def per_device(expert_ids, gates, hidden, weight, out_grad):
    count = lax.axis_size("expert")
    peers = 1 << ((count.bit_length() - 1) // 2)
    planes = count // peers
    tokens, top = expert_ids.shape
    cap = hidden.shape[1] // count
    width, inside = out_grad.shape[1], hidden.shape[2]
    fold = 1
    while fold * cap % 16:
        fold *= 2
    groups = planes // fold
    group_rows, group_tokens = fold * cap, fold * tokens
    rows = planes * cap
    tile = min(512, width // 2)
    steps = width // tile
    half = steps // 2
    last = peers - 1
    anywhere = pl.BlockSpec(memory_space=pl.ANY)
    glance = pl.BlockSpec((16, 128), lambda *i: (0, 0))

    me = lax.axis_index("expert")
    core = lax.axis_index("dp")
    column, plane = me % peers, me // peers
    meta = jnp.stack([column, plane // fold, (plane % fold) * cap, me, core, plane]).astype(jnp.int32)

    def swap(value, distance):
        return lax.ppermute(value, "expert", [(e, e ^ distance) for e in range(count)])

    def exchange(value):
        return lax.ppermute(value, "dp", [(0, 1), (1, 0)])

    matrix = weight[0]
    if fold == 1:
        blocks = hidden.reshape(planes, peers, cap, inside)
    else:
        blocks = hidden.reshape(planes, peers, cap, inside).transpose(1, 0, 2, 3).reshape(1, peers, rows, inside)
    block = (blocks.shape[0], 1, blocks.shape[2], inside)

    columns = [[p * peers + c for p in range(planes)] for c in range(peers)]
    token_rows = lax.all_gather(out_grad, "expert", axis_index_groups=columns, tiled=True)

    ids_turned = expert_ids.T
    table = call(
        table_body, "table", (1,),
        [pl.BlockSpec((top, tokens), lambda i, m: (0, 0)), pl.BlockSpec((top, tokens), lambda i, m: (0, 0))],
        pl.BlockSpec((2 * count, tokens), lambda i, m: (0, 0)),
        jax.ShapeDtypeStruct((2 * count, tokens), F32),
        meta, (ids_turned, gates.T),
    )
    tables = lax.all_gather(table, "expert", axis_index_groups=columns)

    def forward(peer, after):
        return call(
            lambda meta, *refs: forward_body(meta, refs[0], refs[1], refs[-1]), f"forward{peer}", (steps,),
            [
                pl.BlockSpec(block, lambda i, m: (0, lax.bitwise_xor(m[0], peer), 0, 0)),
                pl.BlockSpec((inside, tile), lambda i, m: (0, i)),
            ]
            + [glance] * len(after),
            pl.BlockSpec((rows, tile), lambda i, m: (0, i)),
            jax.ShapeDtypeStruct((rows, width), BF16),
            meta, (blocks, matrix, *after),
        )

    outputs, after = {}, ()
    for peer in list(range(1, peers)) + [0]:
        outputs[peer] = forward(peer, after)
        after = (outputs[peer],)
    returned = [outputs[0]] + [swap(outputs[peer], peer) for peer in range(1, last)]
    final_output = follow(outputs[last], *returned[1:])
    returned.append(swap(final_output, last))

    turned, hidden_last = call(
        turn_body, "turn", (peers,),
        [pl.BlockSpec(block, lambda i, m: (0, lax.bitwise_xor(m[0], i), 0, 0)), glance],
        [pl.BlockSpec((1, inside, rows), lambda i, m: (i, 0, 0)), pl.BlockSpec((rows, inside), lambda i, m: (0, 0))],
        [jax.ShapeDtypeStruct((peers, inside, rows), BF16), jax.ShapeDtypeStruct((rows, inside), BF16)],
        meta, (blocks, outputs[0]),
    )

    table_spec = pl.BlockSpec(tables.shape, lambda i, m: (0, 0, 0))

    def turned_column(i, m):
        return lax.bitwise_xor(i, (1 - m[4]) * half)

    grad_rows = call(
        lambda meta, tables, tokens, after, *refs: grad_rows_body(peers, groups, fold, meta, tables, tokens, *refs),
        "grad_rows", (steps,),
        [table_spec, pl.BlockSpec((planes * tokens, tile), lambda i, m: (0, turned_column(i, m))), glance],
        [pl.BlockSpec((rows, tile), lambda i, m: (0, turned_column(i, m)))] * last
        + [pl.BlockSpec((rows, tile), lambda i, m: (i // half, i % half))],
        [jax.ShapeDtypeStruct((rows, width), BF16)] * last + [jax.ShapeDtypeStruct((2 * rows, width // 2), BF16)],
        meta, (tables, token_rows, final_output),
        scratch=[
            pltpu.VMEM((groups, peers * group_rows, group_tokens), BF16),
            pltpu.VMEM((groups, peers * group_rows, 128), F32),
        ],
    )
    arrived = [grad_rows[0]] + [swap(grad_rows[peer], peer) for peer in range(1, last)]

    padded = width + -(-3 * count // 128) * 128

    def combine(number, stride, offset, dtype, after):
        def part_of(k, i, m):
            return (lax.bitwise_xor(m[1], k * stride + offset), jnp.minimum(i, steps - 1))

        return call(
            lambda meta, tables, after, *refs: combine_body(peers, fold, stride, offset, meta, tables, *refs),
            f"combine{offset}", (number, steps + 1),
            [pl.BlockSpec(tables.shape, lambda k, i, m: (0, 0, 0)), glance, pl.BlockSpec((group_tokens, tile), part_of)]
            + [pl.BlockSpec((group_rows, tile), part_of)] * peers,
            pl.BlockSpec((group_tokens, tile), lambda k, i, m: (k, i)),
            jax.ShapeDtypeStruct((number * group_tokens, padded), dtype),
            meta, (tables, after, token_rows, *returned),
            scratch=[
                pltpu.VMEM((peers * group_rows, 2 * group_tokens), BF16),
                pltpu.VMEM((peers * group_rows, group_tokens), F32),
                pltpu.VMEM((peers, group_tokens), F32),
            ],
        )

    if fold == 1:
        leaving = combine(planes // 2, 2, 1, BF16, grad_rows[0])
        staying = combine(planes // 2, 2, 0, F32, leaving)
        sums = [staying[k * tokens : (k + 1) * tokens] for k in range(planes // 2)]
        combine_done = staying
    else:
        combine_done = combine(groups, 1, 0, F32, grad_rows[0])
        sums = []
        for k in range(planes):
            at = k // fold * fold + lax.bitwise_xor(plane % fold, k % fold)
            sums.append(lax.dynamic_slice_in_dim(combine_done, at * tokens, tokens))
        leaving = jnp.concatenate(sums[1::2], 0).astype(BF16)
        sums = sums[0::2]
    distance = 1
    first_sums = None
    while len(sums) > 1:
        got = swap(leaving, peers * distance)
        pieces = [got[k * tokens : (k + 1) * tokens].astype(F32) for k in range(len(sums))]
        sums = [mine + piece for mine, piece in zip(sums, pieces)]
        leaving = [value.astype(BF16) for value in sums[1::2]]
        leaving = leaving[0] if len(leaving) == 1 else jnp.concatenate(leaving, 0)
        sums = sums[0::2]
        first_sums = leaving if first_sums is None else first_sums
        distance *= 2
    got = swap(leaving, peers * distance)

    turned_other = call(
        turn_other_body, "turn_other", (1,),
        [pl.BlockSpec((rows, inside), lambda i, m: (0, 0))],
        pl.BlockSpec((inside, rows), lambda i, m: (0, 0)),
        jax.ShapeDtypeStruct((inside, rows), BF16),
        meta, (exchange(hidden_last),),
    )
    final_rows = follow(grad_rows[last], *arrived[1:last], combine_done, turned_other)
    arrived.append(swap(final_rows, last))

    grads_shape = jax.ShapeDtypeStruct(blocks.shape, BF16)
    half_shape = jax.ShapeDtypeStruct((inside, width // 2), F32)
    side_specs = [
        pl.BlockSpec((inside, tile), lambda i, m: (0, jnp.minimum(i, half - 1))),
        pl.BlockSpec((inside, tile), lambda i, m: (0, jnp.maximum(i - half, 0))),
    ]
    weight_spec = pl.BlockSpec((inside, tile), lambda i, m: (0, turned_column(i, m)))

    def expert(peer, earlier, after):
        return call(
            functools.partial(expert_body, bool(earlier)), f"expert{peer}", (steps,),
            [
                pl.BlockSpec((1, inside, rows), lambda i, m: (peer, 0, 0)),
                pl.BlockSpec((rows, tile), lambda i, m: (0, turned_column(i, m))),
                weight_spec,
            ]
            + (side_specs + [anywhere] if earlier else [])
            + [glance] * len(after),
            side_specs + [pl.BlockSpec(block, lambda i, m: (0, lax.bitwise_xor(m[0], peer), 0, 0))],
            [jax.ShapeDtypeStruct(half_shape.shape, BF16 if peer == last - 1 else F32), half_shape, grads_shape],
            meta, (turned, arrived[peer], matrix, *earlier, *after),
            scratch=[pltpu.VMEM((rows, inside), F32)],
            aliases={6: 2} if earlier else None,
        )

    earlier = ()
    for peer in range(last):
        earlier = expert(peer, earlier, (final_rows, first_sums) if peer else ())
    total_other, total_own, hidden_grads = earlier
    total_other = exchange(total_other)
    rows_other = exchange(follow(arrived[last][:rows], got))

    combined, gate_grads = call(
        functools.partial(finish_body, count), "finish", (1,),
        [
            glance, pl.BlockSpec((top, tokens), lambda i, m: (0, 0)),
            pl.BlockSpec((tokens, padded), lambda i, m: (0, 0)), pl.BlockSpec((tokens, padded), lambda i, m: (0, 0)),
        ],
        [pl.BlockSpec((tokens, width), lambda i, m: (0, 0)), pl.BlockSpec((top, tokens), lambda i, m: (0, 0))],
        [jax.ShapeDtypeStruct((tokens, width), BF16), jax.ShapeDtypeStruct((top, tokens), F32)],
        meta, (total_own, ids_turned, sums[0], got),
    )
    hidden_grads = call(
        inside_body, "inside", (steps,),
        [pl.BlockSpec((rows, tile), lambda i, m: (i // half, i % half)), weight_spec, anywhere, glance],
        pl.BlockSpec(block, lambda i, m: (0, lax.bitwise_xor(m[0], last), 0, 0)),
        grads_shape,
        meta, (arrived[last], matrix, hidden_grads, combined),
        scratch=[pltpu.VMEM((rows, inside), F32)],
        aliases={3: 0},
    )
    half_spec = pl.BlockSpec((inside, tile), lambda i, m: (0, i))
    weight_grads = call(
        last_body, "last", (half,),
        [
            pl.BlockSpec((1, inside, rows), lambda i, m: (last, 0, 0)),
            pl.BlockSpec((rows, tile), lambda i, m: (1, i)),
            pl.BlockSpec((inside, rows), lambda i, m: (0, 0)),
            pl.BlockSpec((rows, tile), lambda i, m: (0, i)),
            half_spec, half_spec, glance,
        ],
        half_spec,
        jax.ShapeDtypeStruct((inside, width // 2), BF16),
        meta, (turned, arrived[last], turned_other, rows_other, total_own, total_other, combined),
    )

    if fold > 1:
        hidden_grads = hidden_grads.reshape(peers, planes, cap, inside).transpose(1, 0, 2, 3)
    return combined, gate_grads.T, hidden_grads.reshape(hidden.shape), weight_grads[None]


def solution(mesh):
    placed = (
        P(("expert", "dp"), None),
        P(("expert", "dp"), None),
        P("expert", "dp", None),
        P("expert", None, None),
        P(("expert", "dp"), None),
    )
    return jax.shard_map(
        per_device,
        mesh=mesh,
        in_specs=placed,
        out_specs=(
            P(("expert", "dp"), None),
            P(("expert", "dp"), None),
            P("expert", "dp", None),
            P("expert", None, "dp"),
        ),
        check_vma=False,
    )
```

```python
import functools

import jax
import jax.numpy as jnp
from jax import lax
from jax.experimental import pallas as pl
from jax.experimental.pallas import tpu as pltpu
from jax.sharding import PartitionSpec as P

F32 = jnp.float32
BF16 = jnp.bfloat16
VMEM_BYTES = 16 * 1024 * 1024
COST = 1024


def call(body, name, grid, in_specs, out_specs, out_shape, scalars, operands, scratch=(), aliases=None, room=1):
    return pl.pallas_call(
        body,
        name=name,
        grid_spec=pltpu.PrefetchScalarGridSpec(
            num_scalar_prefetch=1, grid=grid, in_specs=in_specs, out_specs=out_specs, scratch_shapes=scratch
        ),
        out_shape=out_shape,
        input_output_aliases=aliases or {},
        cost_estimate=pl.CostEstimate(flops=COST, bytes_accessed=COST, transcendentals=0),
        compiler_params=pltpu.CompilerParams(vmem_limit_bytes=room * VMEM_BYTES),
    )(scalars, *operands)


def follow(value, *earlier):
    anywhere = pl.BlockSpec(memory_space=pl.ANY)
    return pl.pallas_call(
        lambda *refs: None,
        name="follow",
        grid=(1,),
        in_specs=[anywhere] + [pl.BlockSpec((16, 128), lambda i: (0, 0))] * len(earlier),
        out_specs=anywhere,
        out_shape=jax.ShapeDtypeStruct(value.shape, value.dtype),
        input_output_aliases={0: 0},
        cost_estimate=pl.CostEstimate(flops=COST, bytes_accessed=COST, transcendentals=0),
        compiler_params=pltpu.CompilerParams(vmem_limit_bytes=VMEM_BYTES),
    )(value, *earlier)


def table_body(meta, ids, gates, table):
    count = table.shape[0] // 2
    tokens = table.shape[1]
    expert = lax.broadcasted_iota(jnp.int32, (count, tokens), 0)
    named = jnp.zeros((count, tokens), F32)
    gate = jnp.zeros((count, tokens), F32)
    for choice in range(ids.shape[0]):
        hit = ids[choice : choice + 1, :] == expert
        named = named + jnp.where(hit, 1.0, 0.0)
        gate = gate + jnp.where(hit, gates[choice : choice + 1, :], 0.0)
    before = lax.broadcasted_iota(jnp.int32, (tokens, tokens), 0) < lax.broadcasted_iota(jnp.int32, (tokens, tokens), 1)
    earlier = jnp.dot(named.astype(BF16), jnp.where(before, 1.0, 0.0).astype(BF16), preferred_element_type=F32)
    offset = meta[2].astype(F32)
    table[:count, :] = jnp.where(named > 0.0, earlier + offset, -1.0)
    table[count:, :] = gate


def forward_body(meta, hidden, weight, out):
    rows = hidden[:, 0].reshape(out.shape[0], hidden.shape[3])
    out[...] = jnp.dot(rows, weight[...], preferred_element_type=F32).astype(BF16)


def turn_body(meta, hidden, after, out, final):
    value = hidden[:, 0].reshape(final.shape)
    out[0] = value.T
    final[...] = value


def turn_other_body(meta, hidden, out):
    out[...] = hidden[...].T


def selection(tables, expert, rows, planes):
    count = tables.shape[1] // 2
    place = jnp.concatenate([tables[plane, pl.ds(expert, 1), :] for plane in planes], 1)
    gate = jnp.concatenate([tables[plane, pl.ds(expert + count, 1), :] for plane in planes], 1)
    row = lax.broadcasted_iota(jnp.int32, (rows, place.shape[1]), 0).astype(F32)
    return row == place, gate


def grad_rows_body(peers, groups, fold, meta, tables, tokens, *refs):
    outs, (choices, row_gates) = refs[:-2], refs[-2:]
    rows, group_tokens = outs[0].shape[0] // groups, tokens.shape[0] // groups

    @pl.when(pl.program_id(0) == 0)
    def _():
        for group in range(groups):
            planes = [group * fold + k for k in range(fold)]
            for peer in range(peers):
                match, gate = selection(tables, lax.bitwise_xor(meta[3], peer), rows, planes)
                part = pl.ds(peer * rows, rows)
                row_gates[group, part, :] = jnp.broadcast_to(
                    jnp.sum(jnp.where(match, gate, 0.0), 1, keepdims=True), (rows, 128)
                )
                choices[group, part, :] = jnp.where(match, 1.0, 0.0).astype(BF16)

    for group in range(groups):
        grad = tokens[group * group_tokens : (group + 1) * group_tokens, :]
        picked = jnp.dot(choices[group], grad, preferred_element_type=F32)
        value = (picked * row_gates[group][:, :1]).astype(BF16)
        place = pl.ds(group * rows, rows)
        for peer in range(peers):
            outs[peer][place, :] = value[peer * rows : (peer + 1) * rows]


def combine_body(peers, fold, stride, offset, meta, tables, token, *refs):
    returned, (part, weights, marks, inner) = refs[:peers], refs[peers:]
    rows, tokens = returned[0].shape[0], token.shape[0]
    count = tables.shape[1] // 2
    step, last = pl.program_id(1), pl.num_programs(1) - 1
    group = lax.bitwise_xor(meta[1], pl.program_id(0) * stride + offset)

    @pl.when(step == 0)
    def _():
        inner[...] = jnp.zeros(inner.shape, F32)
        planes = [group * fold + k for k in range(fold)]
        highs, lows = [], []
        for peer in range(peers):
            match, gate = selection(tables, lax.bitwise_xor(meta[3], peer), rows, planes)
            high = gate.astype(BF16).astype(F32)
            marks[pl.ds(peer * rows, rows), :] = jnp.where(match, 1.0, 0.0)
            highs.append(jnp.where(match, high, 0.0))
            lows.append(jnp.where(match, gate - high, 0.0))
        weights[:tokens, :] = jnp.concatenate(highs, 0).T.astype(BF16)
        weights[tokens:, :] = jnp.concatenate(lows, 0).T.astype(BF16)

    @pl.when(step < last)
    def _():
        value = jnp.concatenate([ref[...] for ref in returned], 0)
        total = jnp.dot(weights[...], value, preferred_element_type=F32)
        part[...] = (total[:tokens] + total[tokens:]).astype(part.dtype)
        products = lax.dot_general(value, token[...], (((1,), (1,)), ((), ())), preferred_element_type=F32)
        products = products * marks[...]
        for peer in range(peers):
            inner[peer : peer + 1, :] += jnp.sum(products[peer * rows : (peer + 1) * rows], 0, keepdims=True)

    @pl.when(step == last)
    def _():
        value = inner[...]
        high = value.astype(BF16).astype(F32)
        middle = (value - high).astype(BF16).astype(F32)
        pieces = (high, middle, value - high - middle)
        extent = -(-3 * count // 128) * 128
        row = lax.broadcasted_iota(jnp.int32, (extent, tokens), 0)
        placed = jnp.zeros((extent, tokens), F32)
        for number, piece in enumerate(pieces):
            for peer in range(peers):
                at = number * count + lax.bitwise_xor(meta[3], peer)
                placed = jnp.where(row == at, piece[peer : peer + 1, :], placed)
        part[:, :extent] = placed.T.astype(part.dtype)


def inside_body(meta, rows, weight, *refs):
    hidden_grads, token, inside = refs[-3:]
    token[...] = jnp.zeros(token.shape, F32)
    share = lax.dot_general(rows[...], weight[...], (((1,), (1,)), ((), ())), preferred_element_type=F32)
    step = pl.program_id(0)

    @pl.when(step == 0)
    def _():
        inside[...] = share

    @pl.when(step > 0)
    def _():
        inside[...] += share

    @pl.when(step == pl.num_programs(0) - 1)
    def _():
        hidden_grads[:, 0] = inside[...].astype(BF16).reshape(hidden_grads.shape[0], *hidden_grads.shape[2:])


def weight_grad_body(number, meta, turned, *refs):
    rows, sums = refs[:number], refs[-2:]
    value = jnp.dot(turned[0], rows[0][...], preferred_element_type=F32)
    for peer in range(1, number):
        value = value + jnp.dot(turned[peer], rows[peer][...], preferred_element_type=F32)
    half = pl.num_programs(0) // 2
    for side in range(2):

        @pl.when(pl.program_id(0) // half == side)
        def _():
            sums[side][...] = value.astype(sums[side].dtype)


def last_body(meta, turned, rows, turned_other, rows_other, earlier, earlier_other, done, grads):
    value = jnp.dot(turned[0], rows[...], preferred_element_type=F32)
    value = value + jnp.dot(turned_other[...], rows_other[...], preferred_element_type=F32)
    grads[...] = (value + earlier[...] + earlier_other[...].astype(F32)).astype(BF16)


def finish_body(count, meta, after, ids, kept, arrived, combined, gate_grads):
    width = combined.shape[1]
    combined[...] = (kept[:, :width] + arrived[:, :width].astype(F32)).astype(BF16)
    pieces = (kept[:, width:] + arrived[:, width:].astype(F32)).T
    inner = pieces[:count] + pieces[count : 2 * count] + pieces[2 * count : 3 * count]
    named = ids[...]
    found = jnp.zeros(gate_grads.shape, F32)
    for expert in range(count):
        found = found + jnp.where(named == expert, inner[expert : expert + 1, :], 0.0)
    gate_grads[...] = found


def per_device(expert_ids, gates, hidden, weight, out_grad):
    count = lax.axis_size("expert")
    peers = 1 << ((count.bit_length() - 1) // 2)
    planes = count // peers
    tokens, top = expert_ids.shape
    cap = hidden.shape[1] // count
    width, inside = out_grad.shape[1], hidden.shape[2]
    fold = 1
    while fold * cap % 16:
        fold *= 2
    groups = planes // fold
    group_rows, group_tokens = fold * cap, fold * tokens
    rows = planes * cap
    tile = min(512, width // 2)
    steps = width // tile
    half = steps // 2
    large = width // 2
    room = 1 if fold == 1 else 3
    last = peers - 1
    anywhere = pl.BlockSpec(memory_space=pl.ANY)
    glance = pl.BlockSpec((16, 128), lambda *i: (0, 0))

    me = lax.axis_index("expert")
    core = lax.axis_index("dp")
    column, plane = me % peers, me // peers
    meta = jnp.stack([column, plane // fold, (plane % fold) * cap, me, core, plane]).astype(jnp.int32)

    def swap(value, distance):
        return lax.ppermute(value, "expert", [(e, e ^ distance) for e in range(count)])

    def exchange(value):
        return lax.ppermute(value, "dp", [(0, 1), (1, 0)])

    matrix = weight[0]
    if fold == 1:
        blocks = hidden.reshape(planes, peers, cap, inside)
    else:
        blocks = hidden.reshape(planes, peers, cap, inside).transpose(1, 0, 2, 3).reshape(1, peers, rows, inside)
    block = (blocks.shape[0], 1, blocks.shape[2], inside)

    columns = [[p * peers + c for p in range(planes)] for c in range(peers)]
    token_rows = lax.all_gather(out_grad, "expert", axis_index_groups=columns, tiled=True)

    ids_turned = expert_ids.T
    table = call(
        table_body, "table", (1,),
        [pl.BlockSpec((top, tokens), lambda i, m: (0, 0)), pl.BlockSpec((top, tokens), lambda i, m: (0, 0))],
        pl.BlockSpec((2 * count, tokens), lambda i, m: (0, 0)),
        jax.ShapeDtypeStruct((2 * count, tokens), F32),
        meta, (ids_turned, gates.T),
    )
    tables = lax.all_gather(table, "expert", axis_index_groups=columns)

    def forward(peer, after):
        return call(
            lambda meta, *refs: forward_body(meta, refs[0], refs[1], refs[-1]), f"forward{peer}", (steps,),
            [
                pl.BlockSpec(block, lambda i, m: (0, lax.bitwise_xor(m[0], peer), 0, 0)),
                pl.BlockSpec((inside, tile), lambda i, m: (0, i)),
            ]
            + [glance] * len(after),
            pl.BlockSpec((rows, tile), lambda i, m: (0, i)),
            jax.ShapeDtypeStruct((rows, width), BF16),
            meta, (blocks, matrix, *after),
        )

    outputs, after = {}, ()
    for peer in list(range(1, peers)) + [0]:
        outputs[peer] = forward(peer, after)
        after = (outputs[peer],)
    returned = [outputs[0]] + [swap(outputs[peer], peer) for peer in range(1, last)]
    turned, hidden_last = call(
        turn_body, "turn", (peers,),
        [pl.BlockSpec(block, lambda i, m: (0, lax.bitwise_xor(m[0], i), 0, 0)), glance],
        [pl.BlockSpec((1, inside, rows), lambda i, m: (i, 0, 0)), pl.BlockSpec((rows, inside), lambda i, m: (0, 0))],
        [jax.ShapeDtypeStruct((peers, inside, rows), BF16), jax.ShapeDtypeStruct((rows, inside), BF16)],
        meta, (blocks, outputs[0]),
    )

    turned_other = call(
        turn_other_body, "turn_other", (1,),
        [pl.BlockSpec((rows, inside), lambda i, m: (0, 0))],
        pl.BlockSpec((inside, rows), lambda i, m: (0, 0)),
        jax.ShapeDtypeStruct((inside, rows), BF16),
        meta, (exchange(hidden_last),),
    )
    final_output = follow(outputs[last], *returned[1:], tables.reshape(-1, tokens), turned_other)
    returned.append(swap(final_output, last))

    table_spec = pl.BlockSpec(tables.shape, lambda i, m: (0, 0, 0))

    def turned_column(i, m):
        return lax.bitwise_xor(i, (1 - m[4]) * half)

    grad_rows = call(
        lambda meta, tables, tokens, after, *refs: grad_rows_body(peers, groups, fold, meta, tables, tokens, *refs),
        "grad_rows", (2,),
        [table_spec, pl.BlockSpec((planes * tokens, large), lambda i, m: (0, lax.bitwise_xor(i, 1 - m[4]))), glance],
        [pl.BlockSpec((rows, large), lambda i, m: (0, lax.bitwise_xor(i, 1 - m[4])))] * last
        + [pl.BlockSpec((rows, large), lambda i, m: (i, 0))],
        [jax.ShapeDtypeStruct((rows, width), BF16)] * last + [jax.ShapeDtypeStruct((2 * rows, width // 2), BF16)],
        meta, (tables, token_rows, final_output),
        scratch=[
            pltpu.VMEM((groups, peers * group_rows, group_tokens), BF16),
            pltpu.VMEM((groups, peers * group_rows, 128), F32),
        ],
        room=room,
    )
    arrived = [grad_rows[0]] + [swap(grad_rows[peer], peer) for peer in range(1, last)]

    padded = width + -(-3 * count // 128) * 128

    def combine(number, stride, offset, dtype, after):
        def part_of(k, i, m):
            return (lax.bitwise_xor(m[1], k * stride + offset), jnp.minimum(i, 1))

        return call(
            lambda meta, tables, after, *refs: combine_body(peers, fold, stride, offset, meta, tables, *refs),
            f"combine{offset}", (number, 3),
            [pl.BlockSpec(tables.shape, lambda k, i, m: (0, 0, 0)), glance, pl.BlockSpec((group_tokens, large), part_of)]
            + [pl.BlockSpec((group_rows, large), part_of)] * peers,
            pl.BlockSpec((group_tokens, large), lambda k, i, m: (k, i)),
            jax.ShapeDtypeStruct((number * group_tokens, padded), dtype),
            meta, (tables, after, token_rows, *returned),
            scratch=[
                pltpu.VMEM((2 * group_tokens, peers * group_rows), BF16),
                pltpu.VMEM((peers * group_rows, group_tokens), F32),
                pltpu.VMEM((peers, group_tokens), F32),
            ],
            room=room,
        )

    if fold == 1:
        leaving = combine(planes // 2, 2, 1, BF16, grad_rows[0])
        staying = combine(planes // 2, 2, 0, F32, leaving)
        sums = [staying[k * tokens : (k + 1) * tokens] for k in range(planes // 2)]
        combine_done = staying
    else:
        combine_done = combine(groups, 1, 0, F32, grad_rows[0])
        sums = []
        for k in range(planes):
            at = k // fold * fold + lax.bitwise_xor(plane % fold, k % fold)
            sums.append(lax.dynamic_slice_in_dim(combine_done, at * tokens, tokens))
        leaving = jnp.concatenate(sums[1::2], 0).astype(BF16)
        sums = sums[0::2]
    distance = 1
    first_sums = None
    while len(sums) > 1:
        got = swap(leaving, peers * distance)
        pieces = [got[k * tokens : (k + 1) * tokens].astype(F32) for k in range(len(sums))]
        sums = [mine + piece for mine, piece in zip(sums, pieces)]
        leaving = [value.astype(BF16) for value in sums[1::2]]
        leaving = leaving[0] if len(leaving) == 1 else jnp.concatenate(leaving, 0)
        sums = sums[0::2]
        first_sums = leaving if first_sums is None else first_sums
        distance *= 2
    got = swap(leaving, peers * distance)

    final_rows = follow(grad_rows[last], *arrived[1:last], combine_done)
    arrived.append(swap(final_rows, last))

    grads_shape = jax.ShapeDtypeStruct(blocks.shape, BF16)
    half_shape = jax.ShapeDtypeStruct((inside, width // 2), F32)
    side_specs = [
        pl.BlockSpec((inside, tile), lambda i, m: (0, jnp.minimum(i, half - 1))),
        pl.BlockSpec((inside, tile), lambda i, m: (0, jnp.maximum(i - half, 0))),
    ]
    weight_spec = pl.BlockSpec((inside, tile), lambda i, m: (0, turned_column(i, m)))

    def inside_grad(peer, earlier, after):
        whole = arrived[peer].shape[1] == width

        def rows_at(i, m):
            return (0, turned_column(i, m)) if whole else (i // half, i % half)

        return call(
            inside_body, f"inside{peer}", (steps,),
            [pl.BlockSpec((rows, tile), rows_at), weight_spec]
            + ([] if earlier is None else [anywhere])
            + [glance] * len(after),
            [
                pl.BlockSpec(block, lambda i, m: (0, lax.bitwise_xor(m[0], peer), 0, 0)),
                pl.BlockSpec((16, 128), lambda i, m: (0, 0)),
            ],
            [grads_shape, jax.ShapeDtypeStruct((16, 128), F32)],
            meta, (arrived[peer], matrix, *(() if earlier is None else (earlier,)), *after),
            scratch=[pltpu.VMEM((rows, inside), F32)],
            aliases=None if earlier is None else {3: 0},
        )

    total_other, total_own = call(
        functools.partial(weight_grad_body, last), "weight_grad", (steps,),
        [pl.BlockSpec((peers, inside, rows), lambda i, m: (0, 0, 0))]
        + [pl.BlockSpec((rows, tile), lambda i, m: (0, turned_column(i, m)))] * last
        + [glance] * 2,
        side_specs,
        [jax.ShapeDtypeStruct(half_shape.shape, BF16), half_shape],
        meta, (turned, *arrived[:last], final_rows, first_sums),
        room=room,
    )
    hidden_grads = None
    for peer in range(last):
        hidden_grads, token = inside_grad(peer, hidden_grads, (total_own,))
    total_other = exchange(total_other)
    rows_other = exchange(follow(arrived[last][:rows], got, token))

    combined, gate_grads = call(
        functools.partial(finish_body, count), "finish", (1,),
        [
            glance, pl.BlockSpec((top, tokens), lambda i, m: (0, 0)),
            pl.BlockSpec((tokens, padded), lambda i, m: (0, 0)), pl.BlockSpec((tokens, padded), lambda i, m: (0, 0)),
        ],
        [pl.BlockSpec((tokens, width), lambda i, m: (0, 0)), pl.BlockSpec((top, tokens), lambda i, m: (0, 0))],
        [jax.ShapeDtypeStruct((tokens, width), BF16), jax.ShapeDtypeStruct((top, tokens), F32)],
        meta, (total_own, ids_turned, sums[0], got),
    )
    hidden_grads, _ = inside_grad(last, hidden_grads, (combined,))
    half_spec = pl.BlockSpec((inside, tile), lambda i, m: (0, i))
    weight_grads = call(
        last_body, "last", (half,),
        [
            pl.BlockSpec((1, inside, rows), lambda i, m: (last, 0, 0)),
            pl.BlockSpec((rows, tile), lambda i, m: (1, i)),
            pl.BlockSpec((inside, rows), lambda i, m: (0, 0)),
            pl.BlockSpec((rows, tile), lambda i, m: (0, i)),
            half_spec, half_spec, glance,
        ],
        half_spec,
        jax.ShapeDtypeStruct((inside, width // 2), BF16),
        meta, (turned, arrived[last], turned_other, rows_other, total_own, total_other, combined),
    )

    if fold > 1:
        hidden_grads = hidden_grads.reshape(peers, planes, cap, inside).transpose(1, 0, 2, 3)
    return combined, gate_grads.T, hidden_grads.reshape(hidden.shape), weight_grads[None]


def solution(mesh):
    placed = (
        P(("expert", "dp"), None),
        P(("expert", "dp"), None),
        P("expert", "dp", None),
        P("expert", None, None),
        P(("expert", "dp"), None),
    )
    return jax.shard_map(
        per_device,
        mesh=mesh,
        in_specs=placed,
        out_specs=(
            P(("expert", "dp"), None),
            P(("expert", "dp"), None),
            P("expert", "dp", None),
            P("expert", None, "dp"),
        ),
        check_vma=False,
    )
```

```python
import functools

import jax
import jax.numpy as jnp
from jax import lax
from jax.experimental import pallas as pl
from jax.experimental.pallas import tpu as pltpu
from jax.sharding import PartitionSpec as P

F32 = jnp.float32
BF16 = jnp.bfloat16
VMEM_BYTES = 16 * 1024 * 1024
COST = 1024


def call(body, name, grid, in_specs, out_specs, out_shape, scalars, operands, scratch=(), aliases=None, room=1):
    return pl.pallas_call(
        body,
        name=name,
        grid_spec=pltpu.PrefetchScalarGridSpec(
            num_scalar_prefetch=1, grid=grid, in_specs=in_specs, out_specs=out_specs, scratch_shapes=scratch
        ),
        out_shape=out_shape,
        input_output_aliases=aliases or {},
        cost_estimate=pl.CostEstimate(flops=COST, bytes_accessed=COST, transcendentals=0),
        compiler_params=pltpu.CompilerParams(vmem_limit_bytes=room * VMEM_BYTES),
    )(scalars, *operands)


def follow(value, *earlier):
    anywhere = pl.BlockSpec(memory_space=pl.ANY)
    return pl.pallas_call(
        lambda *refs: None,
        name="follow",
        grid=(1,),
        in_specs=[anywhere] + [pl.BlockSpec((16, 128), lambda i: (0, 0))] * len(earlier),
        out_specs=anywhere,
        out_shape=jax.ShapeDtypeStruct(value.shape, value.dtype),
        input_output_aliases={0: 0},
        cost_estimate=pl.CostEstimate(flops=COST, bytes_accessed=COST, transcendentals=0),
        compiler_params=pltpu.CompilerParams(vmem_limit_bytes=VMEM_BYTES),
    )(value, *earlier)


def pieces_of(value):
    high = value.astype(BF16).astype(F32)
    middle = (value - high).astype(BF16).astype(F32)
    return high, middle, value - high - middle


def pack_body(meta, ids, gates, grad, out):
    width, tokens = grad.shape[1], grad.shape[0]
    extent = out.shape[1] - width
    count = meta[6]
    expert = lax.broadcasted_iota(jnp.int32, (extent, tokens), 0)
    piece = jnp.zeros((extent, tokens), jnp.int32)
    for number in range(1, 4):
        piece = piece + jnp.where(expert >= number * count, 1, 0)
    local = expert - piece * count
    named = jnp.zeros((extent, tokens), F32)
    gate = jnp.zeros((extent, tokens), F32)
    for choice in range(ids.shape[0]):
        hit = ids[choice : choice + 1, :] == local
        named = named + jnp.where(hit, 1.0, 0.0)
        gate = gate + jnp.where(hit, gates[choice : choice + 1, :], 0.0)
    before = lax.broadcasted_iota(jnp.int32, (tokens, tokens), 0) < lax.broadcasted_iota(jnp.int32, (tokens, tokens), 1)
    earlier = jnp.dot(named.astype(BF16), jnp.where(before, 1.0, 0.0).astype(BF16), preferred_element_type=F32)
    place = jnp.where(named > 0.0, earlier + meta[2].astype(F32), -1.0)
    high, middle, low = pieces_of(gate)
    table = jnp.where(piece == 0, place, jnp.where(piece == 1, high, jnp.where(piece == 2, middle, low)))
    out[:, :width] = grad[...]
    out[:, width:] = table.T.astype(BF16)


def forward_body(meta, hidden, weight, out):
    rows = hidden[:, 0].reshape(out.shape[0], hidden.shape[3])
    out[...] = jnp.dot(rows, weight[...], preferred_element_type=F32).astype(BF16)


def turn_body(meta, hidden, after, out, final):
    value = hidden[:, 0].reshape(final.shape)
    out[0] = value.T
    final[...] = value


def turn_other_body(meta, hidden, out):
    out[...] = hidden[...].T


def selection(table, count, expert, rows):
    place = table[pl.ds(expert, 1), :]
    gate = table[pl.ds(expert + count, 1), :] + table[pl.ds(expert + 2 * count, 1), :]
    gate = gate + table[pl.ds(expert + 3 * count, 1), :]
    row = lax.broadcasted_iota(jnp.int32, (rows, place.shape[1]), 0).astype(F32)
    return row == place, gate


def grad_rows_body(peers, count, groups, meta, *refs):
    packed, tokens = refs[:groups], refs[groups : 2 * groups]
    outs, (table, choices, row_gates) = refs[2 * groups + 2 : -3], refs[-3:]
    rows = outs[0].shape[0] // groups

    @pl.when(pl.program_id(0) == 0)
    def _():
        for group in range(groups):
            table[...] = packed[group][...].astype(F32).T
            for peer in range(peers):
                match, gate = selection(table, count, lax.bitwise_xor(meta[3], peer), rows)
                part = pl.ds(peer * rows, rows)
                row_gates[group, part, :] = jnp.broadcast_to(
                    jnp.sum(jnp.where(match, gate, 0.0), 1, keepdims=True), (rows, 128)
                )
                choices[group, part, :] = jnp.where(match, 1.0, 0.0).astype(BF16)

    for group in range(groups):
        picked = jnp.dot(choices[group], tokens[group][...], preferred_element_type=F32)
        value = (picked * row_gates[group][:, :1]).astype(BF16)
        place = pl.ds(pl.multiple_of(lax.bitwise_xor(meta[1], group) * rows, rows), rows)
        for peer in range(peers):
            outs[peer][place, :] = value[peer * rows : (peer + 1) * rows]


def combine_body(peers, count, number, meta, *refs):
    packed, tokens, returned = refs[:number], refs[number : 2 * number], refs[2 * number + 1 : 2 * number + 1 + peers]
    part, table, weights, marks, inner = refs[-5:]
    rows, length = returned[0].shape[0], tokens[0].shape[0]
    step, last = pl.program_id(1), pl.num_programs(1) - 1

    def chosen(options):
        value = options[0][...]
        for at in range(1, number):
            value = jnp.where(pl.program_id(0) == at, options[at][...], value)
        return value

    @pl.when(step == 0)
    def _():
        inner[...] = jnp.zeros(inner.shape, F32)
        table[...] = chosen(packed).astype(F32).T
        highs, lows = [], []
        for peer in range(peers):
            match, gate = selection(table, count, lax.bitwise_xor(meta[3], peer), rows)
            high = gate.astype(BF16).astype(F32)
            marks[pl.ds(peer * rows, rows), :] = jnp.where(match, 1.0, 0.0)
            highs.append(jnp.where(match, high, 0.0))
            lows.append(jnp.where(match, gate - high, 0.0))
        weights[:length, :] = jnp.concatenate(highs, 0).T.astype(BF16)
        weights[length:, :] = jnp.concatenate(lows, 0).T.astype(BF16)

    @pl.when(step < last)
    def _():
        value = jnp.concatenate([ref[...] for ref in returned], 0)
        chunk = min(512, value.shape[1])
        for start in range(0, value.shape[1], chunk):
            total = jnp.dot(weights[...], value[:, start : start + chunk], preferred_element_type=F32)
            part[:, start : start + chunk] = (total[:length] + total[length:]).astype(part.dtype)
        products = lax.dot_general(value, chosen(tokens), (((1,), (1,)), ((), ())), preferred_element_type=F32)
        products = products * marks[...]
        for peer in range(peers):
            inner[peer : peer + 1, :] += jnp.sum(products[peer * rows : (peer + 1) * rows], 0, keepdims=True)

    @pl.when(step == last)
    def _():
        extent = -(-3 * count // 128) * 128
        row = lax.broadcasted_iota(jnp.int32, (extent, length), 0)
        placed = jnp.zeros((extent, length), F32)
        for at, piece in enumerate(pieces_of(inner[...])):
            for peer in range(peers):
                place = at * count + lax.bitwise_xor(meta[3], peer)
                placed = jnp.where(row == place, piece[peer : peer + 1, :], placed)
        part[:, :extent] = placed.T.astype(part.dtype)


def inside_body(halves, meta, *refs):
    rows, weights, (out, token) = refs[:halves], refs[halves : 2 * halves], refs[-2:]
    contract = (((1,), (1,)), ((), ()))
    value = lax.dot_general(rows[0][...], weights[0][...], contract, preferred_element_type=F32)
    for half in range(1, halves):
        value = value + lax.dot_general(rows[half][...], weights[half][...], contract, preferred_element_type=F32)
    out[:, 0] = value.astype(BF16).reshape(out.shape[0], out.shape[2], out.shape[3])
    token[...] = jnp.zeros(token.shape, F32)


def weight_grad_body(number, half, meta, turned, *refs):
    rows, others, own = refs[:number], refs[-half - 1 : -1], refs[-1]
    value = jnp.dot(turned[0], rows[0][...], preferred_element_type=F32)
    for peer in range(1, number):
        value = value + jnp.dot(turned[peer], rows[peer][...], preferred_element_type=F32)
    step = pl.program_id(0)
    for at in range(half):

        @pl.when(step == at)
        def _():
            others[at][...] = value.astype(BF16)

    @pl.when(step >= half)
    def _():
        own[...] = value


def last_body(half, meta, turned, rows, turned_other, rows_other, earlier, *refs):
    others, grads = refs[:half], refs[-1]
    value = jnp.dot(turned[0], rows[...], preferred_element_type=F32)
    value = value + jnp.dot(turned_other[...], rows_other[...], preferred_element_type=F32) + earlier[...]
    for at in range(half):

        @pl.when(pl.program_id(0) * half // pl.num_programs(0) == at)
        def _():
            grads[...] = (value + others[at][...].astype(F32)).astype(BF16)


def finish_body(count, meta, after, ids, kept, arrived, combined, gate_grads):
    width = combined.shape[1]
    combined[...] = (kept[:, :width] + arrived[:, :width].astype(F32)).astype(BF16)
    pieces = (kept[:, width:] + arrived[:, width:].astype(F32)).T
    inner = pieces[:count] + pieces[count : 2 * count] + pieces[2 * count : 3 * count]
    named = ids[...]
    found = jnp.zeros(gate_grads.shape, F32)
    for expert in range(count):
        found = found + jnp.where(named == expert, inner[expert : expert + 1, :], 0.0)
    gate_grads[...] = found


def per_device(expert_ids, gates, hidden, weight, out_grad):
    count = lax.axis_size("expert")
    peers = 1 << ((count.bit_length() - 1) // 2)
    planes = count // peers
    tokens, top = expert_ids.shape
    cap = hidden.shape[1] // count
    width, inside = out_grad.shape[1], hidden.shape[2]
    fold = 1
    while fold * cap % 16:
        fold *= 2
    groups = planes // fold
    group_rows, group_tokens = fold * cap, fold * tokens
    rows = planes * cap
    tile = min(512, width // 2)
    steps = width // tile
    half = steps // 2
    large = width // 2
    room = 1 if fold == 1 else 3
    last = peers - 1
    anywhere = pl.BlockSpec(memory_space=pl.ANY)
    glance = pl.BlockSpec((16, 128), lambda *i: (0, 0))

    me = lax.axis_index("expert")
    core = lax.axis_index("dp")
    column, plane = me % peers, me // peers
    meta = jnp.stack([column, plane // fold, (plane % fold) * cap, me, core, plane, count]).astype(jnp.int32)

    def swap(value, distance):
        return lax.ppermute(value, "expert", [(e, e ^ distance) for e in range(count)])

    def exchange(value):
        return lax.ppermute(value, "dp", [(0, 1), (1, 0)])

    matrix = weight[0]
    if fold == 1:
        blocks = hidden.reshape(planes, peers, cap, inside)
    else:
        blocks = hidden.reshape(planes, peers, cap, inside).transpose(1, 0, 2, 3).reshape(1, peers, rows, inside)
    block = (blocks.shape[0], 1, blocks.shape[2], inside)

    ids_turned = expert_ids.T
    extent = -(-4 * count // 128) * 128
    short = pl.BlockSpec((top, tokens), lambda i, m: (0, 0))
    packed = call(
        pack_body, "pack", (1,),
        [short, short, pl.BlockSpec((tokens, width), lambda i, m: (0, 0))],
        pl.BlockSpec((tokens, width + extent), lambda i, m: (0, 0)),
        jax.ShapeDtypeStruct((tokens, width + extent), BF16),
        meta, (ids_turned, gates.T, out_grad),
        room=room,
    )
    gathered = [packed]
    for k in range(1, planes):
        lowest = k & -k
        gathered.append(swap(gathered[k ^ lowest], peers * lowest))
    early = gathered[1:3]
    if fold > 1:
        gathered = [jnp.concatenate(gathered[g * fold : (g + 1) * fold], 0) for g in range(groups)]

    def forward(peer, after):
        return call(
            lambda meta, *refs: forward_body(meta, refs[0], refs[1], refs[-1]), f"forward{peer}", (steps,),
            [
                pl.BlockSpec(block, lambda i, m: (0, lax.bitwise_xor(m[0], peer), 0, 0)),
                pl.BlockSpec((inside, tile), lambda i, m: (0, i)),
            ]
            + [glance] * len(after),
            pl.BlockSpec((rows, tile), lambda i, m: (0, i)),
            jax.ShapeDtypeStruct((rows, width), BF16),
            meta, (blocks, matrix, *after),
        )

    outputs, after = {}, ()
    for peer in list(range(1, peers)) + [0]:
        outputs[peer] = forward(peer, after)
        after = (outputs[peer], packed)
    returned = [outputs[0]] + [swap(outputs[peer], peer) for peer in range(1, last)]
    turned, hidden_last = call(
        turn_body, "turn", (peers,),
        [pl.BlockSpec(block, lambda i, m: (0, lax.bitwise_xor(m[0], i), 0, 0)), glance],
        [pl.BlockSpec((1, inside, rows), lambda i, m: (i, 0, 0)), pl.BlockSpec((rows, inside), lambda i, m: (0, 0))],
        [jax.ShapeDtypeStruct((peers, inside, rows), BF16), jax.ShapeDtypeStruct((rows, inside), BF16)],
        meta, (blocks, outputs[0]),
    )

    turned_other = call(
        turn_other_body, "turn_other", (1,),
        [pl.BlockSpec((rows, inside), lambda i, m: (0, 0))],
        pl.BlockSpec((inside, rows), lambda i, m: (0, 0)),
        jax.ShapeDtypeStruct((inside, rows), BF16),
        meta, (exchange(hidden_last),),
    )
    final_output = follow(outputs[last], *returned[1:], turned_other, *early)
    returned.append(swap(final_output, last))

    def turned_column(i, m):
        return lax.bitwise_xor(i, (1 - m[4]) * half)

    def turned_half(i, m):
        return lax.bitwise_xor(i, 1 - m[4])

    grad_rows = call(
        functools.partial(grad_rows_body, peers, count, groups), "grad_rows", (2,),
        [pl.BlockSpec((group_tokens, extent), lambda i, m: (0, width // extent))] * groups
        + [pl.BlockSpec((group_tokens, large), lambda i, m: (0, turned_half(i, m)))] * groups
        + [glance] * 2,
        [pl.BlockSpec((rows, large), lambda i, m: (0, turned_half(i, m)))] * last
        + [pl.BlockSpec((rows, large), lambda i, m: (i, 0))],
        [jax.ShapeDtypeStruct((rows, width), BF16)] * last + [jax.ShapeDtypeStruct((2 * rows, large), BF16)],
        meta, (*gathered, *gathered, final_output, turned_other),
        scratch=[
            pltpu.VMEM((extent, group_tokens), F32),
            pltpu.VMEM((groups, peers * group_rows, group_tokens), BF16),
            pltpu.VMEM((groups, peers * group_rows, 128), F32),
        ],
        room=room,
    )
    arrived = [grad_rows[0]] + [swap(grad_rows[peer], peer) for peer in range(1, last)]

    padded = width + -(-3 * count // 128) * 128

    def combine(chosen, dtype, after):
        first, stride = chosen[0], len(chosen) > 1 and chosen[1] - chosen[0]
        columns = width if fold == 1 else large

        def part_of(k, i, m):
            return (lax.bitwise_xor(m[1], k * stride + first), jnp.minimum(i, width // columns - 1))

        blocks_of = [gathered[group] for group in chosen]
        return call(
            functools.partial(combine_body, peers, count, len(chosen)), f"combine{first}", (len(chosen), width // columns + 1),
            [pl.BlockSpec((group_tokens, extent), lambda k, i, m: (0, width // extent))] * len(chosen)
            + [pl.BlockSpec((group_tokens, columns), lambda k, i, m: (0, jnp.minimum(i, width // columns - 1)))] * len(chosen)
            + [glance]
            + [pl.BlockSpec((group_rows, columns), part_of)] * peers,
            pl.BlockSpec((group_tokens, columns), lambda k, i, m: (k, i)),
            jax.ShapeDtypeStruct((len(chosen) * group_tokens, padded), dtype),
            meta, (*blocks_of, *blocks_of, after, *returned),
            scratch=[
                pltpu.VMEM((extent, group_tokens), F32),
                pltpu.VMEM((2 * group_tokens, peers * group_rows), BF16),
                pltpu.VMEM((peers * group_rows, group_tokens), F32),
                pltpu.VMEM((peers, group_tokens), F32),
            ],
            room=room,
        )

    if fold == 1:
        leaving = combine(range(1, planes, 2), BF16, grad_rows[0])
        combine_done = combine(range(0, planes, 2), F32, leaving)
        sums = [combine_done[k * tokens : (k + 1) * tokens] for k in range(planes // 2)]
    else:
        parts = [combine([group], F32, grad_rows[0]) for group in range(groups)]
        combine_done = parts[-1]
        sums = [parts[k // fold][k % fold * tokens : (k % fold + 1) * tokens] for k in range(planes)]
        leaving = jnp.concatenate(sums[1::2], 0).astype(BF16)
        sums = sums[0::2]
    distance = 1
    first_sums = None
    while len(sums) > 1:
        got = swap(leaving, peers * distance)
        pieces = [got[k * tokens : (k + 1) * tokens].astype(F32) for k in range(len(sums))]
        sums = [mine + piece for mine, piece in zip(sums, pieces)]
        leaving = [value.astype(BF16) for value in sums[1::2]]
        leaving = leaving[0] if len(leaving) == 1 else jnp.concatenate(leaving, 0)
        sums = sums[0::2]
        first_sums = leaving if first_sums is None else first_sums
        distance *= 2
    got = swap(leaving, peers * distance)

    final_rows = follow(grad_rows[last], *arrived[1:last], combine_done)
    arrived.append(swap(final_rows, last))

    grads_shape = jax.ShapeDtypeStruct(blocks.shape, BF16)
    depth = min(256, inside)

    def inside_grad(peer, earlier, after):
        halves = width // arrived[peer].shape[1]

        def weight_at(half):
            if halves == 1:
                return lambda i, m: (i, 0)
            return lambda i, m: (i, lax.bitwise_xor(1 - m[4], half))

        return call(
            functools.partial(inside_body, halves), f"inside{peer}", (inside // depth,),
            [pl.BlockSpec((rows, width // halves), lambda i, m, half=half: (half, 0)) for half in range(halves)]
            + [pl.BlockSpec((depth, width // halves), weight_at(half)) for half in range(halves)]
            + ([] if earlier is None else [anywhere])
            + [glance] * len(after),
            [
                pl.BlockSpec(block[:3] + (depth,), lambda i, m: (0, lax.bitwise_xor(m[0], peer), 0, i)),
                pl.BlockSpec((16, 128), lambda i, m: (0, 0)),
            ],
            [grads_shape, jax.ShapeDtypeStruct((16, 128), F32)],
            meta,
            (*[arrived[peer]] * halves, *[matrix] * halves, *(() if earlier is None else (earlier,)), *after),
            aliases=None if earlier is None else {1 + 2 * halves: 0},
        )

    *totals_other, total_own = call(
        functools.partial(weight_grad_body, last, half), "weight_grad", (steps,),
        [pl.BlockSpec((peers, inside, rows), lambda i, m: (0, 0, 0))]
        + [pl.BlockSpec((rows, tile), lambda i, m: (0, turned_column(i, m)))] * last
        + [glance] * 2,
        [pl.BlockSpec((inside, tile), lambda i, m: (0, 0))] * half
        + [pl.BlockSpec((inside, tile), lambda i, m: (0, jnp.maximum(i - half, 0)))],
        [jax.ShapeDtypeStruct((inside, tile), BF16)] * half + [jax.ShapeDtypeStruct((inside, large), F32)],
        meta, (turned, *arrived[:last], final_rows, first_sums),
        room=room,
    )
    hidden_grads = None
    for peer in range(last):
        hidden_grads, token = inside_grad(peer, hidden_grads, (total_own,))
    totals_other = [exchange(value) for value in totals_other]
    rows_other = exchange(follow(arrived[last][:rows], got, token))

    combined, gate_grads = call(
        functools.partial(finish_body, count), "finish", (1,),
        [
            glance, pl.BlockSpec((top, tokens), lambda i, m: (0, 0)),
            pl.BlockSpec((tokens, padded), lambda i, m: (0, 0)), pl.BlockSpec((tokens, padded), lambda i, m: (0, 0)),
        ],
        [pl.BlockSpec((tokens, width), lambda i, m: (0, 0)), pl.BlockSpec((top, tokens), lambda i, m: (0, 0))],
        [jax.ShapeDtypeStruct((tokens, width), BF16), jax.ShapeDtypeStruct((top, tokens), F32)],
        meta, (total_own, ids_turned, sums[0], got),
    )
    hidden_grads, _ = inside_grad(last, hidden_grads, ())
    fine = tile // 2 if tile >= 256 else tile
    each = tile // fine
    fine_spec = pl.BlockSpec((inside, fine), lambda i, m: (0, i))
    weight_grads = call(
        functools.partial(last_body, half), "last", (large // fine,),
        [
            pl.BlockSpec((1, inside, rows), lambda i, m: (last, 0, 0)),
            pl.BlockSpec((rows, fine), lambda i, m: (1, i)),
            pl.BlockSpec((inside, rows), lambda i, m: (0, 0)),
            pl.BlockSpec((rows, fine), lambda i, m: (0, i)),
            fine_spec,
        ]
        + [
            pl.BlockSpec((inside, fine), lambda i, m, at=at: (0, jnp.clip(i - at * each, 0, each - 1)))
            for at in range(half)
        ],
        fine_spec,
        jax.ShapeDtypeStruct((inside, large), BF16),
        meta, (turned, arrived[last], turned_other, rows_other, total_own, *totals_other),
        room=room,
    )

    if fold > 1:
        hidden_grads = hidden_grads.reshape(peers, planes, cap, inside).transpose(1, 0, 2, 3)
    return combined, gate_grads.T, hidden_grads.reshape(hidden.shape), weight_grads[None]


def solution(mesh):
    placed = (
        P(("expert", "dp"), None),
        P(("expert", "dp"), None),
        P("expert", "dp", None),
        P("expert", None, None),
        P(("expert", "dp"), None),
    )
    return jax.shard_map(
        per_device,
        mesh=mesh,
        in_specs=placed,
        out_specs=(
            P(("expert", "dp"), None),
            P(("expert", "dp"), None),
            P("expert", "dp", None),
            P("expert", None, "dp"),
        ),
        check_vma=False,
    )
```

```python
import functools

import jax
import jax.numpy as jnp
from jax import lax
from jax.experimental import pallas as pl
from jax.experimental.pallas import tpu as pltpu
from jax.sharding import PartitionSpec as P

F32 = jnp.float32
BF16 = jnp.bfloat16
VMEM_BYTES = 16 * 1024 * 1024
COST = 1024
NEAR_COST = 10**10


def call(body, name, grid, in_specs, out_specs, out_shape, scalars, operands, scratch=(), aliases=None, room=1, cost=COST):
    return pl.pallas_call(
        body,
        name=name,
        grid_spec=pltpu.PrefetchScalarGridSpec(
            num_scalar_prefetch=1, grid=grid, in_specs=in_specs, out_specs=out_specs, scratch_shapes=scratch
        ),
        out_shape=out_shape,
        input_output_aliases=aliases or {},
        cost_estimate=pl.CostEstimate(flops=cost, bytes_accessed=COST, transcendentals=0),
        compiler_params=pltpu.CompilerParams(vmem_limit_bytes=room * VMEM_BYTES),
    )(scalars, *operands)


def follow(value, *earlier):
    anywhere = pl.BlockSpec(memory_space=pl.ANY)
    return pl.pallas_call(
        lambda *refs: None,
        name="follow",
        grid=(1,),
        in_specs=[anywhere] + [pl.BlockSpec((16, 128), lambda i: (0, 0))] * len(earlier),
        out_specs=anywhere,
        out_shape=jax.ShapeDtypeStruct(value.shape, value.dtype),
        input_output_aliases={0: 0},
        cost_estimate=pl.CostEstimate(flops=COST, bytes_accessed=COST, transcendentals=0),
        compiler_params=pltpu.CompilerParams(vmem_limit_bytes=VMEM_BYTES),
    )(value, *earlier)


def pieces_of(value):
    high = value.astype(BF16).astype(F32)
    middle = (value - high).astype(BF16).astype(F32)
    return high, middle, value - high - middle


def pack_body(meta, ids, gates, grad, out, *sides):
    width, tokens = grad.shape[1], grad.shape[0]
    extent = out.shape[1] - width
    count = meta[6]
    expert = lax.broadcasted_iota(jnp.int32, (extent, tokens), 0)
    piece = jnp.zeros((extent, tokens), jnp.int32)
    for number in range(1, 4):
        piece = piece + jnp.where(expert >= number * count, 1, 0)
    local = expert - piece * count
    named = jnp.zeros((extent, tokens), F32)
    gate = jnp.zeros((extent, tokens), F32)
    for choice in range(ids.shape[0]):
        hit = ids[choice : choice + 1, :] == local
        named = named + jnp.where(hit, 1.0, 0.0)
        gate = gate + jnp.where(hit, gates[choice : choice + 1, :], 0.0)
    before = lax.broadcasted_iota(jnp.int32, (tokens, tokens), 0) < lax.broadcasted_iota(jnp.int32, (tokens, tokens), 1)
    earlier = jnp.dot(named.astype(BF16), jnp.where(before, 1.0, 0.0).astype(BF16), preferred_element_type=F32)
    place = jnp.where(named > 0.0, earlier + meta[2].astype(F32), -1.0)
    high, middle, low = pieces_of(gate)
    table = jnp.where(piece == 0, place, jnp.where(piece == 1, high, jnp.where(piece == 2, middle, low)))
    table = table.T.astype(BF16)
    out[:, :width] = grad[...]
    out[:, width:] = table
    large = width // 2
    for number, side in enumerate(sides):
        start = pl.multiple_of(lax.bitwise_xor(1 - meta[4], number) * large, large)
        side[:, :large] = grad[:, pl.ds(start, large)]
        side[:, large:] = table


def collect_body(number, meta, *refs):
    tables, sides, outs = refs[:number], (refs[number : 2 * number], refs[2 * number : 3 * number]), refs[-2:]
    tokens = tables[0].shape[0]
    for side, out in zip(sides, outs):
        large = side[0].shape[1]
        for k in range(number):
            out[k * tokens : (k + 1) * tokens, :large] = side[k][...]
            out[k * tokens : (k + 1) * tokens, large:] = tables[k][...]


def forward_body(meta, hidden, weight, out):
    rows = hidden[:, 0].reshape(out.shape[0], hidden.shape[3])
    out[...] = jnp.dot(rows, weight[...], preferred_element_type=F32).astype(BF16)


def turn_body(meta, hidden, after, out, final):
    value = hidden[:, 0].reshape(final.shape)
    out[0] = value.T
    final[...] = value


def turn_other_body(meta, hidden, out):
    out[...] = hidden[...].T


def selection(table, count, expert, rows):
    place = table[pl.ds(expert, 1), :]
    gate = table[pl.ds(expert + count, 1), :] + table[pl.ds(expert + 2 * count, 1), :]
    gate = gate + table[pl.ds(expert + 3 * count, 1), :]
    row = lax.broadcasted_iota(jnp.int32, (rows, place.shape[1]), 0).astype(F32)
    return row == place, gate


def grad_rows_body(plan, jobs, count, groups, meta, *refs):
    number = jobs * groups
    tables, tokens, outs, table = refs[:number], refs[number : 2 * number], refs[-1 - len(plan) : -1], refs[-1]
    rows = outs[0].shape[0] // len(plan[0][1]) // groups
    for job in range(jobs):
        asked = [(out, peer, parts.index(job)) for out, (peer, parts) in zip(outs, plan) if job in parts]
        for group in range(groups):
            table[...] = tables[job * groups + group][...].astype(F32).T
            choices, row_gates = [], []
            for _, peer, _ in asked:
                match, gate = selection(table, count, lax.bitwise_xor(meta[3], peer), rows)
                choices.append(jnp.where(match, 1.0, 0.0))
                row_gates.append(jnp.sum(jnp.where(match, gate, 0.0), 1, keepdims=True))
            choice = jnp.concatenate(choices, 0).astype(BF16)
            picked = jnp.dot(choice, tokens[job * groups + group][...], preferred_element_type=F32)
            value = (picked * jnp.concatenate(row_gates, 0)).astype(BF16)
            place = pl.multiple_of(lax.bitwise_xor(meta[1], group) * rows, rows)
            for at, (out, _, part) in enumerate(asked):
                out[pl.ds(place + part * groups * rows, rows), :] = value[at * rows : (at + 1) * rows]


def combine_body(peers, count, number, meta, *refs):
    packed, tokens, returned = refs[:number], refs[number : 2 * number], refs[2 * number + 1 : 2 * number + 1 + peers]
    part, table, weights, marks, inner = refs[-5:]
    rows, length = returned[0].shape[0], tokens[0].shape[0]
    step, last = pl.program_id(1), pl.num_programs(1) - 1

    def chosen(options):
        value = options[0][...]
        for at in range(1, number):
            value = jnp.where(pl.program_id(0) == at, options[at][...], value)
        return value

    @pl.when(step == 0)
    def _():
        inner[...] = jnp.zeros(inner.shape, F32)
        table[...] = chosen(packed).astype(F32).T
        highs, lows = [], []
        for peer in range(peers):
            match, gate = selection(table, count, lax.bitwise_xor(meta[3], peer), rows)
            high = gate.astype(BF16).astype(F32)
            marks[pl.ds(peer * rows, rows), :] = jnp.where(match, 1.0, 0.0)
            highs.append(jnp.where(match, high, 0.0))
            lows.append(jnp.where(match, gate - high, 0.0))
        weights[:length, :] = jnp.concatenate(highs, 0).T.astype(BF16)
        weights[length:, :] = jnp.concatenate(lows, 0).T.astype(BF16)

    @pl.when(step < last)
    def _():
        value = jnp.concatenate([ref[...] for ref in returned], 0)
        chunk = min(512, value.shape[1])
        for start in range(0, value.shape[1], chunk):
            total = jnp.dot(weights[...], value[:, start : start + chunk], preferred_element_type=F32)
            part[:, start : start + chunk] = (total[:length] + total[length:]).astype(part.dtype)
        products = lax.dot_general(value, chosen(tokens), (((1,), (1,)), ((), ())), preferred_element_type=F32)
        products = products * marks[...]
        for peer in range(peers):
            inner[peer : peer + 1, :] += jnp.sum(products[peer * rows : (peer + 1) * rows], 0, keepdims=True)

    @pl.when(step == last)
    def _():
        extent = -(-3 * count // 128) * 128
        row = lax.broadcasted_iota(jnp.int32, (extent, length), 0)
        placed = jnp.zeros((extent, length), F32)
        for at, piece in enumerate(pieces_of(inner[...])):
            for peer in range(peers):
                place = at * count + lax.bitwise_xor(meta[3], peer)
                placed = jnp.where(row == place, piece[peer : peer + 1, :], placed)
        part[:, :extent] = placed.T.astype(part.dtype)


def inside_body(halves, meta, *refs):
    rows, weights, (out, token) = refs[:halves], refs[halves : 2 * halves], refs[-2:]
    contract = (((1,), (1,)), ((), ()))
    value = lax.dot_general(rows[0][...], weights[0][...], contract, preferred_element_type=F32)
    for half in range(1, halves):
        value = value + lax.dot_general(rows[half][...], weights[half][...], contract, preferred_element_type=F32)
    out[:, 0] = value.astype(BF16).reshape(out.shape[0], out.shape[2], out.shape[3])
    token[...] = jnp.zeros(token.shape, F32)


def weight_grad_body(number, half, meta, turned, *refs):
    sides, others, own = (refs[:number], refs[number : 2 * number]), refs[-half - 1 : -1], refs[-1]
    step = pl.program_id(0)

    def value_of(side):
        value = jnp.dot(turned[0], side[0][...], preferred_element_type=F32)
        for peer in range(1, number):
            value = value + jnp.dot(turned[peer], side[peer][...], preferred_element_type=F32)
        return value

    for at in range(half):

        @pl.when(step == at)
        def _():
            others[at][...] = value_of(sides[0]).astype(BF16)

    @pl.when(step >= half)
    def _():
        own[...] = value_of(sides[1])


def last_body(half, meta, turned, rows, turned_other, rows_other, earlier, *refs):
    others, grads = refs[:half], refs[-1]
    value = jnp.dot(turned[0], rows[...], preferred_element_type=F32)
    value = value + jnp.dot(turned_other[...], rows_other[...], preferred_element_type=F32) + earlier[...]
    for at in range(half):

        @pl.when(pl.program_id(0) * half // pl.num_programs(0) == at)
        def _():
            grads[...] = (value + others[at][...].astype(F32)).astype(BF16)


def finish_body(count, meta, after, ids, kept, arrived, combined, gate_grads):
    width = combined.shape[1]
    combined[...] = (kept[:, :width] + arrived[:, :width].astype(F32)).astype(BF16)
    pieces = (kept[:, width:] + arrived[:, width:].astype(F32)).T
    inner = pieces[:count] + pieces[count : 2 * count] + pieces[2 * count : 3 * count]
    named = ids[...]
    found = jnp.zeros(gate_grads.shape, F32)
    for expert in range(count):
        found = found + jnp.where(named == expert, inner[expert : expert + 1, :], 0.0)
    gate_grads[...] = found


def per_device(expert_ids, gates, hidden, weight, out_grad):
    count = lax.axis_size("expert")
    peers = 1 << ((count.bit_length() - 1) // 2)
    planes = count // peers
    tokens, top = expert_ids.shape
    cap = hidden.shape[1] // count
    width, inside = out_grad.shape[1], hidden.shape[2]
    fold = 1
    while fold * cap % 16:
        fold *= 2
    groups = planes // fold
    group_rows, group_tokens = fold * cap, fold * tokens
    rows = planes * cap
    tile = min(512, width // 2)
    steps = width // tile
    half = steps // 2
    large = width // 2
    room = 1 if fold == 1 else 3
    last = peers - 1
    anywhere = pl.BlockSpec(memory_space=pl.ANY)
    glance = pl.BlockSpec((16, 128), lambda *i: (0, 0))

    me = lax.axis_index("expert")
    core = lax.axis_index("dp")
    column, plane = me % peers, me // peers
    meta = jnp.stack([column, plane // fold, (plane % fold) * cap, me, core, plane, count]).astype(jnp.int32)

    def swap(value, distance):
        return lax.ppermute(value, "expert", [(e, e ^ distance) for e in range(count)])

    def exchange(value):
        return lax.ppermute(value, "dp", [(0, 1), (1, 0)])

    matrix = weight[0]
    if fold == 1:
        blocks = hidden.reshape(planes, peers, cap, inside)
    else:
        blocks = hidden.reshape(planes, peers, cap, inside).transpose(1, 0, 2, 3).reshape(1, peers, rows, inside)
    block = (blocks.shape[0], 1, blocks.shape[2], inside)

    ids_turned = expert_ids.T
    extent = -(-4 * count // 128) * 128
    short = pl.BlockSpec((top, tokens), lambda i, m: (0, 0))
    relay = peers == 4 and fold == 1
    packed, *near = call(
        pack_body, "pack", (1,),
        [short, short, pl.BlockSpec((tokens, width), lambda i, m: (0, 0))],
        [pl.BlockSpec((tokens, width + extent), lambda i, m: (0, 0))]
        + [pl.BlockSpec((tokens, large + extent), lambda i, m: (0, 0))] * (2 * relay),
        [jax.ShapeDtypeStruct((tokens, width + extent), BF16)]
        + [jax.ShapeDtypeStruct((tokens, large + extent), BF16)] * (2 * relay),
        meta, (ids_turned, gates.T, out_grad),
        room=room,
    )
    near = [swap(value, 1 << number) for number, value in enumerate(near)]
    gathered = [packed]
    for k in range(1, planes):
        lowest = k & -k
        gathered.append(swap(gathered[k ^ lowest], peers * lowest))
    early = gathered[1:3]
    if fold > 1:
        gathered = [jnp.concatenate(gathered[g * fold : (g + 1) * fold], 0) for g in range(groups)]

    def forward(peer, after):
        return call(
            lambda meta, *refs: forward_body(meta, refs[0], refs[1], refs[-1]), f"forward{peer}", (steps,),
            [
                pl.BlockSpec(block, lambda i, m: (0, lax.bitwise_xor(m[0], peer), 0, 0)),
                pl.BlockSpec((inside, tile), lambda i, m: (0, i)),
            ]
            + [glance] * len(after),
            pl.BlockSpec((rows, tile), lambda i, m: (0, i)),
            jax.ShapeDtypeStruct((rows, width), BF16),
            meta, (blocks, matrix, *after),
        )

    outputs, after = {}, (packed,)
    for peer in list(range(1, peers)) + [0]:
        outputs[peer] = forward(peer, after)
        after = (outputs[peer], *near)
    returned = [outputs[0]] + [swap(outputs[peer], peer) for peer in range(1, last)]
    turned, hidden_last = call(
        turn_body, "turn", (peers,),
        [pl.BlockSpec(block, lambda i, m: (0, lax.bitwise_xor(m[0], i), 0, 0)), glance],
        [pl.BlockSpec((1, inside, rows), lambda i, m: (i, 0, 0)), pl.BlockSpec((rows, inside), lambda i, m: (0, 0))],
        [jax.ShapeDtypeStruct((peers, inside, rows), BF16), jax.ShapeDtypeStruct((rows, inside), BF16)],
        meta, (blocks, outputs[0]),
    )

    turned_other = call(
        turn_other_body, "turn_other", (1,),
        [pl.BlockSpec((rows, inside), lambda i, m: (0, 0))],
        pl.BlockSpec((inside, rows), lambda i, m: (0, 0)),
        jax.ShapeDtypeStruct((inside, rows), BF16),
        meta, (exchange(hidden_last),),
    )
    final_output = follow(outputs[last], *returned[1:], turned_other, *early)
    returned.append(swap(final_output, last))

    def other_half(i, m):
        return (0, 1 - m[4])

    def own_half(i, m):
        return (0, m[4])

    def build_rows(name, plan, jobs, after, cost=COST):
        sources = [source for job in jobs for source in job]
        return call(
            functools.partial(grad_rows_body, plan, len(jobs), count, groups), name, (1,),
            [pl.BlockSpec((group_tokens, extent), table_at) for _, table_at, _ in sources]
            + [pl.BlockSpec((group_tokens, large), data_at) for _, _, data_at in sources]
            + [glance] * len(after),
            [pl.BlockSpec((len(parts) * rows, large), lambda i, m: (0, 0)) for _, parts in plan],
            [jax.ShapeDtypeStruct((len(parts) * rows, large), BF16) for _, parts in plan],
            meta, (*[value for value, _, _ in sources] * 2, *after),
            scratch=[pltpu.VMEM((extent, group_tokens), F32)],
            room=room, cost=cost,
        )

    def beside(i, m):
        return (0, width // extent)

    jobs = [[(value, beside, at) for value in gathered] for at in (other_half, own_half)]
    if relay:
        collected = call(
            functools.partial(collect_body, planes - 1), "collect", (1,),
            [pl.BlockSpec((tokens, extent), beside)] * (planes - 1)
            + [pl.BlockSpec((tokens, large), other_half)] * (planes - 1)
            + [pl.BlockSpec((tokens, large), own_half)] * (planes - 1)
            + [glance],
            [pl.BlockSpec(((planes - 1) * tokens, large + extent), lambda i, m: (0, 0))] * 2,
            [jax.ShapeDtypeStruct(((planes - 1) * tokens, large + extent), BF16)] * 2,
            meta, (*gathered[1:] * 3, final_output),
            room=room,
        )
        rest = [swap(value, 1 << number) for number, value in enumerate(collected)]
        made = build_rows("own_rows", ((0, (0, 1)), (1, (1,)), (2, (0,))), jobs, (collected[0],))
        arrived = [
            [(made[0], 0), (made[0], 1)], [None, (swap(made[1], 1), 0)], [(swap(made[2], 2), 0), None], [None, None],
        ]
    else:
        made = build_rows("own_rows", tuple((peer, (0, 1)) for peer in range(peers)), jobs, (final_output,))
        arrived = [[(made[0], 0), (made[0], 1)]]
        for peer in range(1, peers):
            got = swap(made[peer], peer)
            arrived.append([(got, 0), (got, 1)])

    padded = width + -(-3 * count // 128) * 128

    def combine(chosen, dtype, after):
        first, stride = chosen[0], len(chosen) > 1 and chosen[1] - chosen[0]
        columns = width if fold == 1 else large

        def part_of(k, i, m):
            return (lax.bitwise_xor(m[1], k * stride + first), jnp.minimum(i, width // columns - 1))

        blocks_of = [gathered[group] for group in chosen]
        return call(
            functools.partial(combine_body, peers, count, len(chosen)), f"combine{first}", (len(chosen), width // columns + 1),
            [pl.BlockSpec((group_tokens, extent), lambda k, i, m: (0, width // extent))] * len(chosen)
            + [pl.BlockSpec((group_tokens, columns), lambda k, i, m: (0, jnp.minimum(i, width // columns - 1)))] * len(chosen)
            + [glance]
            + [pl.BlockSpec((group_rows, columns), part_of)] * peers,
            pl.BlockSpec((group_tokens, columns), lambda k, i, m: (k, i)),
            jax.ShapeDtypeStruct((len(chosen) * group_tokens, padded), dtype),
            meta, (*blocks_of, *blocks_of, after, *returned),
            scratch=[
                pltpu.VMEM((extent, group_tokens), F32),
                pltpu.VMEM((2 * group_tokens, peers * group_rows), BF16),
                pltpu.VMEM((peers * group_rows, group_tokens), F32),
                pltpu.VMEM((peers, group_tokens), F32),
            ],
            room=room,
        )

    if fold == 1:
        leaving = combine(range(1, planes, 2), BF16, made[0])
        combine_done = combine(range(0, planes, 2), F32, leaving)
        sums = [combine_done[k * tokens : (k + 1) * tokens] for k in range(planes // 2)]
    else:
        parts = [combine([group], F32, made[0]) for group in range(groups)]
        combine_done = parts[-1]
        sums = [parts[k // fold][k % fold * tokens : (k % fold + 1) * tokens] for k in range(planes)]
        leaving = jnp.concatenate(sums[1::2], 0).astype(BF16)
        sums = sums[0::2]
    distance = 1
    first_sums = None
    while len(sums) > 1:
        got = swap(leaving, peers * distance)
        pieces = [got[k * tokens : (k + 1) * tokens].astype(F32) for k in range(len(sums))]
        sums = [mine + piece for mine, piece in zip(sums, pieces)]
        leaving = [value.astype(BF16) for value in sums[1::2]]
        leaving = leaving[0] if len(leaving) == 1 else jnp.concatenate(leaving, 0)
        sums = sums[0::2]
        first_sums = leaving if first_sums is None else first_sums
        distance *= 2
    summed = swap(leaving, peers * distance)

    if relay:
        near_jobs = [
            [(first, lambda i, m: (0, large // extent), lambda i, m: (0, 0))]
            + [(others, lambda i, m, k=k: (k, large // extent), lambda i, m, k=k: (k, 0)) for k in range(planes - 1)]
            for first, others in zip(near, rest)
        ]
        plan = ((0, (0,)), (2, (0,)), (0, (1,)), (1, (1,)))
        made = build_rows("near_rows", plan, near_jobs, (combine_done,), NEAR_COST)
        arrived[1][0], arrived[2][1] = (made[0], 0), (made[2], 0)
        arrived[3] = [(swap(made[1], 2), 0), (swap(made[3], 1), 0)]

    grads_shape = jax.ShapeDtypeStruct(blocks.shape, BF16)
    depth = min(256, inside)

    def inside_grad(peer, earlier, after):
        return call(
            functools.partial(inside_body, 2), f"inside{peer}", (inside // depth,),
            [pl.BlockSpec((rows, large), lambda i, m, at=at: (at, 0)) for _, at in arrived[peer]]
            + [pl.BlockSpec((depth, large), lambda i, m: (i, 1 - m[4])), pl.BlockSpec((depth, large), lambda i, m: (i, m[4]))]
            + ([] if earlier is None else [anywhere])
            + [glance] * len(after),
            [
                pl.BlockSpec(block[:3] + (depth,), lambda i, m: (0, lax.bitwise_xor(m[0], peer), 0, i)),
                pl.BlockSpec((16, 128), lambda i, m: (0, 0)),
            ],
            [grads_shape, jax.ShapeDtypeStruct((16, 128), F32)],
            meta,
            (*[value for value, _ in arrived[peer]], matrix, matrix, *(() if earlier is None else (earlier,)), *after),
            aliases=None if earlier is None else {5: 0},
        )

    *totals_other, total_own = call(
        functools.partial(weight_grad_body, last, half), "weight_grad", (steps,),
        [pl.BlockSpec((peers, inside, rows), lambda i, m: (0, 0, 0))]
        + [
            pl.BlockSpec((rows, tile), lambda i, m, at=arrived[peer][0][1]: (at, jnp.minimum(i, half - 1)))
            for peer in range(last)
        ]
        + [
            pl.BlockSpec((rows, tile), lambda i, m, at=arrived[peer][1][1]: (at, jnp.maximum(i - half, 0)))
            for peer in range(last)
        ]
        + [glance] * 2,
        [pl.BlockSpec((inside, tile), lambda i, m: (0, 0))] * half
        + [pl.BlockSpec((inside, tile), lambda i, m: (0, jnp.maximum(i - half, 0)))],
        [jax.ShapeDtypeStruct((inside, tile), BF16)] * half + [jax.ShapeDtypeStruct((inside, large), F32)],
        meta, (turned, *[arrived[peer][side][0] for side in range(2) for peer in range(last)], made[1], first_sums),
        room=room,
    )
    hidden_grads = None
    for peer in range(last):
        hidden_grads, token = inside_grad(peer, hidden_grads, (total_own,))
    totals_other = [exchange(value) for value in totals_other]
    last_other, last_own = arrived[last]
    rows_other = last_other[0] if relay else last_other[0][:rows]
    rows_other = exchange(follow(rows_other, summed, token))

    combined, gate_grads = call(
        functools.partial(finish_body, count), "finish", (1,),
        [
            glance, pl.BlockSpec((top, tokens), lambda i, m: (0, 0)),
            pl.BlockSpec((tokens, padded), lambda i, m: (0, 0)), pl.BlockSpec((tokens, padded), lambda i, m: (0, 0)),
        ],
        [pl.BlockSpec((tokens, width), lambda i, m: (0, 0)), pl.BlockSpec((top, tokens), lambda i, m: (0, 0))],
        [jax.ShapeDtypeStruct((tokens, width), BF16), jax.ShapeDtypeStruct((top, tokens), F32)],
        meta, (total_own, ids_turned, sums[0], summed),
    )
    hidden_grads, _ = inside_grad(last, hidden_grads, ())
    fine = tile // 2 if tile >= 256 else tile
    each = tile // fine
    fine_spec = pl.BlockSpec((inside, fine), lambda i, m: (0, i))
    weight_grads = call(
        functools.partial(last_body, half), "last", (large // fine,),
        [
            pl.BlockSpec((1, inside, rows), lambda i, m: (last, 0, 0)),
            pl.BlockSpec((rows, fine), lambda i, m: (last_own[1], i)),
            pl.BlockSpec((inside, rows), lambda i, m: (0, 0)),
            pl.BlockSpec((rows, fine), lambda i, m: (0, i)),
            fine_spec,
        ]
        + [
            pl.BlockSpec((inside, fine), lambda i, m, at=at: (0, jnp.clip(i - at * each, 0, each - 1)))
            for at in range(half)
        ],
        fine_spec,
        jax.ShapeDtypeStruct((inside, large), BF16),
        meta, (turned, last_own[0], turned_other, rows_other, total_own, *totals_other),
        room=room,
    )

    if fold > 1:
        hidden_grads = hidden_grads.reshape(peers, planes, cap, inside).transpose(1, 0, 2, 3)
    return combined, gate_grads.T, hidden_grads.reshape(hidden.shape), weight_grads[None]


def solution(mesh):
    placed = (
        P(("expert", "dp"), None),
        P(("expert", "dp"), None),
        P("expert", "dp", None),
        P("expert", None, None),
        P(("expert", "dp"), None),
    )
    return jax.shard_map(
        per_device,
        mesh=mesh,
        in_specs=placed,
        out_specs=(
            P(("expert", "dp"), None),
            P(("expert", "dp"), None),
            P("expert", "dp", None),
            P("expert", None, "dp"),
        ),
        check_vma=False,
    )
```

```python
import functools

import jax
import jax.numpy as jnp
from jax import lax
from jax.experimental import pallas as pl
from jax.experimental.pallas import tpu as pltpu
from jax.sharding import PartitionSpec as P

F32 = jnp.float32
BF16 = jnp.bfloat16
VMEM_BYTES = 16 * 1024 * 1024
COST = 1024
NEAR_COST = 10**10


def call(body, name, grid, in_specs, out_specs, out_shape, scalars, operands, scratch=(), aliases=None, room=1, cost=COST):
    return pl.pallas_call(
        body,
        name=name,
        grid_spec=pltpu.PrefetchScalarGridSpec(
            num_scalar_prefetch=1, grid=grid, in_specs=in_specs, out_specs=out_specs, scratch_shapes=scratch
        ),
        out_shape=out_shape,
        input_output_aliases=aliases or {},
        cost_estimate=pl.CostEstimate(flops=cost, bytes_accessed=COST, transcendentals=0),
        compiler_params=pltpu.CompilerParams(vmem_limit_bytes=room * VMEM_BYTES),
    )(scalars, *operands)


def follow(value, *earlier):
    anywhere = pl.BlockSpec(memory_space=pl.ANY)
    return pl.pallas_call(
        lambda *refs: None,
        name="follow",
        grid=(1,),
        in_specs=[anywhere] + [pl.BlockSpec((16, 128), lambda i: (0, 0))] * len(earlier),
        out_specs=anywhere,
        out_shape=jax.ShapeDtypeStruct(value.shape, value.dtype),
        input_output_aliases={0: 0},
        cost_estimate=pl.CostEstimate(flops=COST, bytes_accessed=COST, transcendentals=0),
        compiler_params=pltpu.CompilerParams(vmem_limit_bytes=VMEM_BYTES),
    )(value, *earlier)


def pieces_of(value):
    high = value.astype(BF16).astype(F32)
    middle = (value - high).astype(BF16).astype(F32)
    return high, middle, value - high - middle


def pack_body(meta, ids, gates, grad, out):
    width, tokens = grad.shape[1], grad.shape[0]
    extent = out.shape[1] - width
    count = meta[6]
    expert = lax.broadcasted_iota(jnp.int32, (extent, tokens), 0)
    piece = jnp.zeros((extent, tokens), jnp.int32)
    for number in range(1, 4):
        piece = piece + jnp.where(expert >= number * count, 1, 0)
    local = expert - piece * count
    named = jnp.zeros((extent, tokens), F32)
    gate = jnp.zeros((extent, tokens), F32)
    for choice in range(ids.shape[0]):
        hit = ids[choice : choice + 1, :] == local
        named = named + jnp.where(hit, 1.0, 0.0)
        gate = gate + jnp.where(hit, gates[choice : choice + 1, :], 0.0)
    before = lax.broadcasted_iota(jnp.int32, (tokens, tokens), 0) < lax.broadcasted_iota(jnp.int32, (tokens, tokens), 1)
    earlier = jnp.dot(named.astype(BF16), jnp.where(before, 1.0, 0.0).astype(BF16), preferred_element_type=F32)
    place = jnp.where(named > 0.0, earlier + meta[2].astype(F32), -1.0)
    high, middle, low = pieces_of(gate)
    table = jnp.where(piece == 0, place, jnp.where(piece == 1, high, jnp.where(piece == 2, middle, low)))
    out[:, :width] = grad[...]
    out[:, width:] = table.T.astype(BF16)


def collect_body(number, meta, *refs):
    tables, sides, outs = refs[:number], (refs[number : 2 * number], refs[2 * number : 3 * number]), refs[-2:]
    tokens = tables[0].shape[0]
    for side, out in zip(sides, outs):
        large = side[0].shape[1]
        for k in range(number):
            out[k * tokens : (k + 1) * tokens, :large] = side[k][...]
            out[k * tokens : (k + 1) * tokens, large:] = tables[k][...]


def forward_body(meta, hidden, weight, out):
    rows = hidden[:, 0].reshape(out.shape[0], hidden.shape[3])
    out[...] = jnp.dot(rows, weight[...], preferred_element_type=F32).astype(BF16)


def turn_body(meta, hidden, after, out, final, final_turned):
    value = hidden[:, 0].reshape(final.shape)
    out[0] = value.T
    final[...] = value
    final_turned[...] = value.T


def turn_other_body(meta, hidden, out):
    out[...] = hidden[...].T


def selection(table, count, expert, rows):
    place = table[pl.ds(expert, 1), :]
    gate = table[pl.ds(expert + count, 1), :] + table[pl.ds(expert + 2 * count, 1), :]
    gate = gate + table[pl.ds(expert + 3 * count, 1), :]
    row = lax.broadcasted_iota(jnp.int32, (rows, place.shape[1]), 0).astype(F32)
    return row == place, gate


def grad_rows_body(plan, jobs, count, groups, meta, *refs):
    number = jobs * groups
    tables, tokens, outs, table = refs[:number], refs[number : 2 * number], refs[-1 - len(plan) : -1], refs[-1]
    rows = outs[0].shape[0] // len(plan[0][1]) // groups
    for job in range(jobs):
        asked = [(out, peer, parts.index(job)) for out, (peer, parts) in zip(outs, plan) if job in parts]
        for group in range(groups):
            table[...] = tables[job * groups + group][...].astype(F32).T
            choices, row_gates = [], []
            for _, peer, _ in asked:
                match, gate = selection(table, count, lax.bitwise_xor(meta[3], peer), rows)
                choices.append(jnp.where(match, 1.0, 0.0))
                row_gates.append(jnp.sum(jnp.where(match, gate, 0.0), 1, keepdims=True))
            choice = jnp.concatenate(choices, 0).astype(BF16)
            picked = jnp.dot(choice, tokens[job * groups + group][...], preferred_element_type=F32)
            value = (picked * jnp.concatenate(row_gates, 0)).astype(BF16)
            place = pl.multiple_of(lax.bitwise_xor(meta[1], group) * rows, rows)
            for at, (out, _, part) in enumerate(asked):
                out[pl.ds(place + part * groups * rows, rows), :] = value[at * rows : (at + 1) * rows]


def combine_body(peers, count, number, meta, *refs):
    packed, tokens, returned = refs[:number], refs[number : 2 * number], refs[2 * number + 1 : 2 * number + 1 + peers]
    part, table, weights, marks, inner = refs[-5:]
    rows, length = returned[0].shape[0], tokens[0].shape[0]
    step, last = pl.program_id(1), pl.num_programs(1) - 1

    def chosen(options):
        value = options[0][...]
        for at in range(1, number):
            value = jnp.where(pl.program_id(0) == at, options[at][...], value)
        return value

    @pl.when(step == 0)
    def _():
        inner[...] = jnp.zeros(inner.shape, F32)
        table[...] = chosen(packed).astype(F32).T
        highs, lows = [], []
        for peer in range(peers):
            match, gate = selection(table, count, lax.bitwise_xor(meta[3], peer), rows)
            high = gate.astype(BF16).astype(F32)
            marks[pl.ds(peer * rows, rows), :] = jnp.where(match, 1.0, 0.0)
            highs.append(jnp.where(match, high, 0.0))
            lows.append(jnp.where(match, gate - high, 0.0))
        weights[:length, :] = jnp.concatenate(highs, 0).T.astype(BF16)
        weights[length:, :] = jnp.concatenate(lows, 0).T.astype(BF16)

    @pl.when(step < last)
    def _():
        value = jnp.concatenate([ref[...] for ref in returned], 0)
        chunk = min(512, value.shape[1])
        for start in range(0, value.shape[1], chunk):
            total = jnp.dot(weights[...], value[:, start : start + chunk], preferred_element_type=F32)
            part[:, start : start + chunk] = (total[:length] + total[length:]).astype(part.dtype)
        products = lax.dot_general(value, chosen(tokens), (((1,), (1,)), ((), ())), preferred_element_type=F32)
        products = products * marks[...]
        for peer in range(peers):
            inner[peer : peer + 1, :] += jnp.sum(products[peer * rows : (peer + 1) * rows], 0, keepdims=True)

    @pl.when(step == last)
    def _():
        extent = -(-3 * count // 128) * 128
        row = lax.broadcasted_iota(jnp.int32, (extent, length), 0)
        placed = jnp.zeros((extent, length), F32)
        for at, piece in enumerate(pieces_of(inner[...])):
            for peer in range(peers):
                place = at * count + lax.bitwise_xor(meta[3], peer)
                placed = jnp.where(row == place, piece[peer : peer + 1, :], placed)
        part[:, :extent] = placed.T.astype(part.dtype)


def inside_body(peers, meta, *refs):
    number = len(peers)
    rows, weights, (out, token) = refs[: 2 * number], refs[2 * number : 2 * number + 2], refs[-2:]
    contract = (((1,), (1,)), ((), ()))
    for at, peer in enumerate(peers):
        value = lax.dot_general(rows[2 * at][...], weights[0][...], contract, preferred_element_type=F32)
        value = value + lax.dot_general(rows[2 * at + 1][...], weights[1][...], contract, preferred_element_type=F32)
        value = value.astype(BF16).reshape(out.shape[0], out.shape[2], out.shape[3])
        if number > 1:
            out[:, pl.ds(lax.bitwise_xor(meta[0], peer), 1)] = value[:, None]
        else:
            out[:, 0] = value
    token[...] = jnp.zeros(token.shape, F32)


def weight_grad_body(number, half, meta, turned, *refs):
    sides, others, own = (refs[:number], refs[number : 2 * number]), refs[-half - 1 : -1], refs[-1]
    step = pl.program_id(0)

    def value_of(side):
        value = jnp.dot(turned[0], side[0][...], preferred_element_type=F32)
        for peer in range(1, number):
            value = value + jnp.dot(turned[peer], side[peer][...], preferred_element_type=F32)
        return value

    for at in range(half):

        @pl.when(step == at)
        def _():
            others[at][...] = value_of(sides[0]).astype(BF16)

    @pl.when(step >= half)
    def _():
        own[...] = value_of(sides[1])


def last_body(half, meta, turned, rows, turned_other, rows_other, earlier, *refs):
    others, grads = refs[:half], refs[-1]
    tile = others[0].shape[1]
    for at in range(half):
        columns = slice(at * tile, (at + 1) * tile)
        value = jnp.dot(turned[...], rows[:, columns], preferred_element_type=F32)
        value = value + jnp.dot(turned_other[...], rows_other[:, columns], preferred_element_type=F32)
        grads[:, columns] = (value + earlier[:, columns] + others[at][...].astype(F32)).astype(BF16)


def finish_body(count, meta, after, ids, kept, arrived, combined, gate_grads):
    width = combined.shape[1]
    combined[...] = (kept[:, :width] + arrived[:, :width].astype(F32)).astype(BF16)
    pieces = (kept[:, width:] + arrived[:, width:].astype(F32)).T
    inner = pieces[:count] + pieces[count : 2 * count] + pieces[2 * count : 3 * count]
    named = ids[...]
    found = jnp.zeros(gate_grads.shape, F32)
    for expert in range(count):
        found = found + jnp.where(named == expert, inner[expert : expert + 1, :], 0.0)
    gate_grads[...] = found


def per_device(expert_ids, gates, hidden, weight, out_grad):
    count = lax.axis_size("expert")
    peers = 1 << ((count.bit_length() - 1) // 2)
    planes = count // peers
    tokens, top = expert_ids.shape
    cap = hidden.shape[1] // count
    width, inside = out_grad.shape[1], hidden.shape[2]
    fold = 1
    while fold * cap % 16:
        fold *= 2
    groups = planes // fold
    group_rows, group_tokens = fold * cap, fold * tokens
    rows = planes * cap
    tile = min(512, width // 2)
    steps = width // tile
    half = steps // 2
    large = width // 2
    room = 1 if fold == 1 else 3
    last = peers - 1
    anywhere = pl.BlockSpec(memory_space=pl.ANY)
    glance = pl.BlockSpec((16, 128), lambda *i: (0, 0))

    me = lax.axis_index("expert")
    core = lax.axis_index("dp")
    column, plane = me % peers, me // peers
    meta = jnp.stack([column, plane // fold, (plane % fold) * cap, me, core, plane, count]).astype(jnp.int32)

    def swap(value, distance):
        return lax.ppermute(value, "expert", [(e, e ^ distance) for e in range(count)])

    def exchange(value):
        return lax.ppermute(value, "dp", [(0, 1), (1, 0)])

    matrix = weight[0]
    if fold == 1:
        blocks = hidden.reshape(planes, peers, cap, inside)
    else:
        blocks = hidden.reshape(planes, peers, cap, inside).transpose(1, 0, 2, 3).reshape(1, peers, rows, inside)
    block = (blocks.shape[0], 1, blocks.shape[2], inside)

    ids_turned = expert_ids.T
    extent = -(-4 * count // 128) * 128
    short = pl.BlockSpec((top, tokens), lambda i, m: (0, 0))
    relay = peers == 4 and fold == 1
    packed = call(
        pack_body, "pack", (1,),
        [short, short, pl.BlockSpec((tokens, width), lambda i, m: (0, 0))],
        pl.BlockSpec((tokens, width + extent), lambda i, m: (0, 0)),
        jax.ShapeDtypeStruct((tokens, width + extent), BF16),
        meta, (ids_turned, gates.T, out_grad),
        room=room,
    )
    gathered = [packed]
    for k in range(1, planes):
        if k & (k - 1) == 0:
            gathered.append(swap(packed, peers * k))
        else:
            gathered.append(None)
    early = [gathered[1 << k] for k in range((planes - 1).bit_length())]

    def forward(peer, after):
        return call(
            lambda meta, *refs: forward_body(meta, refs[0], refs[1], refs[-1]), f"forward{peer}", (steps,),
            [
                pl.BlockSpec(block, lambda i, m: (0, lax.bitwise_xor(m[0], peer), 0, 0)),
                pl.BlockSpec((inside, tile), lambda i, m: (0, i)),
            ]
            + [glance] * len(after),
            pl.BlockSpec((rows, tile), lambda i, m: (0, i)),
            jax.ShapeDtypeStruct((rows, width), BF16),
            meta, (blocks, matrix, *after),
        )

    outputs, after = {}, ()
    for peer in list(range(1, peers)) + [0]:
        outputs[peer] = forward(peer, after)
        after = (outputs[peer], packed)
    returned = [outputs[0]] + [swap(outputs[peer], peer) for peer in range(1, last)]
    turned, hidden_last, turned_last = call(
        turn_body, "turn", (peers,),
        [pl.BlockSpec(block, lambda i, m: (0, lax.bitwise_xor(m[0], i), 0, 0)), glance],
        [pl.BlockSpec((1, inside, rows), lambda i, m: (i, 0, 0)), pl.BlockSpec((rows, inside), lambda i, m: (0, 0)),
         pl.BlockSpec((inside, rows), lambda i, m: (0, 0))],
        [
            jax.ShapeDtypeStruct((peers, inside, rows), BF16), jax.ShapeDtypeStruct((rows, inside), BF16),
            jax.ShapeDtypeStruct((inside, rows), BF16),
        ],
        meta, (blocks, outputs[0]),
    )

    turned_other = call(
        turn_other_body, "turn_other", (1,),
        [pl.BlockSpec((rows, inside), lambda i, m: (0, 0))],
        pl.BlockSpec((inside, rows), lambda i, m: (0, 0)),
        jax.ShapeDtypeStruct((inside, rows), BF16),
        meta, (exchange(hidden_last),),
    )
    final_output = follow(outputs[last], *returned[:0:-1], turned_other, *early)
    returned.append(swap(final_output, last))
    for k in range(1, planes):
        lowest = k & -k
        if k != lowest:
            forwarded = gathered[k ^ lowest]
            forwarded = follow(forwarded, final_output) if relay else forwarded
            gathered[k] = swap(forwarded, peers * lowest)
    if fold > 1:
        gathered = [jnp.concatenate(gathered[g * fold : (g + 1) * fold], 0) for g in range(groups)]

    def other_half(i, m):
        return (0, 1 - m[4])

    def own_half(i, m):
        return (0, m[4])

    def build_rows(name, plan, jobs, after, cost=COST):
        sources = [source for job in jobs for source in job]
        return call(
            functools.partial(grad_rows_body, plan, len(jobs), count, groups), name, (1,),
            [pl.BlockSpec((group_tokens, extent), table_at) for _, table_at, _ in sources]
            + [pl.BlockSpec((group_tokens, large), data_at) for _, _, data_at in sources]
            + [glance] * len(after),
            [pl.BlockSpec((len(parts) * rows, large), lambda i, m: (0, 0)) for _, parts in plan],
            [jax.ShapeDtypeStruct((len(parts) * rows, large), BF16) for _, parts in plan],
            meta, (*[value for value, _, _ in sources] * 2, *after),
            scratch=[pltpu.VMEM((extent, group_tokens), F32)],
            room=room, cost=cost,
        )

    def beside(i, m):
        return (0, width // extent)

    jobs = [[(value, beside, at) for value in gathered] for at in (other_half, own_half)]
    if relay:
        collected = call(
            functools.partial(collect_body, planes), "collect", (1,),
            [pl.BlockSpec((tokens, extent), beside)] * planes
            + [pl.BlockSpec((tokens, large), other_half)] * planes
            + [pl.BlockSpec((tokens, large), own_half)] * planes
            + [glance],
            [pl.BlockSpec((planes * tokens, large + extent), lambda i, m: (0, 0))] * 2,
            [jax.ShapeDtypeStruct((planes * tokens, large + extent), BF16)] * 2,
            meta, (*gathered * 3, final_output),
            room=room,
        )
        near = [swap(value, 1 << number) for number, value in enumerate(collected)]
        made = build_rows("own_rows", ((0, (0, 1)), (1, (1,)), (2, (0,))), jobs, (collected[0],))
        arrived = [
            [(made[0], 0), (made[0], 1)], [None, (swap(made[1], 1), 0)], [(swap(made[2], 2), 0), None], [None, None],
        ]
    else:
        made = build_rows("own_rows", tuple((peer, (0, 1)) for peer in range(peers)), jobs, (final_output,))
        arrived = [[(made[0], 0), (made[0], 1)]]
        for peer in range(1, peers):
            got = swap(made[peer], peer)
            arrived.append([(got, 0), (got, 1)])

    padded = width + -(-3 * count // 128) * 128

    def combine(chosen, dtype, after):
        first, stride = chosen[0], len(chosen) > 1 and chosen[1] - chosen[0]
        columns = width if fold == 1 else large

        def part_of(k, i, m):
            return (lax.bitwise_xor(m[1], k * stride + first), jnp.minimum(i, width // columns - 1))

        blocks_of = [gathered[group] for group in chosen]
        return call(
            functools.partial(combine_body, peers, count, len(chosen)), f"combine{first}", (len(chosen), width // columns + 1),
            [pl.BlockSpec((group_tokens, extent), lambda k, i, m: (0, width // extent))] * len(chosen)
            + [pl.BlockSpec((group_tokens, columns), lambda k, i, m: (0, jnp.minimum(i, width // columns - 1)))] * len(chosen)
            + [glance]
            + [pl.BlockSpec((group_rows, columns), part_of)] * peers,
            pl.BlockSpec((group_tokens, columns), lambda k, i, m: (k, i)),
            jax.ShapeDtypeStruct((len(chosen) * group_tokens, padded), dtype),
            meta, (*blocks_of, *blocks_of, after, *returned),
            scratch=[
                pltpu.VMEM((extent, group_tokens), F32),
                pltpu.VMEM((2 * group_tokens, peers * group_rows), BF16),
                pltpu.VMEM((peers * group_rows, group_tokens), F32),
                pltpu.VMEM((peers, group_tokens), F32),
            ],
            room=room,
        )

    if fold == 1:
        leaving = combine(range(1, planes, 2), BF16, made[0])
        combine_done = combine(range(0, planes, 2), F32, leaving)
        sums = [combine_done[k * tokens : (k + 1) * tokens] for k in range(planes // 2)]
    else:
        parts = [combine([group], F32, made[0]) for group in range(groups)]
        combine_done = parts[-1]
        sums = [parts[k // fold][k % fold * tokens : (k % fold + 1) * tokens] for k in range(planes)]
        leaving = jnp.concatenate(sums[1::2], 0).astype(BF16)
        sums = sums[0::2]
    distance = 1
    first_sums = None
    while len(sums) > 1:
        got = swap(leaving, peers * distance)
        pieces = [got[k * tokens : (k + 1) * tokens].astype(F32) for k in range(len(sums))]
        sums = [mine + piece for mine, piece in zip(sums, pieces)]
        leaving = [value.astype(BF16) for value in sums[1::2]]
        leaving = leaving[0] if len(leaving) == 1 else jnp.concatenate(leaving, 0)
        sums = sums[0::2]
        first_sums = leaving if first_sums is None else first_sums
        distance *= 2
    summed = swap(leaving, peers * distance)

    if relay:
        near_jobs = [
            [(value, lambda i, m, k=k: (k, large // extent), lambda i, m, k=k: (k, 0)) for k in range(planes)]
            for value in near
        ]
        plan = ((0, (0,)), (2, (0,)), (0, (1,)), (1, (1,)))
        made = build_rows("near_rows", plan, near_jobs, (combine_done,), NEAR_COST)
        arrived[1][0], arrived[2][1] = (made[0], 0), (made[2], 0)
        arrived[3] = [(swap(made[1], 2), 0), (swap(made[3], 1), 0)]

    grads_shape = jax.ShapeDtypeStruct(blocks.shape, BF16)
    depth = min(256, inside)

    def inside_grad(chosen, earlier, after):
        operands = [part for peer in chosen for part in arrived[peer]]
        if len(chosen) > 1:
            out = pl.BlockSpec((block[0], peers, block[2], depth), lambda i, m: (0, 0, 0, i))
        else:
            out = pl.BlockSpec(block[:3] + (depth,), lambda i, m: (0, lax.bitwise_xor(m[0], chosen[0]), 0, i))
        return call(
            functools.partial(inside_body, chosen), f"inside{chosen[0]}", (inside // depth,),
            [pl.BlockSpec((rows, large), lambda i, m, at=at: (at, 0)) for _, at in operands]
            + [pl.BlockSpec((depth, large), lambda i, m: (i, 1 - m[4])), pl.BlockSpec((depth, large), lambda i, m: (i, m[4]))]
            + ([] if earlier is None else [anywhere])
            + [glance] * len(after),
            [out, pl.BlockSpec((16, 128), lambda i, m: (0, 0))],
            [grads_shape, jax.ShapeDtypeStruct((16, 128), F32)],
            meta,
            (*[value for value, _ in operands], matrix, matrix, *(() if earlier is None else (earlier,)), *after),
            aliases=None if earlier is None else {3 + 2 * len(chosen): 0},
            room=room if len(chosen) == 1 else room + 1,
        )

    hidden_grads, token = inside_grad(range(last), None, (made[1], first_sums))
    *totals_other, total_own = call(
        functools.partial(weight_grad_body, last, half), "weight_grad", (steps,),
        [pl.BlockSpec((peers, inside, rows), lambda i, m: (0, 0, 0))]
        + [
            pl.BlockSpec((rows, tile), lambda i, m, at=arrived[peer][0][1]: (at, jnp.minimum(i, half - 1)))
            for peer in range(last)
        ]
        + [
            pl.BlockSpec((rows, tile), lambda i, m, at=arrived[peer][1][1]: (at, jnp.maximum(i - half, 0)))
            for peer in range(last)
        ]
        + [glance] * 2,
        [pl.BlockSpec((inside, tile), lambda i, m: (0, 0))] * half
        + [pl.BlockSpec((inside, tile), lambda i, m: (0, jnp.maximum(i - half, 0)))],
        [jax.ShapeDtypeStruct((inside, tile), BF16)] * half + [jax.ShapeDtypeStruct((inside, large), F32)],
        meta, (turned, *[arrived[peer][side][0] for side in range(2) for peer in range(last)], made[1], token),
        room=room,
    )
    totals_other = [exchange(value) for value in totals_other]
    last_other, last_own = arrived[last]
    rows_own = last_own[0] if relay else last_own[0][rows:]
    rows_other = last_other[0] if relay else last_other[0][:rows]
    followed = follow(rows_other, summed, last_own[0])
    rows_other = exchange(followed)

    combined, gate_grads = call(
        functools.partial(finish_body, count), "finish", (1,),
        [
            glance, pl.BlockSpec((top, tokens), lambda i, m: (0, 0)),
            pl.BlockSpec((tokens, padded), lambda i, m: (0, 0)), pl.BlockSpec((tokens, padded), lambda i, m: (0, 0)),
        ],
        [pl.BlockSpec((tokens, width), lambda i, m: (0, 0)), pl.BlockSpec((top, tokens), lambda i, m: (0, 0))],
        [jax.ShapeDtypeStruct((tokens, width), BF16), jax.ShapeDtypeStruct((top, tokens), F32)],
        meta, (total_own, ids_turned, sums[0], summed),
    )
    hidden_grads, _ = inside_grad([last], hidden_grads, (followed,))
    weight_grads = pl.pallas_call(
        functools.partial(last_body, half, None),
        name="last",
        out_shape=jax.ShapeDtypeStruct((inside, large), BF16),
        cost_estimate=pl.CostEstimate(flops=COST, bytes_accessed=COST, transcendentals=0),
        compiler_params=pltpu.CompilerParams(vmem_limit_bytes=room * VMEM_BYTES),
    )(turned_last, rows_own, turned_other, rows_other, total_own, *totals_other)

    if fold > 1:
        hidden_grads = hidden_grads.reshape(peers, planes, cap, inside).transpose(1, 0, 2, 3)
    return combined, gate_grads.T, hidden_grads.reshape(hidden.shape), weight_grads[None]


def solution(mesh):
    placed = (
        P(("expert", "dp"), None),
        P(("expert", "dp"), None),
        P("expert", "dp", None),
        P("expert", None, None),
        P(("expert", "dp"), None),
    )
    return jax.shard_map(
        per_device,
        mesh=mesh,
        in_specs=placed,
        out_specs=(
            P(("expert", "dp"), None),
            P(("expert", "dp"), None),
            P("expert", "dp", None),
            P("expert", None, "dp"),
        ),
        check_vma=False,
    )
```

```python
import functools

import jax
import jax.numpy as jnp
from jax import lax
from jax.experimental import pallas as pl
from jax.experimental.pallas import tpu as pltpu
from jax.sharding import PartitionSpec as P

F32 = jnp.float32
BF16 = jnp.bfloat16
VMEM_BYTES = 16 * 1024 * 1024
COST = 1024
NEAR_COST = 10**10


def call(body, name, grid, in_specs, out_specs, out_shape, scalars, operands, scratch=(), aliases=None, room=1, cost=COST):
    return pl.pallas_call(
        body,
        name=name,
        grid_spec=pltpu.PrefetchScalarGridSpec(
            num_scalar_prefetch=1, grid=grid, in_specs=in_specs, out_specs=out_specs, scratch_shapes=scratch
        ),
        out_shape=out_shape,
        input_output_aliases=aliases or {},
        cost_estimate=pl.CostEstimate(flops=cost, bytes_accessed=COST, transcendentals=0),
        compiler_params=pltpu.CompilerParams(vmem_limit_bytes=room * VMEM_BYTES),
    )(scalars, *operands)


def direct(body, name, out_shape, scalars, operands, out_specs=None, scratch=(), aliases=None, places=None, room=1):
    places = places or {}
    vmem, smem = pl.BlockSpec(memory_space=pltpu.VMEM), pl.BlockSpec(memory_space=pltpu.SMEM)
    several = isinstance(out_shape, (list, tuple))
    return pl.pallas_call(
        body,
        name=name,
        in_specs=[smem] + [places.get(at, vmem) for at in range(len(operands))],
        out_specs=out_specs or ([vmem] * len(out_shape) if several else vmem),
        out_shape=out_shape,
        scratch_shapes=scratch,
        input_output_aliases=aliases or {},
        cost_estimate=pl.CostEstimate(flops=COST, bytes_accessed=COST, transcendentals=0),
        compiler_params=pltpu.CompilerParams(vmem_limit_bytes=int(room * VMEM_BYTES)),
    )(scalars, *operands)


def follow(value, *earlier):
    anywhere = pl.BlockSpec(memory_space=pl.ANY)
    return pl.pallas_call(
        lambda *refs: None,
        name="follow",
        grid=(1,),
        in_specs=[anywhere] + [pl.BlockSpec((16, 128), lambda i: (0, 0))] * len(earlier),
        out_specs=anywhere,
        out_shape=jax.ShapeDtypeStruct(value.shape, value.dtype),
        input_output_aliases={0: 0},
        cost_estimate=pl.CostEstimate(flops=COST, bytes_accessed=COST, transcendentals=0),
        compiler_params=pltpu.CompilerParams(vmem_limit_bytes=VMEM_BYTES),
    )(value, *earlier)


def pieces_of(value):
    high = value.astype(BF16).astype(F32)
    middle = (value - high).astype(BF16).astype(F32)
    return high, middle, value - high - middle


def pack_body(meta, ids, gates, grad, out):
    width, tokens = grad.shape[1], grad.shape[0]
    extent = out.shape[1] - width
    count = meta[6]
    expert = lax.broadcasted_iota(jnp.int32, (extent, tokens), 0)
    piece = jnp.zeros((extent, tokens), jnp.int32)
    for number in range(1, 4):
        piece = piece + jnp.where(expert >= number * count, 1, 0)
    local = expert - piece * count
    named = jnp.zeros((extent, tokens), F32)
    gate = jnp.zeros((extent, tokens), F32)
    for choice in range(ids.shape[0]):
        hit = ids[choice : choice + 1, :] == local
        named = named + jnp.where(hit, 1.0, 0.0)
        gate = gate + jnp.where(hit, gates[choice : choice + 1, :], 0.0)
    before = lax.broadcasted_iota(jnp.int32, (tokens, tokens), 0) < lax.broadcasted_iota(jnp.int32, (tokens, tokens), 1)
    earlier = jnp.dot(named.astype(BF16), jnp.where(before, 1.0, 0.0).astype(BF16), preferred_element_type=F32)
    place = jnp.where(named > 0.0, earlier + meta[2].astype(F32), -1.0)
    high, middle, low = pieces_of(gate)
    table = jnp.where(piece == 0, place, jnp.where(piece == 1, high, jnp.where(piece == 2, middle, low)))
    out[:, :width] = grad[...]
    out[:, width:] = table.T.astype(BF16)


def collect_body(number, meta, *refs):
    tables, sides, outs = refs[:number], (refs[number : 2 * number], refs[2 * number : 3 * number]), refs[-2:]
    tokens = tables[0].shape[0]
    for side, out in zip(sides, outs):
        large = side[0].shape[1]
        for k in range(number):
            out[k * tokens : (k + 1) * tokens, :large] = side[k][...]
            out[k * tokens : (k + 1) * tokens, large:] = tables[k][...]


def forward_body(meta, hidden, weight, out):
    rows = hidden[:, 0].reshape(out.shape[0], hidden.shape[3])
    out[...] = jnp.dot(rows, weight[...], preferred_element_type=F32).astype(BF16)


def forward_first_body(peers, meta, hidden, weight, *refs):
    outs, (rows, matrix, sems) = refs[: len(peers)], refs[len(peers) :]
    tile = matrix.shape[2]
    copies = []
    for at, peer in enumerate(peers):
        part = hidden.at[:, lax.bitwise_xor(meta[0], peer)]
        copies.append(pltpu.make_async_copy(part, rows.at[at], sems.at[at]))
    for at in range(matrix.shape[0]):
        part = weight.at[:, at * tile : (at + 1) * tile]
        copies.append(pltpu.make_async_copy(part, matrix.at[at], sems.at[len(peers) + at]))
    for copy in copies:
        copy.start()
    for copy in copies[: len(peers)]:
        copy.wait()
    length = outs[0].shape[0]
    value = rows[...].reshape(len(peers) * length, rows.shape[3])
    for at in range(matrix.shape[0]):
        copies[len(peers) + at].wait()
        product = jnp.dot(value, matrix[at], preferred_element_type=F32).astype(BF16)
        for number, out in enumerate(outs):
            out[:, at * tile : (at + 1) * tile] = product[number * length : (number + 1) * length]


def turn_body(meta, hidden, after, out, final, final_turned):
    value = hidden[:, 0].reshape(final.shape)
    out[0] = value.T
    final[...] = value
    final_turned[...] = value.T


def turn_other_body(meta, hidden, out):
    out[...] = hidden[...].T


def selection(table, count, expert, rows):
    place = table[pl.ds(expert, 1), :]
    gate = table[pl.ds(expert + count, 1), :] + table[pl.ds(expert + 2 * count, 1), :]
    gate = gate + table[pl.ds(expert + 3 * count, 1), :]
    row = lax.broadcasted_iota(jnp.int32, (rows, place.shape[1]), 0).astype(F32)
    return row == place, gate


def grad_rows_body(plan, jobs, count, groups, meta, *refs):
    number = jobs * groups
    tables, tokens, outs, table = refs[:number], refs[number : 2 * number], refs[-1 - len(plan) : -1], refs[-1]
    rows = outs[0].shape[0] // len(plan[0][1]) // groups
    for job in range(jobs):
        asked = [(out, peer, parts.index(job)) for out, (peer, parts) in zip(outs, plan) if job in parts]
        for group in range(groups):
            table[...] = tables[job * groups + group][...].astype(F32).T
            choices, row_gates = [], []
            for _, peer, _ in asked:
                match, gate = selection(table, count, lax.bitwise_xor(meta[3], peer), rows)
                choices.append(jnp.where(match, 1.0, 0.0))
                row_gates.append(jnp.sum(jnp.where(match, gate, 0.0), 1, keepdims=True))
            choice = jnp.concatenate(choices, 0).astype(BF16)
            picked = jnp.dot(choice, tokens[job * groups + group][...], preferred_element_type=F32)
            value = (picked * jnp.concatenate(row_gates, 0)).astype(BF16)
            place = pl.multiple_of(lax.bitwise_xor(meta[1], group) * rows, rows)
            for at, (out, _, part) in enumerate(asked):
                out[pl.ds(place + part * groups * rows, rows), :] = value[at * rows : (at + 1) * rows]


def combine_body(peers, count, number, meta, *refs):
    packed, tokens, returned = refs[:number], refs[number : 2 * number], refs[2 * number + 1 : 2 * number + 1 + peers]
    part, table, weights, marks, inner = refs[-5:]
    rows, length = returned[0].shape[0], tokens[0].shape[0]
    step, last = pl.program_id(1), pl.num_programs(1) - 1

    def chosen(options):
        value = options[0][...]
        for at in range(1, number):
            value = jnp.where(pl.program_id(0) == at, options[at][...], value)
        return value

    @pl.when(step == 0)
    def _():
        inner[...] = jnp.zeros(inner.shape, F32)
        table[...] = chosen(packed).astype(F32).T
        highs, lows = [], []
        for peer in range(peers):
            match, gate = selection(table, count, lax.bitwise_xor(meta[3], peer), rows)
            high = gate.astype(BF16).astype(F32)
            marks[pl.ds(peer * rows, rows), :] = jnp.where(match, 1.0, 0.0)
            highs.append(jnp.where(match, high, 0.0))
            lows.append(jnp.where(match, gate - high, 0.0))
        weights[:length, :] = jnp.concatenate(highs, 0).T.astype(BF16)
        weights[length:, :] = jnp.concatenate(lows, 0).T.astype(BF16)

    @pl.when(step < last)
    def _():
        value = jnp.concatenate([ref[...] for ref in returned], 0)
        chunk = min(512, value.shape[1])
        for start in range(0, value.shape[1], chunk):
            total = jnp.dot(weights[...], value[:, start : start + chunk], preferred_element_type=F32)
            part[:, start : start + chunk] = (total[:length] + total[length:]).astype(part.dtype)
        products = lax.dot_general(value, chosen(tokens), (((1,), (1,)), ((), ())), preferred_element_type=F32)
        products = products * marks[...]
        for peer in range(peers):
            inner[peer : peer + 1, :] += jnp.sum(products[peer * rows : (peer + 1) * rows], 0, keepdims=True)

    @pl.when(step == last)
    def _():
        extent = -(-3 * count // 128) * 128
        row = lax.broadcasted_iota(jnp.int32, (extent, length), 0)
        placed = jnp.zeros((extent, length), F32)
        for at, piece in enumerate(pieces_of(inner[...])):
            for peer in range(peers):
                place = at * count + lax.bitwise_xor(meta[3], peer)
                placed = jnp.where(row == place, piece[peer : peer + 1, :], placed)
        part[:, :extent] = placed.T.astype(part.dtype)


def inside_body(plan, meta, weight, *refs):
    number = 1 + max(at for _, parts in plan for at, _ in parts)
    rows, out, token, (store, sems) = refs[:number], refs[-4], refs[-3], refs[-2:]
    shape = store.shape[1:]
    length, large = shape[0] * shape[1], weight.shape[1] // 2
    contract = (((1,), (1,)), ((), ()))
    copies = []
    for at, (peer, parts) in enumerate(plan):
        value = jnp.zeros((length, weight.shape[0]), F32)
        for half, (operand, start) in enumerate(parts):
            columns = pl.ds(pl.multiple_of(lax.bitwise_xor(1 - meta[4], half) * large, large), large)
            part = rows[operand][start : start + length, :]
            value = value + lax.dot_general(part, weight[:, columns], contract, preferred_element_type=F32)
        store[at] = value.astype(BF16).reshape(shape)
        copies.append(pltpu.make_async_copy(store.at[at], out.at[:, lax.bitwise_xor(meta[0], peer)], sems.at[at]))
        copies[-1].start()
    token[...] = jnp.zeros(token.shape, F32)
    for copy in copies:
        copy.wait()


def weight_grad_body(plan, number, half, meta, turned, *refs):
    rows, others, own = refs[:number], refs[-half - 1 : -1], refs[-1]
    length, tile = turned.shape[2], others[0].shape[1]

    def value_of(side, at):
        value = jnp.zeros((turned.shape[1], tile), F32)
        for peer, parts in plan:
            operand, start = parts[side]
            part = rows[operand][start : start + length, at * tile : (at + 1) * tile]
            value = value + jnp.dot(turned[peer], part, preferred_element_type=F32)
        return value

    for at in range(half):
        others[at][...] = value_of(0, at).astype(BF16)
        own[:, at * tile : (at + 1) * tile] = value_of(1, at)


def last_body(half, meta, turned, rows, turned_other, rows_other, earlier, *refs):
    others, grads = refs[:half], refs[-1]
    tile = others[0].shape[1]
    for at in range(half):
        columns = slice(at * tile, (at + 1) * tile)
        value = jnp.dot(turned[...], rows[:, columns], preferred_element_type=F32)
        value = value + jnp.dot(turned_other[...], rows_other[:, columns], preferred_element_type=F32)
        grads[:, columns] = (value + earlier[:, columns] + others[at][...].astype(F32)).astype(BF16)


def finish_body(count, meta, ids, kept, arrived, combined, gate_grads):
    width = combined.shape[1]
    combined[...] = (kept[:, :width] + arrived[:, :width].astype(F32)).astype(BF16)
    pieces = (kept[:, width:] + arrived[:, width:].astype(F32)).T
    inner = pieces[:count] + pieces[count : 2 * count] + pieces[2 * count : 3 * count]
    named = ids[...]
    found = jnp.zeros(gate_grads.shape, F32)
    for expert in range(count):
        found = found + jnp.where(named == expert, inner[expert : expert + 1, :], 0.0)
    gate_grads[...] = found


def per_device(expert_ids, gates, hidden, weight, out_grad):
    count = lax.axis_size("expert")
    peers = 1 << ((count.bit_length() - 1) // 2)
    planes = count // peers
    tokens, top = expert_ids.shape
    cap = hidden.shape[1] // count
    width, inside = out_grad.shape[1], hidden.shape[2]
    fold = 1
    while fold * cap % 16:
        fold *= 2
    groups = planes // fold
    group_rows, group_tokens = fold * cap, fold * tokens
    rows = planes * cap
    tile = min(512, width // 2)
    steps = width // tile
    half = steps // 2
    large = width // 2
    room = 1 if fold == 1 else 3
    last = peers - 1
    anywhere = pl.BlockSpec(memory_space=pl.ANY)
    glance = pl.BlockSpec((16, 128), lambda *i: (0, 0))

    me = lax.axis_index("expert")
    core = lax.axis_index("dp")
    column, plane = me % peers, me // peers
    meta = jnp.stack([column, plane // fold, (plane % fold) * cap, me, core, plane, count]).astype(jnp.int32)

    def swap(value, distance):
        return lax.ppermute(value, "expert", [(e, e ^ distance) for e in range(count)])

    def exchange(value):
        return lax.ppermute(value, "dp", [(0, 1), (1, 0)])

    matrix = weight[0]
    if fold == 1:
        blocks = hidden.reshape(planes, peers, cap, inside)
    else:
        blocks = hidden.reshape(planes, peers, cap, inside).transpose(1, 0, 2, 3).reshape(1, peers, rows, inside)
    block = (blocks.shape[0], 1, blocks.shape[2], inside)

    ids_turned = expert_ids.T
    extent = -(-4 * count // 128) * 128
    short = pl.BlockSpec((top, tokens), lambda i, m: (0, 0))
    relay = peers == 4 and fold == 1
    packed = call(
        pack_body, "pack", (1,),
        [short, short, pl.BlockSpec((tokens, width), lambda i, m: (0, 0))],
        pl.BlockSpec((tokens, width + extent), lambda i, m: (0, 0)),
        jax.ShapeDtypeStruct((tokens, width + extent), BF16),
        meta, (ids_turned, gates.T, out_grad),
        room=room,
    )
    gathered = [packed]
    for k in range(1, planes):
        if k & (k - 1) == 0:
            gathered.append(swap(packed, peers * k))
        else:
            gathered.append(None)
    early = [gathered[1 << k] for k in range((planes - 1).bit_length())]

    def forward(peer, after):
        return call(
            lambda meta, *refs: forward_body(meta, refs[0], refs[1], refs[-1]), f"forward{peer}", (steps,),
            [
                pl.BlockSpec(block, lambda i, m: (0, lax.bitwise_xor(m[0], peer), 0, 0)),
                pl.BlockSpec((inside, tile), lambda i, m: (0, i)),
            ]
            + [glance] * len(after),
            pl.BlockSpec((rows, tile), lambda i, m: (0, i)),
            jax.ShapeDtypeStruct((rows, width), BF16),
            meta, (blocks, matrix, *after),
        )

    outputs, after = {}, ()
    if relay:
        outputs[1], outputs[2] = direct(
            functools.partial(forward_first_body, (1, 2)), "forward1", [jax.ShapeDtypeStruct((rows, width), BF16)] * 2,
            meta, (blocks, matrix),
            scratch=[
                pltpu.VMEM((2, planes, cap, inside), BF16),
                pltpu.VMEM((steps, inside, tile), BF16),
                pltpu.SemaphoreType.DMA((2 + steps,)),
            ],
            places={0: anywhere, 1: anywhere}, room=3.75,
        )
        after = (outputs[2], packed)
    for peer in [peer for peer in list(range(1, peers)) + [0] if peer not in outputs]:
        outputs[peer] = forward(peer, after)
        after = (outputs[peer], packed)
    returned = [outputs[0]] + [swap(outputs[peer], peer) for peer in range(1, last)]
    turned, hidden_last, turned_last = call(
        turn_body, "turn", (peers,),
        [pl.BlockSpec(block, lambda i, m: (0, lax.bitwise_xor(m[0], i), 0, 0)), glance],
        [pl.BlockSpec((1, inside, rows), lambda i, m: (i, 0, 0)), pl.BlockSpec((rows, inside), lambda i, m: (0, 0)),
         pl.BlockSpec((inside, rows), lambda i, m: (0, 0))],
        [
            jax.ShapeDtypeStruct((peers, inside, rows), BF16), jax.ShapeDtypeStruct((rows, inside), BF16),
            jax.ShapeDtypeStruct((inside, rows), BF16),
        ],
        meta, (blocks, outputs[0]),
    )

    turned_other = call(
        turn_other_body, "turn_other", (1,),
        [pl.BlockSpec((rows, inside), lambda i, m: (0, 0))],
        pl.BlockSpec((inside, rows), lambda i, m: (0, 0)),
        jax.ShapeDtypeStruct((inside, rows), BF16),
        meta, (exchange(hidden_last),),
    )
    final_output = follow(outputs[last], *returned[:0:-1], turned_other, *early)
    returned.append(swap(final_output, last))
    for k in range(1, planes):
        lowest = k & -k
        if k != lowest:
            forwarded = gathered[k ^ lowest]
            forwarded = follow(forwarded, final_output) if relay else forwarded
            gathered[k] = swap(forwarded, peers * lowest)
    if fold > 1:
        gathered = [jnp.concatenate(gathered[g * fold : (g + 1) * fold], 0) for g in range(groups)]

    def other_half(i, m):
        return (0, 1 - m[4])

    def own_half(i, m):
        return (0, m[4])

    def build_rows(name, plan, jobs, after, cost=COST):
        sources = [source for job in jobs for source in job]
        return call(
            functools.partial(grad_rows_body, plan, len(jobs), count, groups), name, (1,),
            [pl.BlockSpec((group_tokens, extent), table_at) for _, table_at, _ in sources]
            + [pl.BlockSpec((group_tokens, large), data_at) for _, _, data_at in sources]
            + [glance] * len(after),
            [pl.BlockSpec((len(parts) * rows, large), lambda i, m: (0, 0)) for _, parts in plan],
            [jax.ShapeDtypeStruct((len(parts) * rows, large), BF16) for _, parts in plan],
            meta, (*[value for value, _, _ in sources] * 2, *after),
            scratch=[pltpu.VMEM((extent, group_tokens), F32)],
            room=room, cost=cost,
        )

    def beside(i, m):
        return (0, width // extent)

    jobs = [[(value, beside, at) for value in gathered] for at in (other_half, own_half)]
    if relay:
        collected = call(
            functools.partial(collect_body, planes), "collect", (1,),
            [pl.BlockSpec((tokens, extent), beside)] * planes
            + [pl.BlockSpec((tokens, large), other_half)] * planes
            + [pl.BlockSpec((tokens, large), own_half)] * planes
            + [glance],
            [pl.BlockSpec((planes * tokens, large + extent), lambda i, m: (0, 0))] * 2,
            [jax.ShapeDtypeStruct((planes * tokens, large + extent), BF16)] * 2,
            meta, (*gathered * 3, final_output),
            room=room,
        )
        near = [swap(value, 1 << number) for number, value in enumerate(collected)]
        made = build_rows("own_rows", ((0, (0, 1)), (1, (1,)), (2, (0,))), jobs, (collected[0],))
        arrived = [
            [(made[0], 0), (made[0], 1)], [None, (swap(made[1], 1), 0)], [(swap(made[2], 2), 0), None], [None, None],
        ]
    else:
        made = build_rows("own_rows", tuple((peer, (0, 1)) for peer in range(peers)), jobs, (final_output,))
        arrived = [[(made[0], 0), (made[0], 1)]]
        for peer in range(1, peers):
            got = swap(made[peer], peer)
            arrived.append([(got, 0), (got, 1)])

    padded = width + -(-3 * count // 128) * 128

    def combine(chosen, dtype, after):
        first, stride = chosen[0], len(chosen) > 1 and chosen[1] - chosen[0]
        columns = width if fold == 1 else large

        def part_of(k, i, m):
            return (lax.bitwise_xor(m[1], k * stride + first), jnp.minimum(i, width // columns - 1))

        blocks_of = [gathered[group] for group in chosen]
        return call(
            functools.partial(combine_body, peers, count, len(chosen)), f"combine{first}", (len(chosen), width // columns + 1),
            [pl.BlockSpec((group_tokens, extent), lambda k, i, m: (0, width // extent))] * len(chosen)
            + [pl.BlockSpec((group_tokens, columns), lambda k, i, m: (0, jnp.minimum(i, width // columns - 1)))] * len(chosen)
            + [glance]
            + [pl.BlockSpec((group_rows, columns), part_of)] * peers,
            pl.BlockSpec((group_tokens, columns), lambda k, i, m: (k, i)),
            jax.ShapeDtypeStruct((len(chosen) * group_tokens, padded), dtype),
            meta, (*blocks_of, *blocks_of, after, *returned),
            scratch=[
                pltpu.VMEM((extent, group_tokens), F32),
                pltpu.VMEM((2 * group_tokens, peers * group_rows), BF16),
                pltpu.VMEM((peers * group_rows, group_tokens), F32),
                pltpu.VMEM((peers, group_tokens), F32),
            ],
            room=room,
        )

    if fold == 1:
        leaving = combine(range(1, planes, 2), BF16, made[0])
        combine_done = combine(range(0, planes, 2), F32, leaving)
        sums = [combine_done[k * tokens : (k + 1) * tokens] for k in range(planes // 2)]
    else:
        parts = [combine([group], F32, made[0]) for group in range(groups)]
        combine_done = parts[-1]
        sums = [parts[k // fold][k % fold * tokens : (k % fold + 1) * tokens] for k in range(planes)]
        leaving = jnp.concatenate(sums[1::2], 0).astype(BF16)
        sums = sums[0::2]
    distance = 1
    first_sums = None
    while len(sums) > 1:
        got = swap(leaving, peers * distance)
        pieces = [got[k * tokens : (k + 1) * tokens].astype(F32) for k in range(len(sums))]
        sums = [mine + piece for mine, piece in zip(sums, pieces)]
        leaving = [value.astype(BF16) for value in sums[1::2]]
        leaving = leaving[0] if len(leaving) == 1 else jnp.concatenate(leaving, 0)
        sums = sums[0::2]
        first_sums = leaving if first_sums is None else first_sums
        distance *= 2
    summed = swap(leaving, peers * distance)

    if relay:
        near_jobs = [
            [(value, lambda i, m, k=k: (k, large // extent), lambda i, m, k=k: (k, 0)) for k in range(planes)]
            for value in near
        ]
        plan = ((0, (0,)), (2, (0,)), (0, (1,)), (1, (1,)))
        made = build_rows("near_rows", plan, near_jobs, (combine_done,), NEAR_COST)
        arrived[1][0], arrived[2][1] = (made[0], 0), (made[2], 0)
        arrived[3] = [(swap(made[1], 2), 0), (swap(made[3], 1), 0)]

    grads_shape = jax.ShapeDtypeStruct(blocks.shape, BF16)
    def rows_of(chosen):
        arrays, plan = [], []
        for peer in chosen:
            parts = []
            for value, at in arrived[peer]:
                known = [number for number, array in enumerate(arrays) if array is value]
                if not known:
                    arrays.append(value)
                parts.append((known[0] if known else len(arrays) - 1, at * rows))
            plan.append((peer, tuple(parts)))
        return arrays, tuple(plan)

    def inside_grad(chosen, earlier, after):
        arrays, plan = rows_of(chosen)
        operands = [matrix, *arrays, *after] + ([] if earlier is None else [earlier])
        return direct(
            functools.partial(inside_body, plan), f"inside{chosen[0]}",
            [grads_shape, jax.ShapeDtypeStruct((16, 128), F32)],
            meta, operands,
            out_specs=[anywhere, pl.BlockSpec(memory_space=pltpu.VMEM)],
            scratch=[
                pltpu.VMEM((len(chosen), block[0], block[2], inside), BF16),
                pltpu.SemaphoreType.DMA((len(chosen),)),
            ],
            aliases=None if earlier is None else {len(operands): 0},
            places={} if earlier is None else {len(operands) - 1: anywhere},
        )

    hidden_grads, token = inside_grad(range(last), None, (made[1][:16, :128], first_sums[:16, :128]))
    arrays, plan = rows_of(range(last))
    *totals_other, total_own = direct(
        functools.partial(weight_grad_body, plan, len(arrays), half), "weight_grad",
        [jax.ShapeDtypeStruct((inside, tile), BF16)] * half + [jax.ShapeDtypeStruct((inside, large), F32)],
        meta, (turned, *arrays, token),
    )
    totals_other = [exchange(value) for value in totals_other]
    last_other, last_own = arrived[last]
    rows_own = last_own[0] if relay else last_own[0][rows:]
    rows_other = last_other[0] if relay else last_other[0][:rows]
    followed = follow(rows_other, summed, last_own[0])
    rows_other = exchange(followed)

    combined, gate_grads = direct(
        functools.partial(finish_body, count), "finish",
        [jax.ShapeDtypeStruct((tokens, width), BF16), jax.ShapeDtypeStruct((top, tokens), F32)],
        meta, (ids_turned, sums[0], summed),
    )
    hidden_grads, _ = inside_grad([last], hidden_grads, (followed,))
    weight_grads = pl.pallas_call(
        functools.partial(last_body, half, None),
        name="last",
        out_shape=jax.ShapeDtypeStruct((inside, large), BF16),
        cost_estimate=pl.CostEstimate(flops=COST, bytes_accessed=COST, transcendentals=0),
        compiler_params=pltpu.CompilerParams(vmem_limit_bytes=room * VMEM_BYTES),
    )(turned_last, rows_own, turned_other, rows_other, total_own, *totals_other)

    if fold > 1:
        hidden_grads = hidden_grads.reshape(peers, planes, cap, inside).transpose(1, 0, 2, 3)
    return combined, gate_grads.T, hidden_grads.reshape(hidden.shape), weight_grads[None]


def solution(mesh):
    placed = (
        P(("expert", "dp"), None),
        P(("expert", "dp"), None),
        P("expert", "dp", None),
        P("expert", None, None),
        P(("expert", "dp"), None),
    )
    return jax.shard_map(
        per_device,
        mesh=mesh,
        in_specs=placed,
        out_specs=(
            P(("expert", "dp"), None),
            P(("expert", "dp"), None),
            P("expert", "dp", None),
            P("expert", None, "dp"),
        ),
        check_vma=False,
    )
```

```python
import functools

import jax
import jax.numpy as jnp
from jax import lax
from jax.experimental import pallas as pl
from jax.experimental.pallas import tpu as pltpu
from jax.sharding import PartitionSpec as P

F32 = jnp.float32
BF16 = jnp.bfloat16
VMEM_BYTES = 16 * 1024 * 1024
COST = 1024
NEAR_COST = 10**10


def call(body, name, grid, in_specs, out_specs, out_shape, scalars, operands, scratch=(), aliases=None, room=1, cost=COST):
    return pl.pallas_call(
        body,
        name=name,
        grid_spec=pltpu.PrefetchScalarGridSpec(
            num_scalar_prefetch=1, grid=grid, in_specs=in_specs, out_specs=out_specs, scratch_shapes=scratch
        ),
        out_shape=out_shape,
        input_output_aliases=aliases or {},
        cost_estimate=pl.CostEstimate(flops=cost, bytes_accessed=COST, transcendentals=0),
        compiler_params=pltpu.CompilerParams(vmem_limit_bytes=room * VMEM_BYTES),
    )(scalars, *operands)


def direct(body, name, out_shape, scalars, operands, out_specs=None, scratch=(), aliases=None, places=None, room=1, cost=COST):
    places = places or {}
    vmem, smem = pl.BlockSpec(memory_space=pltpu.VMEM), pl.BlockSpec(memory_space=pltpu.SMEM)
    several = isinstance(out_shape, (list, tuple))
    return pl.pallas_call(
        body,
        name=name,
        in_specs=[smem] + [places.get(at, vmem) for at in range(len(operands))],
        out_specs=out_specs or ([vmem] * len(out_shape) if several else vmem),
        out_shape=out_shape,
        scratch_shapes=scratch,
        input_output_aliases=aliases or {},
        cost_estimate=pl.CostEstimate(flops=cost, bytes_accessed=COST, transcendentals=0),
        compiler_params=pltpu.CompilerParams(vmem_limit_bytes=int(room * VMEM_BYTES)),
    )(scalars, *operands)


def follow(value, *earlier):
    anywhere = pl.BlockSpec(memory_space=pl.ANY)
    return pl.pallas_call(
        lambda *refs: None,
        name="follow",
        grid=(1,),
        in_specs=[anywhere] + [pl.BlockSpec((16, 128), lambda i: (0, 0))] * len(earlier),
        out_specs=anywhere,
        out_shape=jax.ShapeDtypeStruct(value.shape, value.dtype),
        input_output_aliases={0: 0},
        cost_estimate=pl.CostEstimate(flops=COST, bytes_accessed=COST, transcendentals=0),
        compiler_params=pltpu.CompilerParams(vmem_limit_bytes=VMEM_BYTES),
    )(value, *earlier)


def pieces_of(value):
    high = value.astype(BF16).astype(F32)
    middle = (value - high).astype(BF16).astype(F32)
    return high, middle, value - high - middle


def pack_body(meta, ids, gates, grad, out):
    width, tokens = grad.shape[1], grad.shape[0]
    extent = out.shape[1] - width
    count = meta[6]
    expert = lax.broadcasted_iota(jnp.int32, (extent, tokens), 0)
    piece = jnp.zeros((extent, tokens), jnp.int32)
    for number in range(1, 4):
        piece = piece + jnp.where(expert >= number * count, 1, 0)
    local = expert - piece * count
    named = jnp.zeros((extent, tokens), F32)
    gate = jnp.zeros((extent, tokens), F32)
    for choice in range(ids.shape[0]):
        hit = ids[choice : choice + 1, :] == local
        named = named + jnp.where(hit, 1.0, 0.0)
        gate = gate + jnp.where(hit, gates[choice : choice + 1, :], 0.0)
    before = lax.broadcasted_iota(jnp.int32, (tokens, tokens), 0) < lax.broadcasted_iota(jnp.int32, (tokens, tokens), 1)
    earlier = jnp.dot(named.astype(BF16), jnp.where(before, 1.0, 0.0).astype(BF16), preferred_element_type=F32)
    place = jnp.where(named > 0.0, earlier + meta[2].astype(F32), -1.0)
    high, middle, low = pieces_of(gate)
    table = jnp.where(piece == 0, place, jnp.where(piece == 1, high, jnp.where(piece == 2, middle, low)))
    out[:, :width] = grad[...]
    out[:, width:] = table.T.astype(BF16)


def collect_body(number, meta, *refs):
    blocks, outs = refs[:number], refs[-2:]
    tokens = blocks[0].shape[0]
    extent = 2 * outs[0].shape[1] - blocks[0].shape[1]
    large = outs[0].shape[1] - extent
    for half, out in enumerate(outs):
        start = pl.multiple_of(lax.bitwise_xor(1 - meta[4], half) * large, large)
        for k in range(number):
            out[k * tokens : (k + 1) * tokens, :large] = blocks[k][:, pl.ds(start, large)]
            out[k * tokens : (k + 1) * tokens, large:] = blocks[k][:, 2 * large :]


def forward_body(meta, hidden, weight, out):
    rows = hidden[:, 0].reshape(out.shape[0], hidden.shape[3])
    out[...] = jnp.dot(rows, weight[...], preferred_element_type=F32).astype(BF16)


def forward_first_body(peers, meta, hidden, weight, *refs):
    outs, (rows, matrix, sems) = refs[: len(peers)], refs[len(peers) :]
    tile = matrix.shape[2]
    copies = []
    for at, peer in enumerate(peers):
        part = hidden.at[:, lax.bitwise_xor(meta[0], peer)]
        copies.append(pltpu.make_async_copy(part, rows.at[at], sems.at[at]))
    for at in range(matrix.shape[0]):
        part = weight.at[:, at * tile : (at + 1) * tile]
        copies.append(pltpu.make_async_copy(part, matrix.at[at], sems.at[len(peers) + at]))
    for copy in copies:
        copy.start()
    for copy in copies[: len(peers)]:
        copy.wait()
    length = outs[0].shape[0]
    value = rows[...].reshape(len(peers) * length, rows.shape[3])
    for at in range(matrix.shape[0]):
        copies[len(peers) + at].wait()
        product = jnp.dot(value, matrix[at], preferred_element_type=F32).astype(BF16)
        for number, out in enumerate(outs):
            out[:, at * tile : (at + 1) * tile] = product[number * length : (number + 1) * length]


def turn_body(meta, hidden, after, out, final, final_turned):
    value = hidden[:, 0].reshape(final.shape)
    out[0] = value.T
    final[...] = value
    final_turned[...] = value.T


def turn_other_body(meta, hidden, out):
    out[...] = hidden[...].T


def selection(table, count, expert, rows):
    place = table[pl.ds(expert, 1), :]
    gate = table[pl.ds(expert + count, 1), :] + table[pl.ds(expert + 2 * count, 1), :]
    gate = gate + table[pl.ds(expert + 3 * count, 1), :]
    row = lax.broadcasted_iota(jnp.int32, (rows, place.shape[1]), 0).astype(F32)
    return row == place, gate


def grad_rows_body(plan, jobs, count, groups, meta, *refs):
    number = jobs * groups
    tables, tokens, outs, table = refs[:number], refs[number : 2 * number], refs[-1 - len(plan) : -1], refs[-1]
    rows = outs[0].shape[0] // len(plan[0][1]) // groups
    for job in range(jobs):
        asked = [(out, peer, parts.index(job)) for out, (peer, parts) in zip(outs, plan) if job in parts]
        for group in range(groups):
            table[...] = tables[job * groups + group][...].astype(F32).T
            choices, row_gates = [], []
            for _, peer, _ in asked:
                match, gate = selection(table, count, lax.bitwise_xor(meta[3], peer), rows)
                choices.append(jnp.where(match, 1.0, 0.0))
                row_gates.append(jnp.sum(jnp.where(match, gate, 0.0), 1, keepdims=True))
            choice = jnp.concatenate(choices, 0).astype(BF16)
            picked = jnp.dot(choice, tokens[job * groups + group][...], preferred_element_type=F32)
            value = (picked * jnp.concatenate(row_gates, 0)).astype(BF16)
            place = pl.multiple_of(lax.bitwise_xor(meta[1], group) * rows, rows)
            for at, (out, _, part) in enumerate(asked):
                out[pl.ds(place + part * groups * rows, rows), :] = value[at * rows : (at + 1) * rows]


def direct_rows_body(plan, jobs, number, count, meta, *refs):
    arrays, outs, table = refs[:number], refs[-1 - len(plan) : -1], refs[-1]
    extent, tokens = table.shape
    large = outs[0].shape[1]
    rows = outs[0].shape[0] // len(plan[0][1]) // len(jobs[0])
    for job, sources in enumerate(jobs):
        asked = [(out, peer, parts.index(job)) for out, (peer, parts) in zip(outs, plan) if job in parts]
        for group, (operand, first, whole) in enumerate(sources):
            here = slice(first, first + tokens)
            wide = 2 * large if whole else large
            table[...] = arrays[operand][here, wide : wide + extent].astype(F32).T
            choices, row_gates = [], []
            for _, peer, _ in asked:
                match, gate = selection(table, count, lax.bitwise_xor(meta[3], peer), rows)
                choices.append(jnp.where(match, 1.0, 0.0))
                row_gates.append(jnp.sum(jnp.where(match, gate, 0.0), 1, keepdims=True))
            if whole:
                columns = pl.ds(pl.multiple_of(lax.bitwise_xor(1 - meta[4], job) * large, large), large)
            else:
                columns = slice(0, large)
            choice = jnp.concatenate(choices, 0).astype(BF16)
            picked = jnp.dot(choice, arrays[operand][here, columns], preferred_element_type=F32)
            value = (picked * jnp.concatenate(row_gates, 0)).astype(BF16)
            place = pl.multiple_of(lax.bitwise_xor(meta[1], group) * rows, rows)
            for at, (out, _, part) in enumerate(asked):
                out[pl.ds(place + part * len(sources) * rows, rows), :] = value[at * rows : (at + 1) * rows]


def direct_combine_body(peers, count, cap, chosen, meta, *refs):
    blocks, returned, (part, table) = refs[: len(chosen)], refs[len(chosen) + 1 : -2], refs[-2:]
    extent, length = table.shape
    width = returned[0].shape[1]
    chunk = min(512, width)
    for number, k in enumerate(chosen):
        here = slice(number * length, (number + 1) * length)
        table[...] = blocks[number][:, width:].astype(F32).T
        start = pl.multiple_of(lax.bitwise_xor(meta[1], k) * cap, cap)
        highs, lows, marks = [], [], []
        for peer in range(peers):
            match, gate = selection(table, count, lax.bitwise_xor(meta[3], peer), cap)
            high = gate.astype(BF16).astype(F32)
            marks.append(jnp.where(match, 1.0, 0.0))
            highs.append(jnp.where(match, high, 0.0))
            lows.append(jnp.where(match, gate - high, 0.0))
        weights = jnp.concatenate([jnp.concatenate(highs, 0).T, jnp.concatenate(lows, 0).T], 0).astype(BF16)
        products = jnp.zeros((peers * cap, length), F32)
        for at in range(0, width, chunk):
            columns = slice(at, at + chunk)
            value = jnp.concatenate([ref[pl.ds(start, cap), columns] for ref in returned], 0)
            total = jnp.dot(weights, value, preferred_element_type=F32)
            part[here, columns] = (total[:length] + total[length:]).astype(part.dtype)
            products = products + lax.dot_general(
                value, blocks[number][:, columns], (((1,), (1,)), ((), ())), preferred_element_type=F32
            )
        products = products * jnp.concatenate(marks, 0)
        inner = [jnp.sum(products[peer * cap : (peer + 1) * cap], 0, keepdims=True) for peer in range(peers)]
        beside = part.shape[1] - width
        row = lax.broadcasted_iota(jnp.int32, (beside, length), 0)
        placed = jnp.zeros((beside, length), F32)
        for peer in range(peers):
            for at, piece in enumerate(pieces_of(inner[peer])):
                placed = jnp.where(row == at * count + lax.bitwise_xor(meta[3], peer), piece, placed)
        part[here, width:] = placed.T.astype(part.dtype)


def combine_body(peers, count, number, meta, *refs):
    packed, tokens, returned = refs[:number], refs[number : 2 * number], refs[2 * number + 1 : 2 * number + 1 + peers]
    part, table, weights, marks, inner = refs[-5:]
    rows, length = returned[0].shape[0], tokens[0].shape[0]
    step, last = pl.program_id(1), pl.num_programs(1) - 1

    def chosen(options):
        value = options[0][...]
        for at in range(1, number):
            value = jnp.where(pl.program_id(0) == at, options[at][...], value)
        return value

    @pl.when(step == 0)
    def _():
        inner[...] = jnp.zeros(inner.shape, F32)
        table[...] = chosen(packed).astype(F32).T
        highs, lows = [], []
        for peer in range(peers):
            match, gate = selection(table, count, lax.bitwise_xor(meta[3], peer), rows)
            high = gate.astype(BF16).astype(F32)
            marks[pl.ds(peer * rows, rows), :] = jnp.where(match, 1.0, 0.0)
            highs.append(jnp.where(match, high, 0.0))
            lows.append(jnp.where(match, gate - high, 0.0))
        weights[:length, :] = jnp.concatenate(highs, 0).T.astype(BF16)
        weights[length:, :] = jnp.concatenate(lows, 0).T.astype(BF16)

    @pl.when(step < last)
    def _():
        value = jnp.concatenate([ref[...] for ref in returned], 0)
        chunk = min(512, value.shape[1])
        for start in range(0, value.shape[1], chunk):
            total = jnp.dot(weights[...], value[:, start : start + chunk], preferred_element_type=F32)
            part[:, start : start + chunk] = (total[:length] + total[length:]).astype(part.dtype)
        products = lax.dot_general(value, chosen(tokens), (((1,), (1,)), ((), ())), preferred_element_type=F32)
        products = products * marks[...]
        for peer in range(peers):
            inner[peer : peer + 1, :] += jnp.sum(products[peer * rows : (peer + 1) * rows], 0, keepdims=True)

    @pl.when(step == last)
    def _():
        extent = -(-3 * count // 128) * 128
        row = lax.broadcasted_iota(jnp.int32, (extent, length), 0)
        placed = jnp.zeros((extent, length), F32)
        for at, piece in enumerate(pieces_of(inner[...])):
            for peer in range(peers):
                place = at * count + lax.bitwise_xor(meta[3], peer)
                placed = jnp.where(row == place, piece[peer : peer + 1, :], placed)
        part[:, :extent] = placed.T.astype(part.dtype)


def inside_body(plan, meta, weight, *refs):
    number = 1 + max(at for _, parts in plan for at, _ in parts)
    rows, out, token, (store, sems) = refs[:number], refs[-4], refs[-3], refs[-2:]
    shape = store.shape[1:]
    length, large = shape[0] * shape[1], weight.shape[1] // 2
    contract = (((1,), (1,)), ((), ()))
    copies = []
    for at, (peer, parts) in enumerate(plan):
        value = jnp.zeros((length, weight.shape[0]), F32)
        for half, (operand, start) in enumerate(parts):
            columns = pl.ds(pl.multiple_of(lax.bitwise_xor(1 - meta[4], half) * large, large), large)
            part = rows[operand][start : start + length, :]
            value = value + lax.dot_general(part, weight[:, columns], contract, preferred_element_type=F32)
        store[at] = value.astype(BF16).reshape(shape)
        copies.append(pltpu.make_async_copy(store.at[at], out.at[:, lax.bitwise_xor(meta[0], peer)], sems.at[at]))
        copies[-1].start()
    token[...] = jnp.zeros(token.shape, F32)
    for copy in copies:
        copy.wait()


def weight_grad_body(plan, number, half, meta, turned, *refs):
    rows, others, own = refs[:number], refs[-half - 1 : -1], refs[-1]
    length, tile = turned.shape[2], others[0].shape[1]

    def value_of(side, at):
        value = jnp.zeros((turned.shape[1], tile), F32)
        for peer, parts in plan:
            operand, start = parts[side]
            part = rows[operand][start : start + length, at * tile : (at + 1) * tile]
            value = value + jnp.dot(turned[peer], part, preferred_element_type=F32)
        return value

    for at in range(half):
        others[at][...] = value_of(0, at).astype(BF16)
        own[:, at * tile : (at + 1) * tile] = value_of(1, at)


def last_body(half, meta, turned, rows, turned_other, rows_other, earlier, *refs):
    others, (grads, store, sems) = refs[:half], refs[half:]
    tile = others[0].shape[1]
    copies = []
    for at in range(half):
        columns = slice(at * tile, (at + 1) * tile)
        value = jnp.dot(turned[...], rows[:, columns], preferred_element_type=F32)
        value = value + jnp.dot(turned_other[...], rows_other[:, columns], preferred_element_type=F32)
        store[at] = (value + earlier[:, columns] + others[at][...].astype(F32)).astype(BF16)
        copies.append(pltpu.make_async_copy(store.at[at], grads.at[:, columns], sems.at[at]))
        copies[-1].start()
    for copy in copies:
        copy.wait()


def finish_body(count, meta, ids, kept, arrived, combined, gate_grads, token):
    width = combined.shape[1]
    combined[...] = (kept[:, :width] + arrived[:, :width].astype(F32)).astype(BF16)
    pieces = (kept[:, width:] + arrived[:, width:].astype(F32)).T
    inner = pieces[:count] + pieces[count : 2 * count] + pieces[2 * count : 3 * count]
    named = ids[...]
    found = jnp.zeros(gate_grads.shape, F32)
    for expert in range(count):
        found = found + jnp.where(named == expert, inner[expert : expert + 1, :], 0.0)
    gate_grads[...] = found
    token[...] = jnp.zeros(token.shape, F32)


def per_device(expert_ids, gates, hidden, weight, out_grad):
    count = lax.axis_size("expert")
    peers = 1 << ((count.bit_length() - 1) // 2)
    planes = count // peers
    tokens, top = expert_ids.shape
    cap = hidden.shape[1] // count
    width, inside = out_grad.shape[1], hidden.shape[2]
    fold = 1
    while fold * cap % 16:
        fold *= 2
    groups = planes // fold
    group_rows, group_tokens = fold * cap, fold * tokens
    rows = planes * cap
    tile = min(512, width // 2)
    steps = width // tile
    half = steps // 2
    large = width // 2
    room = 1 if fold == 1 else 3
    last = peers - 1
    anywhere = pl.BlockSpec(memory_space=pl.ANY)
    glance = pl.BlockSpec((16, 128), lambda *i: (0, 0))

    me = lax.axis_index("expert")
    core = lax.axis_index("dp")
    column, plane = me % peers, me // peers
    meta = jnp.stack([column, plane // fold, (plane % fold) * cap, me, core, plane, count]).astype(jnp.int32)

    def swap(value, distance):
        return lax.ppermute(value, "expert", [(e, e ^ distance) for e in range(count)])

    def exchange(value):
        return lax.ppermute(value, "dp", [(0, 1), (1, 0)])

    matrix = weight[0]
    if fold == 1:
        blocks = hidden.reshape(planes, peers, cap, inside)
    else:
        blocks = hidden.reshape(planes, peers, cap, inside).transpose(1, 0, 2, 3).reshape(1, peers, rows, inside)
    block = (blocks.shape[0], 1, blocks.shape[2], inside)

    ids_turned = expert_ids.T
    extent = -(-4 * count // 128) * 128
    short = pl.BlockSpec((top, tokens), lambda i, m: (0, 0))
    relay = peers == 4 and fold == 1
    packed = call(
        pack_body, "pack", (1,),
        [short, short, pl.BlockSpec((tokens, width), lambda i, m: (0, 0))],
        pl.BlockSpec((tokens, width + extent), lambda i, m: (0, 0)),
        jax.ShapeDtypeStruct((tokens, width + extent), BF16),
        meta, (ids_turned, gates.T, out_grad),
        room=room,
    )
    gathered = [packed]
    for k in range(1, planes):
        if k & (k - 1) == 0:
            gathered.append(swap(packed, peers * k))
        else:
            gathered.append(None)
    early = [gathered[1 << k] for k in range((planes - 1).bit_length())]

    def forward(peer, after):
        return call(
            lambda meta, *refs: forward_body(meta, refs[0], refs[1], refs[-1]), f"forward{peer}", (steps,),
            [
                pl.BlockSpec(block, lambda i, m: (0, lax.bitwise_xor(m[0], peer), 0, 0)),
                pl.BlockSpec((inside, tile), lambda i, m: (0, i)),
            ]
            + [glance] * len(after),
            pl.BlockSpec((rows, tile), lambda i, m: (0, i)),
            jax.ShapeDtypeStruct((rows, width), BF16),
            meta, (blocks, matrix, *after),
        )

    outputs, after = {}, ()
    if relay:
        outputs[1], outputs[2] = direct(
            functools.partial(forward_first_body, (1, 2)), "forward1", [jax.ShapeDtypeStruct((rows, width), BF16)] * 2,
            meta, (blocks, matrix),
            scratch=[
                pltpu.VMEM((2, planes, cap, inside), BF16),
                pltpu.VMEM((steps, inside, tile), BF16),
                pltpu.SemaphoreType.DMA((2 + steps,)),
            ],
            places={0: anywhere, 1: anywhere}, room=3.75,
        )
        after = (outputs[2], packed)
    for peer in [peer for peer in list(range(1, peers)) + [0] if peer not in outputs]:
        outputs[peer] = forward(peer, after)
        after = (outputs[peer], packed)
    returned = [outputs[0]] + [swap(outputs[peer], peer) for peer in range(1, last)]
    turned, hidden_last, turned_last = call(
        turn_body, "turn", (peers,),
        [pl.BlockSpec(block, lambda i, m: (0, lax.bitwise_xor(m[0], i), 0, 0)), glance],
        [pl.BlockSpec((1, inside, rows), lambda i, m: (i, 0, 0)), pl.BlockSpec((rows, inside), lambda i, m: (0, 0)),
         pl.BlockSpec((inside, rows), lambda i, m: (0, 0))],
        [
            jax.ShapeDtypeStruct((peers, inside, rows), BF16), jax.ShapeDtypeStruct((rows, inside), BF16),
            jax.ShapeDtypeStruct((inside, rows), BF16),
        ],
        meta, (blocks, outputs[0]),
    )

    turned_other = call(
        turn_other_body, "turn_other", (1,),
        [pl.BlockSpec((rows, inside), lambda i, m: (0, 0))],
        pl.BlockSpec((inside, rows), lambda i, m: (0, 0)),
        jax.ShapeDtypeStruct((inside, rows), BF16),
        meta, (exchange(hidden_last),),
    )
    final_output = follow(outputs[last], *returned[:0:-1], turned_other, *early)
    returned.append(swap(final_output, last))
    for k in range(1, planes):
        lowest = k & -k
        if k != lowest:
            gathered[k] = swap(gathered[k ^ lowest], peers * lowest)
    if fold > 1:
        gathered = [jnp.concatenate(gathered[g * fold : (g + 1) * fold], 0) for g in range(groups)]

    def other_half(i, m):
        return (0, 1 - m[4])

    def own_half(i, m):
        return (0, m[4])

    def build_rows(name, plan, jobs, after, cost=COST):
        sources = [source for job in jobs for source in job]
        return call(
            functools.partial(grad_rows_body, plan, len(jobs), count, groups), name, (1,),
            [pl.BlockSpec((group_tokens, extent), table_at) for _, table_at, _ in sources]
            + [pl.BlockSpec((group_tokens, large), data_at) for _, _, data_at in sources]
            + [glance] * len(after),
            [pl.BlockSpec((len(parts) * rows, large), lambda i, m: (0, 0)) for _, parts in plan],
            [jax.ShapeDtypeStruct((len(parts) * rows, large), BF16) for _, parts in plan],
            meta, (*[value for value, _, _ in sources] * 2, *after),
            scratch=[pltpu.VMEM((extent, group_tokens), F32)],
            room=room, cost=cost,
        )

    def beside(i, m):
        return (0, width // extent)

    jobs = [[(value, beside, at) for value in gathered] for at in (other_half, own_half)]
    if relay:
        beside_shape = jax.ShapeDtypeStruct((planes * tokens, large + extent), BF16)
        collected = direct(
            functools.partial(collect_body, planes), "collect", [beside_shape] * 2, meta, (*gathered, final_output),
        )
        near = [swap(value, 1 << number) for number, value in enumerate(collected)]
        plan = ((0, (0, 1)), (1, (1,)), (2, (0,)))
        own_jobs = [[(k, 0, True) for k in range(planes)]] * 2
        made = direct(
            functools.partial(direct_rows_body, plan, own_jobs, planes, count), "own_rows",
            [jax.ShapeDtypeStruct((len(parts) * rows, large), BF16) for _, parts in plan],
            meta, (*gathered, collected[0]), scratch=[pltpu.VMEM((extent, tokens), F32)],
        )
        arrived = [
            [(made[0], 0), (made[0], 1)], [None, (swap(made[1], 1), 0)], [(swap(made[2], 2), 0), None], [None, None],
        ]
    else:
        made = build_rows("own_rows", tuple((peer, (0, 1)) for peer in range(peers)), jobs, (final_output,))
        arrived = [[(made[0], 0), (made[0], 1)]]
        for peer in range(1, peers):
            got = swap(made[peer], peer)
            arrived.append([(got, 0), (got, 1)])

    padded = width + -(-3 * count // 128) * 128

    def combine(chosen, dtype, after):
        first, stride = chosen[0], len(chosen) > 1 and chosen[1] - chosen[0]
        columns = width if fold == 1 else large

        def part_of(k, i, m):
            return (lax.bitwise_xor(m[1], k * stride + first), jnp.minimum(i, width // columns - 1))

        blocks_of = [gathered[group] for group in chosen]
        return call(
            functools.partial(combine_body, peers, count, len(chosen)), f"combine{first}", (len(chosen), width // columns + 1),
            [pl.BlockSpec((group_tokens, extent), lambda k, i, m: (0, width // extent))] * len(chosen)
            + [pl.BlockSpec((group_tokens, columns), lambda k, i, m: (0, jnp.minimum(i, width // columns - 1)))] * len(chosen)
            + [glance]
            + [pl.BlockSpec((group_rows, columns), part_of)] * peers,
            pl.BlockSpec((group_tokens, columns), lambda k, i, m: (k, i)),
            jax.ShapeDtypeStruct((len(chosen) * group_tokens, padded), dtype),
            meta, (*blocks_of, *blocks_of, after, *returned),
            scratch=[
                pltpu.VMEM((extent, group_tokens), F32),
                pltpu.VMEM((2 * group_tokens, peers * group_rows), BF16),
                pltpu.VMEM((peers * group_rows, group_tokens), F32),
                pltpu.VMEM((peers, group_tokens), F32),
            ],
            room=room,
        )

    def direct_combine(chosen, dtype, after):
        return direct(
            functools.partial(direct_combine_body, peers, count, cap, tuple(chosen)), f"combine{chosen[0]}",
            jax.ShapeDtypeStruct((len(chosen) * tokens, padded), dtype),
            meta, (*[gathered[k] for k in chosen], after, *returned),
            scratch=[pltpu.VMEM((extent, tokens), F32)],
        )

    if relay:
        combine = direct_combine
    if fold == 1:
        leaving = combine(range(1, planes, 2), BF16, made[0])
        combine_done = combine(range(0, planes, 2), F32, leaving)
        sums = [combine_done[k * tokens : (k + 1) * tokens] for k in range(planes // 2)]
    else:
        parts = [combine([group], F32, made[0]) for group in range(groups)]
        combine_done = parts[-1]
        sums = [parts[k // fold][k % fold * tokens : (k % fold + 1) * tokens] for k in range(planes)]
        leaving = jnp.concatenate(sums[1::2], 0).astype(BF16)
        sums = sums[0::2]
    distance = 1
    first_sums = None
    while len(sums) > 1:
        got = swap(leaving, peers * distance)
        pieces = [got[k * tokens : (k + 1) * tokens].astype(F32) for k in range(len(sums))]
        sums = [mine + piece for mine, piece in zip(sums, pieces)]
        leaving = [value.astype(BF16) for value in sums[1::2]]
        leaving = leaving[0] if len(leaving) == 1 else jnp.concatenate(leaving, 0)
        sums = sums[0::2]
        first_sums = leaving if first_sums is None else first_sums
        distance *= 2
    summed = swap(leaving, peers * distance)

    if relay:
        plan = ((0, (0,)), (2, (0,)), (0, (1,)), (1, (1,)))
        near_jobs = [[(job, k * tokens, False) for k in range(planes)] for job in range(2)]
        made = direct(
            functools.partial(direct_rows_body, plan, near_jobs, 2, count), "near_rows",
            [jax.ShapeDtypeStruct((rows, large), BF16)] * 4,
            meta, (*near, combine_done), scratch=[pltpu.VMEM((extent, tokens), F32)], cost=NEAR_COST,
        )
        arrived[1][0], arrived[2][1] = (made[0], 0), (made[2], 0)
        arrived[3] = [(swap(made[1], 2), 0), (swap(made[3], 1), 0)]

    grads_shape = jax.ShapeDtypeStruct(blocks.shape, BF16)
    def rows_of(chosen):
        arrays, plan = [], []
        for peer in chosen:
            parts = []
            for value, at in arrived[peer]:
                known = [number for number, array in enumerate(arrays) if array is value]
                if not known:
                    arrays.append(value)
                parts.append((known[0] if known else len(arrays) - 1, at * rows))
            plan.append((peer, tuple(parts)))
        return arrays, tuple(plan)

    def inside_grad(chosen, earlier, after):
        arrays, plan = rows_of(chosen)
        operands = [matrix, *arrays, *after] + ([] if earlier is None else [earlier])
        return direct(
            functools.partial(inside_body, plan), f"inside{chosen[0]}",
            [grads_shape, jax.ShapeDtypeStruct((16, 128), F32)],
            meta, operands,
            out_specs=[anywhere, pl.BlockSpec(memory_space=pltpu.VMEM)],
            scratch=[
                pltpu.VMEM((len(chosen), block[0], block[2], inside), BF16),
                pltpu.SemaphoreType.DMA((len(chosen),)),
            ],
            aliases=None if earlier is None else {len(operands): 0},
            places={} if earlier is None else {len(operands) - 1: anywhere},
        )

    hidden_grads, token = inside_grad(range(last), None, (made[1][:16, :128], first_sums[:16, :128]))
    arrays, plan = rows_of(range(last))
    *totals_other, total_own = direct(
        functools.partial(weight_grad_body, plan, len(arrays), half), "weight_grad",
        [jax.ShapeDtypeStruct((inside, tile), BF16)] * half + [jax.ShapeDtypeStruct((inside, large), F32)],
        meta, (turned, *arrays, token),
    )
    totals_other = [exchange(value) for value in totals_other]
    last_other, last_own = arrived[last]
    rows_own = last_own[0] if relay else last_own[0][rows:]
    rows_other = last_other[0] if relay else last_other[0][:rows]

    combined, gate_grads, finished = direct(
        functools.partial(finish_body, count), "finish",
        [
            jax.ShapeDtypeStruct((tokens, width), BF16), jax.ShapeDtypeStruct((top, tokens), F32),
            jax.ShapeDtypeStruct((16, 128), F32),
        ],
        meta, (ids_turned, sums[0], summed),
    )
    followed = follow(rows_other, finished, last_own[0])
    rows_other = exchange(followed)
    if relay:
        arrived[last][0] = (followed, 0)
    hidden_grads, _ = inside_grad([last], hidden_grads, ())
    weight_grads = direct(
        functools.partial(last_body, half), "last", jax.ShapeDtypeStruct((inside, large), BF16),
        meta, (turned_last, rows_own, turned_other, rows_other, total_own, *totals_other),
        out_specs=anywhere,
        scratch=[pltpu.VMEM((half, inside, tile), BF16), pltpu.SemaphoreType.DMA((half,))],
    )

    if fold > 1:
        hidden_grads = hidden_grads.reshape(peers, planes, cap, inside).transpose(1, 0, 2, 3)
    return combined, gate_grads.T, hidden_grads.reshape(hidden.shape), weight_grads[None]


def solution(mesh):
    placed = (
        P(("expert", "dp"), None),
        P(("expert", "dp"), None),
        P("expert", "dp", None),
        P("expert", None, None),
        P(("expert", "dp"), None),
    )
    return jax.shard_map(
        per_device,
        mesh=mesh,
        in_specs=placed,
        out_specs=(
            P(("expert", "dp"), None),
            P(("expert", "dp"), None),
            P("expert", "dp", None),
            P("expert", None, "dp"),
        ),
        check_vma=False,
    )
```

```python
import functools

import jax
import jax.numpy as jnp
from jax import lax
from jax.experimental import pallas as pl
from jax.experimental.pallas import tpu as pltpu
from jax.sharding import PartitionSpec as P

F32 = jnp.float32
BF16 = jnp.bfloat16
VMEM_BYTES = 16 * 1024 * 1024
COST = 1024
NEAR_COST = 10**10


def call(body, name, grid, in_specs, out_specs, out_shape, scalars, operands, scratch=(), aliases=None, room=1, cost=COST):
    return pl.pallas_call(
        body,
        name=name,
        grid_spec=pltpu.PrefetchScalarGridSpec(
            num_scalar_prefetch=1, grid=grid, in_specs=in_specs, out_specs=out_specs, scratch_shapes=scratch
        ),
        out_shape=out_shape,
        input_output_aliases=aliases or {},
        cost_estimate=pl.CostEstimate(flops=cost, bytes_accessed=COST, transcendentals=0),
        compiler_params=pltpu.CompilerParams(vmem_limit_bytes=room * VMEM_BYTES),
    )(scalars, *operands)


def direct(body, name, out_shape, scalars, operands, out_specs=None, scratch=(), aliases=None, places=None, room=1, cost=COST):
    places = places or {}
    vmem, smem = pl.BlockSpec(memory_space=pltpu.VMEM), pl.BlockSpec(memory_space=pltpu.SMEM)
    several = isinstance(out_shape, (list, tuple))
    return pl.pallas_call(
        body,
        name=name,
        in_specs=[smem] + [places.get(at, vmem) for at in range(len(operands))],
        out_specs=out_specs or ([vmem] * len(out_shape) if several else vmem),
        out_shape=out_shape,
        scratch_shapes=scratch,
        input_output_aliases=aliases or {},
        cost_estimate=pl.CostEstimate(flops=cost, bytes_accessed=COST, transcendentals=0),
        compiler_params=pltpu.CompilerParams(vmem_limit_bytes=int(room * VMEM_BYTES)),
    )(scalars, *operands)


def follow(value, *earlier):
    anywhere = pl.BlockSpec(memory_space=pl.ANY)
    return pl.pallas_call(
        lambda *refs: None,
        name="follow",
        grid=(1,),
        in_specs=[anywhere] + [pl.BlockSpec((16, 128), lambda i: (0, 0))] * len(earlier),
        out_specs=anywhere,
        out_shape=jax.ShapeDtypeStruct(value.shape, value.dtype),
        input_output_aliases={0: 0},
        cost_estimate=pl.CostEstimate(flops=COST, bytes_accessed=COST, transcendentals=0),
        compiler_params=pltpu.CompilerParams(vmem_limit_bytes=VMEM_BYTES),
    )(value, *earlier)


def token_body(meta, *refs):
    refs[-1][...] = jnp.zeros(refs[-1].shape, F32)


def pieces_of(value):
    high = value.astype(BF16).astype(F32)
    middle = (value - high).astype(BF16).astype(F32)
    return high, middle, value - high - middle


def pack_body(meta, ids, gates, grad, out):
    width, tokens = grad.shape[1], grad.shape[0]
    extent = out.shape[1] - width
    count = meta[6]
    expert = lax.broadcasted_iota(jnp.int32, (extent, tokens), 0)
    piece = jnp.zeros((extent, tokens), jnp.int32)
    for number in range(1, 4):
        piece = piece + jnp.where(expert >= number * count, 1, 0)
    local = expert - piece * count
    named = jnp.zeros((extent, tokens), F32)
    gate = jnp.zeros((extent, tokens), F32)
    for choice in range(ids.shape[0]):
        hit = ids[choice : choice + 1, :] == local
        named = named + jnp.where(hit, 1.0, 0.0)
        gate = gate + jnp.where(hit, gates[choice : choice + 1, :], 0.0)
    before = lax.broadcasted_iota(jnp.int32, (tokens, tokens), 0) < lax.broadcasted_iota(jnp.int32, (tokens, tokens), 1)
    earlier = jnp.dot(named.astype(BF16), jnp.where(before, 1.0, 0.0).astype(BF16), preferred_element_type=F32)
    place = jnp.where(named > 0.0, earlier + meta[2].astype(F32), -1.0)
    high, middle, low = pieces_of(gate)
    table = jnp.where(piece == 0, place, jnp.where(piece == 1, high, jnp.where(piece == 2, middle, low)))
    out[:, :width] = grad[...]
    out[:, width:] = table.T.astype(BF16)


def collect_body(number, meta, *refs):
    blocks, outs = refs[:number], refs[-2:]
    tokens = blocks[0].shape[0]
    extent = 2 * outs[0].shape[1] - blocks[0].shape[1]
    large = outs[0].shape[1] - extent
    for half, out in enumerate(outs):
        start = pl.multiple_of(lax.bitwise_xor(1 - meta[4], half) * large, large)
        for k in range(number):
            out[k * tokens : (k + 1) * tokens, :large] = blocks[k][:, pl.ds(start, large)]
            out[k * tokens : (k + 1) * tokens, large:] = blocks[k][:, 2 * large :]


def forward_body(meta, hidden, weight, out):
    rows = hidden[:, 0].reshape(out.shape[0], hidden.shape[3])
    out[...] = jnp.dot(rows, weight[...], preferred_element_type=F32).astype(BF16)


def forward_first_body(peers, meta, hidden, weight, *refs):
    outs, (rows, matrix, store, sems, out_sems) = refs[: len(peers)], refs[len(peers) :]
    tile = matrix.shape[2]
    copies = []
    for at, peer in enumerate(peers):
        part = hidden.at[:, lax.bitwise_xor(meta[0], peer)]
        copies.append(pltpu.make_async_copy(part, rows.at[at], sems.at[at]))
    for at in range(matrix.shape[0]):
        part = weight.at[:, at * tile : (at + 1) * tile]
        copies.append(pltpu.make_async_copy(part, matrix.at[at], sems.at[len(peers) + at]))
    for copy in copies:
        copy.start()
    for copy in copies[: len(peers)]:
        copy.wait()
    length = outs[0].shape[0]
    value = rows[...].reshape(len(peers) * length, rows.shape[3])
    results = []
    for at in range(matrix.shape[0]):
        copies[len(peers) + at].wait()
        product = jnp.dot(value, matrix[at], preferred_element_type=F32).astype(BF16)
        for number, out in enumerate(outs):
            store[at, number] = product[number * length : (number + 1) * length]
            target = out.at[:, at * tile : (at + 1) * tile]
            results.append(pltpu.make_async_copy(store.at[at, number], target, out_sems.at[at, number]))
            results[-1].start()
    for copy in results:
        copy.wait()


def turn_body(meta, hidden, after, out, final, final_turned):
    value = hidden[:, 0].reshape(final.shape)
    out[0] = value.T
    final[...] = value
    final_turned[...] = value.T


def turn_other_body(meta, hidden, out):
    out[...] = hidden[...].T


def selection(table, count, expert, rows):
    place = table[pl.ds(expert, 1), :]
    gate = table[pl.ds(expert + count, 1), :] + table[pl.ds(expert + 2 * count, 1), :]
    gate = gate + table[pl.ds(expert + 3 * count, 1), :]
    row = lax.broadcasted_iota(jnp.int32, (rows, place.shape[1]), 0).astype(F32)
    return row == place, gate


def grad_rows_body(plan, jobs, count, groups, meta, *refs):
    number = jobs * groups
    tables, tokens, outs, table = refs[:number], refs[number : 2 * number], refs[-1 - len(plan) : -1], refs[-1]
    rows = outs[0].shape[0] // len(plan[0][1]) // groups
    for job in range(jobs):
        asked = [(out, peer, parts.index(job)) for out, (peer, parts) in zip(outs, plan) if job in parts]
        for group in range(groups):
            table[...] = tables[job * groups + group][...].astype(F32).T
            choices, row_gates = [], []
            for _, peer, _ in asked:
                match, gate = selection(table, count, lax.bitwise_xor(meta[3], peer), rows)
                choices.append(jnp.where(match, 1.0, 0.0))
                row_gates.append(jnp.sum(jnp.where(match, gate, 0.0), 1, keepdims=True))
            choice = jnp.concatenate(choices, 0).astype(BF16)
            picked = jnp.dot(choice, tokens[job * groups + group][...], preferred_element_type=F32)
            value = (picked * jnp.concatenate(row_gates, 0)).astype(BF16)
            place = pl.multiple_of(lax.bitwise_xor(meta[1], group) * rows, rows)
            for at, (out, _, part) in enumerate(asked):
                out[pl.ds(place + part * groups * rows, rows), :] = value[at * rows : (at + 1) * rows]


def direct_rows_body(plan, jobs, number, count, meta, *refs):
    arrays, outs, table = refs[:number], refs[-1 - len(plan) : -1], refs[-1]
    extent, tokens = table.shape
    large = outs[0].shape[1]
    rows = outs[0].shape[0] // len(plan[0][1]) // len(jobs[0])
    for job, sources in enumerate(jobs):
        asked = [(out, peer, parts.index(job)) for out, (peer, parts) in zip(outs, plan) if job in parts]
        for group, (operand, first, whole) in enumerate(sources):
            here = slice(first, first + tokens)
            wide = 2 * large if whole else large
            table[...] = arrays[operand][here, wide : wide + extent].astype(F32).T
            choices, row_gates = [], []
            for _, peer, _ in asked:
                match, gate = selection(table, count, lax.bitwise_xor(meta[3], peer), rows)
                choices.append(jnp.where(match, 1.0, 0.0))
                row_gates.append(jnp.sum(jnp.where(match, gate, 0.0), 1, keepdims=True))
            if whole:
                columns = pl.ds(pl.multiple_of(lax.bitwise_xor(1 - meta[4], job) * large, large), large)
            else:
                columns = slice(0, large)
            choice = jnp.concatenate(choices, 0).astype(BF16)
            picked = jnp.dot(choice, arrays[operand][here, columns], preferred_element_type=F32)
            value = (picked * jnp.concatenate(row_gates, 0)).astype(BF16)
            place = pl.multiple_of(lax.bitwise_xor(meta[1], group) * rows, rows)
            for at, (out, _, part) in enumerate(asked):
                out[pl.ds(place + part * len(sources) * rows, rows), :] = value[at * rows : (at + 1) * rows]


def direct_combine_body(peers, count, cap, chosen, meta, *refs):
    blocks, returned, (part, table) = refs[: len(chosen)], refs[len(chosen) + 1 : -2], refs[-2:]
    extent, length = table.shape
    width = returned[0].shape[1]
    chunk = min(512, width)
    for number, k in enumerate(chosen):
        here = slice(number * length, (number + 1) * length)
        table[...] = blocks[number][:, width:].astype(F32).T
        start = pl.multiple_of(lax.bitwise_xor(meta[1], k) * cap, cap)
        highs, lows, marks = [], [], []
        for peer in range(peers):
            match, gate = selection(table, count, lax.bitwise_xor(meta[3], peer), cap)
            high = gate.astype(BF16).astype(F32)
            marks.append(jnp.where(match, 1.0, 0.0))
            highs.append(jnp.where(match, high, 0.0))
            lows.append(jnp.where(match, gate - high, 0.0))
        weights = jnp.concatenate([jnp.concatenate(highs, 0).T, jnp.concatenate(lows, 0).T], 0).astype(BF16)
        products = jnp.zeros((peers * cap, length), F32)
        for at in range(0, width, chunk):
            columns = slice(at, at + chunk)
            value = jnp.concatenate([ref[pl.ds(start, cap), columns] for ref in returned], 0)
            total = jnp.dot(weights, value, preferred_element_type=F32)
            part[here, columns] = (total[:length] + total[length:]).astype(part.dtype)
            products = products + lax.dot_general(
                value, blocks[number][:, columns], (((1,), (1,)), ((), ())), preferred_element_type=F32
            )
        products = products * jnp.concatenate(marks, 0)
        inner = [jnp.sum(products[peer * cap : (peer + 1) * cap], 0, keepdims=True) for peer in range(peers)]
        beside = part.shape[1] - width
        row = lax.broadcasted_iota(jnp.int32, (beside, length), 0)
        placed = jnp.zeros((beside, length), F32)
        for peer in range(peers):
            for at, piece in enumerate(pieces_of(inner[peer])):
                placed = jnp.where(row == at * count + lax.bitwise_xor(meta[3], peer), piece, placed)
        part[here, width:] = placed.T.astype(part.dtype)


def combine_body(peers, count, number, meta, *refs):
    packed, tokens, returned = refs[:number], refs[number : 2 * number], refs[2 * number + 1 : 2 * number + 1 + peers]
    part, table, weights, marks, inner = refs[-5:]
    rows, length = returned[0].shape[0], tokens[0].shape[0]
    step, last = pl.program_id(1), pl.num_programs(1) - 1

    def chosen(options):
        value = options[0][...]
        for at in range(1, number):
            value = jnp.where(pl.program_id(0) == at, options[at][...], value)
        return value

    @pl.when(step == 0)
    def _():
        inner[...] = jnp.zeros(inner.shape, F32)
        table[...] = chosen(packed).astype(F32).T
        highs, lows = [], []
        for peer in range(peers):
            match, gate = selection(table, count, lax.bitwise_xor(meta[3], peer), rows)
            high = gate.astype(BF16).astype(F32)
            marks[pl.ds(peer * rows, rows), :] = jnp.where(match, 1.0, 0.0)
            highs.append(jnp.where(match, high, 0.0))
            lows.append(jnp.where(match, gate - high, 0.0))
        weights[:length, :] = jnp.concatenate(highs, 0).T.astype(BF16)
        weights[length:, :] = jnp.concatenate(lows, 0).T.astype(BF16)

    @pl.when(step < last)
    def _():
        value = jnp.concatenate([ref[...] for ref in returned], 0)
        chunk = min(512, value.shape[1])
        for start in range(0, value.shape[1], chunk):
            total = jnp.dot(weights[...], value[:, start : start + chunk], preferred_element_type=F32)
            part[:, start : start + chunk] = (total[:length] + total[length:]).astype(part.dtype)
        products = lax.dot_general(value, chosen(tokens), (((1,), (1,)), ((), ())), preferred_element_type=F32)
        products = products * marks[...]
        for peer in range(peers):
            inner[peer : peer + 1, :] += jnp.sum(products[peer * rows : (peer + 1) * rows], 0, keepdims=True)

    @pl.when(step == last)
    def _():
        extent = -(-3 * count // 128) * 128
        row = lax.broadcasted_iota(jnp.int32, (extent, length), 0)
        placed = jnp.zeros((extent, length), F32)
        for at, piece in enumerate(pieces_of(inner[...])):
            for peer in range(peers):
                place = at * count + lax.bitwise_xor(meta[3], peer)
                placed = jnp.where(row == place, piece[peer : peer + 1, :], placed)
        part[:, :extent] = placed.T.astype(part.dtype)


def inside_body(plan, meta, weight, *refs):
    number = 1 + max(at for _, parts in plan for at, _ in parts)
    rows, out, token, (store, sems) = refs[:number], refs[-4], refs[-3], refs[-2:]
    shape = store.shape[1:]
    length, large = shape[0] * shape[1], weight.shape[1] // 2
    contract = (((1,), (1,)), ((), ()))
    copies = []
    for at, (peer, parts) in enumerate(plan):
        value = jnp.zeros((length, weight.shape[0]), F32)
        for half, (operand, start) in enumerate(parts):
            columns = pl.ds(pl.multiple_of(lax.bitwise_xor(1 - meta[4], half) * large, large), large)
            part = rows[operand][start : start + length, :]
            value = value + lax.dot_general(part, weight[:, columns], contract, preferred_element_type=F32)
        store[at] = value.astype(BF16).reshape(shape)
        copies.append(pltpu.make_async_copy(store.at[at], out.at[:, lax.bitwise_xor(meta[0], peer)], sems.at[at]))
        copies[-1].start()
    token[...] = jnp.zeros(token.shape, F32)
    for copy in copies:
        copy.wait()


def weight_grad_body(plan, number, half, meta, turned, *refs):
    rows, others, own = refs[:number], refs[-half - 1 : -1], refs[-1]
    length, tile = turned.shape[2], others[0].shape[1]

    def value_of(side, at):
        value = jnp.zeros((turned.shape[1], tile), F32)
        for peer, parts in plan:
            operand, start = parts[side]
            part = rows[operand][start : start + length, at * tile : (at + 1) * tile]
            value = value + jnp.dot(turned[peer], part, preferred_element_type=F32)
        return value

    for at in range(half):
        others[at][...] = value_of(0, at).astype(BF16)
        own[:, at * tile : (at + 1) * tile] = value_of(1, at)


def last_body(half, meta, turned, rows, turned_other, rows_other, earlier, *refs):
    others, (grads, store, sems) = refs[:half], refs[half:]
    tile = others[0].shape[1]
    copies = []
    for at in range(half):
        columns = slice(at * tile, (at + 1) * tile)
        value = jnp.dot(turned[...], rows[:, columns], preferred_element_type=F32)
        value = value + jnp.dot(turned_other[...], rows_other[:, columns], preferred_element_type=F32)
        store[at] = (value + earlier[:, columns] + others[at][...].astype(F32)).astype(BF16)
        copies.append(pltpu.make_async_copy(store.at[at], grads.at[:, columns], sems.at[at]))
        copies[-1].start()
    for copy in copies:
        copy.wait()


def finish_body(count, meta, ids, kept, arrived, combined, gate_grads, token):
    width = combined.shape[1]
    combined[...] = (kept[:, :width] + arrived[:, :width].astype(F32)).astype(BF16)
    pieces = (kept[:, width:] + arrived[:, width:].astype(F32)).T
    inner = pieces[:count] + pieces[count : 2 * count] + pieces[2 * count : 3 * count]
    named = ids[...]
    found = jnp.zeros(gate_grads.shape, F32)
    for expert in range(count):
        found = found + jnp.where(named == expert, inner[expert : expert + 1, :], 0.0)
    gate_grads[...] = found
    token[...] = jnp.zeros(token.shape, F32)


def per_device(expert_ids, gates, hidden, weight, out_grad):
    count = lax.axis_size("expert")
    peers = 1 << ((count.bit_length() - 1) // 2)
    planes = count // peers
    tokens, top = expert_ids.shape
    cap = hidden.shape[1] // count
    width, inside = out_grad.shape[1], hidden.shape[2]
    fold = 1
    while fold * cap % 16:
        fold *= 2
    groups = planes // fold
    group_rows, group_tokens = fold * cap, fold * tokens
    rows = planes * cap
    tile = min(512, width // 2)
    steps = width // tile
    half = steps // 2
    large = width // 2
    room = 1 if fold == 1 else 3
    last = peers - 1
    anywhere = pl.BlockSpec(memory_space=pl.ANY)
    glance = pl.BlockSpec((16, 128), lambda *i: (0, 0))

    me = lax.axis_index("expert")
    core = lax.axis_index("dp")
    column, plane = me % peers, me // peers
    meta = jnp.stack([column, plane // fold, (plane % fold) * cap, me, core, plane, count]).astype(jnp.int32)

    def swap(value, distance):
        return lax.ppermute(value, "expert", [(e, e ^ distance) for e in range(count)])

    def exchange(value):
        return lax.ppermute(value, "dp", [(0, 1), (1, 0)])

    matrix = weight[0]
    if fold == 1:
        blocks = hidden.reshape(planes, peers, cap, inside)
    else:
        blocks = hidden.reshape(planes, peers, cap, inside).transpose(1, 0, 2, 3).reshape(1, peers, rows, inside)
    block = (blocks.shape[0], 1, blocks.shape[2], inside)

    ids_turned = expert_ids.T
    extent = -(-4 * count // 128) * 128
    short = pl.BlockSpec((top, tokens), lambda i, m: (0, 0))
    relay = peers == 4 and fold == 1
    packed = call(
        pack_body, "pack", (1,),
        [short, short, pl.BlockSpec((tokens, width), lambda i, m: (0, 0))],
        pl.BlockSpec((tokens, width + extent), lambda i, m: (0, 0)),
        jax.ShapeDtypeStruct((tokens, width + extent), BF16),
        meta, (ids_turned, gates.T, out_grad),
        room=room,
    )
    gathered = [packed]
    for k in range(1, planes):
        if k & (k - 1) == 0:
            gathered.append(swap(packed, peers * k))
        else:
            gathered.append(None)

    def forward(peer, after):
        return call(
            lambda meta, *refs: forward_body(meta, refs[0], refs[1], refs[-1]), f"forward{peer}", (steps,),
            [
                pl.BlockSpec(block, lambda i, m: (0, lax.bitwise_xor(m[0], peer), 0, 0)),
                pl.BlockSpec((inside, tile), lambda i, m: (0, i)),
            ]
            + [glance] * len(after),
            pl.BlockSpec((rows, tile), lambda i, m: (0, i)),
            jax.ShapeDtypeStruct((rows, width), BF16),
            meta, (blocks, matrix, *after),
        )

    outputs, after = {}, ()
    if relay:
        outputs[1], outputs[2] = direct(
            functools.partial(forward_first_body, (1, 2)), "forward1", [jax.ShapeDtypeStruct((rows, width), BF16)] * 2,
            meta, (blocks, matrix),
            scratch=[
                pltpu.VMEM((2, planes, cap, inside), BF16),
                pltpu.VMEM((steps, inside, tile), BF16),
                pltpu.VMEM((steps, 2, rows, tile), BF16),
                pltpu.SemaphoreType.DMA((2 + steps,)),
                pltpu.SemaphoreType.DMA((steps, 2)),
            ],
            out_specs=[anywhere, anywhere],
            places={0: anywhere, 1: anywhere}, room=3.75,
        )
        after = (outputs[2], packed)
    for peer in [peer for peer in list(range(1, peers)) + [0] if peer not in outputs]:
        outputs[peer] = forward(peer, after)
        after = (outputs[peer], packed)
    returned = [outputs[0]] + [swap(outputs[peer], peer) for peer in range(1, peers)]
    turned, hidden_last, turned_last = call(
        turn_body, "turn", (peers,),
        [pl.BlockSpec(block, lambda i, m: (0, lax.bitwise_xor(m[0], i), 0, 0)), glance],
        [pl.BlockSpec((1, inside, rows), lambda i, m: (i, 0, 0)), pl.BlockSpec((rows, inside), lambda i, m: (0, 0)),
         pl.BlockSpec((inside, rows), lambda i, m: (0, 0))],
        [
            jax.ShapeDtypeStruct((peers, inside, rows), BF16), jax.ShapeDtypeStruct((rows, inside), BF16),
            jax.ShapeDtypeStruct((inside, rows), BF16),
        ],
        meta, (blocks, outputs[0]),
    )

    turned_other = call(
        turn_other_body, "turn_other", (1,),
        [pl.BlockSpec((rows, inside), lambda i, m: (0, 0))],
        pl.BlockSpec((inside, rows), lambda i, m: (0, 0)),
        jax.ShapeDtypeStruct((inside, rows), BF16),
        meta, (exchange(hidden_last),),
    )
    for k in range(1, planes):
        lowest = k & -k
        if k != lowest:
            gathered[k] = swap(gathered[k ^ lowest], peers * lowest)
    if fold > 1:
        gathered = [jnp.concatenate(gathered[g * fold : (g + 1) * fold], 0) for g in range(groups)]

    def other_half(i, m):
        return (0, 1 - m[4])

    def own_half(i, m):
        return (0, m[4])

    def build_rows(name, plan, jobs, after, cost=COST):
        sources = [source for job in jobs for source in job]
        return call(
            functools.partial(grad_rows_body, plan, len(jobs), count, groups), name, (1,),
            [pl.BlockSpec((group_tokens, extent), table_at) for _, table_at, _ in sources]
            + [pl.BlockSpec((group_tokens, large), data_at) for _, _, data_at in sources]
            + [glance] * len(after),
            [pl.BlockSpec((len(parts) * rows, large), lambda i, m: (0, 0)) for _, parts in plan],
            [jax.ShapeDtypeStruct((len(parts) * rows, large), BF16) for _, parts in plan],
            meta, (*[value for value, _, _ in sources] * 2, *after),
            scratch=[pltpu.VMEM((extent, group_tokens), F32)],
            room=room, cost=cost,
        )

    def beside(i, m):
        return (0, width // extent)

    jobs = [[(value, beside, at) for value in gathered] for at in (other_half, own_half)]
    if relay:
        plan = ((0, (0, 1)), (1, (1,)), (2, (0,)))
        own_jobs = [[(k, 0, True) for k in range(planes)]] * 2
        made = direct(
            functools.partial(direct_rows_body, plan, own_jobs, planes, count), "own_rows",
            [jax.ShapeDtypeStruct((len(parts) * rows, large), BF16) for _, parts in plan],
            meta, gathered, scratch=[pltpu.VMEM((extent, tokens), F32)],
        )
        beside_shape = jax.ShapeDtypeStruct((planes * tokens, large + extent), BF16)
        arrival = call(
            token_body, "arrival", (1,), [glance] * (last + 3), glance, jax.ShapeDtypeStruct((16, 128), F32), meta,
            (*returned[1:], outputs[0], turned_other, made[1]),
        )
        collected = direct(
            functools.partial(collect_body, planes), "collect", [beside_shape] * 2, meta, (*gathered, arrival),
        )
        near = [swap(value, 1 << number) for number, value in enumerate(collected)]
        arrived = [
            [(made[0], 0), (made[0], 1)], [None, (swap(made[1], 1), 0)], [(swap(made[2], 2), 0), None], [None, None],
        ]
    else:
        made = build_rows("own_rows", tuple((peer, (0, 1)) for peer in range(peers)), jobs, (outputs[0],))
        arrived = [[(made[0], 0), (made[0], 1)]]
        for peer in range(1, peers):
            got = swap(made[peer], peer)
            arrived.append([(got, 0), (got, 1)])

    padded = width + -(-3 * count // 128) * 128

    def combine(chosen, dtype, after):
        first, stride = chosen[0], len(chosen) > 1 and chosen[1] - chosen[0]
        columns = width if fold == 1 else large

        def part_of(k, i, m):
            return (lax.bitwise_xor(m[1], k * stride + first), jnp.minimum(i, width // columns - 1))

        blocks_of = [gathered[group] for group in chosen]
        return call(
            functools.partial(combine_body, peers, count, len(chosen)), f"combine{first}", (len(chosen), width // columns + 1),
            [pl.BlockSpec((group_tokens, extent), lambda k, i, m: (0, width // extent))] * len(chosen)
            + [pl.BlockSpec((group_tokens, columns), lambda k, i, m: (0, jnp.minimum(i, width // columns - 1)))] * len(chosen)
            + [glance]
            + [pl.BlockSpec((group_rows, columns), part_of)] * peers,
            pl.BlockSpec((group_tokens, columns), lambda k, i, m: (k, i)),
            jax.ShapeDtypeStruct((len(chosen) * group_tokens, padded), dtype),
            meta, (*blocks_of, *blocks_of, after, *returned),
            scratch=[
                pltpu.VMEM((extent, group_tokens), F32),
                pltpu.VMEM((2 * group_tokens, peers * group_rows), BF16),
                pltpu.VMEM((peers * group_rows, group_tokens), F32),
                pltpu.VMEM((peers, group_tokens), F32),
            ],
            room=room,
        )

    def direct_combine(chosen, dtype, after):
        return direct(
            functools.partial(direct_combine_body, peers, count, cap, tuple(chosen)), f"combine{chosen[0]}",
            jax.ShapeDtypeStruct((len(chosen) * tokens, padded), dtype),
            meta, (*[gathered[k] for k in chosen], after, *returned),
            scratch=[pltpu.VMEM((extent, tokens), F32)],
        )

    if relay:
        combine = direct_combine
    if fold == 1:
        leaving = combine(range(1, planes, 2), BF16, made[0])
        combine_done = combine(range(0, planes, 2), F32, leaving)
        sums = [combine_done[k * tokens : (k + 1) * tokens] for k in range(planes // 2)]
    else:
        parts = [combine([group], F32, made[0]) for group in range(groups)]
        combine_done = parts[-1]
        sums = [parts[k // fold][k % fold * tokens : (k % fold + 1) * tokens] for k in range(planes)]
        leaving = jnp.concatenate(sums[1::2], 0).astype(BF16)
        sums = sums[0::2]
    distance = 1
    first_sums = None
    while len(sums) > 1:
        got = swap(leaving, peers * distance)
        pieces = [got[k * tokens : (k + 1) * tokens].astype(F32) for k in range(len(sums))]
        sums = [mine + piece for mine, piece in zip(sums, pieces)]
        leaving = [value.astype(BF16) for value in sums[1::2]]
        leaving = leaving[0] if len(leaving) == 1 else jnp.concatenate(leaving, 0)
        sums = sums[0::2]
        first_sums = leaving if first_sums is None else first_sums
        distance *= 2
    summed = swap(leaving, peers * distance)

    if relay:
        plan = ((0, (0,)), (2, (0,)), (0, (1,)), (1, (1,)))
        near_jobs = [[(job, k * tokens, False) for k in range(planes)] for job in range(2)]
        made = direct(
            functools.partial(direct_rows_body, plan, near_jobs, 2, count), "near_rows",
            [jax.ShapeDtypeStruct((rows, large), BF16)] * 4,
            meta, (*near, combine_done), scratch=[pltpu.VMEM((extent, tokens), F32)], cost=NEAR_COST,
        )
        arrived[1][0], arrived[2][1] = (made[0], 0), (made[2], 0)
        arrived[3] = [(swap(made[1], 2), 0), (swap(made[3], 1), 0)]

    grads_shape = jax.ShapeDtypeStruct(blocks.shape, BF16)
    def rows_of(chosen):
        arrays, plan = [], []
        for peer in chosen:
            parts = []
            for value, at in arrived[peer]:
                known = [number for number, array in enumerate(arrays) if array is value]
                if not known:
                    arrays.append(value)
                parts.append((known[0] if known else len(arrays) - 1, at * rows))
            plan.append((peer, tuple(parts)))
        return arrays, tuple(plan)

    def inside_grad(chosen, earlier, after):
        arrays, plan = rows_of(chosen)
        operands = [matrix, *arrays, *after] + ([] if earlier is None else [earlier])
        return direct(
            functools.partial(inside_body, plan), f"inside{chosen[0]}",
            [grads_shape, jax.ShapeDtypeStruct((16, 128), F32)],
            meta, operands,
            out_specs=[anywhere, pl.BlockSpec(memory_space=pltpu.VMEM)],
            scratch=[
                pltpu.VMEM((len(chosen), block[0], block[2], inside), BF16),
                pltpu.SemaphoreType.DMA((len(chosen),)),
            ],
            aliases=None if earlier is None else {len(operands): 0},
            places={} if earlier is None else {len(operands) - 1: anywhere},
        )

    hidden_grads, token = inside_grad(range(last), None, (made[1][:16, :128], first_sums[:16, :128]))
    arrays, plan = rows_of(range(last))
    *totals_other, total_own = direct(
        functools.partial(weight_grad_body, plan, len(arrays), half), "weight_grad",
        [jax.ShapeDtypeStruct((inside, tile), BF16)] * half + [jax.ShapeDtypeStruct((inside, large), F32)],
        meta, (turned, *arrays, token),
    )
    totals_other = [exchange(value) for value in totals_other]
    last_other, last_own = arrived[last]
    rows_own = last_own[0] if relay else last_own[0][rows:]
    rows_other = last_other[0] if relay else last_other[0][:rows]

    combined, gate_grads, finished = direct(
        functools.partial(finish_body, count), "finish",
        [
            jax.ShapeDtypeStruct((tokens, width), BF16), jax.ShapeDtypeStruct((top, tokens), F32),
            jax.ShapeDtypeStruct((16, 128), F32),
        ],
        meta, (ids_turned, sums[0], summed),
    )
    followed = follow(rows_other, finished, last_own[0])
    rows_other = exchange(followed)
    if relay:
        arrived[last][0] = (followed, 0)
    hidden_grads, _ = inside_grad([last], hidden_grads, ())
    weight_grads = direct(
        functools.partial(last_body, half), "last", jax.ShapeDtypeStruct((inside, large), BF16),
        meta, (turned_last, rows_own, turned_other, rows_other, total_own, *totals_other),
        out_specs=anywhere,
        scratch=[pltpu.VMEM((half, inside, tile), BF16), pltpu.SemaphoreType.DMA((half,))],
    )

    if fold > 1:
        hidden_grads = hidden_grads.reshape(peers, planes, cap, inside).transpose(1, 0, 2, 3)
    return combined, gate_grads.T, hidden_grads.reshape(hidden.shape), weight_grads[None]


def solution(mesh):
    placed = (
        P(("expert", "dp"), None),
        P(("expert", "dp"), None),
        P("expert", "dp", None),
        P("expert", None, None),
        P(("expert", "dp"), None),
    )
    return jax.shard_map(
        per_device,
        mesh=mesh,
        in_specs=placed,
        out_specs=(
            P(("expert", "dp"), None),
            P(("expert", "dp"), None),
            P("expert", "dp", None),
            P("expert", None, "dp"),
        ),
        check_vma=False,
    )
```

```python
import functools

import jax
import jax.numpy as jnp
from jax import lax
from jax.experimental import pallas as pl
from jax.experimental.pallas import tpu as pltpu
from jax.sharding import PartitionSpec as P

F32 = jnp.float32
BF16 = jnp.bfloat16
VMEM_BYTES = 16 * 1024 * 1024
COST = 1024
NEAR_COST = 10**10
LONG_COST = 10**11


def call(body, name, grid, in_specs, out_specs, out_shape, scalars, operands, scratch=(), aliases=None, room=1, cost=COST):
    return pl.pallas_call(
        body,
        name=name,
        grid_spec=pltpu.PrefetchScalarGridSpec(
            num_scalar_prefetch=1, grid=grid, in_specs=in_specs, out_specs=out_specs, scratch_shapes=scratch
        ),
        out_shape=out_shape,
        input_output_aliases=aliases or {},
        cost_estimate=pl.CostEstimate(flops=cost, bytes_accessed=COST, transcendentals=0),
        compiler_params=pltpu.CompilerParams(vmem_limit_bytes=room * VMEM_BYTES),
    )(scalars, *operands)


def direct(body, name, out_shape, scalars, operands, out_specs=None, scratch=(), aliases=None, places=None, room=1, cost=COST):
    places = places or {}
    vmem, smem = pl.BlockSpec(memory_space=pltpu.VMEM), pl.BlockSpec(memory_space=pltpu.SMEM)
    several = isinstance(out_shape, (list, tuple))
    return pl.pallas_call(
        body,
        name=name,
        in_specs=[smem] + [places.get(at, vmem) for at in range(len(operands))],
        out_specs=out_specs or ([vmem] * len(out_shape) if several else vmem),
        out_shape=out_shape,
        scratch_shapes=scratch,
        input_output_aliases=aliases or {},
        cost_estimate=pl.CostEstimate(flops=cost, bytes_accessed=COST, transcendentals=0),
        compiler_params=pltpu.CompilerParams(vmem_limit_bytes=int(room * VMEM_BYTES)),
    )(scalars, *operands)


def follow(value, *earlier):
    anywhere = pl.BlockSpec(memory_space=pl.ANY)
    return pl.pallas_call(
        lambda *refs: None,
        name="follow",
        grid=(1,),
        in_specs=[anywhere] + [pl.BlockSpec((16, 128), lambda i: (0, 0))] * len(earlier),
        out_specs=anywhere,
        out_shape=jax.ShapeDtypeStruct(value.shape, value.dtype),
        input_output_aliases={0: 0},
        cost_estimate=pl.CostEstimate(flops=COST, bytes_accessed=COST, transcendentals=0),
        compiler_params=pltpu.CompilerParams(vmem_limit_bytes=VMEM_BYTES),
    )(value, *earlier)


def token_body(meta, *refs):
    refs[-1][...] = jnp.zeros(refs[-1].shape, F32)


def pieces_of(value):
    high = value.astype(BF16).astype(F32)
    middle = (value - high).astype(BF16).astype(F32)
    return high, middle, value - high - middle


def pack_body(meta, ids, gates, grad, out):
    width, tokens = grad.shape[1], grad.shape[0]
    extent = out.shape[1] - width
    count = meta[6]
    expert = lax.broadcasted_iota(jnp.int32, (extent, tokens), 0)
    piece = jnp.zeros((extent, tokens), jnp.int32)
    for number in range(1, 4):
        piece = piece + jnp.where(expert >= number * count, 1, 0)
    local = expert - piece * count
    named = jnp.zeros((extent, tokens), F32)
    gate = jnp.zeros((extent, tokens), F32)
    for choice in range(ids.shape[0]):
        hit = ids[choice : choice + 1, :] == local
        named = named + jnp.where(hit, 1.0, 0.0)
        gate = gate + jnp.where(hit, gates[choice : choice + 1, :], 0.0)
    before = lax.broadcasted_iota(jnp.int32, (tokens, tokens), 0) < lax.broadcasted_iota(jnp.int32, (tokens, tokens), 1)
    earlier = jnp.dot(named.astype(BF16), jnp.where(before, 1.0, 0.0).astype(BF16), preferred_element_type=F32)
    place = jnp.where(named > 0.0, earlier + meta[2].astype(F32), -1.0)
    high, middle, low = pieces_of(gate)
    table = jnp.where(piece == 0, place, jnp.where(piece == 1, high, jnp.where(piece == 2, middle, low)))
    out[:, :width] = grad[...]
    out[:, width:] = table.T.astype(BF16)


def collect_body(number, meta, *refs):
    blocks, outs = refs[:number], refs[-2:]
    tokens = blocks[0].shape[0]
    extent = 2 * outs[0].shape[1] - blocks[0].shape[1]
    large = outs[0].shape[1] - extent
    for half, out in enumerate(outs):
        start = pl.multiple_of(lax.bitwise_xor(1 - meta[4], half) * large, large)
        for k in range(number):
            out[k * tokens : (k + 1) * tokens, :large] = blocks[k][:, pl.ds(start, large)]
            out[k * tokens : (k + 1) * tokens, large:] = blocks[k][:, 2 * large :]


def forward_body(meta, hidden, weight, out):
    rows = hidden[:, 0].reshape(out.shape[0], hidden.shape[3])
    out[...] = jnp.dot(rows, weight[...], preferred_element_type=F32).astype(BF16)


def forward_first_body(peers, meta, hidden, weight, *refs):
    outs, (rows, matrix, store, sems, out_sems) = refs[: len(peers)], refs[len(peers) :]
    tile = matrix.shape[2]
    copies = []
    for at, peer in enumerate(peers):
        part = hidden.at[:, lax.bitwise_xor(meta[0], peer)]
        copies.append(pltpu.make_async_copy(part, rows.at[at], sems.at[at]))
    for at in range(matrix.shape[0]):
        part = weight.at[:, at * tile : (at + 1) * tile]
        copies.append(pltpu.make_async_copy(part, matrix.at[at], sems.at[len(peers) + at]))
    for copy in copies:
        copy.start()
    for copy in copies[: len(peers)]:
        copy.wait()
    length = outs[0].shape[0]
    value = rows[...].reshape(len(peers) * length, rows.shape[3])
    results = []
    for at in range(matrix.shape[0]):
        copies[len(peers) + at].wait()
        product = jnp.dot(value, matrix[at], preferred_element_type=F32).astype(BF16)
        for number, out in enumerate(outs):
            store[at, number] = product[number * length : (number + 1) * length]
            target = out.at[:, at * tile : (at + 1) * tile]
            results.append(pltpu.make_async_copy(store.at[at, number], target, out_sems.at[at, number]))
            results[-1].start()
    for copy in results:
        copy.wait()


def turn_body(meta, hidden, after, out, final, final_turned):
    value = hidden[:, 0].reshape(final.shape)
    out[0] = value.T
    final[...] = value
    final_turned[...] = value.T


def turn_other_body(meta, hidden, out):
    out[...] = hidden[...].T


def selection(table, count, expert, rows):
    place = table[pl.ds(expert, 1), :]
    gate = table[pl.ds(expert + count, 1), :] + table[pl.ds(expert + 2 * count, 1), :]
    gate = gate + table[pl.ds(expert + 3 * count, 1), :]
    row = lax.broadcasted_iota(jnp.int32, (rows, place.shape[1]), 0).astype(F32)
    return row == place, gate


def grad_rows_body(plan, jobs, count, groups, meta, *refs):
    number = jobs * groups
    tables, tokens, outs, table = refs[:number], refs[number : 2 * number], refs[-1 - len(plan) : -1], refs[-1]
    rows = outs[0].shape[0] // len(plan[0][1]) // groups
    for job in range(jobs):
        asked = [(out, peer, parts.index(job)) for out, (peer, parts) in zip(outs, plan) if job in parts]
        for group in range(groups):
            table[...] = tables[job * groups + group][...].astype(F32).T
            choices, row_gates = [], []
            for _, peer, _ in asked:
                match, gate = selection(table, count, lax.bitwise_xor(meta[3], peer), rows)
                choices.append(jnp.where(match, 1.0, 0.0))
                row_gates.append(jnp.sum(jnp.where(match, gate, 0.0), 1, keepdims=True))
            choice = jnp.concatenate(choices, 0).astype(BF16)
            picked = jnp.dot(choice, tokens[job * groups + group][...], preferred_element_type=F32)
            value = (picked * jnp.concatenate(row_gates, 0)).astype(BF16)
            place = pl.multiple_of(lax.bitwise_xor(meta[1], group) * rows, rows)
            for at, (out, _, part) in enumerate(asked):
                out[pl.ds(place + part * groups * rows, rows), :] = value[at * rows : (at + 1) * rows]


def direct_rows_body(plan, jobs, number, count, meta, *refs):
    arrays, outs, table = refs[:number], refs[-1 - len(plan) : -1], refs[-1]
    extent, tokens = table.shape
    large = outs[0].shape[1]
    rows = outs[0].shape[0] // len(plan[0][1]) // len(jobs[0])
    for job, sources in enumerate(jobs):
        asked = [(out, peer, parts.index(job)) for out, (peer, parts) in zip(outs, plan) if job in parts]
        for group, (operand, first, whole) in enumerate(sources):
            here = slice(first, first + tokens)
            wide = 2 * large if whole else large
            table[...] = arrays[operand][here, wide : wide + extent].astype(F32).T
            choices, row_gates = [], []
            for _, peer, _ in asked:
                match, gate = selection(table, count, lax.bitwise_xor(meta[3], peer), rows)
                choices.append(jnp.where(match, 1.0, 0.0))
                row_gates.append(jnp.sum(jnp.where(match, gate, 0.0), 1, keepdims=True))
            if whole:
                columns = pl.ds(pl.multiple_of(lax.bitwise_xor(1 - meta[4], job) * large, large), large)
            else:
                columns = slice(0, large)
            choice = jnp.concatenate(choices, 0).astype(BF16)
            picked = jnp.dot(choice, arrays[operand][here, columns], preferred_element_type=F32)
            value = (picked * jnp.concatenate(row_gates, 0)).astype(BF16)
            place = pl.multiple_of(lax.bitwise_xor(meta[1], group) * rows, rows)
            for at, (out, _, part) in enumerate(asked):
                out[pl.ds(place + part * len(sources) * rows, rows), :] = value[at * rows : (at + 1) * rows]


def direct_combine_body(peers, count, cap, chosen, meta, *refs):
    blocks, returned, (part, table) = refs[: len(chosen)], refs[len(chosen) + 1 : -2], refs[-2:]
    extent, length = table.shape
    width = returned[0].shape[1]
    chunk = min(512, width)
    for number, k in enumerate(chosen):
        here = slice(number * length, (number + 1) * length)
        table[...] = blocks[number][:, width:].astype(F32).T
        start = pl.multiple_of(lax.bitwise_xor(meta[1], k) * cap, cap)
        highs, lows, marks = [], [], []
        for peer in range(peers):
            match, gate = selection(table, count, lax.bitwise_xor(meta[3], peer), cap)
            high = gate.astype(BF16).astype(F32)
            marks.append(jnp.where(match, 1.0, 0.0))
            highs.append(jnp.where(match, high, 0.0))
            lows.append(jnp.where(match, gate - high, 0.0))
        weights = jnp.concatenate([jnp.concatenate(highs, 0).T, jnp.concatenate(lows, 0).T], 0).astype(BF16)
        products = jnp.zeros((peers * cap, length), F32)
        for at in range(0, width, chunk):
            columns = slice(at, at + chunk)
            value = jnp.concatenate([ref[pl.ds(start, cap), columns] for ref in returned], 0)
            total = jnp.dot(weights, value, preferred_element_type=F32)
            part[here, columns] = (total[:length] + total[length:]).astype(part.dtype)
            products = products + lax.dot_general(
                value, blocks[number][:, columns], (((1,), (1,)), ((), ())), preferred_element_type=F32
            )
        products = products * jnp.concatenate(marks, 0)
        inner = [jnp.sum(products[peer * cap : (peer + 1) * cap], 0, keepdims=True) for peer in range(peers)]
        beside = part.shape[1] - width
        row = lax.broadcasted_iota(jnp.int32, (beside, length), 0)
        placed = jnp.zeros((beside, length), F32)
        for peer in range(peers):
            for at, piece in enumerate(pieces_of(inner[peer])):
                placed = jnp.where(row == at * count + lax.bitwise_xor(meta[3], peer), piece, placed)
        part[here, width:] = placed.T.astype(part.dtype)


def combine_body(peers, count, number, meta, *refs):
    packed, tokens, returned = refs[:number], refs[number : 2 * number], refs[2 * number + 1 : 2 * number + 1 + peers]
    part, table, weights, marks, inner = refs[-5:]
    rows, length = returned[0].shape[0], tokens[0].shape[0]
    step, last = pl.program_id(1), pl.num_programs(1) - 1

    def chosen(options):
        value = options[0][...]
        for at in range(1, number):
            value = jnp.where(pl.program_id(0) == at, options[at][...], value)
        return value

    @pl.when(step == 0)
    def _():
        inner[...] = jnp.zeros(inner.shape, F32)
        table[...] = chosen(packed).astype(F32).T
        highs, lows = [], []
        for peer in range(peers):
            match, gate = selection(table, count, lax.bitwise_xor(meta[3], peer), rows)
            high = gate.astype(BF16).astype(F32)
            marks[pl.ds(peer * rows, rows), :] = jnp.where(match, 1.0, 0.0)
            highs.append(jnp.where(match, high, 0.0))
            lows.append(jnp.where(match, gate - high, 0.0))
        weights[:length, :] = jnp.concatenate(highs, 0).T.astype(BF16)
        weights[length:, :] = jnp.concatenate(lows, 0).T.astype(BF16)

    @pl.when(step < last)
    def _():
        value = jnp.concatenate([ref[...] for ref in returned], 0)
        chunk = min(512, value.shape[1])
        for start in range(0, value.shape[1], chunk):
            total = jnp.dot(weights[...], value[:, start : start + chunk], preferred_element_type=F32)
            part[:, start : start + chunk] = (total[:length] + total[length:]).astype(part.dtype)
        products = lax.dot_general(value, chosen(tokens), (((1,), (1,)), ((), ())), preferred_element_type=F32)
        products = products * marks[...]
        for peer in range(peers):
            inner[peer : peer + 1, :] += jnp.sum(products[peer * rows : (peer + 1) * rows], 0, keepdims=True)

    @pl.when(step == last)
    def _():
        extent = -(-3 * count // 128) * 128
        row = lax.broadcasted_iota(jnp.int32, (extent, length), 0)
        placed = jnp.zeros((extent, length), F32)
        for at, piece in enumerate(pieces_of(inner[...])):
            for peer in range(peers):
                place = at * count + lax.bitwise_xor(meta[3], peer)
                placed = jnp.where(row == place, piece[peer : peer + 1, :], placed)
        part[:, :extent] = placed.T.astype(part.dtype)


def inside_body(plan, meta, weight, *refs):
    number = 1 + max(at for _, parts in plan for at, _ in parts)
    rows, out, token, (store, sems) = refs[:number], refs[-4], refs[-3], refs[-2:]
    shape = store.shape[1:]
    length, large = shape[0] * shape[1], weight.shape[1] // 2
    contract = (((1,), (1,)), ((), ()))
    copies = []
    for at, (peer, parts) in enumerate(plan):
        value = jnp.zeros((length, weight.shape[0]), F32)
        for half, (operand, start) in enumerate(parts):
            columns = pl.ds(pl.multiple_of(lax.bitwise_xor(1 - meta[4], half) * large, large), large)
            part = rows[operand][start : start + length, :]
            value = value + lax.dot_general(part, weight[:, columns], contract, preferred_element_type=F32)
        store[at] = value.astype(BF16).reshape(shape)
        copies.append(pltpu.make_async_copy(store.at[at], out.at[:, lax.bitwise_xor(meta[0], peer)], sems.at[at]))
        copies[-1].start()
    token[...] = jnp.zeros(token.shape, F32)
    for copy in copies:
        copy.wait()


def weight_grad_body(plan, number, has_earlier, half, meta, turned, *refs):
    rows, (other, own, token) = refs[:number], refs[-3:]
    length, tile = turned.shape[2], own.shape[1] // half
    for side, out in enumerate((other, own)):
        for at in range(half):
            columns = slice(at * tile, (at + 1) * tile)
            value = refs[number + side][:, columns] if has_earlier else jnp.zeros((turned.shape[1], tile), F32)
            for peer, parts in plan:
                operand, start = parts[side]
                part = rows[operand][start : start + length, columns]
                value = value + jnp.dot(turned[peer], part, preferred_element_type=F32)
            out[:, columns] = value.astype(out.dtype)
    token[...] = jnp.zeros(token.shape, F32)


def last_body(half, meta, turned, rows, turned_other, rows_other, earlier, earlier_other, done, grads, store, sems):
    tile = store.shape[2]
    copies = []
    for at in range(half):
        columns = slice(at * tile, (at + 1) * tile)
        value = jnp.dot(turned[...], rows[:, columns], preferred_element_type=F32)
        value = value + jnp.dot(turned_other[...], rows_other[:, columns], preferred_element_type=F32)
        store[at] = (value + earlier[:, columns] + earlier_other[:, columns].astype(F32)).astype(BF16)
        copies.append(pltpu.make_async_copy(store.at[at], grads.at[:, columns], sems.at[at]))
        copies[-1].start()
    for copy in copies:
        copy.wait()


def finish_body(count, meta, ids, kept, arrived, after, combined, gate_grads, token):
    width = combined.shape[1]
    combined[...] = (kept[:, :width] + arrived[:, :width].astype(F32)).astype(BF16)
    pieces = (kept[:, width:] + arrived[:, width:].astype(F32)).T
    inner = pieces[:count] + pieces[count : 2 * count] + pieces[2 * count : 3 * count]
    named = ids[...]
    found = jnp.zeros(gate_grads.shape, F32)
    for expert in range(count):
        found = found + jnp.where(named == expert, inner[expert : expert + 1, :], 0.0)
    gate_grads[...] = found
    token[...] = jnp.zeros(token.shape, F32)


def per_device(expert_ids, gates, hidden, weight, out_grad):
    count = lax.axis_size("expert")
    peers = 1 << ((count.bit_length() - 1) // 2)
    planes = count // peers
    tokens, top = expert_ids.shape
    cap = hidden.shape[1] // count
    width, inside = out_grad.shape[1], hidden.shape[2]
    fold = 1
    while fold * cap % 16:
        fold *= 2
    groups = planes // fold
    group_rows, group_tokens = fold * cap, fold * tokens
    rows = planes * cap
    tile = min(512, width // 2)
    steps = width // tile
    half = steps // 2
    large = width // 2
    room = 1 if fold == 1 else 3
    last = peers - 1
    anywhere = pl.BlockSpec(memory_space=pl.ANY)
    glance = pl.BlockSpec((16, 128), lambda *i: (0, 0))

    me = lax.axis_index("expert")
    core = lax.axis_index("dp")
    column, plane = me % peers, me // peers
    meta = jnp.stack([column, plane // fold, (plane % fold) * cap, me, core, plane, count]).astype(jnp.int32)

    def swap(value, distance):
        return lax.ppermute(value, "expert", [(e, e ^ distance) for e in range(count)])

    def exchange(value):
        return lax.ppermute(value, "dp", [(0, 1), (1, 0)])

    matrix = weight[0]
    if fold == 1:
        blocks = hidden.reshape(planes, peers, cap, inside)
    else:
        blocks = hidden.reshape(planes, peers, cap, inside).transpose(1, 0, 2, 3).reshape(1, peers, rows, inside)
    block = (blocks.shape[0], 1, blocks.shape[2], inside)

    ids_turned = expert_ids.T
    extent = -(-4 * count // 128) * 128
    short = pl.BlockSpec((top, tokens), lambda i, m: (0, 0))
    relay = peers == 4 and fold == 1
    packed = call(
        pack_body, "pack", (1,),
        [short, short, pl.BlockSpec((tokens, width), lambda i, m: (0, 0))],
        pl.BlockSpec((tokens, width + extent), lambda i, m: (0, 0)),
        jax.ShapeDtypeStruct((tokens, width + extent), BF16),
        meta, (ids_turned, gates.T, out_grad),
        room=room,
    )
    gathered = [packed]
    for k in range(1, planes):
        if k & (k - 1) == 0:
            gathered.append(swap(packed, peers * k))
        else:
            gathered.append(None)

    def forward(peer, after):
        return call(
            lambda meta, *refs: forward_body(meta, refs[0], refs[1], refs[-1]), f"forward{peer}", (steps,),
            [
                pl.BlockSpec(block, lambda i, m: (0, lax.bitwise_xor(m[0], peer), 0, 0)),
                pl.BlockSpec((inside, tile), lambda i, m: (0, i)),
            ]
            + [glance] * len(after),
            pl.BlockSpec((rows, tile), lambda i, m: (0, i)),
            jax.ShapeDtypeStruct((rows, width), BF16),
            meta, (blocks, matrix, *after),
        )

    outputs, after = {}, ()
    if relay:
        outputs[1], outputs[2] = direct(
            functools.partial(forward_first_body, (1, 2)), "forward1", [jax.ShapeDtypeStruct((rows, width), BF16)] * 2,
            meta, (blocks, matrix),
            scratch=[
                pltpu.VMEM((2, planes, cap, inside), BF16),
                pltpu.VMEM((steps, inside, tile), BF16),
                pltpu.VMEM((steps, 2, rows, tile), BF16),
                pltpu.SemaphoreType.DMA((2 + steps,)),
                pltpu.SemaphoreType.DMA((steps, 2)),
            ],
            out_specs=[anywhere, anywhere],
            places={0: anywhere, 1: anywhere}, room=3.75,
        )
        after = (outputs[2], packed)
    for peer in [peer for peer in list(range(1, peers)) + [0] if peer not in outputs]:
        outputs[peer] = forward(peer, after)
        after = (outputs[peer], packed)
    returned = [outputs[0]] + [swap(outputs[peer], peer) for peer in range(1, peers)]
    turned, hidden_last, turned_last = call(
        turn_body, "turn", (peers,),
        [pl.BlockSpec(block, lambda i, m: (0, lax.bitwise_xor(m[0], i), 0, 0)), glance],
        [pl.BlockSpec((1, inside, rows), lambda i, m: (i, 0, 0)), pl.BlockSpec((rows, inside), lambda i, m: (0, 0)),
         pl.BlockSpec((inside, rows), lambda i, m: (0, 0))],
        [
            jax.ShapeDtypeStruct((peers, inside, rows), BF16), jax.ShapeDtypeStruct((rows, inside), BF16),
            jax.ShapeDtypeStruct((inside, rows), BF16),
        ],
        meta, (blocks, outputs[0]),
    )

    turned_other = call(
        turn_other_body, "turn_other", (1,),
        [pl.BlockSpec((rows, inside), lambda i, m: (0, 0))],
        pl.BlockSpec((inside, rows), lambda i, m: (0, 0)),
        jax.ShapeDtypeStruct((inside, rows), BF16),
        meta, (exchange(hidden_last),),
    )
    for k in range(1, planes):
        lowest = k & -k
        if k != lowest:
            gathered[k] = swap(gathered[k ^ lowest], peers * lowest)
    if fold > 1:
        gathered = [jnp.concatenate(gathered[g * fold : (g + 1) * fold], 0) for g in range(groups)]

    def other_half(i, m):
        return (0, 1 - m[4])

    def own_half(i, m):
        return (0, m[4])

    def build_rows(name, plan, jobs, after, cost=COST):
        sources = [source for job in jobs for source in job]
        return call(
            functools.partial(grad_rows_body, plan, len(jobs), count, groups), name, (1,),
            [pl.BlockSpec((group_tokens, extent), table_at) for _, table_at, _ in sources]
            + [pl.BlockSpec((group_tokens, large), data_at) for _, _, data_at in sources]
            + [glance] * len(after),
            [pl.BlockSpec((len(parts) * rows, large), lambda i, m: (0, 0)) for _, parts in plan],
            [jax.ShapeDtypeStruct((len(parts) * rows, large), BF16) for _, parts in plan],
            meta, (*[value for value, _, _ in sources] * 2, *after),
            scratch=[pltpu.VMEM((extent, group_tokens), F32)],
            room=room, cost=cost,
        )

    def beside(i, m):
        return (0, width // extent)

    jobs = [[(value, beside, at) for value in gathered] for at in (other_half, own_half)]
    if relay:
        plan = ((0, (0, 1)), (1, (1,)), (2, (0,)))
        own_jobs = [[(k, 0, True) for k in range(planes)]] * 2
        made = direct(
            functools.partial(direct_rows_body, plan, own_jobs, planes, count), "own_rows",
            [jax.ShapeDtypeStruct((len(parts) * rows, large), BF16) for _, parts in plan],
            meta, gathered, scratch=[pltpu.VMEM((extent, tokens), F32)],
        )
        beside_shape = jax.ShapeDtypeStruct((planes * tokens, large + extent), BF16)
        arrival = made[1]
        for group in ((outputs[0], turned_other, *returned[1:last]), returned[last:]):
            arrival = call(
                token_body, "arrival", (1,), [glance] * (len(group) + 1), glance,
                jax.ShapeDtypeStruct((16, 128), F32), meta, (*group, arrival),
            )
        collected = direct(
            functools.partial(collect_body, planes), "collect", [beside_shape] * 2, meta, (*gathered, arrival),
        )
        near = [swap(value, 1 << number) for number, value in enumerate(collected)]
        arrived = [
            [(made[0], 0), (made[0], 1)], [None, (swap(made[1], 1), 0)], [(swap(made[2], 2), 0), None], [None, None],
        ]
    else:
        made = build_rows("own_rows", tuple((peer, (0, 1)) for peer in range(peers)), jobs, (outputs[0],))
        arrived = [[(made[0], 0), (made[0], 1)]]
        for peer in range(1, peers):
            got = swap(made[peer], peer)
            arrived.append([(got, 0), (got, 1)])

    padded = width + -(-3 * count // 128) * 128

    def combine(chosen, dtype, after):
        first, stride = chosen[0], len(chosen) > 1 and chosen[1] - chosen[0]
        columns = width if fold == 1 else large

        def part_of(k, i, m):
            return (lax.bitwise_xor(m[1], k * stride + first), jnp.minimum(i, width // columns - 1))

        blocks_of = [gathered[group] for group in chosen]
        return call(
            functools.partial(combine_body, peers, count, len(chosen)), f"combine{first}", (len(chosen), width // columns + 1),
            [pl.BlockSpec((group_tokens, extent), lambda k, i, m: (0, width // extent))] * len(chosen)
            + [pl.BlockSpec((group_tokens, columns), lambda k, i, m: (0, jnp.minimum(i, width // columns - 1)))] * len(chosen)
            + [glance]
            + [pl.BlockSpec((group_rows, columns), part_of)] * peers,
            pl.BlockSpec((group_tokens, columns), lambda k, i, m: (k, i)),
            jax.ShapeDtypeStruct((len(chosen) * group_tokens, padded), dtype),
            meta, (*blocks_of, *blocks_of, after, *returned),
            scratch=[
                pltpu.VMEM((extent, group_tokens), F32),
                pltpu.VMEM((2 * group_tokens, peers * group_rows), BF16),
                pltpu.VMEM((peers * group_rows, group_tokens), F32),
                pltpu.VMEM((peers, group_tokens), F32),
            ],
            room=room,
        )

    def direct_combine(chosen, dtype, after):
        return direct(
            functools.partial(direct_combine_body, peers, count, cap, tuple(chosen)), f"combine{chosen[0]}",
            jax.ShapeDtypeStruct((len(chosen) * tokens, padded), dtype),
            meta, (*[gathered[k] for k in chosen], after, *returned),
            scratch=[pltpu.VMEM((extent, tokens), F32)],
        )

    if relay:
        combine = direct_combine
    if fold == 1:
        leaving = combine(range(1, planes, 2), BF16, made[0])
        combine_done = combine(range(0, planes, 2), F32, leaving)
        sums = [combine_done[k * tokens : (k + 1) * tokens] for k in range(planes // 2)]
    else:
        parts = [combine([group], F32, made[0]) for group in range(groups)]
        combine_done = parts[-1]
        sums = [parts[k // fold][k % fold * tokens : (k % fold + 1) * tokens] for k in range(planes)]
        leaving = jnp.concatenate(sums[1::2], 0).astype(BF16)
        sums = sums[0::2]
    distance = 1
    first_sums = None
    while len(sums) > 1:
        got = swap(leaving, peers * distance)
        pieces = [got[k * tokens : (k + 1) * tokens].astype(F32) for k in range(len(sums))]
        sums = [mine + piece for mine, piece in zip(sums, pieces)]
        leaving = [value.astype(BF16) for value in sums[1::2]]
        leaving = leaving[0] if len(leaving) == 1 else jnp.concatenate(leaving, 0)
        sums = sums[0::2]
        first_sums = leaving if first_sums is None else first_sums
        distance *= 2
    summed = swap(leaving, peers * distance)

    grads_shape = jax.ShapeDtypeStruct(blocks.shape, BF16)
    def rows_of(chosen):
        arrays, plan = [], []
        for peer in chosen:
            parts = []
            for value, at in arrived[peer]:
                known = [number for number, array in enumerate(arrays) if array is value]
                if not known:
                    arrays.append(value)
                parts.append((known[0] if known else len(arrays) - 1, at * rows))
            plan.append((peer, tuple(parts)))
        return arrays, tuple(plan)

    def inside_grad(chosen, earlier, after):
        arrays, plan = rows_of(chosen)
        operands = [matrix, *arrays, *after] + ([] if earlier is None else [earlier])
        return direct(
            functools.partial(inside_body, plan), f"inside{chosen[0]}",
            [grads_shape, jax.ShapeDtypeStruct((16, 128), F32)],
            meta, operands,
            out_specs=[anywhere, pl.BlockSpec(memory_space=pltpu.VMEM)],
            scratch=[
                pltpu.VMEM((len(chosen), block[0], block[2], inside), BF16),
                pltpu.SemaphoreType.DMA((len(chosen),)),
            ],
            aliases=None if earlier is None else {len(operands): 0},
            places={} if earlier is None else {len(operands) - 1: anywhere},
        )

    def weight_grad(chosen, earlier, after, kind):
        arrays, plan = rows_of(chosen)
        shape = (inside, large)
        return direct(
            functools.partial(weight_grad_body, plan, len(arrays), bool(earlier), half), f"weight_grad{chosen[0]}",
            [jax.ShapeDtypeStruct(shape, kind), jax.ShapeDtypeStruct(shape, F32), jax.ShapeDtypeStruct((16, 128), F32)],
            meta, (turned, *arrays, *earlier, *after),
        )

    hidden_grads, token = inside_grad([0], None, ())
    total_other, total_own, own_token = weight_grad([0], (), (token,), F32)

    if relay:
        plan = ((0, (0,)), (2, (0,)), (0, (1,)), (1, (1,)))
        near_jobs = [[(job, k * tokens, False) for k in range(planes)] for job in range(2)]
        made = direct(
            functools.partial(direct_rows_body, plan, near_jobs, 2, count), "near_rows",
            [jax.ShapeDtypeStruct((rows, large), BF16)] * 4,
            meta, (*near, combine_done, own_token), scratch=[pltpu.VMEM((extent, tokens), F32)], cost=NEAR_COST,
        )
        arrived[1][0], arrived[2][1] = (made[0], 0), (made[2], 0)
        arrived[3] = [(swap(made[1], 2), 0), (swap(made[3], 1), 0)]

    hidden_grads, token = inside_grad(range(1, last), hidden_grads, (made[1][:16, :128], first_sums[:16, :128]))
    total_other, total_own, _ = weight_grad(range(1, last), (total_other, total_own), (token,), BF16)
    total_other = exchange(total_other)
    last_other, last_own = arrived[last]
    rows_own = last_own[0] if relay else last_own[0][rows:]
    rows_other = last_other[0] if relay else last_other[0][:rows]

    followed = follow(rows_other, last_own[0])
    rows_other = exchange(followed)
    if relay:
        arrived[last][0] = (followed, 0)
    hidden_grads, token = inside_grad([last], hidden_grads, ())
    combined, gate_grads, finished = direct(
        functools.partial(finish_body, count), "finish",
        [
            jax.ShapeDtypeStruct((tokens, width), BF16), jax.ShapeDtypeStruct((top, tokens), F32),
            jax.ShapeDtypeStruct((16, 128), F32),
        ],
        meta, (ids_turned, sums[0], summed, token), cost=LONG_COST,
    )
    weight_grads = direct(
        functools.partial(last_body, half), "last", jax.ShapeDtypeStruct((inside, large), BF16),
        meta, (turned_last, rows_own, turned_other, rows_other, total_own, total_other, finished),
        out_specs=anywhere,
        scratch=[pltpu.VMEM((half, inside, tile), BF16), pltpu.SemaphoreType.DMA((half,))],
    )

    if fold > 1:
        hidden_grads = hidden_grads.reshape(peers, planes, cap, inside).transpose(1, 0, 2, 3)
    return combined, gate_grads.T, hidden_grads.reshape(hidden.shape), weight_grads[None]


def solution(mesh):
    placed = (
        P(("expert", "dp"), None),
        P(("expert", "dp"), None),
        P("expert", "dp", None),
        P("expert", None, None),
        P(("expert", "dp"), None),
    )
    return jax.shard_map(
        per_device,
        mesh=mesh,
        in_specs=placed,
        out_specs=(
            P(("expert", "dp"), None),
            P(("expert", "dp"), None),
            P("expert", "dp", None),
            P("expert", None, "dp"),
        ),
        check_vma=False,
    )
```

```python
import functools

import jax
import jax.numpy as jnp
from jax import lax
from jax.experimental import pallas as pl
from jax.experimental.pallas import tpu as pltpu
from jax.sharding import PartitionSpec as P

F32 = jnp.float32
BF16 = jnp.bfloat16
VMEM_BYTES = 16 * 1024 * 1024
COST = 1024
NEAR_COST = 10**10
LONG_COST = 10**11


def call(body, name, grid, in_specs, out_specs, out_shape, scalars, operands, scratch=(), aliases=None, room=1, cost=COST):
    return pl.pallas_call(
        body,
        name=name,
        grid_spec=pltpu.PrefetchScalarGridSpec(
            num_scalar_prefetch=1, grid=grid, in_specs=in_specs, out_specs=out_specs, scratch_shapes=scratch
        ),
        out_shape=out_shape,
        input_output_aliases=aliases or {},
        cost_estimate=pl.CostEstimate(flops=cost, bytes_accessed=COST, transcendentals=0),
        compiler_params=pltpu.CompilerParams(vmem_limit_bytes=room * VMEM_BYTES),
    )(scalars, *operands)


def direct(body, name, out_shape, scalars, operands, out_specs=None, scratch=(), aliases=None, places=None, room=1, cost=COST):
    places = places or {}
    vmem, smem = pl.BlockSpec(memory_space=pltpu.VMEM), pl.BlockSpec(memory_space=pltpu.SMEM)
    several = isinstance(out_shape, (list, tuple))
    return pl.pallas_call(
        body,
        name=name,
        in_specs=[smem] + [places.get(at, vmem) for at in range(len(operands))],
        out_specs=out_specs or ([vmem] * len(out_shape) if several else vmem),
        out_shape=out_shape,
        scratch_shapes=scratch,
        input_output_aliases=aliases or {},
        cost_estimate=pl.CostEstimate(flops=cost, bytes_accessed=COST, transcendentals=0),
        compiler_params=pltpu.CompilerParams(vmem_limit_bytes=int(room * VMEM_BYTES)),
    )(scalars, *operands)


def follow(value, *earlier):
    anywhere = pl.BlockSpec(memory_space=pl.ANY)
    return pl.pallas_call(
        lambda *refs: None,
        name="follow",
        grid=(1,),
        in_specs=[anywhere] + [pl.BlockSpec((16, 128), lambda i: (0, 0))] * len(earlier),
        out_specs=anywhere,
        out_shape=jax.ShapeDtypeStruct(value.shape, value.dtype),
        input_output_aliases={0: 0},
        cost_estimate=pl.CostEstimate(flops=COST, bytes_accessed=COST, transcendentals=0),
        compiler_params=pltpu.CompilerParams(vmem_limit_bytes=VMEM_BYTES),
    )(value, *earlier)


def token_body(meta, *refs):
    refs[-1][...] = jnp.zeros(refs[-1].shape, F32)


def pieces_of(value):
    high = value.astype(BF16).astype(F32)
    middle = (value - high).astype(BF16).astype(F32)
    return high, middle, value - high - middle


def pack_body(meta, ids, gates, grad, out):
    width, tokens = grad.shape[1], grad.shape[0]
    extent = out.shape[1] - width
    count = meta[6]
    expert = lax.broadcasted_iota(jnp.int32, (extent, tokens), 0)
    piece = jnp.zeros((extent, tokens), jnp.int32)
    for number in range(1, 4):
        piece = piece + jnp.where(expert >= number * count, 1, 0)
    local = expert - piece * count
    named = jnp.zeros((extent, tokens), F32)
    gate = jnp.zeros((extent, tokens), F32)
    for choice in range(ids.shape[0]):
        hit = ids[choice : choice + 1, :] == local
        named = named + jnp.where(hit, 1.0, 0.0)
        gate = gate + jnp.where(hit, gates[choice : choice + 1, :], 0.0)
    before = lax.broadcasted_iota(jnp.int32, (tokens, tokens), 0) < lax.broadcasted_iota(jnp.int32, (tokens, tokens), 1)
    earlier = jnp.dot(named.astype(BF16), jnp.where(before, 1.0, 0.0).astype(BF16), preferred_element_type=F32)
    place = jnp.where(named > 0.0, earlier + meta[2].astype(F32), -1.0)
    high, middle, low = pieces_of(gate)
    table = jnp.where(piece == 0, place, jnp.where(piece == 1, high, jnp.where(piece == 2, middle, low)))
    out[:, :width] = grad[...]
    out[:, width:] = table.T.astype(BF16)


def collect_body(number, count, meta, *refs):
    blocks, outs, table = refs[:number], refs[-3:-1], refs[-1]
    tokens, large = blocks[0].shape[0], outs[0].shape[1]
    strips = ([], [])
    for k in range(number):
        table[...] = blocks[k][:, 2 * large :].astype(F32).T
        for side, out in enumerate(outs):
            start = pl.multiple_of(lax.bitwise_xor(1 - meta[4], side) * large, large)
            out[k * tokens : (k + 1) * tokens, :] = blocks[k][:, pl.ds(start, large)]
            receiver = lax.bitwise_xor(meta[3], 1 << side)
            experts = (receiver, lax.bitwise_xor(receiver, 2 >> side))
            lines = [table[pl.ds(expert + at * count, 1), :] for expert in experts for at in range(4)]
            strips[side].append(jnp.concatenate(lines, 0))
    for strip, out in zip(strips, outs):
        if large > number * tokens:
            strip.append(jnp.zeros((8, large - number * tokens), F32))
        strip = jnp.concatenate(strip, 1)
        out[number * tokens :, :] = jnp.concatenate([strip, jnp.zeros(strip.shape, F32)], 0).astype(BF16)


def forward_body(meta, hidden, weight, out):
    rows = hidden[:, 0].reshape(out.shape[0], hidden.shape[3])
    out[...] = jnp.dot(rows, weight[...], preferred_element_type=F32).astype(BF16)


def forward_first_body(peers, meta, hidden, weight, *refs):
    outs, (rows, matrix, store, sems, out_sems) = refs[: len(peers)], refs[len(peers) :]
    tile = matrix.shape[2]
    copies = []
    for at, peer in enumerate(peers):
        part = hidden.at[:, lax.bitwise_xor(meta[0], peer)]
        copies.append(pltpu.make_async_copy(part, rows.at[at], sems.at[at]))
    for at in range(matrix.shape[0]):
        part = weight.at[:, at * tile : (at + 1) * tile]
        copies.append(pltpu.make_async_copy(part, matrix.at[at], sems.at[len(peers) + at]))
    for copy in copies:
        copy.start()
    for copy in copies[: len(peers)]:
        copy.wait()
    length = outs[0].shape[0]
    value = rows[...].reshape(len(peers) * length, rows.shape[3])
    results = []
    for at in range(matrix.shape[0]):
        copies[len(peers) + at].wait()
        product = jnp.dot(value, matrix[at], preferred_element_type=F32).astype(BF16)
        for number, out in enumerate(outs):
            store[at, number] = product[number * length : (number + 1) * length]
            target = out.at[:, at * tile : (at + 1) * tile]
            results.append(pltpu.make_async_copy(store.at[at, number], target, out_sems.at[at, number]))
            results[-1].start()
    for copy in results:
        copy.wait()


def turn_body(meta, hidden, after, out, final, final_turned):
    value = hidden[:, 0].reshape(final.shape)
    out[0] = value.T
    final[...] = value
    final_turned[...] = value.T


def turn_other_body(meta, hidden, out):
    out[...] = hidden[...].T


def selection(table, count, expert, rows):
    lines = [table[pl.ds(expert + at * count, 1), :] for at in range(4)]
    return selection_of(lines, rows)


def selection_of(lines, rows):
    place, gate = lines[0], lines[1] + lines[2] + lines[3]
    row = lax.broadcasted_iota(jnp.int32, (rows, place.shape[1]), 0).astype(F32)
    return row == place, gate


def grad_rows_body(plan, jobs, count, groups, meta, *refs):
    number = jobs * groups
    tables, tokens, outs, table = refs[:number], refs[number : 2 * number], refs[-1 - len(plan) : -1], refs[-1]
    rows = outs[0].shape[0] // len(plan[0][1]) // groups
    for job in range(jobs):
        asked = [(out, peer, parts.index(job)) for out, (peer, parts) in zip(outs, plan) if job in parts]
        for group in range(groups):
            table[...] = tables[job * groups + group][...].astype(F32).T
            choices, row_gates = [], []
            for _, peer, _ in asked:
                match, gate = selection(table, count, lax.bitwise_xor(meta[3], peer), rows)
                choices.append(jnp.where(match, 1.0, 0.0))
                row_gates.append(jnp.sum(jnp.where(match, gate, 0.0), 1, keepdims=True))
            choice = jnp.concatenate(choices, 0).astype(BF16)
            picked = jnp.dot(choice, tokens[job * groups + group][...], preferred_element_type=F32)
            value = (picked * jnp.concatenate(row_gates, 0)).astype(BF16)
            place = pl.multiple_of(lax.bitwise_xor(meta[1], group) * rows, rows)
            for at, (out, _, part) in enumerate(asked):
                out[pl.ds(place + part * groups * rows, rows), :] = value[at * rows : (at + 1) * rows]


def direct_rows_body(plan, jobs, number, count, meta, *refs):
    arrays, outs, table = refs[:number], refs[-1 - len(plan) : -1], refs[-1]
    tokens = table.shape[1]
    large = outs[0].shape[1]
    rows = outs[0].shape[0] // len(plan[0][1]) // len(jobs[0])
    for job, sources in enumerate(jobs):
        asked = [(out, peer, parts.index(job)) for out, (peer, parts) in zip(outs, plan) if job in parts]
        for group, (operand, first, whole) in enumerate(sources):
            array, here = arrays[operand], slice(first, first + tokens)
            if whole:
                table[...] = array[here, 2 * large :].astype(F32).T
                columns = pl.ds(pl.multiple_of(lax.bitwise_xor(1 - meta[4], job) * large, large), large)
            else:
                strip = array[array.shape[0] - 16 :, group * tokens : (group + 1) * tokens].astype(F32)
                columns = slice(0, large)
            choices, row_gates = [], []
            for _, peer, _ in asked:
                if whole:
                    match, gate = selection(table, count, lax.bitwise_xor(meta[3], peer), rows)
                else:
                    top = 4 if peer else 0
                    match, gate = selection_of([strip[top + at : top + at + 1] for at in range(4)], rows)
                choices.append(jnp.where(match, 1.0, 0.0))
                row_gates.append(jnp.sum(jnp.where(match, gate, 0.0), 1, keepdims=True))
            choice = jnp.concatenate(choices, 0).astype(BF16)
            picked = jnp.dot(choice, array[here, columns], preferred_element_type=F32)
            value = (picked * jnp.concatenate(row_gates, 0)).astype(BF16)
            place = pl.multiple_of(lax.bitwise_xor(meta[1], group) * rows, rows)
            for at, (out, _, part) in enumerate(asked):
                out[pl.ds(place + part * len(sources) * rows, rows), :] = value[at * rows : (at + 1) * rows]


def direct_combine_body(peers, count, cap, chosen, meta, *refs):
    blocks, returned, (part, table) = refs[: len(chosen)], refs[len(chosen) + 1 : -2], refs[-2:]
    extent, length = table.shape
    width = returned[0].shape[1]
    chunk = min(512, width)
    for number, k in enumerate(chosen):
        here = slice(number * length, (number + 1) * length)
        table[...] = blocks[number][:, width:].astype(F32).T
        start = pl.multiple_of(lax.bitwise_xor(meta[1], k) * cap, cap)
        highs, lows, marks = [], [], []
        for peer in range(peers):
            match, gate = selection(table, count, lax.bitwise_xor(meta[3], peer), cap)
            high = gate.astype(BF16).astype(F32)
            marks.append(jnp.where(match, 1.0, 0.0))
            highs.append(jnp.where(match, high, 0.0))
            lows.append(jnp.where(match, gate - high, 0.0))
        weights = jnp.concatenate([jnp.concatenate(highs, 0).T, jnp.concatenate(lows, 0).T], 0).astype(BF16)
        products = jnp.zeros((peers * cap, length), F32)
        for at in range(0, width, chunk):
            columns = slice(at, at + chunk)
            value = jnp.concatenate([ref[pl.ds(start, cap), columns] for ref in returned], 0)
            total = jnp.dot(weights, value, preferred_element_type=F32)
            part[here, columns] = (total[:length] + total[length:]).astype(part.dtype)
            products = products + lax.dot_general(
                value, blocks[number][:, columns], (((1,), (1,)), ((), ())), preferred_element_type=F32
            )
        products = products * jnp.concatenate(marks, 0)
        inner = [jnp.sum(products[peer * cap : (peer + 1) * cap], 0, keepdims=True) for peer in range(peers)]
        beside = part.shape[1] - width
        row = lax.broadcasted_iota(jnp.int32, (beside, length), 0)
        placed = jnp.zeros((beside, length), F32)
        for peer in range(peers):
            for at, piece in enumerate(pieces_of(inner[peer])):
                placed = jnp.where(row == at * count + lax.bitwise_xor(meta[3], peer), piece, placed)
        part[here, width:] = placed.T.astype(part.dtype)


def combine_body(peers, count, number, meta, *refs):
    packed, tokens, returned = refs[:number], refs[number : 2 * number], refs[2 * number + 1 : 2 * number + 1 + peers]
    part, table, weights, marks, inner = refs[-5:]
    rows, length = returned[0].shape[0], tokens[0].shape[0]
    step, last = pl.program_id(1), pl.num_programs(1) - 1

    def chosen(options):
        value = options[0][...]
        for at in range(1, number):
            value = jnp.where(pl.program_id(0) == at, options[at][...], value)
        return value

    @pl.when(step == 0)
    def _():
        inner[...] = jnp.zeros(inner.shape, F32)
        table[...] = chosen(packed).astype(F32).T
        highs, lows = [], []
        for peer in range(peers):
            match, gate = selection(table, count, lax.bitwise_xor(meta[3], peer), rows)
            high = gate.astype(BF16).astype(F32)
            marks[pl.ds(peer * rows, rows), :] = jnp.where(match, 1.0, 0.0)
            highs.append(jnp.where(match, high, 0.0))
            lows.append(jnp.where(match, gate - high, 0.0))
        weights[:length, :] = jnp.concatenate(highs, 0).T.astype(BF16)
        weights[length:, :] = jnp.concatenate(lows, 0).T.astype(BF16)

    @pl.when(step < last)
    def _():
        value = jnp.concatenate([ref[...] for ref in returned], 0)
        chunk = min(512, value.shape[1])
        for start in range(0, value.shape[1], chunk):
            total = jnp.dot(weights[...], value[:, start : start + chunk], preferred_element_type=F32)
            part[:, start : start + chunk] = (total[:length] + total[length:]).astype(part.dtype)
        products = lax.dot_general(value, chosen(tokens), (((1,), (1,)), ((), ())), preferred_element_type=F32)
        products = products * marks[...]
        for peer in range(peers):
            inner[peer : peer + 1, :] += jnp.sum(products[peer * rows : (peer + 1) * rows], 0, keepdims=True)

    @pl.when(step == last)
    def _():
        extent = -(-3 * count // 128) * 128
        row = lax.broadcasted_iota(jnp.int32, (extent, length), 0)
        placed = jnp.zeros((extent, length), F32)
        for at, piece in enumerate(pieces_of(inner[...])):
            for peer in range(peers):
                place = at * count + lax.bitwise_xor(meta[3], peer)
                placed = jnp.where(row == place, piece[peer : peer + 1, :], placed)
        part[:, :extent] = placed.T.astype(part.dtype)


def send_inside(plan, meta, weight, rows, out, store, sems):
    shape = store.shape[1:]
    length, large = shape[0] * shape[1], weight.shape[1] // 2
    contract = (((1,), (1,)), ((), ()))
    copies = []
    for at, (peer, parts) in enumerate(plan):
        value = jnp.zeros((length, weight.shape[0]), F32)
        for half, (operand, start) in enumerate(parts):
            columns = pl.ds(pl.multiple_of(lax.bitwise_xor(1 - meta[4], half) * large, large), large)
            part = rows[operand][start : start + length, :]
            value = value + lax.dot_general(part, weight[:, columns], contract, preferred_element_type=F32)
        store[at] = value.astype(BF16).reshape(shape)
        copies.append(pltpu.make_async_copy(store.at[at], out.at[:, lax.bitwise_xor(meta[0], peer)], sems.at[at]))
        copies[-1].start()
    return copies


def inside_body(plan, meta, weight, *refs):
    number = 1 + max(at for _, parts in plan for at, _ in parts)
    out, token, store, sems = refs[-4:]
    copies = send_inside(plan, meta, weight, refs[:number], out, store, sems)
    token[...] = jnp.zeros(token.shape, F32)
    for copy in copies:
        copy.wait()


def tail_body(plan, count, meta, weight, *refs):
    number = 1 + max(at for _, parts in plan for at, _ in parts)
    ids, kept, arrived = refs[number : number + 3]
    out, combined, gate_grads, token, store, sums, sems, sum_sems = refs[-8:]
    copies = send_inside(plan, meta, weight, refs[:number], out, store, sems)
    width, part = combined.shape[1], sums.shape[2]
    for at in range(sums.shape[0]):
        columns = slice(at * part, (at + 1) * part)
        sums[at] = (kept[:, columns] + arrived[:, columns].astype(F32)).astype(BF16)
        copies.append(pltpu.make_async_copy(sums.at[at], combined.at[:, columns], sum_sems.at[at]))
        copies[-1].start()
    pieces = (kept[:, width:] + arrived[:, width:].astype(F32)).T
    inner = pieces[:count] + pieces[count : 2 * count] + pieces[2 * count : 3 * count]
    named = ids[...]
    found = jnp.zeros(gate_grads.shape, F32)
    for expert in range(count):
        found = found + jnp.where(named == expert, inner[expert : expert + 1, :], 0.0)
    gate_grads[...] = found
    token[...] = jnp.zeros(token.shape, F32)
    for copy in copies:
        copy.wait()


def weight_grad_body(plan, number, has_earlier, half, meta, turned, *refs):
    rows, (other, own, token) = refs[:number], refs[-3:]
    length, tile = turned.shape[2], own.shape[1] // half
    for side, out in enumerate((other, own)):
        for at in range(half):
            columns = slice(at * tile, (at + 1) * tile)
            value = refs[number + side][:, columns] if has_earlier else jnp.zeros((turned.shape[1], tile), F32)
            for peer, parts in plan:
                operand, start = parts[side]
                part = rows[operand][start : start + length, columns]
                value = value + jnp.dot(turned[peer], part, preferred_element_type=F32)
            out[:, columns] = value.astype(out.dtype)
    token[...] = jnp.zeros(token.shape, F32)


def last_body(half, meta, turned, rows, turned_other, rows_other, earlier, earlier_other, done, grads, store, sems):
    tile = store.shape[2]
    copies = []
    for at in range(half):
        columns = slice(at * tile, (at + 1) * tile)
        value = jnp.dot(turned[...], rows[:, columns], preferred_element_type=F32)
        value = value + jnp.dot(turned_other[...], rows_other[:, columns], preferred_element_type=F32)
        store[at] = (value + earlier[:, columns] + earlier_other[:, columns].astype(F32)).astype(BF16)
        copies.append(pltpu.make_async_copy(store.at[at], grads.at[:, columns], sems.at[at]))
        copies[-1].start()
    for copy in copies:
        copy.wait()


def per_device(expert_ids, gates, hidden, weight, out_grad):
    count = lax.axis_size("expert")
    peers = 1 << ((count.bit_length() - 1) // 2)
    planes = count // peers
    tokens, top = expert_ids.shape
    cap = hidden.shape[1] // count
    width, inside = out_grad.shape[1], hidden.shape[2]
    fold = 1
    while fold * cap % 16:
        fold *= 2
    groups = planes // fold
    group_rows, group_tokens = fold * cap, fold * tokens
    rows = planes * cap
    tile = min(512, width // 2)
    steps = width // tile
    half = steps // 2
    large = width // 2
    room = 1 if fold == 1 else 3
    last = peers - 1
    anywhere = pl.BlockSpec(memory_space=pl.ANY)
    glance = pl.BlockSpec((16, 128), lambda *i: (0, 0))

    me = lax.axis_index("expert")
    core = lax.axis_index("dp")
    column, plane = me % peers, me // peers
    meta = jnp.stack([column, plane // fold, (plane % fold) * cap, me, core, plane, count]).astype(jnp.int32)

    def swap(value, distance):
        return lax.ppermute(value, "expert", [(e, e ^ distance) for e in range(count)])

    def exchange(value):
        return lax.ppermute(value, "dp", [(0, 1), (1, 0)])

    matrix = weight[0]
    if fold == 1:
        blocks = hidden.reshape(planes, peers, cap, inside)
    else:
        blocks = hidden.reshape(planes, peers, cap, inside).transpose(1, 0, 2, 3).reshape(1, peers, rows, inside)
    block = (blocks.shape[0], 1, blocks.shape[2], inside)

    ids_turned = expert_ids.T
    extent = -(-4 * count // 128) * 128
    short = pl.BlockSpec((top, tokens), lambda i, m: (0, 0))
    relay = peers == 4 and fold == 1 and planes * tokens <= large
    packed = call(
        pack_body, "pack", (1,),
        [short, short, pl.BlockSpec((tokens, width), lambda i, m: (0, 0))],
        pl.BlockSpec((tokens, width + extent), lambda i, m: (0, 0)),
        jax.ShapeDtypeStruct((tokens, width + extent), BF16),
        meta, (ids_turned, gates.T, out_grad),
        room=room,
    )
    gathered = [packed]
    for k in range(1, planes):
        if k & (k - 1) == 0:
            gathered.append(swap(packed, peers * k))
        else:
            gathered.append(None)

    def forward(peer, after):
        return call(
            lambda meta, *refs: forward_body(meta, refs[0], refs[1], refs[-1]), f"forward{peer}", (steps,),
            [
                pl.BlockSpec(block, lambda i, m: (0, lax.bitwise_xor(m[0], peer), 0, 0)),
                pl.BlockSpec((inside, tile), lambda i, m: (0, i)),
            ]
            + [glance] * len(after),
            pl.BlockSpec((rows, tile), lambda i, m: (0, i)),
            jax.ShapeDtypeStruct((rows, width), BF16),
            meta, (blocks, matrix, *after),
        )

    outputs, after = {}, ()
    if relay:
        outputs[1], outputs[2] = direct(
            functools.partial(forward_first_body, (1, 2)), "forward1", [jax.ShapeDtypeStruct((rows, width), BF16)] * 2,
            meta, (blocks, matrix),
            scratch=[
                pltpu.VMEM((2, planes, cap, inside), BF16),
                pltpu.VMEM((steps, inside, tile), BF16),
                pltpu.VMEM((steps, 2, rows, tile), BF16),
                pltpu.SemaphoreType.DMA((2 + steps,)),
                pltpu.SemaphoreType.DMA((steps, 2)),
            ],
            out_specs=[anywhere, anywhere],
            places={0: anywhere, 1: anywhere}, room=3.75,
        )
        after = (outputs[2], packed)
    for peer in [peer for peer in list(range(1, peers)) + [0] if peer not in outputs]:
        outputs[peer] = forward(peer, after)
        after = (outputs[peer], packed)
    returned = [outputs[0]] + [swap(outputs[peer], peer) for peer in range(1, peers)]
    turned, hidden_last, turned_last = call(
        turn_body, "turn", (peers,),
        [pl.BlockSpec(block, lambda i, m: (0, lax.bitwise_xor(m[0], i), 0, 0)), glance],
        [pl.BlockSpec((1, inside, rows), lambda i, m: (i, 0, 0)), pl.BlockSpec((rows, inside), lambda i, m: (0, 0)),
         pl.BlockSpec((inside, rows), lambda i, m: (0, 0))],
        [
            jax.ShapeDtypeStruct((peers, inside, rows), BF16), jax.ShapeDtypeStruct((rows, inside), BF16),
            jax.ShapeDtypeStruct((inside, rows), BF16),
        ],
        meta, (blocks, outputs[0]),
    )

    turned_other = call(
        turn_other_body, "turn_other", (1,),
        [pl.BlockSpec((rows, inside), lambda i, m: (0, 0))],
        pl.BlockSpec((inside, rows), lambda i, m: (0, 0)),
        jax.ShapeDtypeStruct((inside, rows), BF16),
        meta, (exchange(hidden_last),),
    )
    for k in range(1, planes):
        lowest = k & -k
        if k != lowest:
            gathered[k] = swap(gathered[k ^ lowest], peers * lowest)
    if fold > 1:
        gathered = [jnp.concatenate(gathered[g * fold : (g + 1) * fold], 0) for g in range(groups)]

    def other_half(i, m):
        return (0, 1 - m[4])

    def own_half(i, m):
        return (0, m[4])

    def build_rows(name, plan, jobs, after, cost=COST):
        sources = [source for job in jobs for source in job]
        return call(
            functools.partial(grad_rows_body, plan, len(jobs), count, groups), name, (1,),
            [pl.BlockSpec((group_tokens, extent), table_at) for _, table_at, _ in sources]
            + [pl.BlockSpec((group_tokens, large), data_at) for _, _, data_at in sources]
            + [glance] * len(after),
            [pl.BlockSpec((len(parts) * rows, large), lambda i, m: (0, 0)) for _, parts in plan],
            [jax.ShapeDtypeStruct((len(parts) * rows, large), BF16) for _, parts in plan],
            meta, (*[value for value, _, _ in sources] * 2, *after),
            scratch=[pltpu.VMEM((extent, group_tokens), F32)],
            room=room, cost=cost,
        )

    def beside(i, m):
        return (0, width // extent)

    jobs = [[(value, beside, at) for value in gathered] for at in (other_half, own_half)]
    if relay:
        plan = ((0, (0, 1)), (1, (1,)), (2, (0,)))
        own_jobs = [[(k, 0, True) for k in range(planes)]] * 2
        made = direct(
            functools.partial(direct_rows_body, plan, own_jobs, planes, count), "own_rows",
            [jax.ShapeDtypeStruct((len(parts) * rows, large), BF16) for _, parts in plan],
            meta, gathered, scratch=[pltpu.VMEM((extent, tokens), F32)],
        )
        beside_shape = jax.ShapeDtypeStruct((planes * tokens + 16, large), BF16)
        collected = direct(
            functools.partial(collect_body, planes, count), "collect", [beside_shape] * 2, meta, gathered,
            scratch=[pltpu.VMEM((extent, tokens), F32)],
        )
        before = (outputs[0], turned_other, made[1], collected[0], *returned[1:last])
        arrival = call(
            token_body, "arrival", (1,), [glance] * len(before), glance, jax.ShapeDtypeStruct((16, 128), F32), meta, before,
        )
        near = [swap(follow(value, arrival, returned[last]), 1 << number) for number, value in enumerate(collected)]
        arrived = [
            [(made[0], 0), (made[0], 1)], [None, (swap(made[1], 1), 0)], [(swap(made[2], 2), 0), None], [None, None],
        ]
    else:
        made = build_rows("own_rows", tuple((peer, (0, 1)) for peer in range(peers)), jobs, (outputs[0],))
        arrived = [[(made[0], 0), (made[0], 1)]]
        for peer in range(1, peers):
            got = swap(made[peer], peer)
            arrived.append([(got, 0), (got, 1)])

    padded = width + -(-3 * count // 128) * 128

    def combine(chosen, dtype, after):
        first, stride = chosen[0], len(chosen) > 1 and chosen[1] - chosen[0]
        columns = width if fold == 1 else large

        def part_of(k, i, m):
            return (lax.bitwise_xor(m[1], k * stride + first), jnp.minimum(i, width // columns - 1))

        blocks_of = [gathered[group] for group in chosen]
        return call(
            functools.partial(combine_body, peers, count, len(chosen)), f"combine{first}", (len(chosen), width // columns + 1),
            [pl.BlockSpec((group_tokens, extent), lambda k, i, m: (0, width // extent))] * len(chosen)
            + [pl.BlockSpec((group_tokens, columns), lambda k, i, m: (0, jnp.minimum(i, width // columns - 1)))] * len(chosen)
            + [glance]
            + [pl.BlockSpec((group_rows, columns), part_of)] * peers,
            pl.BlockSpec((group_tokens, columns), lambda k, i, m: (k, i)),
            jax.ShapeDtypeStruct((len(chosen) * group_tokens, padded), dtype),
            meta, (*blocks_of, *blocks_of, after, *returned),
            scratch=[
                pltpu.VMEM((extent, group_tokens), F32),
                pltpu.VMEM((2 * group_tokens, peers * group_rows), BF16),
                pltpu.VMEM((peers * group_rows, group_tokens), F32),
                pltpu.VMEM((peers, group_tokens), F32),
            ],
            room=room,
        )

    def direct_combine(chosen, dtype, after):
        return direct(
            functools.partial(direct_combine_body, peers, count, cap, tuple(chosen)), f"combine{chosen[0]}",
            jax.ShapeDtypeStruct((len(chosen) * tokens, padded), dtype),
            meta, (*[gathered[k] for k in chosen], after, *returned),
            scratch=[pltpu.VMEM((extent, tokens), F32)],
        )

    if relay:
        combine = direct_combine
    if fold == 1:
        leaving = combine(range(1, planes, 2), BF16, made[0])
        combine_done = combine(range(0, planes, 2), F32, leaving)
        sums = [combine_done[k * tokens : (k + 1) * tokens] for k in range(planes // 2)]
    else:
        parts = [combine([group], F32, made[0]) for group in range(groups)]
        combine_done = parts[-1]
        sums = [parts[k // fold][k % fold * tokens : (k % fold + 1) * tokens] for k in range(planes)]
        leaving = jnp.concatenate(sums[1::2], 0).astype(BF16)
        sums = sums[0::2]
    distance = 1
    first_sums = None
    while len(sums) > 1:
        got = swap(leaving, peers * distance)
        pieces = [got[k * tokens : (k + 1) * tokens].astype(F32) for k in range(len(sums))]
        sums = [mine + piece for mine, piece in zip(sums, pieces)]
        leaving = [value.astype(BF16) for value in sums[1::2]]
        leaving = leaving[0] if len(leaving) == 1 else jnp.concatenate(leaving, 0)
        sums = sums[0::2]
        first_sums = leaving if first_sums is None else first_sums
        distance *= 2
    summed = swap(leaving, peers * distance)

    grads_shape = jax.ShapeDtypeStruct(blocks.shape, BF16)
    def rows_of(chosen):
        arrays, plan = [], []
        for peer in chosen:
            parts = []
            for value, at in arrived[peer]:
                known = [number for number, array in enumerate(arrays) if array is value]
                if not known:
                    arrays.append(value)
                parts.append((known[0] if known else len(arrays) - 1, at * rows))
            plan.append((peer, tuple(parts)))
        return arrays, tuple(plan)

    def inside_grad(chosen, earlier, after):
        arrays, plan = rows_of(chosen)
        operands = [matrix, *arrays, *after] + ([] if earlier is None else [earlier])
        return direct(
            functools.partial(inside_body, plan), f"inside{chosen[0]}",
            [grads_shape, jax.ShapeDtypeStruct((16, 128), F32)],
            meta, operands,
            out_specs=[anywhere, pl.BlockSpec(memory_space=pltpu.VMEM)],
            scratch=[
                pltpu.VMEM((len(chosen), block[0], block[2], inside), BF16),
                pltpu.SemaphoreType.DMA((len(chosen),)),
            ],
            aliases=None if earlier is None else {len(operands): 0},
            places={} if earlier is None else {len(operands) - 1: anywhere},
        )

    def weight_grad(chosen, earlier, after, kind):
        arrays, plan = rows_of(chosen)
        shape = (inside, large)
        return direct(
            functools.partial(weight_grad_body, plan, len(arrays), bool(earlier), half), f"weight_grad{chosen[0]}",
            [jax.ShapeDtypeStruct(shape, kind), jax.ShapeDtypeStruct(shape, F32), jax.ShapeDtypeStruct((16, 128), F32)],
            meta, (turned, *arrays, *earlier, *after),
        )

    hidden_grads, token = inside_grad([0], None, ())
    total_other, total_own, own_token = weight_grad([0], (), (token,), F32)

    if relay:
        plan = ((0, (0,)), (2, (0,)), (0, (1,)), (1, (1,)))
        near_jobs = [[(job, k * tokens, False) for k in range(planes)] for job in range(2)]
        made = direct(
            functools.partial(direct_rows_body, plan, near_jobs, 2, count), "near_rows",
            [jax.ShapeDtypeStruct((rows, large), BF16)] * 4,
            meta, (*near, combine_done, own_token), scratch=[pltpu.VMEM((extent, tokens), F32)], cost=NEAR_COST,
        )
        arrived[1][0], arrived[2][1] = (made[0], 0), (made[2], 0)
        arrived[3] = [(swap(made[1], 2), 0), (swap(made[3], 1), 0)]

    hidden_grads, token = inside_grad(range(1, last), hidden_grads, (made[1][:16, :128], first_sums[:16, :128]))
    total_other, total_own, _ = weight_grad(range(1, last), (total_other, total_own), (token,), BF16)
    total_other = exchange(total_other)
    last_other, last_own = arrived[last]
    rows_own = last_own[0] if relay else last_own[0][rows:]
    rows_other = last_other[0] if relay else last_other[0][:rows]

    followed = follow(rows_other, last_own[0])
    rows_other = exchange(followed)
    if relay:
        arrived[last][0] = (followed, 0)
    arrays, plan = rows_of([last])
    vmem = pl.BlockSpec(memory_space=pltpu.VMEM)
    hidden_grads, combined, gate_grads, finished = direct(
        functools.partial(tail_body, plan, count), "tail",
        [
            grads_shape, jax.ShapeDtypeStruct((tokens, width), BF16), jax.ShapeDtypeStruct((top, tokens), F32),
            jax.ShapeDtypeStruct((16, 128), F32),
        ],
        meta, (matrix, *arrays, ids_turned, sums[0], summed, hidden_grads),
        out_specs=[anywhere, anywhere, vmem, vmem],
        scratch=[
            pltpu.VMEM((1, block[0], block[2], inside), BF16), pltpu.VMEM((2, tokens, large), BF16),
            pltpu.SemaphoreType.DMA((1,)), pltpu.SemaphoreType.DMA((2,)),
        ],
        aliases={len(arrays) + 5: 0}, places={len(arrays) + 4: anywhere}, cost=LONG_COST,
    )
    weight_grads = direct(
        functools.partial(last_body, 2 * half), "last", jax.ShapeDtypeStruct((inside, large), BF16),
        meta, (turned_last, rows_own, turned_other, rows_other, total_own, total_other, finished),
        out_specs=anywhere,
        scratch=[pltpu.VMEM((2 * half, inside, tile // 2), BF16), pltpu.SemaphoreType.DMA((2 * half,))],
    )

    if fold > 1:
        hidden_grads = hidden_grads.reshape(peers, planes, cap, inside).transpose(1, 0, 2, 3)
    return combined, gate_grads.T, hidden_grads.reshape(hidden.shape), weight_grads[None]


def solution(mesh):
    placed = (
        P(("expert", "dp"), None),
        P(("expert", "dp"), None),
        P("expert", "dp", None),
        P("expert", None, None),
        P(("expert", "dp"), None),
    )
    return jax.shard_map(
        per_device,
        mesh=mesh,
        in_specs=placed,
        out_specs=(
            P(("expert", "dp"), None),
            P(("expert", "dp"), None),
            P("expert", "dp", None),
            P("expert", None, "dp"),
        ),
        check_vma=False,
    )
```

```python
import functools

import jax
import jax.numpy as jnp
from jax import lax
from jax.experimental import pallas as pl
from jax.experimental.pallas import tpu as pltpu
from jax.sharding import PartitionSpec as P

F32 = jnp.float32
BF16 = jnp.bfloat16
VMEM_BYTES = 16 * 1024 * 1024
COST = 1024
NEAR_COST = 10**10
LONG_COST = 10**11


def call(body, name, grid, in_specs, out_specs, out_shape, scalars, operands, scratch=(), aliases=None, room=1, cost=COST):
    return pl.pallas_call(
        body,
        name=name,
        grid_spec=pltpu.PrefetchScalarGridSpec(
            num_scalar_prefetch=1, grid=grid, in_specs=in_specs, out_specs=out_specs, scratch_shapes=scratch
        ),
        out_shape=out_shape,
        input_output_aliases=aliases or {},
        cost_estimate=pl.CostEstimate(flops=cost, bytes_accessed=COST, transcendentals=0),
        compiler_params=pltpu.CompilerParams(vmem_limit_bytes=room * VMEM_BYTES),
    )(scalars, *operands)


def direct(body, name, out_shape, scalars, operands, out_specs=None, scratch=(), aliases=None, places=None, room=1, cost=COST):
    places = places or {}
    vmem, smem = pl.BlockSpec(memory_space=pltpu.VMEM), pl.BlockSpec(memory_space=pltpu.SMEM)
    several = isinstance(out_shape, (list, tuple))
    return pl.pallas_call(
        body,
        name=name,
        in_specs=[smem] + [places.get(at, vmem) for at in range(len(operands))],
        out_specs=out_specs or ([vmem] * len(out_shape) if several else vmem),
        out_shape=out_shape,
        scratch_shapes=scratch,
        input_output_aliases=aliases or {},
        cost_estimate=pl.CostEstimate(flops=cost, bytes_accessed=COST, transcendentals=0),
        compiler_params=pltpu.CompilerParams(vmem_limit_bytes=int(room * VMEM_BYTES)),
    )(scalars, *operands)


def follow(value, *earlier):
    anywhere = pl.BlockSpec(memory_space=pl.ANY)
    return pl.pallas_call(
        lambda *refs: None,
        name="follow",
        grid=(1,),
        in_specs=[anywhere] + [pl.BlockSpec((16, 128), lambda i: (0, 0))] * len(earlier),
        out_specs=anywhere,
        out_shape=jax.ShapeDtypeStruct(value.shape, value.dtype),
        input_output_aliases={0: 0},
        cost_estimate=pl.CostEstimate(flops=COST, bytes_accessed=COST, transcendentals=0),
        compiler_params=pltpu.CompilerParams(vmem_limit_bytes=VMEM_BYTES),
    )(value, *earlier)


def token_body(meta, *refs):
    refs[-1][...] = jnp.zeros(refs[-1].shape, F32)


def pieces_of(value):
    high = value.astype(BF16).astype(F32)
    middle = (value - high).astype(BF16).astype(F32)
    return high, middle, value - high - middle


def pack_body(meta, ids, gates, grad, out):
    width, tokens = grad.shape[1], grad.shape[0]
    extent = out.shape[1] - width
    count = meta[6]
    expert = lax.broadcasted_iota(jnp.int32, (extent, tokens), 0)
    piece = jnp.zeros((extent, tokens), jnp.int32)
    for number in range(1, 4):
        piece = piece + jnp.where(expert >= number * count, 1, 0)
    local = expert - piece * count
    named = jnp.zeros((extent, tokens), F32)
    gate = jnp.zeros((extent, tokens), F32)
    for choice in range(ids.shape[0]):
        hit = ids[choice : choice + 1, :] == local
        named = named + jnp.where(hit, 1.0, 0.0)
        gate = gate + jnp.where(hit, gates[choice : choice + 1, :], 0.0)
    before = lax.broadcasted_iota(jnp.int32, (tokens, tokens), 0) < lax.broadcasted_iota(jnp.int32, (tokens, tokens), 1)
    earlier = jnp.dot(named.astype(BF16), jnp.where(before, 1.0, 0.0).astype(BF16), preferred_element_type=F32)
    place = jnp.where(named > 0.0, earlier + meta[2].astype(F32), -1.0)
    high, middle, low = pieces_of(gate)
    table = jnp.where(piece == 0, place, jnp.where(piece == 1, high, jnp.where(piece == 2, middle, low)))
    out[:, :width] = grad[...]
    out[:, width:] = table.T.astype(BF16)


def collect_body(number, count, meta, *refs):
    blocks, outs, table = refs[:number], refs[-3:-1], refs[-1]
    tokens, large = blocks[0].shape[0], outs[0].shape[1]
    strips = ([], [])
    for k in range(number):
        table[...] = blocks[k][:, 2 * large :].astype(F32).T
        for side, out in enumerate(outs):
            start = pl.multiple_of(lax.bitwise_xor(1 - meta[4], side) * large, large)
            out[k * tokens : (k + 1) * tokens, :] = blocks[k][:, pl.ds(start, large)]
            receiver = lax.bitwise_xor(meta[3], 1 << side)
            experts = (receiver, lax.bitwise_xor(receiver, 2 >> side))
            lines = [table[pl.ds(expert + at * count, 1), :] for expert in experts for at in range(4)]
            strips[side].append(jnp.concatenate(lines, 0))
    for strip, out in zip(strips, outs):
        if large > number * tokens:
            strip.append(jnp.zeros((8, large - number * tokens), F32))
        strip = jnp.concatenate(strip, 1)
        out[number * tokens :, :] = jnp.concatenate([strip, jnp.zeros(strip.shape, F32)], 0).astype(BF16)


def forward_body(meta, hidden, weight, out):
    rows = hidden[:, 0].reshape(out.shape[0], hidden.shape[3])
    out[...] = jnp.dot(rows, weight[...], preferred_element_type=F32).astype(BF16)


def forward_first_body(peers, meta, hidden, weight, *refs):
    outs, (rows, matrix, store, sems, out_sems) = refs[: len(peers)], refs[len(peers) :]
    tile = matrix.shape[2]
    copies = []
    for at, peer in enumerate(peers):
        part = hidden.at[:, lax.bitwise_xor(lax.bitwise_and(meta[0], 3), peer)]
        copies.append(pltpu.make_async_copy(part, rows.at[at], sems.at[at]))
    for at in range(matrix.shape[0]):
        part = weight.at[:, at * tile : (at + 1) * tile]
        copies.append(pltpu.make_async_copy(part, matrix.at[at], sems.at[len(peers) + at]))
    for copy in copies:
        copy.start()
    for copy in copies[: len(peers)]:
        copy.wait()
    length = outs[0].shape[0]
    value = rows[...].reshape(len(peers) * length, rows.shape[3])
    results = []
    for at in range(matrix.shape[0]):
        copies[len(peers) + at].wait()
        product = jnp.dot(value, matrix[at], preferred_element_type=F32).astype(BF16)
        for number, out in enumerate(outs):
            store[at, number] = product[number * length : (number + 1) * length]
            target = out.at[:, at * tile : (at + 1) * tile]
            results.append(pltpu.make_async_copy(store.at[at, number], target, out_sems.at[at, number]))
            results[-1].start()
    for copy in results:
        copy.wait()


def turn_body(meta, hidden, after, out, final, final_turned):
    value = hidden[:, 0].reshape(final.shape)
    out[0] = value.T
    final[...] = value
    final_turned[...] = value.T


def turn_other_body(meta, hidden, out):
    out[...] = hidden[...].T


def selection(table, count, expert, rows):
    lines = [table[pl.ds(expert + at * count, 1), :] for at in range(4)]
    return selection_of(lines, rows)


def selection_of(lines, rows):
    place, gate = lines[0], lines[1] + lines[2] + lines[3]
    row = lax.broadcasted_iota(jnp.int32, (rows, place.shape[1]), 0).astype(F32)
    return row == place, gate


def grad_rows_body(plan, jobs, count, groups, meta, *refs):
    number = jobs * groups
    tables, tokens, outs, table = refs[:number], refs[number : 2 * number], refs[-1 - len(plan) : -1], refs[-1]
    rows = outs[0].shape[0] // len(plan[0][1]) // groups
    for job in range(jobs):
        asked = [(out, peer, parts.index(job)) for out, (peer, parts) in zip(outs, plan) if job in parts]
        for group in range(groups):
            table[...] = tables[job * groups + group][...].astype(F32).T
            choices, row_gates = [], []
            for _, peer, _ in asked:
                match, gate = selection(table, count, lax.bitwise_xor(meta[3], peer), rows)
                choices.append(jnp.where(match, 1.0, 0.0))
                row_gates.append(jnp.sum(jnp.where(match, gate, 0.0), 1, keepdims=True))
            choice = jnp.concatenate(choices, 0).astype(BF16)
            picked = jnp.dot(choice, tokens[job * groups + group][...], preferred_element_type=F32)
            value = (picked * jnp.concatenate(row_gates, 0)).astype(BF16)
            place = pl.multiple_of(lax.bitwise_xor(meta[1], group) * rows, rows)
            for at, (out, _, part) in enumerate(asked):
                out[pl.ds(place + part * groups * rows, rows), :] = value[at * rows : (at + 1) * rows]


def direct_rows_body(plan, jobs, number, count, meta, *refs):
    arrays, outs, table = refs[:number], refs[-1 - len(plan) : -1], refs[-1]
    tokens = table.shape[1]
    large = outs[0].shape[1]
    rows = outs[0].shape[0] // len(plan[0][1]) // len(jobs[0])
    for job, sources in enumerate(jobs):
        asked = [(out, peer, parts.index(job)) for out, (peer, parts) in zip(outs, plan) if job in parts]
        for group, (operand, first, whole) in enumerate(sources):
            array, here = arrays[operand], slice(first, first + tokens)
            if whole:
                table[...] = array[here, 2 * large :].astype(F32).T
                columns = pl.ds(pl.multiple_of(lax.bitwise_xor(1 - meta[4], job) * large, large), large)
            else:
                strip = array[array.shape[0] - 16 :, group * tokens : (group + 1) * tokens].astype(F32)
                columns = slice(0, large)
            choices, row_gates = [], []
            for _, peer, _ in asked:
                if whole:
                    match, gate = selection(table, count, lax.bitwise_xor(meta[3], peer), rows)
                else:
                    top = 4 if peer else 0
                    match, gate = selection_of([strip[top + at : top + at + 1] for at in range(4)], rows)
                choices.append(jnp.where(match, 1.0, 0.0))
                row_gates.append(jnp.sum(jnp.where(match, gate, 0.0), 1, keepdims=True))
            choice = jnp.concatenate(choices, 0).astype(BF16)
            picked = jnp.dot(choice, array[here, columns], preferred_element_type=F32)
            value = (picked * jnp.concatenate(row_gates, 0)).astype(BF16)
            place = pl.multiple_of(lax.bitwise_xor(meta[1], group) * rows, rows)
            for at, (out, _, part) in enumerate(asked):
                out[pl.ds(place + part * len(sources) * rows, rows), :] = value[at * rows : (at + 1) * rows]


def direct_combine_body(peers, count, cap, chosen, meta, *refs):
    blocks, returned, (part, table) = refs[: len(chosen)], refs[len(chosen) + 1 : -2], refs[-2:]
    extent, length = table.shape
    width = returned[0].shape[1]
    chunk = min(512, width)
    for number, k in enumerate(chosen):
        here = slice(number * length, (number + 1) * length)
        table[...] = blocks[number][:, width:].astype(F32).T
        start = pl.multiple_of(lax.bitwise_xor(meta[1], k) * cap, cap)
        highs, lows, marks = [], [], []
        for peer in range(peers):
            match, gate = selection(table, count, lax.bitwise_xor(meta[3], peer), cap)
            high = gate.astype(BF16).astype(F32)
            marks.append(jnp.where(match, 1.0, 0.0))
            highs.append(jnp.where(match, high, 0.0))
            lows.append(jnp.where(match, gate - high, 0.0))
        weights = jnp.concatenate([jnp.concatenate(highs, 0).T, jnp.concatenate(lows, 0).T], 0).astype(BF16)
        products = jnp.zeros((peers * cap, length), F32)
        for at in range(0, width, chunk):
            columns = slice(at, at + chunk)
            value = jnp.concatenate([ref[pl.ds(start, cap), columns] for ref in returned], 0)
            total = jnp.dot(weights, value, preferred_element_type=F32)
            part[here, columns] = (total[:length] + total[length:]).astype(part.dtype)
            products = products + lax.dot_general(
                value, blocks[number][:, columns], (((1,), (1,)), ((), ())), preferred_element_type=F32
            )
        products = products * jnp.concatenate(marks, 0)
        inner = [jnp.sum(products[peer * cap : (peer + 1) * cap], 0, keepdims=True) for peer in range(peers)]
        beside = part.shape[1] - width
        row = lax.broadcasted_iota(jnp.int32, (beside, length), 0)
        placed = jnp.zeros((beside, length), F32)
        for peer in range(peers):
            for at, piece in enumerate(pieces_of(inner[peer])):
                placed = jnp.where(row == at * count + lax.bitwise_xor(meta[3], peer), piece, placed)
        part[here, width:] = placed.T.astype(part.dtype)


def combine_body(peers, count, number, meta, *refs):
    packed, tokens, returned = refs[:number], refs[number : 2 * number], refs[2 * number + 1 : 2 * number + 1 + peers]
    part, table, weights, marks, inner = refs[-5:]
    rows, length = returned[0].shape[0], tokens[0].shape[0]
    step, last = pl.program_id(1), pl.num_programs(1) - 1

    def chosen(options):
        value = options[0][...]
        for at in range(1, number):
            value = jnp.where(pl.program_id(0) == at, options[at][...], value)
        return value

    @pl.when(step == 0)
    def _():
        inner[...] = jnp.zeros(inner.shape, F32)
        table[...] = chosen(packed).astype(F32).T
        highs, lows = [], []
        for peer in range(peers):
            match, gate = selection(table, count, lax.bitwise_xor(meta[3], peer), rows)
            high = gate.astype(BF16).astype(F32)
            marks[pl.ds(peer * rows, rows), :] = jnp.where(match, 1.0, 0.0)
            highs.append(jnp.where(match, high, 0.0))
            lows.append(jnp.where(match, gate - high, 0.0))
        weights[:length, :] = jnp.concatenate(highs, 0).T.astype(BF16)
        weights[length:, :] = jnp.concatenate(lows, 0).T.astype(BF16)

    @pl.when(step < last)
    def _():
        value = jnp.concatenate([ref[...] for ref in returned], 0)
        chunk = min(512, value.shape[1])
        for start in range(0, value.shape[1], chunk):
            total = jnp.dot(weights[...], value[:, start : start + chunk], preferred_element_type=F32)
            part[:, start : start + chunk] = (total[:length] + total[length:]).astype(part.dtype)
        products = lax.dot_general(value, chosen(tokens), (((1,), (1,)), ((), ())), preferred_element_type=F32)
        products = products * marks[...]
        for peer in range(peers):
            inner[peer : peer + 1, :] += jnp.sum(products[peer * rows : (peer + 1) * rows], 0, keepdims=True)

    @pl.when(step == last)
    def _():
        extent = -(-3 * count // 128) * 128
        row = lax.broadcasted_iota(jnp.int32, (extent, length), 0)
        placed = jnp.zeros((extent, length), F32)
        for at, piece in enumerate(pieces_of(inner[...])):
            for peer in range(peers):
                place = at * count + lax.bitwise_xor(meta[3], peer)
                placed = jnp.where(row == place, piece[peer : peer + 1, :], placed)
        part[:, :extent] = placed.T.astype(part.dtype)


def send_inside(plan, meta, weight, rows, out, store, sems):
    shape = store.shape[1:]
    length, large = shape[0] * shape[1], weight.shape[1] // 2
    contract = (((1,), (1,)), ((), ()))
    copies = []
    for at, (peer, parts) in enumerate(plan):
        value = jnp.zeros((length, weight.shape[0]), F32)
        for half, (operand, start) in enumerate(parts):
            columns = pl.ds(pl.multiple_of(lax.bitwise_xor(1 - meta[4], half) * large, large), large)
            part = rows[operand][start : start + length, :]
            value = value + lax.dot_general(part, weight[:, columns], contract, preferred_element_type=F32)
        store[at] = value.astype(BF16).reshape(shape)
        copies.append(pltpu.make_async_copy(store.at[at], out.at[:, lax.bitwise_xor(meta[0], peer)], sems.at[at]))
        copies[-1].start()
    return copies


def inside_body(plan, meta, weight, *refs):
    number = 1 + max(at for _, parts in plan for at, _ in parts)
    out, token, store, sems = refs[-4:]
    copies = send_inside(plan, meta, weight, refs[:number], out, store, sems)
    token[...] = jnp.zeros(token.shape, F32)
    for copy in copies:
        copy.wait()


def tail_body(plan, count, meta, weight, *refs):
    number = 1 + max(at for _, parts in plan for at, _ in parts)
    ids, kept, arrived, turned, earlier = refs[number : number + 5]
    out, combined, gate_grads, total, store, sums, sems, sum_sems = refs[-8:]
    copies = send_inside(plan, meta, weight, refs[:number], out, store, sems)
    width, part = combined.shape[1], sums.shape[2]
    for at in range(sums.shape[0]):
        columns = slice(at * part, (at + 1) * part)
        sums[at] = (kept[:, columns] + arrived[:, columns].astype(F32)).astype(BF16)
        copies.append(pltpu.make_async_copy(sums.at[at], combined.at[:, columns], sum_sems.at[at]))
        copies[-1].start()
    pieces = (kept[:, width:] + arrived[:, width:].astype(F32)).T
    inner = pieces[:count] + pieces[count : 2 * count] + pieces[2 * count : 3 * count]
    named = ids[...]
    found = jnp.zeros(gate_grads.shape, F32)
    for expert in range(count):
        found = found + jnp.where(named == expert, inner[expert : expert + 1, :], 0.0)
    gate_grads[...] = found
    operand, start = plan[0][1][1]
    chunk = min(512, total.shape[1])
    for at in range(0, total.shape[1], chunk):
        columns = slice(at, at + chunk)
        part = refs[operand][start : start + turned.shape[1], columns]
        total[:, columns] = jnp.dot(turned[...], part, preferred_element_type=F32) + earlier[:, columns]
    for copy in copies:
        copy.wait()


def weight_grad_body(plan, number, has_earlier, half, meta, turned, *refs):
    rows, (other, own, token) = refs[:number], refs[-3:]
    length, tile = turned.shape[2], own.shape[1] // half
    for side, out in enumerate((other, own)):
        for at in range(half):
            columns = slice(at * tile, (at + 1) * tile)
            value = refs[number + side][:, columns] if has_earlier else jnp.zeros((turned.shape[1], tile), F32)
            for peer, parts in plan:
                operand, start = parts[side]
                part = rows[operand][start : start + length, columns]
                value = value + jnp.dot(turned[peer], part, preferred_element_type=F32)
            out[:, columns] = value.astype(out.dtype)
    token[...] = jnp.zeros(token.shape, F32)


def last_body(parts, meta, turned, rows, earlier, earlier_other, grads, store, sems):
    tile = store.shape[2]
    copies = []
    for at in range(parts):
        columns = slice(at * tile, (at + 1) * tile)
        value = jnp.dot(turned[...], rows[:, columns], preferred_element_type=F32)
        store[at] = (value + earlier[:, columns] + earlier_other[:, columns].astype(F32)).astype(BF16)
        copies.append(pltpu.make_async_copy(store.at[at], grads.at[:, columns], sems.at[at]))
        copies[-1].start()
    for copy in copies:
        copy.wait()


def per_device(expert_ids, gates, hidden, weight, out_grad):
    count = lax.axis_size("expert")
    peers = 1 << ((count.bit_length() - 1) // 2)
    planes = count // peers
    tokens, top = expert_ids.shape
    cap = hidden.shape[1] // count
    width, inside = out_grad.shape[1], hidden.shape[2]
    fold = 1
    while fold * cap % 16:
        fold *= 2
    groups = planes // fold
    group_rows, group_tokens = fold * cap, fold * tokens
    rows = planes * cap
    tile = min(512, width // 2)
    steps = width // tile
    half = steps // 2
    large = width // 2
    room = 1 if fold == 1 else 3
    last = peers - 1
    anywhere = pl.BlockSpec(memory_space=pl.ANY)
    glance = pl.BlockSpec((16, 128), lambda *i: (0, 0))

    me = lax.axis_index("expert")
    core = lax.axis_index("dp")
    column, plane = me % peers, me // peers
    meta = jnp.stack([column, plane // fold, (plane % fold) * cap, me, core, plane, count]).astype(jnp.int32)

    def swap(value, distance):
        return lax.ppermute(value, "expert", [(e, e ^ distance) for e in range(count)])

    def exchange(value):
        return lax.ppermute(value, "dp", [(0, 1), (1, 0)])

    matrix = weight[0]
    if fold == 1:
        blocks = hidden.reshape(planes, peers, cap, inside)
    else:
        blocks = hidden.reshape(planes, peers, cap, inside).transpose(1, 0, 2, 3).reshape(1, peers, rows, inside)
    block = (blocks.shape[0], 1, blocks.shape[2], inside)

    ids_turned = expert_ids.T
    extent = -(-4 * count // 128) * 128
    short = pl.BlockSpec((top, tokens), lambda i, m: (0, 0))
    relay = peers == 4 and fold == 1 and planes * tokens <= large
    packed = call(
        pack_body, "pack", (1,),
        [short, short, pl.BlockSpec((tokens, width), lambda i, m: (0, 0))],
        pl.BlockSpec((tokens, width + extent), lambda i, m: (0, 0)),
        jax.ShapeDtypeStruct((tokens, width + extent), BF16),
        meta, (ids_turned, gates.T, out_grad),
        room=room,
    )
    gathered = [packed]
    for k in range(1, planes):
        if k & (k - 1) == 0:
            gathered.append(swap(packed, peers * k))
        else:
            gathered.append(None)

    def forward(peer, after):
        return call(
            lambda meta, *refs: forward_body(meta, refs[0], refs[1], refs[-1]), f"forward{peer}", (steps,),
            [
                pl.BlockSpec(block, lambda i, m: (0, lax.bitwise_xor(m[0], peer), 0, 0)),
                pl.BlockSpec((inside, tile), lambda i, m: (0, i)),
            ]
            + [glance] * len(after),
            pl.BlockSpec((rows, tile), lambda i, m: (0, i)),
            jax.ShapeDtypeStruct((rows, width), BF16),
            meta, (blocks, matrix, *after),
        )

    outputs, after = {}, ()
    if relay:
        outputs[1], outputs[2] = direct(
            functools.partial(forward_first_body, (1, 2)), "forward1", [jax.ShapeDtypeStruct((rows, width), BF16)] * 2,
            me.astype(jnp.int32).reshape(1), (blocks, matrix),
            scratch=[
                pltpu.VMEM((2, planes, cap, inside), BF16),
                pltpu.VMEM((steps, inside, tile), BF16),
                pltpu.VMEM((steps, 2, rows, tile), BF16),
                pltpu.SemaphoreType.DMA((2 + steps,)),
                pltpu.SemaphoreType.DMA((steps, 2)),
            ],
            out_specs=[anywhere, anywhere],
            places={0: anywhere, 1: anywhere}, room=3.75,
        )
        after = (outputs[2], packed)
    for peer in [peer for peer in list(range(1, peers)) + [0] if peer not in outputs]:
        outputs[peer] = forward(peer, after)
        after = (outputs[peer], packed)
    returned = [outputs[0]] + [swap(outputs[peer], peer) for peer in range(1, peers)]
    turned, hidden_last, turned_last = call(
        turn_body, "turn", (peers,),
        [pl.BlockSpec(block, lambda i, m: (0, lax.bitwise_xor(m[0], i), 0, 0)), glance],
        [pl.BlockSpec((1, inside, rows), lambda i, m: (i, 0, 0)), pl.BlockSpec((rows, inside), lambda i, m: (0, 0)),
         pl.BlockSpec((inside, rows), lambda i, m: (0, 0))],
        [
            jax.ShapeDtypeStruct((peers, inside, rows), BF16), jax.ShapeDtypeStruct((rows, inside), BF16),
            jax.ShapeDtypeStruct((inside, rows), BF16),
        ],
        meta, (blocks, outputs[0]),
    )

    turned_other = call(
        turn_other_body, "turn_other", (1,),
        [pl.BlockSpec((rows, inside), lambda i, m: (0, 0))],
        pl.BlockSpec((inside, rows), lambda i, m: (0, 0)),
        jax.ShapeDtypeStruct((inside, rows), BF16),
        meta, (exchange(hidden_last),),
    )
    for k in range(1, planes):
        lowest = k & -k
        if k != lowest:
            gathered[k] = swap(gathered[k ^ lowest], peers * lowest)
    if fold > 1:
        gathered = [jnp.concatenate(gathered[g * fold : (g + 1) * fold], 0) for g in range(groups)]

    def other_half(i, m):
        return (0, 1 - m[4])

    def own_half(i, m):
        return (0, m[4])

    def build_rows(name, plan, jobs, after, cost=COST):
        sources = [source for job in jobs for source in job]
        return call(
            functools.partial(grad_rows_body, plan, len(jobs), count, groups), name, (1,),
            [pl.BlockSpec((group_tokens, extent), table_at) for _, table_at, _ in sources]
            + [pl.BlockSpec((group_tokens, large), data_at) for _, _, data_at in sources]
            + [glance] * len(after),
            [pl.BlockSpec((len(parts) * rows, large), lambda i, m: (0, 0)) for _, parts in plan],
            [jax.ShapeDtypeStruct((len(parts) * rows, large), BF16) for _, parts in plan],
            meta, (*[value for value, _, _ in sources] * 2, *after),
            scratch=[pltpu.VMEM((extent, group_tokens), F32)],
            room=room, cost=cost,
        )

    def beside(i, m):
        return (0, width // extent)

    jobs = [[(value, beside, at) for value in gathered] for at in (other_half, own_half)]
    if relay:
        plan = ((0, (0, 1)), (1, (1,)), (2, (0,)))
        own_jobs = [[(k, 0, True) for k in range(planes)]] * 2
        made = direct(
            functools.partial(direct_rows_body, plan, own_jobs, planes, count), "own_rows",
            [jax.ShapeDtypeStruct((len(parts) * rows, large), BF16) for _, parts in plan],
            meta, gathered, scratch=[pltpu.VMEM((extent, tokens), F32)],
        )
        beside_shape = jax.ShapeDtypeStruct((planes * tokens + 16, large), BF16)
        collected = direct(
            functools.partial(collect_body, planes, count), "collect", [beside_shape] * 2, meta, gathered,
            scratch=[pltpu.VMEM((extent, tokens), F32)],
        )
        before = (outputs[0], turned_other, made[1], collected[0], *returned[1:last])
        arrival = call(
            token_body, "arrival", (1,), [glance] * len(before), glance, jax.ShapeDtypeStruct((16, 128), F32), meta, before,
        )
        near = [swap(follow(value, arrival, returned[last]), 1 << number) for number, value in enumerate(collected)]
        arrived = [
            [(made[0], 0), (made[0], 1)], [None, (swap(made[1], 1), 0)], [(swap(made[2], 2), 0), None], [None, None],
        ]
    else:
        made = build_rows("own_rows", tuple((peer, (0, 1)) for peer in range(peers)), jobs, (outputs[0],))
        arrived = [[(made[0], 0), (made[0], 1)]]
        for peer in range(1, peers):
            got = swap(made[peer], peer)
            arrived.append([(got, 0), (got, 1)])

    padded = width + -(-3 * count // 128) * 128

    def combine(chosen, dtype, after):
        first, stride = chosen[0], len(chosen) > 1 and chosen[1] - chosen[0]
        columns = width if fold == 1 else large

        def part_of(k, i, m):
            return (lax.bitwise_xor(m[1], k * stride + first), jnp.minimum(i, width // columns - 1))

        blocks_of = [gathered[group] for group in chosen]
        return call(
            functools.partial(combine_body, peers, count, len(chosen)), f"combine{first}", (len(chosen), width // columns + 1),
            [pl.BlockSpec((group_tokens, extent), lambda k, i, m: (0, width // extent))] * len(chosen)
            + [pl.BlockSpec((group_tokens, columns), lambda k, i, m: (0, jnp.minimum(i, width // columns - 1)))] * len(chosen)
            + [glance]
            + [pl.BlockSpec((group_rows, columns), part_of)] * peers,
            pl.BlockSpec((group_tokens, columns), lambda k, i, m: (k, i)),
            jax.ShapeDtypeStruct((len(chosen) * group_tokens, padded), dtype),
            meta, (*blocks_of, *blocks_of, after, *returned),
            scratch=[
                pltpu.VMEM((extent, group_tokens), F32),
                pltpu.VMEM((2 * group_tokens, peers * group_rows), BF16),
                pltpu.VMEM((peers * group_rows, group_tokens), F32),
                pltpu.VMEM((peers, group_tokens), F32),
            ],
            room=room,
        )

    def direct_combine(chosen, dtype, after):
        return direct(
            functools.partial(direct_combine_body, peers, count, cap, tuple(chosen)), f"combine{chosen[0]}",
            jax.ShapeDtypeStruct((len(chosen) * tokens, padded), dtype),
            meta, (*[gathered[k] for k in chosen], after, *returned),
            scratch=[pltpu.VMEM((extent, tokens), F32)],
        )

    if relay:
        combine = direct_combine
    if fold == 1:
        leaving = combine(range(1, planes, 2), BF16, made[0])
        combine_done = combine(range(0, planes, 2), F32, leaving)
        sums = [combine_done[k * tokens : (k + 1) * tokens] for k in range(planes // 2)]
    else:
        parts = [combine([group], F32, made[0]) for group in range(groups)]
        combine_done = parts[-1]
        sums = [parts[k // fold][k % fold * tokens : (k % fold + 1) * tokens] for k in range(planes)]
        leaving = jnp.concatenate(sums[1::2], 0).astype(BF16)
        sums = sums[0::2]
    distance = 1
    first_sums = None
    while len(sums) > 1:
        got = swap(leaving, peers * distance)
        pieces = [got[k * tokens : (k + 1) * tokens].astype(F32) for k in range(len(sums))]
        sums = [mine + piece for mine, piece in zip(sums, pieces)]
        leaving = [value.astype(BF16) for value in sums[1::2]]
        leaving = leaving[0] if len(leaving) == 1 else jnp.concatenate(leaving, 0)
        sums = sums[0::2]
        first_sums = leaving if first_sums is None else first_sums
        distance *= 2
    summed = swap(leaving, peers * distance)

    grads_shape = jax.ShapeDtypeStruct(blocks.shape, BF16)
    def rows_of(chosen):
        arrays, plan = [], []
        for peer in chosen:
            parts = []
            for value, at in arrived[peer]:
                known = [number for number, array in enumerate(arrays) if array is value]
                if not known:
                    arrays.append(value)
                parts.append((known[0] if known else len(arrays) - 1, at * rows))
            plan.append((peer, tuple(parts)))
        return arrays, tuple(plan)

    def inside_grad(chosen, earlier, after):
        arrays, plan = rows_of(chosen)
        operands = [matrix, *arrays, *after] + ([] if earlier is None else [earlier])
        return direct(
            functools.partial(inside_body, plan), f"inside{chosen[0]}",
            [grads_shape, jax.ShapeDtypeStruct((16, 128), F32)],
            meta, operands,
            out_specs=[anywhere, pl.BlockSpec(memory_space=pltpu.VMEM)],
            scratch=[
                pltpu.VMEM((len(chosen), block[0], block[2], inside), BF16),
                pltpu.SemaphoreType.DMA((len(chosen),)),
            ],
            aliases=None if earlier is None else {len(operands): 0},
            places={} if earlier is None else {len(operands) - 1: anywhere},
        )

    def weight_grad(chosen, earlier, after, kind):
        arrays, plan = rows_of(chosen)
        shape = (inside, large)
        return direct(
            functools.partial(weight_grad_body, plan, len(arrays), bool(earlier), half), f"weight_grad{chosen[0]}",
            [jax.ShapeDtypeStruct(shape, kind), jax.ShapeDtypeStruct(shape, F32), jax.ShapeDtypeStruct((16, 128), F32)],
            meta, (turned, *arrays, *earlier, *after),
        )

    hidden_grads, token = inside_grad([0], None, ())
    total_other, total_own, own_token = weight_grad([0], (), (token,), F32)

    if relay:
        plan = ((0, (0,)), (2, (0,)), (0, (1,)), (1, (1,)))
        near_jobs = [[(job, k * tokens, False) for k in range(planes)] for job in range(2)]
        made = direct(
            functools.partial(direct_rows_body, plan, near_jobs, 2, count), "near_rows",
            [jax.ShapeDtypeStruct((rows, large), BF16)] * 4,
            meta, (*near, combine_done, own_token), scratch=[pltpu.VMEM((extent, tokens), F32)], cost=NEAR_COST,
        )
        arrived[1][0], arrived[2][1] = (made[0], 0), (made[2], 0)
        arrived[3] = [(swap(made[1], 2), 0), (swap(made[3], 1), 0)]

    hidden_grads, token = inside_grad(range(1, last), hidden_grads, (made[1][:16, :128], first_sums[:16, :128]))
    total_other, total_own, _ = weight_grad(range(1, last), (total_other, total_own), (token,), BF16)
    total_other = exchange(total_other)
    last_other, _ = arrived[last]
    rows_other = last_other[0] if relay else last_other[0][:rows]

    rows_other = exchange(rows_other)
    arrays, plan = rows_of([last])
    vmem = pl.BlockSpec(memory_space=pltpu.VMEM)
    hidden_grads, combined, gate_grads, total_own = direct(
        functools.partial(tail_body, plan, count), "tail",
        [
            grads_shape, jax.ShapeDtypeStruct((tokens, width), BF16), jax.ShapeDtypeStruct((top, tokens), F32),
            jax.ShapeDtypeStruct((inside, large), F32),
        ],
        meta, (matrix, *arrays, ids_turned, sums[0], summed, turned_last, total_own, hidden_grads),
        out_specs=[anywhere, anywhere, vmem, vmem],
        scratch=[
            pltpu.VMEM((1, block[0], block[2], inside), BF16), pltpu.VMEM((2, tokens, large), BF16),
            pltpu.SemaphoreType.DMA((1,)), pltpu.SemaphoreType.DMA((2,)),
        ],
        aliases={len(arrays) + 7: 0}, places={len(arrays) + 6: anywhere}, cost=LONG_COST,
    )
    weight_grads = direct(
        functools.partial(last_body, 2 * half), "last", jax.ShapeDtypeStruct((inside, large), BF16),
        meta, (turned_other, rows_other, total_own, total_other),
        out_specs=anywhere,
        scratch=[pltpu.VMEM((2 * half, inside, tile // 2), BF16), pltpu.SemaphoreType.DMA((2 * half,))],
    )

    if fold > 1:
        hidden_grads = hidden_grads.reshape(peers, planes, cap, inside).transpose(1, 0, 2, 3)
    return combined, gate_grads.T, hidden_grads.reshape(hidden.shape), weight_grads[None]


def solution(mesh):
    placed = (
        P(("expert", "dp"), None),
        P(("expert", "dp"), None),
        P("expert", "dp", None),
        P("expert", None, None),
        P(("expert", "dp"), None),
    )
    return jax.shard_map(
        per_device,
        mesh=mesh,
        in_specs=placed,
        out_specs=(
            P(("expert", "dp"), None),
            P(("expert", "dp"), None),
            P("expert", "dp", None),
            P("expert", None, "dp"),
        ),
        check_vma=False,
    )
```

```python
import functools

import jax
import jax.numpy as jnp
from jax import lax
from jax.experimental import pallas as pl
from jax.experimental.pallas import tpu as pltpu
from jax.sharding import PartitionSpec as P

F32 = jnp.float32
BF16 = jnp.bfloat16
VMEM_BYTES = 16 * 1024 * 1024
COST = 1024
NEAR_COST = 10**10
LONG_COST = 10**11


def call(body, name, grid, in_specs, out_specs, out_shape, scalars, operands, scratch=(), aliases=None, room=1, cost=COST):
    return pl.pallas_call(
        body,
        name=name,
        grid_spec=pltpu.PrefetchScalarGridSpec(
            num_scalar_prefetch=1, grid=grid, in_specs=in_specs, out_specs=out_specs, scratch_shapes=scratch
        ),
        out_shape=out_shape,
        input_output_aliases=aliases or {},
        cost_estimate=pl.CostEstimate(flops=cost, bytes_accessed=COST, transcendentals=0),
        compiler_params=pltpu.CompilerParams(vmem_limit_bytes=room * VMEM_BYTES),
    )(scalars, *operands)


def direct(body, name, out_shape, scalars, operands, out_specs=None, scratch=(), aliases=None, places=None, room=0.5, cost=COST):
    places = places or {}
    vmem, smem = pl.BlockSpec(memory_space=pltpu.VMEM), pl.BlockSpec(memory_space=pltpu.SMEM)
    several = isinstance(out_shape, (list, tuple))
    return pl.pallas_call(
        body,
        name=name,
        in_specs=[smem] + [places.get(at, vmem) for at in range(len(operands))],
        out_specs=out_specs or ([vmem] * len(out_shape) if several else vmem),
        out_shape=out_shape,
        scratch_shapes=scratch,
        input_output_aliases=aliases or {},
        cost_estimate=pl.CostEstimate(flops=cost, bytes_accessed=COST, transcendentals=0),
        compiler_params=pltpu.CompilerParams(vmem_limit_bytes=int(room * VMEM_BYTES)),
    )(scalars, *operands)


def follow(value, *earlier):
    anywhere = pl.BlockSpec(memory_space=pl.ANY)
    return pl.pallas_call(
        lambda *refs: None,
        name="follow",
        grid=(1,),
        in_specs=[anywhere] + [pl.BlockSpec((16, 128), lambda i: (0, 0))] * len(earlier),
        out_specs=anywhere,
        out_shape=jax.ShapeDtypeStruct(value.shape, value.dtype),
        input_output_aliases={0: 0},
        cost_estimate=pl.CostEstimate(flops=COST, bytes_accessed=COST, transcendentals=0),
        compiler_params=pltpu.CompilerParams(vmem_limit_bytes=VMEM_BYTES),
    )(value, *earlier)


def token_body(meta, *refs):
    refs[-1][...] = jnp.zeros(refs[-1].shape, F32)


def pieces_of(value):
    high = value.astype(BF16).astype(F32)
    middle = (value - high).astype(BF16).astype(F32)
    return high, middle, value - high - middle


def pack_body(meta, ids, gates, grad, out):
    width, tokens = grad.shape[1], grad.shape[0]
    extent = out.shape[1] - width
    count = meta[6]
    expert = lax.broadcasted_iota(jnp.int32, (extent, tokens), 0)
    piece = jnp.zeros((extent, tokens), jnp.int32)
    for number in range(1, 4):
        piece = piece + jnp.where(expert >= number * count, 1, 0)
    local = expert - piece * count
    named = jnp.zeros((extent, tokens), F32)
    gate = jnp.zeros((extent, tokens), F32)
    for choice in range(ids.shape[0]):
        hit = ids[choice : choice + 1, :] == local
        named = named + jnp.where(hit, 1.0, 0.0)
        gate = gate + jnp.where(hit, gates[choice : choice + 1, :], 0.0)
    before = lax.broadcasted_iota(jnp.int32, (tokens, tokens), 0) < lax.broadcasted_iota(jnp.int32, (tokens, tokens), 1)
    earlier = jnp.dot(named.astype(BF16), jnp.where(before, 1.0, 0.0).astype(BF16), preferred_element_type=F32)
    place = jnp.where(named > 0.0, earlier + meta[2].astype(F32), -1.0)
    high, middle, low = pieces_of(gate)
    table = jnp.where(piece == 0, place, jnp.where(piece == 1, high, jnp.where(piece == 2, middle, low)))
    out[:, :width] = grad[...]
    out[:, width:] = table.T.astype(BF16)


def collect_body(number, count, meta, *refs):
    blocks, outs, table = refs[:number], refs[-3:-1], refs[-1]
    tokens, large = blocks[0].shape[0], outs[0].shape[1]
    strips = ([], [])
    for k in range(number):
        table[...] = blocks[k][:, 2 * large :].astype(F32).T
        for side, out in enumerate(outs):
            start = pl.multiple_of(lax.bitwise_xor(1 - meta[4], side) * large, large)
            out[k * tokens : (k + 1) * tokens, :] = blocks[k][:, pl.ds(start, large)]
            receiver = lax.bitwise_xor(meta[3], 1 << side)
            experts = (receiver, lax.bitwise_xor(receiver, 2 >> side))
            lines = [table[pl.ds(expert + at * count, 1), :] for expert in experts for at in range(4)]
            strips[side].append(jnp.concatenate(lines, 0))
    for strip, out in zip(strips, outs):
        if large > number * tokens:
            strip.append(jnp.zeros((8, large - number * tokens), F32))
        strip = jnp.concatenate(strip, 1)
        out[number * tokens :, :] = jnp.concatenate([strip, jnp.zeros(strip.shape, F32)], 0).astype(BF16)


def forward_body(meta, hidden, weight, out):
    rows = hidden[:, 0].reshape(out.shape[0], hidden.shape[3])
    out[...] = jnp.dot(rows, weight[...], preferred_element_type=F32).astype(BF16)


def forward_first_body(peers, meta, hidden, weight, *refs):
    outs, (rows, matrix, store, sems, out_sems) = refs[: len(peers)], refs[len(peers) :]
    tile = matrix.shape[2]
    copies = []
    for at, peer in enumerate(peers):
        part = hidden.at[:, lax.bitwise_xor(lax.bitwise_and(meta[0], 3), peer)]
        copies.append(pltpu.make_async_copy(part, rows.at[at], sems.at[at]))
    for at in range(matrix.shape[0]):
        part = weight.at[:, at * tile : (at + 1) * tile]
        copies.append(pltpu.make_async_copy(part, matrix.at[at], sems.at[len(peers) + at]))
    for copy in copies:
        copy.start()
    for copy in copies[: len(peers)]:
        copy.wait()
    length = outs[0].shape[0]
    value = rows[...].reshape(len(peers) * length, rows.shape[3])
    results = []
    for at in range(matrix.shape[0]):
        copies[len(peers) + at].wait()
        product = jnp.dot(value, matrix[at], preferred_element_type=F32).astype(BF16)
        for number, out in enumerate(outs):
            store[at, number] = product[number * length : (number + 1) * length]
            target = out.at[:, at * tile : (at + 1) * tile]
            results.append(pltpu.make_async_copy(store.at[at, number], target, out_sems.at[at, number]))
            results[-1].start()
    for copy in results:
        copy.wait()


def turn_body(meta, hidden, after, out, final, final_turned):
    value = hidden[:, 0].reshape(final.shape)
    out[0] = value.T
    final[...] = value
    final_turned[...] = value.T


def turn_other_body(meta, hidden, out):
    out[...] = hidden[...].T


def selection(table, count, expert, rows):
    lines = [table[pl.ds(expert + at * count, 1), :] for at in range(4)]
    return selection_of(lines, rows)


def selection_of(lines, rows):
    place, gate = lines[0], lines[1] + lines[2] + lines[3]
    row = lax.broadcasted_iota(jnp.int32, (rows, place.shape[1]), 0).astype(F32)
    return row == place, gate


def grad_rows_body(plan, jobs, count, groups, meta, *refs):
    number = jobs * groups
    tables, tokens, outs, table = refs[:number], refs[number : 2 * number], refs[-1 - len(plan) : -1], refs[-1]
    rows = outs[0].shape[0] // len(plan[0][1]) // groups
    for job in range(jobs):
        asked = [(out, peer, parts.index(job)) for out, (peer, parts) in zip(outs, plan) if job in parts]
        for group in range(groups):
            table[...] = tables[job * groups + group][...].astype(F32).T
            choices, row_gates = [], []
            for _, peer, _ in asked:
                match, gate = selection(table, count, lax.bitwise_xor(meta[3], peer), rows)
                choices.append(jnp.where(match, 1.0, 0.0))
                row_gates.append(jnp.sum(jnp.where(match, gate, 0.0), 1, keepdims=True))
            choice = jnp.concatenate(choices, 0).astype(BF16)
            picked = jnp.dot(choice, tokens[job * groups + group][...], preferred_element_type=F32)
            value = (picked * jnp.concatenate(row_gates, 0)).astype(BF16)
            place = pl.multiple_of(lax.bitwise_xor(meta[1], group) * rows, rows)
            for at, (out, _, part) in enumerate(asked):
                out[pl.ds(place + part * groups * rows, rows), :] = value[at * rows : (at + 1) * rows]


def direct_rows_body(plan, jobs, number, count, meta, *refs):
    arrays, outs, table = refs[:number], refs[-1 - len(plan) : -1], refs[-1]
    tokens = table.shape[1]
    large = outs[0].shape[1]
    rows = outs[0].shape[0] // len(plan[0][1]) // len(jobs[0])
    for job, sources in enumerate(jobs):
        asked = [(out, peer, parts.index(job)) for out, (peer, parts) in zip(outs, plan) if job in parts]
        for group, (operand, first, whole) in enumerate(sources):
            array, here = arrays[operand], slice(first, first + tokens)
            if whole:
                table[...] = array[here, 2 * large :].astype(F32).T
                columns = pl.ds(pl.multiple_of(lax.bitwise_xor(1 - meta[4], job) * large, large), large)
            else:
                strip = array[array.shape[0] - 16 :, group * tokens : (group + 1) * tokens].astype(F32)
                columns = slice(0, large)
            choices, row_gates = [], []
            for _, peer, _ in asked:
                if whole:
                    match, gate = selection(table, count, lax.bitwise_xor(meta[3], peer), rows)
                else:
                    top = 4 if peer else 0
                    match, gate = selection_of([strip[top + at : top + at + 1] for at in range(4)], rows)
                choices.append(jnp.where(match, 1.0, 0.0))
                row_gates.append(jnp.sum(jnp.where(match, gate, 0.0), 1, keepdims=True))
            choice = jnp.concatenate(choices, 0).astype(BF16)
            picked = jnp.dot(choice, array[here, columns], preferred_element_type=F32)
            value = (picked * jnp.concatenate(row_gates, 0)).astype(BF16)
            place = pl.multiple_of(lax.bitwise_xor(meta[1], group) * rows, rows)
            for at, (out, _, part) in enumerate(asked):
                out[pl.ds(place + part * len(sources) * rows, rows), :] = value[at * rows : (at + 1) * rows]


def direct_combine_body(peers, count, cap, chosen, meta, *refs):
    blocks, returned, (part, table) = refs[: len(chosen)], refs[len(chosen) + 1 : -2], refs[-2:]
    extent, length = table.shape
    width = returned[0].shape[1]
    chunk = min(512, width)
    for number, k in enumerate(chosen):
        here = slice(number * length, (number + 1) * length)
        table[...] = blocks[number][:, width:].astype(F32).T
        start = pl.multiple_of(lax.bitwise_xor(meta[1], k) * cap, cap)
        highs, lows, marks = [], [], []
        for peer in range(peers):
            match, gate = selection(table, count, lax.bitwise_xor(meta[3], peer), cap)
            high = gate.astype(BF16).astype(F32)
            marks.append(jnp.where(match, 1.0, 0.0))
            highs.append(jnp.where(match, high, 0.0))
            lows.append(jnp.where(match, gate - high, 0.0))
        weights = jnp.concatenate([jnp.concatenate(highs, 0).T, jnp.concatenate(lows, 0).T], 0).astype(BF16)
        products = jnp.zeros((peers * cap, length), F32)
        for at in range(0, width, chunk):
            columns = slice(at, at + chunk)
            value = jnp.concatenate([ref[pl.ds(start, cap), columns] for ref in returned], 0)
            total = jnp.dot(weights, value, preferred_element_type=F32)
            part[here, columns] = (total[:length] + total[length:]).astype(part.dtype)
            products = products + lax.dot_general(
                value, blocks[number][:, columns], (((1,), (1,)), ((), ())), preferred_element_type=F32
            )
        products = products * jnp.concatenate(marks, 0)
        inner = [jnp.sum(products[peer * cap : (peer + 1) * cap], 0, keepdims=True) for peer in range(peers)]
        beside = part.shape[1] - width
        row = lax.broadcasted_iota(jnp.int32, (beside, length), 0)
        placed = jnp.zeros((beside, length), F32)
        for peer in range(peers):
            for at, piece in enumerate(pieces_of(inner[peer])):
                placed = jnp.where(row == at * count + lax.bitwise_xor(meta[3], peer), piece, placed)
        part[here, width:] = placed.T.astype(part.dtype)


def combine_body(peers, count, number, meta, *refs):
    packed, tokens, returned = refs[:number], refs[number : 2 * number], refs[2 * number + 1 : 2 * number + 1 + peers]
    part, table, weights, marks, inner = refs[-5:]
    rows, length = returned[0].shape[0], tokens[0].shape[0]
    step, last = pl.program_id(1), pl.num_programs(1) - 1

    def chosen(options):
        value = options[0][...]
        for at in range(1, number):
            value = jnp.where(pl.program_id(0) == at, options[at][...], value)
        return value

    @pl.when(step == 0)
    def _():
        inner[...] = jnp.zeros(inner.shape, F32)
        table[...] = chosen(packed).astype(F32).T
        highs, lows = [], []
        for peer in range(peers):
            match, gate = selection(table, count, lax.bitwise_xor(meta[3], peer), rows)
            high = gate.astype(BF16).astype(F32)
            marks[pl.ds(peer * rows, rows), :] = jnp.where(match, 1.0, 0.0)
            highs.append(jnp.where(match, high, 0.0))
            lows.append(jnp.where(match, gate - high, 0.0))
        weights[:length, :] = jnp.concatenate(highs, 0).T.astype(BF16)
        weights[length:, :] = jnp.concatenate(lows, 0).T.astype(BF16)

    @pl.when(step < last)
    def _():
        value = jnp.concatenate([ref[...] for ref in returned], 0)
        chunk = min(512, value.shape[1])
        for start in range(0, value.shape[1], chunk):
            total = jnp.dot(weights[...], value[:, start : start + chunk], preferred_element_type=F32)
            part[:, start : start + chunk] = (total[:length] + total[length:]).astype(part.dtype)
        products = lax.dot_general(value, chosen(tokens), (((1,), (1,)), ((), ())), preferred_element_type=F32)
        products = products * marks[...]
        for peer in range(peers):
            inner[peer : peer + 1, :] += jnp.sum(products[peer * rows : (peer + 1) * rows], 0, keepdims=True)

    @pl.when(step == last)
    def _():
        extent = -(-3 * count // 128) * 128
        row = lax.broadcasted_iota(jnp.int32, (extent, length), 0)
        placed = jnp.zeros((extent, length), F32)
        for at, piece in enumerate(pieces_of(inner[...])):
            for peer in range(peers):
                place = at * count + lax.bitwise_xor(meta[3], peer)
                placed = jnp.where(row == place, piece[peer : peer + 1, :], placed)
        part[:, :extent] = placed.T.astype(part.dtype)


def send_inside(plan, meta, weight, rows, out, store, sems):
    shape = store.shape[1:]
    length, large = shape[0] * shape[1], weight.shape[1] // 2
    contract = (((1,), (1,)), ((), ()))
    copies = []
    for at, (peer, parts) in enumerate(plan):
        value = jnp.zeros((length, weight.shape[0]), F32)
        for half, (operand, start) in enumerate(parts):
            columns = pl.ds(pl.multiple_of(lax.bitwise_xor(1 - meta[4], half) * large, large), large)
            part = rows[operand][start : start + length, :]
            value = value + lax.dot_general(part, weight[:, columns], contract, preferred_element_type=F32)
        store[at] = value.astype(BF16).reshape(shape)
        copies.append(pltpu.make_async_copy(store.at[at], out.at[:, lax.bitwise_xor(meta[0], peer)], sems.at[at]))
        copies[-1].start()
    return copies


def inside_body(plan, meta, weight, *refs):
    number = 1 + max(at for _, parts in plan for at, _ in parts)
    out, token, store, sems = refs[-4:]
    copies = send_inside(plan, meta, weight, refs[:number], out, store, sems)
    token[...] = jnp.zeros(token.shape, F32)
    for copy in copies:
        copy.wait()


def tail_body(plan, count, meta, weight, *refs):
    number = 1 + max(at for _, parts in plan for at, _ in parts)
    ids, kept, arrived, turned, earlier = refs[number : number + 5]
    out, combined, gate_grads, total, store, sums, sems, sum_sems = refs[-8:]
    copies = send_inside(plan, meta, weight, refs[:number], out, store, sems)
    width, part = combined.shape[1], sums.shape[2]
    for at in range(sums.shape[0]):
        columns = slice(at * part, (at + 1) * part)
        sums[at] = (kept[:, columns] + arrived[:, columns].astype(F32)).astype(BF16)
        copies.append(pltpu.make_async_copy(sums.at[at], combined.at[:, columns], sum_sems.at[at]))
        copies[-1].start()
    pieces = (kept[:, width:] + arrived[:, width:].astype(F32)).T
    inner = pieces[:count] + pieces[count : 2 * count] + pieces[2 * count : 3 * count]
    named = ids[...]
    found = jnp.zeros(gate_grads.shape, F32)
    for expert in range(count):
        found = found + jnp.where(named == expert, inner[expert : expert + 1, :], 0.0)
    gate_grads[...] = found
    operand, start = plan[0][1][1]
    chunk = min(512, total.shape[1])
    for at in range(0, total.shape[1], chunk):
        columns = slice(at, at + chunk)
        part = refs[operand][start : start + turned.shape[1], columns]
        total[:, columns] = jnp.dot(turned[...], part, preferred_element_type=F32) + earlier[:, columns]
    for copy in copies:
        copy.wait()


def weight_grad_body(plan, number, has_earlier, half, meta, turned, *refs):
    rows, (other, own, token) = refs[:number], refs[-3:]
    length, tile = turned.shape[2], own.shape[1] // half
    for side, out in enumerate((other, own)):
        for at in range(half):
            columns = slice(at * tile, (at + 1) * tile)
            value = refs[number + side][:, columns] if has_earlier else jnp.zeros((turned.shape[1], tile), F32)
            for peer, parts in plan:
                operand, start = parts[side]
                part = rows[operand][start : start + length, columns]
                value = value + jnp.dot(turned[peer], part, preferred_element_type=F32)
            out[:, columns] = value.astype(out.dtype)
    token[...] = jnp.zeros(token.shape, F32)


def last_body(parts, meta, turned, rows, earlier, earlier_other, grads, store, sems):
    tile = store.shape[2]
    copies = []
    for at in range(parts):
        columns = slice(at * tile, (at + 1) * tile)
        value = jnp.dot(turned[...], rows[:, columns], preferred_element_type=F32)
        store[at] = (value + earlier[:, columns] + earlier_other[:, columns].astype(F32)).astype(BF16)
        copies.append(pltpu.make_async_copy(store.at[at], grads.at[:, columns], sems.at[at]))
        copies[-1].start()
    for copy in copies:
        copy.wait()


def per_device(expert_ids, gates, hidden, weight, out_grad):
    count = lax.axis_size("expert")
    peers = 1 << ((count.bit_length() - 1) // 2)
    planes = count // peers
    tokens, top = expert_ids.shape
    cap = hidden.shape[1] // count
    width, inside = out_grad.shape[1], hidden.shape[2]
    fold = 1
    while fold * cap % 16:
        fold *= 2
    groups = planes // fold
    group_rows, group_tokens = fold * cap, fold * tokens
    rows = planes * cap
    tile = min(512, width // 2)
    steps = width // tile
    half = steps // 2
    large = width // 2
    room = 1 if fold == 1 else 3
    last = peers - 1
    anywhere = pl.BlockSpec(memory_space=pl.ANY)
    glance = pl.BlockSpec((16, 128), lambda *i: (0, 0))

    me = lax.axis_index("expert")
    core = lax.axis_index("dp")
    column, plane = me % peers, me // peers
    meta = jnp.stack([column, plane // fold, (plane % fold) * cap, me, core, plane, count]).astype(jnp.int32)

    def swap(value, distance):
        return lax.ppermute(value, "expert", [(e, e ^ distance) for e in range(count)])

    def exchange(value):
        return lax.ppermute(value, "dp", [(0, 1), (1, 0)])

    matrix = weight[0]
    if fold == 1:
        blocks = hidden.reshape(planes, peers, cap, inside)
    else:
        blocks = hidden.reshape(planes, peers, cap, inside).transpose(1, 0, 2, 3).reshape(1, peers, rows, inside)
    block = (blocks.shape[0], 1, blocks.shape[2], inside)

    ids_turned = expert_ids.T
    extent = -(-4 * count // 128) * 128
    short = pl.BlockSpec((top, tokens), lambda i, m: (0, 0))
    relay = peers == 4 and fold == 1 and planes * tokens <= large
    packed = call(
        pack_body, "pack", (1,),
        [short, short, pl.BlockSpec((tokens, width), lambda i, m: (0, 0))],
        pl.BlockSpec((tokens, width + extent), lambda i, m: (0, 0)),
        jax.ShapeDtypeStruct((tokens, width + extent), BF16),
        meta, (ids_turned, gates.T, out_grad),
        room=room,
    )
    gathered = [packed]
    for k in range(1, planes):
        if k & (k - 1) == 0:
            gathered.append(swap(packed, peers * k))
        else:
            gathered.append(None)

    def forward(peer, after):
        return call(
            lambda meta, *refs: forward_body(meta, refs[0], refs[1], refs[-1]), f"forward{peer}", (steps,),
            [
                pl.BlockSpec(block, lambda i, m: (0, lax.bitwise_xor(m[0], peer), 0, 0)),
                pl.BlockSpec((inside, tile), lambda i, m: (0, i)),
            ]
            + [glance] * len(after),
            pl.BlockSpec((rows, tile), lambda i, m: (0, i)),
            jax.ShapeDtypeStruct((rows, width), BF16),
            meta, (blocks, matrix, *after),
        )

    outputs, after = {}, ()
    if relay:
        outputs[1], outputs[2] = direct(
            functools.partial(forward_first_body, (1, 2)), "forward1", [jax.ShapeDtypeStruct((rows, width), BF16)] * 2,
            me.astype(jnp.int32).reshape(1), (blocks, matrix),
            scratch=[
                pltpu.VMEM((2, planes, cap, inside), BF16),
                pltpu.VMEM((steps, inside, tile), BF16),
                pltpu.VMEM((steps, 2, rows, tile), BF16),
                pltpu.SemaphoreType.DMA((2 + steps,)),
                pltpu.SemaphoreType.DMA((steps, 2)),
            ],
            out_specs=[anywhere, anywhere],
            places={0: anywhere, 1: anywhere}, room=3.75,
        )
        after = (outputs[2], packed)
    for peer in [peer for peer in list(range(1, peers)) + [0] if peer not in outputs]:
        outputs[peer] = forward(peer, after)
        after = (outputs[peer], packed)
    returned = [outputs[0]] + [swap(outputs[peer], peer) for peer in range(1, peers)]
    turned, hidden_last, turned_last = call(
        turn_body, "turn", (peers,),
        [pl.BlockSpec(block, lambda i, m: (0, lax.bitwise_xor(m[0], i), 0, 0)), glance],
        [pl.BlockSpec((1, inside, rows), lambda i, m: (i, 0, 0)), pl.BlockSpec((rows, inside), lambda i, m: (0, 0)),
         pl.BlockSpec((inside, rows), lambda i, m: (0, 0))],
        [
            jax.ShapeDtypeStruct((peers, inside, rows), BF16), jax.ShapeDtypeStruct((rows, inside), BF16),
            jax.ShapeDtypeStruct((inside, rows), BF16),
        ],
        meta, (blocks, outputs[0]),
    )

    turned_other = call(
        turn_other_body, "turn_other", (1,),
        [pl.BlockSpec((rows, inside), lambda i, m: (0, 0))],
        pl.BlockSpec((inside, rows), lambda i, m: (0, 0)),
        jax.ShapeDtypeStruct((inside, rows), BF16),
        meta, (exchange(hidden_last),),
    )
    for k in range(1, planes):
        lowest = k & -k
        if k != lowest:
            gathered[k] = swap(gathered[k ^ lowest], peers * lowest)
    if fold > 1:
        gathered = [jnp.concatenate(gathered[g * fold : (g + 1) * fold], 0) for g in range(groups)]

    def other_half(i, m):
        return (0, 1 - m[4])

    def own_half(i, m):
        return (0, m[4])

    def build_rows(name, plan, jobs, after, cost=COST):
        sources = [source for job in jobs for source in job]
        return call(
            functools.partial(grad_rows_body, plan, len(jobs), count, groups), name, (1,),
            [pl.BlockSpec((group_tokens, extent), table_at) for _, table_at, _ in sources]
            + [pl.BlockSpec((group_tokens, large), data_at) for _, _, data_at in sources]
            + [glance] * len(after),
            [pl.BlockSpec((len(parts) * rows, large), lambda i, m: (0, 0)) for _, parts in plan],
            [jax.ShapeDtypeStruct((len(parts) * rows, large), BF16) for _, parts in plan],
            meta, (*[value for value, _, _ in sources] * 2, *after),
            scratch=[pltpu.VMEM((extent, group_tokens), F32)],
            room=room, cost=cost,
        )

    def beside(i, m):
        return (0, width // extent)

    jobs = [[(value, beside, at) for value in gathered] for at in (other_half, own_half)]
    if relay:
        plan = ((0, (0, 1)), (1, (1,)), (2, (0,)))
        own_jobs = [[(k, 0, True) for k in range(planes)]] * 2
        made = direct(
            functools.partial(direct_rows_body, plan, own_jobs, planes, count), "own_rows",
            [jax.ShapeDtypeStruct((len(parts) * rows, large), BF16) for _, parts in plan],
            meta, gathered, scratch=[pltpu.VMEM((extent, tokens), F32)],
        )
        beside_shape = jax.ShapeDtypeStruct((planes * tokens + 16, large), BF16)
        collected = direct(
            functools.partial(collect_body, planes, count), "collect", [beside_shape] * 2, meta, gathered,
            scratch=[pltpu.VMEM((extent, tokens), F32)],
        )
        before = (outputs[0], turned_other, made[1], collected[0], *returned[1:last])
        arrival = call(
            token_body, "arrival", (1,), [glance] * len(before), glance, jax.ShapeDtypeStruct((16, 128), F32), meta, before,
        )
        near = [swap(follow(value, arrival, returned[last]), 1 << number) for number, value in enumerate(collected)]
        arrived = [
            [(made[0], 0), (made[0], 1)], [None, (swap(made[1], 1), 0)], [(swap(made[2], 2), 0), None], [None, None],
        ]
    else:
        made = build_rows("own_rows", tuple((peer, (0, 1)) for peer in range(peers)), jobs, (outputs[0],))
        arrived = [[(made[0], 0), (made[0], 1)]]
        for peer in range(1, peers):
            got = swap(made[peer], peer)
            arrived.append([(got, 0), (got, 1)])

    padded = width + -(-3 * count // 128) * 128

    def combine(chosen, dtype, after):
        first, stride = chosen[0], len(chosen) > 1 and chosen[1] - chosen[0]
        columns = width if fold == 1 else large

        def part_of(k, i, m):
            return (lax.bitwise_xor(m[1], k * stride + first), jnp.minimum(i, width // columns - 1))

        blocks_of = [gathered[group] for group in chosen]
        return call(
            functools.partial(combine_body, peers, count, len(chosen)), f"combine{first}", (len(chosen), width // columns + 1),
            [pl.BlockSpec((group_tokens, extent), lambda k, i, m: (0, width // extent))] * len(chosen)
            + [pl.BlockSpec((group_tokens, columns), lambda k, i, m: (0, jnp.minimum(i, width // columns - 1)))] * len(chosen)
            + [glance]
            + [pl.BlockSpec((group_rows, columns), part_of)] * peers,
            pl.BlockSpec((group_tokens, columns), lambda k, i, m: (k, i)),
            jax.ShapeDtypeStruct((len(chosen) * group_tokens, padded), dtype),
            meta, (*blocks_of, *blocks_of, after, *returned),
            scratch=[
                pltpu.VMEM((extent, group_tokens), F32),
                pltpu.VMEM((2 * group_tokens, peers * group_rows), BF16),
                pltpu.VMEM((peers * group_rows, group_tokens), F32),
                pltpu.VMEM((peers, group_tokens), F32),
            ],
            room=room,
        )

    def direct_combine(chosen, dtype, after):
        return direct(
            functools.partial(direct_combine_body, peers, count, cap, tuple(chosen)), f"combine{chosen[0]}",
            jax.ShapeDtypeStruct((len(chosen) * tokens, padded), dtype),
            meta, (*[gathered[k] for k in chosen], after, *returned),
            scratch=[pltpu.VMEM((extent, tokens), F32)],
        )

    if relay:
        combine = direct_combine
    if fold == 1:
        leaving = combine(range(1, planes, 2), BF16, made[0])
        combine_done = combine(range(0, planes, 2), F32, leaving)
        sums = [combine_done[k * tokens : (k + 1) * tokens] for k in range(planes // 2)]
    else:
        parts = [combine([group], F32, made[0]) for group in range(groups)]
        combine_done = parts[-1]
        sums = [parts[k // fold][k % fold * tokens : (k % fold + 1) * tokens] for k in range(planes)]
        leaving = jnp.concatenate(sums[1::2], 0).astype(BF16)
        sums = sums[0::2]
    distance = 1
    first_sums = None
    while len(sums) > 1:
        got = swap(leaving, peers * distance)
        pieces = [got[k * tokens : (k + 1) * tokens].astype(F32) for k in range(len(sums))]
        sums = [mine + piece for mine, piece in zip(sums, pieces)]
        leaving = [value.astype(BF16) for value in sums[1::2]]
        leaving = leaving[0] if len(leaving) == 1 else jnp.concatenate(leaving, 0)
        sums = sums[0::2]
        first_sums = leaving if first_sums is None else first_sums
        distance *= 2
    summed = swap(leaving, peers * distance)

    grads_shape = jax.ShapeDtypeStruct(blocks.shape, BF16)
    def rows_of(chosen):
        arrays, plan = [], []
        for peer in chosen:
            parts = []
            for value, at in arrived[peer]:
                known = [number for number, array in enumerate(arrays) if array is value]
                if not known:
                    arrays.append(value)
                parts.append((known[0] if known else len(arrays) - 1, at * rows))
            plan.append((peer, tuple(parts)))
        return arrays, tuple(plan)

    def inside_grad(chosen, earlier, after):
        arrays, plan = rows_of(chosen)
        operands = [matrix, *arrays, *after] + ([] if earlier is None else [earlier])
        return direct(
            functools.partial(inside_body, plan), f"inside{chosen[0]}",
            [grads_shape, jax.ShapeDtypeStruct((16, 128), F32)],
            meta, operands,
            out_specs=[anywhere, pl.BlockSpec(memory_space=pltpu.VMEM)],
            scratch=[
                pltpu.VMEM((len(chosen), block[0], block[2], inside), BF16),
                pltpu.SemaphoreType.DMA((len(chosen),)),
            ],
            aliases=None if earlier is None else {len(operands): 0},
            places={} if earlier is None else {len(operands) - 1: anywhere},
        )

    def weight_grad(chosen, earlier, after, kind):
        arrays, plan = rows_of(chosen)
        shape = (inside, large)
        return direct(
            functools.partial(weight_grad_body, plan, len(arrays), bool(earlier), half), f"weight_grad{chosen[0]}",
            [jax.ShapeDtypeStruct(shape, kind), jax.ShapeDtypeStruct(shape, F32), jax.ShapeDtypeStruct((16, 128), F32)],
            meta, (turned, *arrays, *earlier, *after),
        )

    hidden_grads, token = inside_grad([0], None, ())
    total_other, total_own, own_token = weight_grad([0], (), (token,), F32)

    if relay:
        plan = ((0, (0,)), (2, (0,)), (0, (1,)), (1, (1,)))
        near_jobs = [[(job, k * tokens, False) for k in range(planes)] for job in range(2)]
        made = direct(
            functools.partial(direct_rows_body, plan, near_jobs, 2, count), "near_rows",
            [jax.ShapeDtypeStruct((rows, large), BF16)] * 4,
            meta, (*near, combine_done, own_token), scratch=[pltpu.VMEM((extent, tokens), F32)], cost=NEAR_COST,
        )
        arrived[1][0], arrived[2][1] = (made[0], 0), (made[2], 0)
        arrived[3] = [(swap(made[1], 2), 0), (swap(made[3], 1), 0)]

    hidden_grads, token = inside_grad(range(1, last), hidden_grads, (made[1][:16, :128], first_sums[:16, :128]))
    total_other, total_own, _ = weight_grad(range(1, last), (total_other, total_own), (token,), BF16)
    total_other = exchange(total_other)
    last_other, _ = arrived[last]
    rows_other = last_other[0] if relay else last_other[0][:rows]

    rows_other = exchange(rows_other)
    arrays, plan = rows_of([last])
    vmem = pl.BlockSpec(memory_space=pltpu.VMEM)
    hidden_grads, combined, gate_grads, total_own = direct(
        functools.partial(tail_body, plan, count), "tail",
        [
            grads_shape, jax.ShapeDtypeStruct((tokens, width), BF16), jax.ShapeDtypeStruct((top, tokens), F32),
            jax.ShapeDtypeStruct((inside, large), F32),
        ],
        meta, (matrix, *arrays, ids_turned, sums[0], summed, turned_last, total_own, hidden_grads),
        out_specs=[anywhere, anywhere, vmem, vmem],
        scratch=[
            pltpu.VMEM((1, block[0], block[2], inside), BF16), pltpu.VMEM((2, tokens, large), BF16),
            pltpu.SemaphoreType.DMA((1,)), pltpu.SemaphoreType.DMA((2,)),
        ],
        aliases={len(arrays) + 7: 0}, places={len(arrays) + 6: anywhere}, cost=LONG_COST,
    )
    weight_grads = direct(
        functools.partial(last_body, 2 * half), "last", jax.ShapeDtypeStruct((inside, large), BF16),
        meta, (turned_other, rows_other, total_own, total_other),
        out_specs=anywhere,
        scratch=[pltpu.VMEM((2 * half, inside, tile // 2), BF16), pltpu.SemaphoreType.DMA((2 * half,))],
    )

    if fold > 1:
        hidden_grads = hidden_grads.reshape(peers, planes, cap, inside).transpose(1, 0, 2, 3)
    return combined, gate_grads.T, hidden_grads.reshape(hidden.shape), weight_grads[None]


def solution(mesh):
    placed = (
        P(("expert", "dp"), None),
        P(("expert", "dp"), None),
        P("expert", "dp", None),
        P("expert", None, None),
        P(("expert", "dp"), None),
    )
    return jax.shard_map(
        per_device,
        mesh=mesh,
        in_specs=placed,
        out_specs=(
            P(("expert", "dp"), None),
            P(("expert", "dp"), None),
            P("expert", "dp", None),
            P("expert", None, "dp"),
        ),
        check_vma=False,
    )
```

```python
import functools

import jax
import jax.numpy as jnp
from jax import lax
from jax.experimental import pallas as pl
from jax.experimental.pallas import tpu as pltpu
from jax.sharding import PartitionSpec as P

F32 = jnp.float32
BF16 = jnp.bfloat16
VMEM_BYTES = 16 * 1024 * 1024
COST = 1024
NEAR_COST = 10**10
LONG_COST = 10**11


def call(body, name, grid, in_specs, out_specs, out_shape, scalars, operands, scratch=(), aliases=None, room=1, cost=COST):
    return pl.pallas_call(
        body,
        name=name,
        grid_spec=pltpu.PrefetchScalarGridSpec(
            num_scalar_prefetch=1, grid=grid, in_specs=in_specs, out_specs=out_specs, scratch_shapes=scratch
        ),
        out_shape=out_shape,
        input_output_aliases=aliases or {},
        cost_estimate=pl.CostEstimate(flops=cost, bytes_accessed=COST, transcendentals=0),
        compiler_params=pltpu.CompilerParams(vmem_limit_bytes=room * VMEM_BYTES),
    )(scalars, *operands)


def direct(body, name, out_shape, scalars, operands, out_specs=None, scratch=(), aliases=None, places=None, room=0.5, cost=COST):
    places = places or {}
    vmem, smem = pl.BlockSpec(memory_space=pltpu.VMEM), pl.BlockSpec(memory_space=pltpu.SMEM)
    several = isinstance(out_shape, (list, tuple))
    return pl.pallas_call(
        body,
        name=name,
        in_specs=[smem] + [places.get(at, vmem) for at in range(len(operands))],
        out_specs=out_specs or ([vmem] * len(out_shape) if several else vmem),
        out_shape=out_shape,
        scratch_shapes=scratch,
        input_output_aliases=aliases or {},
        cost_estimate=pl.CostEstimate(flops=cost, bytes_accessed=COST, transcendentals=0),
        compiler_params=pltpu.CompilerParams(vmem_limit_bytes=int(room * VMEM_BYTES)),
    )(scalars, *operands)


def follow(value, *earlier):
    anywhere = pl.BlockSpec(memory_space=pl.ANY)
    return pl.pallas_call(
        lambda *refs: None,
        name="follow",
        grid=(1,),
        in_specs=[anywhere] + [pl.BlockSpec((16, 128), lambda i: (0, 0))] * len(earlier),
        out_specs=anywhere,
        out_shape=jax.ShapeDtypeStruct(value.shape, value.dtype),
        input_output_aliases={0: 0},
        cost_estimate=pl.CostEstimate(flops=COST, bytes_accessed=COST, transcendentals=0),
        compiler_params=pltpu.CompilerParams(vmem_limit_bytes=VMEM_BYTES),
    )(value, *earlier)


def token_body(meta, *refs):
    refs[-1][...] = jnp.zeros(refs[-1].shape, F32)


def pieces_of(value):
    high = value.astype(BF16).astype(F32)
    middle = (value - high).astype(BF16).astype(F32)
    return high, middle, value - high - middle


def pack_body(meta, ids, gates, grad, out):
    width, tokens = grad.shape[1], grad.shape[0]
    extent = out.shape[1] - width
    count = meta[6]
    expert = lax.broadcasted_iota(jnp.int32, (extent, tokens), 0)
    piece = jnp.zeros((extent, tokens), jnp.int32)
    for number in range(1, 4):
        piece = piece + jnp.where(expert >= number * count, 1, 0)
    local = expert - piece * count
    named = jnp.zeros((extent, tokens), F32)
    gate = jnp.zeros((extent, tokens), F32)
    for choice in range(ids.shape[0]):
        hit = ids[choice : choice + 1, :] == local
        named = named + jnp.where(hit, 1.0, 0.0)
        gate = gate + jnp.where(hit, gates[choice : choice + 1, :], 0.0)
    before = lax.broadcasted_iota(jnp.int32, (tokens, tokens), 0) < lax.broadcasted_iota(jnp.int32, (tokens, tokens), 1)
    earlier = jnp.dot(named.astype(BF16), jnp.where(before, 1.0, 0.0).astype(BF16), preferred_element_type=F32)
    place = jnp.where(named > 0.0, earlier + meta[2].astype(F32), -1.0)
    high, middle, low = pieces_of(gate)
    table = jnp.where(piece == 0, place, jnp.where(piece == 1, high, jnp.where(piece == 2, middle, low)))
    out[:, :width] = grad[...]
    out[:, width:] = table.T.astype(BF16)


def collect_body(number, count, meta, *refs):
    blocks, outs, table = refs[:number], refs[-3:-1], refs[-1]
    tokens, large = blocks[0].shape[0], outs[0].shape[1]
    strips = ([], [])
    for k in range(number):
        table[...] = blocks[k][:, 2 * large :].astype(F32).T
        for side, out in enumerate(outs):
            start = pl.multiple_of(lax.bitwise_xor(1 - meta[4], side) * large, large)
            out[k * tokens : (k + 1) * tokens, :] = blocks[k][:, pl.ds(start, large)]
            receiver = lax.bitwise_xor(meta[3], 1 << side)
            experts = (receiver, lax.bitwise_xor(receiver, 2 >> side))
            lines = [table[pl.ds(expert + at * count, 1), :] for expert in experts for at in range(4)]
            strips[side].append(jnp.concatenate(lines, 0))
    for strip, out in zip(strips, outs):
        if large > number * tokens:
            strip.append(jnp.zeros((8, large - number * tokens), F32))
        strip = jnp.concatenate(strip, 1)
        out[number * tokens :, :] = jnp.concatenate([strip, jnp.zeros(strip.shape, F32)], 0).astype(BF16)


def forward_body(meta, hidden, weight, out):
    rows = hidden[:, 0].reshape(out.shape[0], hidden.shape[3])
    out[...] = jnp.dot(rows, weight[...], preferred_element_type=F32).astype(BF16)


def forward_first_body(peers, meta, hidden, weight, *refs):
    outs, (rows, matrix, store, sems, out_sems) = refs[: len(peers)], refs[len(peers) :]
    tile = matrix.shape[2]
    copies = []
    for at, peer in enumerate(peers):
        part = hidden.at[:, lax.bitwise_xor(lax.bitwise_and(meta[0], 3), peer)]
        copies.append(pltpu.make_async_copy(part, rows.at[at], sems.at[at]))
    for at in range(matrix.shape[0]):
        part = weight.at[:, at * tile : (at + 1) * tile]
        copies.append(pltpu.make_async_copy(part, matrix.at[at], sems.at[len(peers) + at]))
    for copy in copies:
        copy.start()
    for copy in copies[: len(peers)]:
        copy.wait()
    length = outs[0].shape[0]
    value = rows[...].reshape(len(peers) * length, rows.shape[3])
    results = []
    for at in range(matrix.shape[0]):
        copies[len(peers) + at].wait()
        product = jnp.dot(value, matrix[at], preferred_element_type=F32).astype(BF16)
        for number, out in enumerate(outs):
            store[at, number] = product[number * length : (number + 1) * length]
            target = out.at[:, at * tile : (at + 1) * tile]
            results.append(pltpu.make_async_copy(store.at[at, number], target, out_sems.at[at, number]))
            results[-1].start()
    for copy in results:
        copy.wait()


def turn_body(meta, hidden, *refs):
    out, final, final_turned = refs[-3:]
    value = hidden[:, 0].reshape(final.shape)
    out[0] = value.T
    final[...] = value
    final_turned[...] = value.T


def turn_other_body(meta, hidden, out):
    out[...] = hidden[...].T


def selection(table, count, expert, rows):
    lines = [table[pl.ds(expert + at * count, 1), :] for at in range(4)]
    return selection_of(lines, rows)


def selection_of(lines, rows):
    place, gate = lines[0], lines[1] + lines[2] + lines[3]
    row = lax.broadcasted_iota(jnp.int32, (rows, place.shape[1]), 0).astype(F32)
    return row == place, gate


def grad_rows_body(plan, jobs, count, groups, meta, *refs):
    number = jobs * groups
    tables, tokens, outs, table = refs[:number], refs[number : 2 * number], refs[-1 - len(plan) : -1], refs[-1]
    rows = outs[0].shape[0] // len(plan[0][1]) // groups
    for job in range(jobs):
        asked = [(out, peer, parts.index(job)) for out, (peer, parts) in zip(outs, plan) if job in parts]
        for group in range(groups):
            table[...] = tables[job * groups + group][...].astype(F32).T
            choices, row_gates = [], []
            for _, peer, _ in asked:
                match, gate = selection(table, count, lax.bitwise_xor(meta[3], peer), rows)
                choices.append(jnp.where(match, 1.0, 0.0))
                row_gates.append(jnp.sum(jnp.where(match, gate, 0.0), 1, keepdims=True))
            choice = jnp.concatenate(choices, 0).astype(BF16)
            picked = jnp.dot(choice, tokens[job * groups + group][...], preferred_element_type=F32)
            value = (picked * jnp.concatenate(row_gates, 0)).astype(BF16)
            place = pl.multiple_of(lax.bitwise_xor(meta[1], group) * rows, rows)
            for at, (out, _, part) in enumerate(asked):
                out[pl.ds(place + part * groups * rows, rows), :] = value[at * rows : (at + 1) * rows]


def direct_rows_body(plan, jobs, number, count, meta, *refs):
    arrays, outs, table = refs[:number], refs[-1 - len(plan) : -1], refs[-1]
    tokens = table.shape[1]
    large = outs[0].shape[1]
    rows = outs[0].shape[0] // len(plan[0][1]) // len(jobs[0])
    for job, sources in enumerate(jobs):
        asked = [(out, peer, parts.index(job)) for out, (peer, parts) in zip(outs, plan) if job in parts]
        for group, (operand, first, whole) in enumerate(sources):
            array, here = arrays[operand], slice(first, first + tokens)
            if whole:
                table[...] = array[here, 2 * large :].astype(F32).T
                columns = pl.ds(pl.multiple_of(lax.bitwise_xor(1 - meta[4], job) * large, large), large)
            else:
                strip = array[array.shape[0] - 16 :, group * tokens : (group + 1) * tokens].astype(F32)
                columns = slice(0, large)
            choices, row_gates = [], []
            for _, peer, _ in asked:
                if whole:
                    match, gate = selection(table, count, lax.bitwise_xor(meta[3], peer), rows)
                else:
                    top = 4 if peer else 0
                    match, gate = selection_of([strip[top + at : top + at + 1] for at in range(4)], rows)
                choices.append(jnp.where(match, 1.0, 0.0))
                row_gates.append(jnp.sum(jnp.where(match, gate, 0.0), 1, keepdims=True))
            choice = jnp.concatenate(choices, 0).astype(BF16)
            picked = jnp.dot(choice, array[here, columns], preferred_element_type=F32)
            value = (picked * jnp.concatenate(row_gates, 0)).astype(BF16)
            place = pl.multiple_of(lax.bitwise_xor(meta[1], group) * rows, rows)
            for at, (out, _, part) in enumerate(asked):
                out[pl.ds(place + part * len(sources) * rows, rows), :] = value[at * rows : (at + 1) * rows]


def direct_combine_body(peers, count, cap, chosen, meta, *refs):
    blocks, returned, (part, table) = refs[: len(chosen)], refs[len(chosen) + 1 : -2], refs[-2:]
    extent, length = table.shape
    width = returned[0].shape[1]
    chunk = min(512, width)
    for number, k in enumerate(chosen):
        here = slice(number * length, (number + 1) * length)
        table[...] = blocks[number][:, width:].astype(F32).T
        start = pl.multiple_of(lax.bitwise_xor(meta[1], k) * cap, cap)
        highs, lows, marks = [], [], []
        for peer in range(peers):
            match, gate = selection(table, count, lax.bitwise_xor(meta[3], peer), cap)
            high = gate.astype(BF16).astype(F32)
            marks.append(jnp.where(match, 1.0, 0.0))
            highs.append(jnp.where(match, high, 0.0))
            lows.append(jnp.where(match, gate - high, 0.0))
        weights = jnp.concatenate([jnp.concatenate(highs, 0).T, jnp.concatenate(lows, 0).T], 0).astype(BF16)
        products = jnp.zeros((peers * cap, length), F32)
        for at in range(0, width, chunk):
            columns = slice(at, at + chunk)
            value = jnp.concatenate([ref[pl.ds(start, cap), columns] for ref in returned], 0)
            total = jnp.dot(weights, value, preferred_element_type=F32)
            part[here, columns] = (total[:length] + total[length:]).astype(part.dtype)
            products = products + lax.dot_general(
                value, blocks[number][:, columns], (((1,), (1,)), ((), ())), preferred_element_type=F32
            )
        products = products * jnp.concatenate(marks, 0)
        inner = [jnp.sum(products[peer * cap : (peer + 1) * cap], 0, keepdims=True) for peer in range(peers)]
        beside = part.shape[1] - width
        row = lax.broadcasted_iota(jnp.int32, (beside, length), 0)
        placed = jnp.zeros((beside, length), F32)
        for peer in range(peers):
            for at, piece in enumerate(pieces_of(inner[peer])):
                placed = jnp.where(row == at * count + lax.bitwise_xor(meta[3], peer), piece, placed)
        part[here, width:] = placed.T.astype(part.dtype)


def combine_body(peers, count, number, meta, *refs):
    packed, tokens, returned = refs[:number], refs[number : 2 * number], refs[2 * number + 1 : 2 * number + 1 + peers]
    part, table, weights, marks, inner = refs[-5:]
    rows, length = returned[0].shape[0], tokens[0].shape[0]
    step, last = pl.program_id(1), pl.num_programs(1) - 1

    def chosen(options):
        value = options[0][...]
        for at in range(1, number):
            value = jnp.where(pl.program_id(0) == at, options[at][...], value)
        return value

    @pl.when(step == 0)
    def _():
        inner[...] = jnp.zeros(inner.shape, F32)
        table[...] = chosen(packed).astype(F32).T
        highs, lows = [], []
        for peer in range(peers):
            match, gate = selection(table, count, lax.bitwise_xor(meta[3], peer), rows)
            high = gate.astype(BF16).astype(F32)
            marks[pl.ds(peer * rows, rows), :] = jnp.where(match, 1.0, 0.0)
            highs.append(jnp.where(match, high, 0.0))
            lows.append(jnp.where(match, gate - high, 0.0))
        weights[:length, :] = jnp.concatenate(highs, 0).T.astype(BF16)
        weights[length:, :] = jnp.concatenate(lows, 0).T.astype(BF16)

    @pl.when(step < last)
    def _():
        value = jnp.concatenate([ref[...] for ref in returned], 0)
        chunk = min(512, value.shape[1])
        for start in range(0, value.shape[1], chunk):
            total = jnp.dot(weights[...], value[:, start : start + chunk], preferred_element_type=F32)
            part[:, start : start + chunk] = (total[:length] + total[length:]).astype(part.dtype)
        products = lax.dot_general(value, chosen(tokens), (((1,), (1,)), ((), ())), preferred_element_type=F32)
        products = products * marks[...]
        for peer in range(peers):
            inner[peer : peer + 1, :] += jnp.sum(products[peer * rows : (peer + 1) * rows], 0, keepdims=True)

    @pl.when(step == last)
    def _():
        extent = -(-3 * count // 128) * 128
        row = lax.broadcasted_iota(jnp.int32, (extent, length), 0)
        placed = jnp.zeros((extent, length), F32)
        for at, piece in enumerate(pieces_of(inner[...])):
            for peer in range(peers):
                place = at * count + lax.bitwise_xor(meta[3], peer)
                placed = jnp.where(row == place, piece[peer : peer + 1, :], placed)
        part[:, :extent] = placed.T.astype(part.dtype)


def send_inside(plan, meta, weight, rows, out, store, sems):
    shape = store.shape[1:]
    length, large = shape[0] * shape[1], weight.shape[1] // 2
    contract = (((1,), (1,)), ((), ()))
    copies = []
    for at, (peer, parts) in enumerate(plan):
        value = jnp.zeros((length, weight.shape[0]), F32)
        for half, (operand, start) in enumerate(parts):
            columns = pl.ds(pl.multiple_of(lax.bitwise_xor(1 - meta[4], half) * large, large), large)
            part = rows[operand][start : start + length, :]
            value = value + lax.dot_general(part, weight[:, columns], contract, preferred_element_type=F32)
        store[at] = value.astype(BF16).reshape(shape)
        copies.append(pltpu.make_async_copy(store.at[at], out.at[:, lax.bitwise_xor(meta[0], peer)], sems.at[at]))
        copies[-1].start()
    return copies


def inside_body(plan, meta, weight, *refs):
    number = 1 + max(at for _, parts in plan for at, _ in parts)
    out, token, store, sems = refs[-4:]
    copies = send_inside(plan, meta, weight, refs[:number], out, store, sems)
    token[...] = jnp.zeros(token.shape, F32)
    for copy in copies:
        copy.wait()


def tail_body(plan, count, meta, weight, *refs):
    number = 1 + max(at for _, parts in plan for at, _ in parts)
    ids, kept, arrived, turned, earlier = refs[number : number + 5]
    out, combined, gate_grads, total, store, sums, sems, sum_sems = refs[-8:]
    copies = send_inside(plan, meta, weight, refs[:number], out, store, sems)
    width, part = combined.shape[1], sums.shape[2]
    for at in range(sums.shape[0]):
        columns = slice(at * part, (at + 1) * part)
        sums[at] = (kept[:, columns] + arrived[:, columns].astype(F32)).astype(BF16)
        copies.append(pltpu.make_async_copy(sums.at[at], combined.at[:, columns], sum_sems.at[at]))
        copies[-1].start()
    pieces = (kept[:, width:] + arrived[:, width:].astype(F32)).T
    inner = pieces[:count] + pieces[count : 2 * count] + pieces[2 * count : 3 * count]
    named = ids[...]
    found = jnp.zeros(gate_grads.shape, F32)
    for expert in range(count):
        found = found + jnp.where(named == expert, inner[expert : expert + 1, :], 0.0)
    gate_grads[...] = found
    operand, start = plan[0][1][1]
    chunk = min(512, total.shape[1])
    for at in range(0, total.shape[1], chunk):
        columns = slice(at, at + chunk)
        part = refs[operand][start : start + turned.shape[1], columns]
        total[:, columns] = jnp.dot(turned[...], part, preferred_element_type=F32) + earlier[:, columns]
    for copy in copies:
        copy.wait()


def weight_grad_body(plan, number, has_earlier, half, meta, turned, *refs):
    rows, (other, own, token) = refs[:number], refs[-3:]
    length, tile = turned.shape[2], own.shape[1] // half
    for side, out in enumerate((other, own)):
        for at in range(half):
            columns = slice(at * tile, (at + 1) * tile)
            value = refs[number + side][:, columns] if has_earlier else jnp.zeros((turned.shape[1], tile), F32)
            for peer, parts in plan:
                operand, start = parts[side]
                part = rows[operand][start : start + length, columns]
                value = value + jnp.dot(turned[peer], part, preferred_element_type=F32)
            out[:, columns] = value.astype(out.dtype)
    token[...] = jnp.zeros(token.shape, F32)


def last_body(parts, meta, turned, rows, earlier, earlier_other, grads, store, sems):
    tile = store.shape[2]
    copies = []
    for at in range(parts):
        columns = slice(at * tile, (at + 1) * tile)
        value = jnp.dot(turned[...], rows[:, columns], preferred_element_type=F32)
        store[at] = (value + earlier[:, columns] + earlier_other[:, columns].astype(F32)).astype(BF16)
        copies.append(pltpu.make_async_copy(store.at[at], grads.at[:, columns], sems.at[at]))
        copies[-1].start()
    for copy in copies:
        copy.wait()


def per_device(expert_ids, gates, hidden, weight, out_grad):
    count = lax.axis_size("expert")
    peers = 1 << ((count.bit_length() - 1) // 2)
    planes = count // peers
    tokens, top = expert_ids.shape
    cap = hidden.shape[1] // count
    width, inside = out_grad.shape[1], hidden.shape[2]
    fold = 1
    while fold * cap % 16:
        fold *= 2
    groups = planes // fold
    group_rows, group_tokens = fold * cap, fold * tokens
    rows = planes * cap
    tile = min(512, width // 2)
    steps = width // tile
    half = steps // 2
    large = width // 2
    room = 1 if fold == 1 else 3
    last = peers - 1
    anywhere = pl.BlockSpec(memory_space=pl.ANY)
    glance = pl.BlockSpec((16, 128), lambda *i: (0, 0))

    me = lax.axis_index("expert")
    core = lax.axis_index("dp")
    column, plane = me % peers, me // peers
    meta = jnp.stack([column, plane // fold, (plane % fold) * cap, me, core, plane, count]).astype(jnp.int32)

    def swap(value, distance):
        return lax.ppermute(value, "expert", [(e, e ^ distance) for e in range(count)])

    def exchange(value):
        return lax.ppermute(value, "dp", [(0, 1), (1, 0)])

    matrix = weight[0]
    if fold == 1:
        blocks = hidden.reshape(planes, peers, cap, inside)
    else:
        blocks = hidden.reshape(planes, peers, cap, inside).transpose(1, 0, 2, 3).reshape(1, peers, rows, inside)
    block = (blocks.shape[0], 1, blocks.shape[2], inside)

    ids_turned = expert_ids.T
    extent = -(-4 * count // 128) * 128
    short = pl.BlockSpec((top, tokens), lambda i, m: (0, 0))
    relay = peers == 4 and fold == 1 and planes * tokens <= large
    def forward(peer, after):
        return call(
            lambda meta, *refs: forward_body(meta, refs[0], refs[1], refs[-1]), f"forward{peer}", (steps,),
            [
                pl.BlockSpec(block, lambda i, m: (0, lax.bitwise_xor(m[0], peer), 0, 0)),
                pl.BlockSpec((inside, tile), lambda i, m: (0, i)),
            ]
            + [glance] * len(after),
            pl.BlockSpec((rows, tile), lambda i, m: (0, i)),
            jax.ShapeDtypeStruct((rows, width), BF16),
            meta, (blocks, matrix, *after),
        )

    outputs, after = {}, ()
    if relay:
        outputs[1], outputs[2] = direct(
            functools.partial(forward_first_body, (1, 2)), "forward1", [jax.ShapeDtypeStruct((rows, width), BF16)] * 2,
            me.astype(jnp.int32).reshape(1), (blocks, matrix),
            scratch=[
                pltpu.VMEM((2, planes, cap, inside), BF16),
                pltpu.VMEM((steps, inside, tile), BF16),
                pltpu.VMEM((steps, 2, rows, tile), BF16),
                pltpu.SemaphoreType.DMA((2 + steps,)),
                pltpu.SemaphoreType.DMA((steps, 2)),
            ],
            out_specs=[anywhere, anywhere],
            places={0: anywhere, 1: anywhere}, room=3.75,
        )
    packed = call(
        lambda meta, *refs: pack_body(meta, *refs[:3], refs[-1]), "pack", (1,),
        [short, short, pl.BlockSpec((tokens, width), lambda i, m: (0, 0))] + [glance] * relay,
        pl.BlockSpec((tokens, width + extent), lambda i, m: (0, 0)),
        jax.ShapeDtypeStruct((tokens, width + extent), BF16),
        meta, (ids_turned, gates.T, out_grad, *([outputs[2]] if relay else [])),
        room=room,
    )
    gathered = [packed]
    for k in range(1, planes):
        if k & (k - 1) == 0:
            gathered.append(swap(packed, peers * k))
        else:
            gathered.append(None)

    after = (outputs[2], packed) if relay else ()
    for peer in [peer for peer in list(range(1, peers)) + [0] if peer not in outputs]:
        outputs[peer] = forward(peer, after)
        after = (outputs[peer], packed)
    returned = [outputs[0]] + [swap(outputs[peer], peer) for peer in range(1, peers)]
    waits = gathered[1:3] if relay else [outputs[0]]
    turned, hidden_last, turned_last = call(
        turn_body, "turn", (peers,),
        [pl.BlockSpec(block, lambda i, m: (0, lax.bitwise_xor(m[0], i), 0, 0))] + [glance] * len(waits),
        [pl.BlockSpec((1, inside, rows), lambda i, m: (i, 0, 0)), pl.BlockSpec((rows, inside), lambda i, m: (0, 0)),
         pl.BlockSpec((inside, rows), lambda i, m: (0, 0))],
        [
            jax.ShapeDtypeStruct((peers, inside, rows), BF16), jax.ShapeDtypeStruct((rows, inside), BF16),
            jax.ShapeDtypeStruct((inside, rows), BF16),
        ],
        meta, (blocks, *waits),
    )

    turned_other = call(
        turn_other_body, "turn_other", (1,),
        [pl.BlockSpec((rows, inside), lambda i, m: (0, 0))],
        pl.BlockSpec((inside, rows), lambda i, m: (0, 0)),
        jax.ShapeDtypeStruct((inside, rows), BF16),
        meta, (exchange(hidden_last),),
    )
    for k in range(1, planes):
        lowest = k & -k
        if k != lowest:
            gathered[k] = swap(gathered[k ^ lowest], peers * lowest)
    if fold > 1:
        gathered = [jnp.concatenate(gathered[g * fold : (g + 1) * fold], 0) for g in range(groups)]

    def other_half(i, m):
        return (0, 1 - m[4])

    def own_half(i, m):
        return (0, m[4])

    def build_rows(name, plan, jobs, after, cost=COST):
        sources = [source for job in jobs for source in job]
        return call(
            functools.partial(grad_rows_body, plan, len(jobs), count, groups), name, (1,),
            [pl.BlockSpec((group_tokens, extent), table_at) for _, table_at, _ in sources]
            + [pl.BlockSpec((group_tokens, large), data_at) for _, _, data_at in sources]
            + [glance] * len(after),
            [pl.BlockSpec((len(parts) * rows, large), lambda i, m: (0, 0)) for _, parts in plan],
            [jax.ShapeDtypeStruct((len(parts) * rows, large), BF16) for _, parts in plan],
            meta, (*[value for value, _, _ in sources] * 2, *after),
            scratch=[pltpu.VMEM((extent, group_tokens), F32)],
            room=room, cost=cost,
        )

    def beside(i, m):
        return (0, width // extent)

    jobs = [[(value, beside, at) for value in gathered] for at in (other_half, own_half)]
    if relay:
        plan = ((0, (0, 1)), (1, (1,)), (2, (0,)))
        own_jobs = [[(k, 0, True) for k in range(planes)]] * 2
        made = direct(
            functools.partial(direct_rows_body, plan, own_jobs, planes, count), "own_rows",
            [jax.ShapeDtypeStruct((len(parts) * rows, large), BF16) for _, parts in plan],
            meta, gathered, scratch=[pltpu.VMEM((extent, tokens), F32)],
        )
        beside_shape = jax.ShapeDtypeStruct((planes * tokens + 16, large), BF16)
        collected = direct(
            functools.partial(collect_body, planes, count), "collect", [beside_shape] * 2, meta, gathered,
            scratch=[pltpu.VMEM((extent, tokens), F32)],
        )
        before = (outputs[0], turned_other, made[1], collected[0], *returned[1:last])
        arrival = call(
            token_body, "arrival", (1,), [glance] * len(before), glance, jax.ShapeDtypeStruct((16, 128), F32), meta, before,
        )
        near = [swap(follow(value, arrival, returned[last]), 1 << number) for number, value in enumerate(collected)]
        arrived = [
            [(made[0], 0), (made[0], 1)], [None, (swap(made[1], 1), 0)], [(swap(made[2], 2), 0), None], [None, None],
        ]
    else:
        made = build_rows("own_rows", tuple((peer, (0, 1)) for peer in range(peers)), jobs, (outputs[0],))
        arrived = [[(made[0], 0), (made[0], 1)]]
        for peer in range(1, peers):
            got = swap(made[peer], peer)
            arrived.append([(got, 0), (got, 1)])

    padded = width + -(-3 * count // 128) * 128

    def combine(chosen, dtype, after):
        first, stride = chosen[0], len(chosen) > 1 and chosen[1] - chosen[0]
        columns = width if fold == 1 else large

        def part_of(k, i, m):
            return (lax.bitwise_xor(m[1], k * stride + first), jnp.minimum(i, width // columns - 1))

        blocks_of = [gathered[group] for group in chosen]
        return call(
            functools.partial(combine_body, peers, count, len(chosen)), f"combine{first}", (len(chosen), width // columns + 1),
            [pl.BlockSpec((group_tokens, extent), lambda k, i, m: (0, width // extent))] * len(chosen)
            + [pl.BlockSpec((group_tokens, columns), lambda k, i, m: (0, jnp.minimum(i, width // columns - 1)))] * len(chosen)
            + [glance]
            + [pl.BlockSpec((group_rows, columns), part_of)] * peers,
            pl.BlockSpec((group_tokens, columns), lambda k, i, m: (k, i)),
            jax.ShapeDtypeStruct((len(chosen) * group_tokens, padded), dtype),
            meta, (*blocks_of, *blocks_of, after, *returned),
            scratch=[
                pltpu.VMEM((extent, group_tokens), F32),
                pltpu.VMEM((2 * group_tokens, peers * group_rows), BF16),
                pltpu.VMEM((peers * group_rows, group_tokens), F32),
                pltpu.VMEM((peers, group_tokens), F32),
            ],
            room=room,
        )

    def direct_combine(chosen, dtype, after):
        return direct(
            functools.partial(direct_combine_body, peers, count, cap, tuple(chosen)), f"combine{chosen[0]}",
            jax.ShapeDtypeStruct((len(chosen) * tokens, padded), dtype),
            meta, (*[gathered[k] for k in chosen], after, *returned),
            scratch=[pltpu.VMEM((extent, tokens), F32)],
        )

    if relay:
        combine = direct_combine
    if fold == 1:
        leaving = combine(range(1, planes, 2), BF16, made[0])
        combine_done = combine(range(0, planes, 2), F32, leaving)
        sums = [combine_done[k * tokens : (k + 1) * tokens] for k in range(planes // 2)]
    else:
        parts = [combine([group], F32, made[0]) for group in range(groups)]
        combine_done = parts[-1]
        sums = [parts[k // fold][k % fold * tokens : (k % fold + 1) * tokens] for k in range(planes)]
        leaving = jnp.concatenate(sums[1::2], 0).astype(BF16)
        sums = sums[0::2]
    distance = 1
    first_sums = None
    while len(sums) > 1:
        got = swap(leaving, peers * distance)
        pieces = [got[k * tokens : (k + 1) * tokens].astype(F32) for k in range(len(sums))]
        sums = [mine + piece for mine, piece in zip(sums, pieces)]
        leaving = [value.astype(BF16) for value in sums[1::2]]
        leaving = leaving[0] if len(leaving) == 1 else jnp.concatenate(leaving, 0)
        sums = sums[0::2]
        first_sums = leaving if first_sums is None else first_sums
        distance *= 2
    summed = swap(leaving, peers * distance)

    grads_shape = jax.ShapeDtypeStruct(blocks.shape, BF16)
    def rows_of(chosen):
        arrays, plan = [], []
        for peer in chosen:
            parts = []
            for value, at in arrived[peer]:
                known = [number for number, array in enumerate(arrays) if array is value]
                if not known:
                    arrays.append(value)
                parts.append((known[0] if known else len(arrays) - 1, at * rows))
            plan.append((peer, tuple(parts)))
        return arrays, tuple(plan)

    def inside_grad(chosen, earlier, after):
        arrays, plan = rows_of(chosen)
        operands = [matrix, *arrays, *after] + ([] if earlier is None else [earlier])
        return direct(
            functools.partial(inside_body, plan), f"inside{chosen[0]}",
            [grads_shape, jax.ShapeDtypeStruct((16, 128), F32)],
            meta, operands,
            out_specs=[anywhere, pl.BlockSpec(memory_space=pltpu.VMEM)],
            scratch=[
                pltpu.VMEM((len(chosen), block[0], block[2], inside), BF16),
                pltpu.SemaphoreType.DMA((len(chosen),)),
            ],
            aliases=None if earlier is None else {len(operands): 0},
            places={} if earlier is None else {len(operands) - 1: anywhere},
        )

    def weight_grad(chosen, earlier, after, kind):
        arrays, plan = rows_of(chosen)
        shape = (inside, large)
        return direct(
            functools.partial(weight_grad_body, plan, len(arrays), bool(earlier), half), f"weight_grad{chosen[0]}",
            [jax.ShapeDtypeStruct(shape, kind), jax.ShapeDtypeStruct(shape, F32), jax.ShapeDtypeStruct((16, 128), F32)],
            meta, (turned, *arrays, *earlier, *after),
        )

    hidden_grads, token = inside_grad([0], None, ())
    total_other, total_own, own_token = weight_grad([0], (), (token,), F32)

    if relay:
        plan = ((0, (0,)), (2, (0,)), (0, (1,)), (1, (1,)))
        near_jobs = [[(job, k * tokens, False) for k in range(planes)] for job in range(2)]
        made = direct(
            functools.partial(direct_rows_body, plan, near_jobs, 2, count), "near_rows",
            [jax.ShapeDtypeStruct((rows, large), BF16)] * 4,
            meta, (*near, combine_done, own_token), scratch=[pltpu.VMEM((extent, tokens), F32)], cost=NEAR_COST,
        )
        arrived[1][0], arrived[2][1] = (made[0], 0), (made[2], 0)
        arrived[3] = [(swap(made[1], 2), 0), (swap(made[3], 1), 0)]

    hidden_grads, token = inside_grad(range(1, last), hidden_grads, (made[1][:16, :128], first_sums[:16, :128]))
    total_other, total_own, _ = weight_grad(range(1, last), (total_other, total_own), (token,), BF16)
    total_other = exchange(total_other)
    last_other, _ = arrived[last]
    rows_other = last_other[0] if relay else last_other[0][:rows]

    rows_other = exchange(rows_other)
    arrays, plan = rows_of([last])
    vmem = pl.BlockSpec(memory_space=pltpu.VMEM)
    hidden_grads, combined, gate_grads, total_own = direct(
        functools.partial(tail_body, plan, count), "tail",
        [
            grads_shape, jax.ShapeDtypeStruct((tokens, width), BF16), jax.ShapeDtypeStruct((top, tokens), F32),
            jax.ShapeDtypeStruct((inside, large), F32),
        ],
        meta, (matrix, *arrays, ids_turned, sums[0], summed, turned_last, total_own, hidden_grads),
        out_specs=[anywhere, anywhere, vmem, vmem],
        scratch=[
            pltpu.VMEM((1, block[0], block[2], inside), BF16), pltpu.VMEM((2, tokens, large), BF16),
            pltpu.SemaphoreType.DMA((1,)), pltpu.SemaphoreType.DMA((2,)),
        ],
        aliases={len(arrays) + 7: 0}, places={len(arrays) + 6: anywhere}, cost=LONG_COST,
    )
    weight_grads = direct(
        functools.partial(last_body, 2 * half), "last", jax.ShapeDtypeStruct((inside, large), BF16),
        meta, (turned_other, rows_other, total_own, total_other),
        out_specs=anywhere,
        scratch=[pltpu.VMEM((2 * half, inside, tile // 2), BF16), pltpu.SemaphoreType.DMA((2 * half,))],
    )

    if fold > 1:
        hidden_grads = hidden_grads.reshape(peers, planes, cap, inside).transpose(1, 0, 2, 3)
    return combined, gate_grads.T, hidden_grads.reshape(hidden.shape), weight_grads[None]


def solution(mesh):
    placed = (
        P(("expert", "dp"), None),
        P(("expert", "dp"), None),
        P("expert", "dp", None),
        P("expert", None, None),
        P(("expert", "dp"), None),
    )
    return jax.shard_map(
        per_device,
        mesh=mesh,
        in_specs=placed,
        out_specs=(
            P(("expert", "dp"), None),
            P(("expert", "dp"), None),
            P("expert", "dp", None),
            P("expert", None, "dp"),
        ),
        check_vma=False,
    )
```
